32 devices in a mesh: groups: 2 (over y), frames: 16 (over z, x, core).
Axes of the slice: x: 2, y: 2, z: 4, core: 2. Of those that a mesh axis runs over, the one named last changes fastest.
Arguments:
- video_frames: bfloat16 [64, 1024, 1024], P(('groups', 'frames')), parts along dimension 0, may hold values from -6 to 6
- segments: int32 [64], P('groups'), parts along dimension 0, may hold values from 0 to 3, never falling along the last dimension, each value on 1 to 29 neighbouring positions
- ref_pick: int32 [8], P('groups'), parts along dimension 0, may hold values from 0 to 4095
- band_taps: bfloat16 [32], replicated, may hold values from -2 to 2
Outputs:
- motion: float32 [64, 256, 256], P(('groups', 'frames')), parts along dimension 0
The draws below stay inside these ranges and needn't reach their ends.
There are 2 independent parts, one for each index of `groups`. The reference program is written for one: setup_inputs(seed, part) draws one part's arguments, and reference() takes and returns one part's arrays. A program takes and returns all parts, laid end to end along the dimension named above; an argument that names none is the same for every part. Nothing has to cross between parts.
Inputs may be any that keep to these rules, and one draw needn't show every extreme that they name: Segment numbers never fall along the frames; each of the 4 segments holds 1 to 29 frames and one holds exactly 29.
All inputs are finite; a program needn't handle non-finite values.
Results may differ from the reference program's by a relative error of at most 0.012.
Values may be sent and summed in bfloat16 or wider, within the bound.
No kernel may reach another device: no remote copies, remote signals or barrier semaphores. Data moves between devices by JAX's collectives and lax.ppermute only.
A program may use at most 128 MiB of HBM per device.

```python
import math
import jax
import jax.numpy as jnp
import numpy as np
from jax import lax

IMG = 1024
ORIENT = 4
TAPS = 32
NSEG = 4
QUART = 256
FRAMES = 32
SEG_MOST = 29


def plant(values, key, least, high):
    longest = values.shape.index(max(values.shape))
    spots = []
    for shift in (0, 1):
        where = [jax.random.randint(jax.random.fold_in(key, axis), (), 0, length) for axis, length in enumerate(values.shape)]
        where[longest] = (where[longest] + shift) % values.shape[longest]
        spots.append(tuple(where))
    return values.at[spots[0]].set(least).at[spots[1]].set(high)


def block_scale(stream_key, dims, shards, low, high):
    def one(dim, parts):
        draws = jax.random.uniform(jax.random.fold_in(jax.random.fold_in(stream_key, 6), dim), (parts,), jnp.float32, low / len(shards), high / len(shards))
        return jnp.repeat(jnp.exp(draws), dims[dim] // parts).reshape((-1,) + (1,) * (len(dims) - dim - 1))

    factor_of = one(*shards[0])
    for cut in shards[1:]:
        factor_of = factor_of * one(*cut)
    return factor_of


def length_profile(number_of, total, limit, lean):
    portions = [(1 << 20) // math.isqrt(rank ** lean) + 1 for rank in range(2, number_of + 1)]
    rest, holding = total - limit - (number_of - 1), [1] * (number_of - 1)
    while rest > 0:
        free = [i for i in range(number_of - 1) if holding[i] < limit]
        mass, remaining = sum([portions[i] for i in free]), rest
        for i in free:
            more = min(limit - holding[i], max(1, remaining * portions[i] // mass), rest)
            holding[i] = holding[i] + more
            rest = rest - more
    return np.array([limit] + holding)


def ragged(rng, amount, total, reach, slope):
    if amount == 2:
        one = jax.random.randint(rng, (), max(1, total - reach), min(reach, total - 1) + 1)
        return jnp.stack([one, total - one])
    tallies = jnp.asarray(length_profile(amount, total, reach, slope), jnp.int32)
    couples = (amount - 1) // 2
    source_of, receiver = tallies[1:1 + 2 * couples:2], tallies[2:2 + 2 * couples:2]
    slack = jnp.minimum(source_of - 1, reach - receiver)
    moved = jax.random.randint(jax.random.fold_in(rng, 1), (couples,), 0, 1 << 20) % (slack + 1)
    tallies = tallies.at[1:1 + 2 * couples:2].set(source_of - moved).at[2:2 + 2 * couples:2].set(receiver + moved)
    return tallies[jax.random.permutation(jax.random.fold_in(rng, 2), amount)]


def scatter_about(stream_key, extent, width, bound, cuts=(), held_as=jnp.bfloat16):
    result = width * jax.random.normal(stream_key, extent, jnp.float32)
    if cuts:
        result = result * block_scale(stream_key, extent, cuts, -0.22, 0.18)
    return jnp.clip(result, -bound, bound).astype(held_as)


def setup_inputs(seed: int = 0, part: int = 0) -> dict:
    seeds = jax.random.split(jax.random.key(seed), 5)
    part_keys = jax.random.split(jax.random.fold_in(seeds[4], part), 5)
    return {
        "video_frames": scatter_about(part_keys[0], (FRAMES, IMG, IMG), 1.0, 6.0, ((0, 16),)),
        "segments": jnp.searchsorted(jnp.cumsum(ragged(part_keys[1], NSEG, FRAMES, SEG_MOST, 1)), jnp.arange(FRAMES), side="right").astype(jnp.int32),
        "ref_pick": plant(jax.random.randint(part_keys[2], (NSEG,), 0, 4096), jax.random.fold_in(part_keys[2], 1), 0, 4095).astype(jnp.int32),
        "band_taps": scatter_about(seeds[3], (TAPS,), 0.35, 2.0),
    }


blur_sigma = 2.0
gabor_sigma = 2.0
wave_number = math.pi / 2.0
gabor_gain = 2.0

def make_down(full_size, quarter):
    position = jnp.arange(quarter, dtype=jnp.float32)[:, None]
    columns = jnp.arange(full_size, dtype=jnp.float32)[None, :]
    offset_grid = columns - 4.0 * position - 1.5
    weight = jnp.exp(-offset_grid * offset_grid / (2.0 * blur_sigma * blur_sigma))
    return (weight / lax.optimization_barrier(jnp.sum(weight, axis=1, keepdims=True))).astype(jnp.bfloat16)

def gabor_tables(quarter, orient):
    position = jnp.arange(quarter, dtype=jnp.float32)
    offset_grid = position[None, :] - position[:, None]
    envelope = gabor_gain * jnp.exp(-offset_grid * offset_grid / (2.0 * gabor_sigma * gabor_sigma))
    angles = jnp.arange(orient, dtype=jnp.float32) * (math.pi / orient)
    wave_x = wave_number * jnp.cos(angles)
    wave_y = wave_number * jnp.sin(angles)
    phase_y = wave_y[:, None, None] * offset_grid[None]
    left_table = jnp.stack([envelope * jnp.cos(phase_y), envelope * jnp.sin(phase_y)], axis=2)
    left_table = left_table.reshape(orient * quarter * 2, quarter).astype(jnp.bfloat16)
    phase_x = wave_x[:, None, None] * (-offset_grid)[None]
    real_part = envelope * jnp.cos(phase_x)
    imag_part = envelope * jnp.sin(phase_x)
    upper_half = jnp.concatenate([real_part, imag_part], axis=2)
    lower_half = jnp.concatenate([-imag_part, real_part], axis=2)
    right_table = jnp.concatenate([upper_half, lower_half], axis=1).astype(jnp.bfloat16)
    return (left_table, right_table)

def frame_coeff(single, down_matrix, left_table, right_table):
    half_done = jnp.dot(single, down_matrix.T, preferred_element_type=jnp.float32).astype(jnp.bfloat16)
    reduced = jnp.dot(down_matrix, half_done, preferred_element_type=jnp.float32).astype(jnp.bfloat16)
    stacked = jnp.dot(left_table, reduced, preferred_element_type=jnp.float32).astype(jnp.bfloat16)
    quarter = reduced.shape[0]
    orient = right_table.shape[0]
    stacked = stacked.reshape(orient, quarter, 2 * quarter)
    return jnp.einsum('oya,oab->oyb', stacked.astype(jnp.float32), right_table.astype(jnp.float32)).astype(jnp.bfloat16)

def phase_terms(coeffs, per_frame):
    quarter = coeffs.shape[-1] // 2
    coeff_real = coeffs[..., :quarter].astype(jnp.float32)
    coeff_imag = coeffs[..., quarter:].astype(jnp.float32)
    ref_real = per_frame[..., :quarter].astype(jnp.float32)
    ref_imag = per_frame[..., quarter:].astype(jnp.float32)
    prod_real = coeff_real * ref_real + coeff_imag * ref_imag
    prod_imag = coeff_imag * ref_real - coeff_real * ref_imag
    phase_signal = (prod_imag / jnp.sqrt(prod_real * prod_real + prod_imag * prod_imag + 1.0)).astype(jnp.bfloat16)
    amplitude = coeff_real * coeff_real + coeff_imag * coeff_imag
    return (phase_signal, amplitude)

def taps_matrix(band_taps, frame_count):
    frame_index = jnp.arange(frame_count, dtype=jnp.int32)
    lag_grid = frame_index[:, None] - frame_index[None, :]
    one_hot = (lag_grid[:, :, None] == jnp.arange(band_taps.shape[0], dtype=jnp.int32)[None, None, :]).astype(jnp.float32)
    return jnp.einsum('tsk,k->ts', one_hot, band_taps.astype(jnp.float32)).astype(jnp.bfloat16)

def segment_refs(segments, ref_pick, segment_count):
    numbers = jnp.arange(segment_count, dtype=jnp.int32)
    starts = lax.optimization_barrier(jnp.sum((segments[None, :] < numbers[:, None]).astype(jnp.int32), axis=1))
    counts = lax.optimization_barrier(jnp.sum((segments[None, :] == numbers[:, None]).astype(jnp.int32), axis=1))
    return (starts + ref_pick % counts).astype(jnp.int32)

def reference(video_frames, segments, ref_pick, band_taps):
    down_matrix = make_down(IMG, QUART)
    left_table, right_table = gabor_tables(QUART, ORIENT)
    coeffs = lax.map(lambda single: frame_coeff(single, down_matrix, left_table, right_table), video_frames)
    ref_frames = segment_refs(segments, ref_pick, NSEG)
    ref_coeffs = coeffs[ref_frames]
    per_frame = ref_coeffs[segments]
    phase_signal, amplitude = phase_terms(coeffs, per_frame)
    matrix = taps_matrix(band_taps, FRAMES)
    filtered = jnp.dot(matrix, phase_signal.reshape(FRAMES, -1), preferred_element_type=jnp.float32)
    filtered = filtered.astype(jnp.bfloat16).reshape(phase_signal.shape).astype(jnp.float32)
    return lax.optimization_barrier(jnp.sum(amplitude * filtered, axis=1)) / (lax.optimization_barrier(jnp.sum(amplitude, axis=1)) + 1.0)
```

```python
import functools
import math

import jax
import jax.numpy as jnp
import numpy as np
from jax import lax
from jax.experimental import pallas as pl
from jax.experimental.pallas import tpu as pltpu
from jax.sharding import PartitionSpec as P

IMG = 1024
ORIENT = 4
NSEG = 4
QUART = 256


blur_sigma = 2.0
gabor_sigma = 2.0
wave_number = math.pi / 2.0
gabor_gain = 2.0

HALO = 32
TILE = 16
VMEM_LIMIT = 56 * 1024 * 1024


def make_down(full_size, quarter):
    position = np.arange(quarter, dtype=np.float32)[:, None]
    columns = np.arange(full_size, dtype=np.float32)[None, :]
    offset_grid = columns - np.float32(4.0) * position - np.float32(1.5)
    weight = np.exp(-offset_grid * offset_grid / np.float32(2.0 * blur_sigma * blur_sigma))
    return (weight / np.sum(weight, axis=1, keepdims=True)).astype(jnp.bfloat16)


def envelope_of(offset_grid):
    return np.float32(gabor_gain) * np.exp(
        -offset_grid * offset_grid / np.float32(2.0 * gabor_sigma * gabor_sigma)
    )


def waves(orient):
    angles = np.arange(orient, dtype=np.float32) * np.float32(math.pi / orient)
    wave_x = np.float32(wave_number) * np.cos(angles)
    wave_y = np.float32(wave_number) * np.sin(angles)
    return wave_x, wave_y


def slab_left_table(rows, halo, orient):
    offset = (
        np.arange(rows + 2 * halo, dtype=np.float32)[None, :]
        - np.float32(halo)
        - np.arange(rows, dtype=np.float32)[:, None]
    )
    wave_y = waves(orient)[1]
    phase = wave_y[:, None, None] * offset[None]
    envelope = envelope_of(offset)[None]
    table = np.stack([envelope * np.cos(phase), envelope * np.sin(phase)], axis=1)
    return table.reshape(orient * 2 * rows, rows + 2 * halo).astype(jnp.bfloat16)


def make_right_table(quarter, orient):
    position = np.arange(quarter, dtype=np.float32)
    offset = position[:, None] - position[None, :]
    wave_x = waves(orient)[0]
    phase_x = wave_x[:, None, None] * offset[None]
    envelope = envelope_of(offset)[None]
    real_part = envelope * np.cos(phase_x)
    imag_part = envelope * np.sin(phase_x)
    upper_half = np.concatenate([real_part, imag_part], axis=2)
    lower_half = np.concatenate([-imag_part, real_part], axis=2)
    return np.concatenate([upper_half, lower_half], axis=1).astype(jnp.bfloat16)


def reduce_kernel(frame_ref, down_t_ref, down_ref, out_ref, total_ref, padded_ref, *, rows, halo):
    step = pl.program_id(1)
    half = jnp.dot(frame_ref[0], down_t_ref[...], preferred_element_type=jnp.float32)
    part = jnp.dot(down_ref[...], half.astype(jnp.bfloat16), preferred_element_type=jnp.float32)

    @pl.when(step == 0)
    def _():
        total_ref[...] = part

    @pl.when(step > 0)
    def _():
        total_ref[...] += part

    @pl.when(step == pl.num_programs(1) - 1)
    def _():
        quarter = total_ref.shape[0]
        edge = jnp.zeros((halo, quarter), jnp.bfloat16)
        padded_ref[0:halo] = edge
        padded_ref[halo + quarter :] = edge
        padded_ref[halo : halo + quarter] = total_ref[...].astype(jnp.bfloat16)
        for slab in range(out_ref.shape[0]):
            out_ref[slab, 0] = padded_ref[slab * rows : slab * rows + rows + 2 * halo]


def reduce_frames(video_frames, slabs, rows, halo):
    count, size, _ = video_frames.shape
    quarter = slabs * rows
    block = quarter
    down = make_down(size, quarter)
    window = rows + 2 * halo
    return pl.pallas_call(
        functools.partial(reduce_kernel, rows=rows, halo=halo),
        grid=(count, size // block),
        in_specs=[
            pl.BlockSpec((1, block, size), lambda f, i: (f, i, 0)),
            pl.BlockSpec((size, quarter), lambda f, i: (0, 0)),
            pl.BlockSpec((quarter, block), lambda f, i: (0, i)),
        ],
        out_specs=pl.BlockSpec((slabs, 1, window, quarter), lambda f, i: (0, f, 0, 0)),
        out_shape=jax.ShapeDtypeStruct((slabs, count, window, quarter), jnp.bfloat16),
        scratch_shapes=[
            pltpu.VMEM((quarter, quarter), jnp.float32),
            pltpu.VMEM((quarter + 2 * halo, quarter), jnp.bfloat16),
        ],
        compiler_params=pltpu.CompilerParams(vmem_limit_bytes=VMEM_LIMIT),
        cost_estimate=pl.CostEstimate(
            flops=2 * count * size * quarter * (size + quarter),
            bytes_accessed=2 * count * size * size,
            transcendentals=0,
        ),
    )(video_frames, jnp.asarray(down.T.copy()), jnp.asarray(down))


def pixel_kernel(
    segments_ref, pick_ref, taps_ref, window_ref, left_ref, right_ref, out_ref,
    stacked_ref, coeff_ref, phase_ref, spread_ref, ref_frame_ref,
):
    frames, _, quarter = window_ref.shape
    rows = out_ref.shape[1]
    orient = right_ref.shape[0]
    nseg = pick_ref.shape[0]
    taps = taps_ref.shape[0]
    both = 2 * quarter

    def count_one(t, totals):
        here = segments_ref[t]
        below = [total + (here < s).astype(jnp.int32) for s, total in enumerate(totals[0])]
        same = [total + (here == s).astype(jnp.int32) for s, total in enumerate(totals[1])]
        return tuple(below), tuple(same)

    zeros = tuple(jnp.int32(0) for _ in range(nseg))
    starts, counts = lax.fori_loop(0, frames, count_one, (zeros, zeros))
    for s in range(nseg):
        ref_frame_ref[s] = starts[s] + lax.rem(pick_ref[s], counts[s])

    lag = lax.broadcasted_iota(jnp.int32, (frames, frames), 0) - lax.broadcasted_iota(
        jnp.int32, (frames, frames), 1
    )
    matrix = jnp.zeros((frames, frames), jnp.float32)
    for k in range(taps):
        matrix = jnp.where(lag == k, taps_ref[k], matrix)
    wide = frames * rows
    repeat_left = (
        lax.broadcasted_iota(jnp.int32, (wide, frames), 0) // rows
        == lax.broadcasted_iota(jnp.int32, (wide, frames), 1)
    ).astype(jnp.bfloat16)
    repeat_right = (
        lax.broadcasted_iota(jnp.int32, (frames, wide), 1) // rows
        == lax.broadcasted_iota(jnp.int32, (frames, wide), 0)
    ).astype(jnp.bfloat16)
    tall = jnp.dot(repeat_left, matrix.astype(jnp.bfloat16), preferred_element_type=jnp.float32)
    tall = tall.astype(jnp.bfloat16)
    chunk = 128
    for start in range(0, wide, chunk):
        piece = jnp.dot(tall[start : start + chunk], repeat_right, preferred_element_type=jnp.float32)
        same_row = (
            lax.broadcasted_iota(jnp.int32, (chunk, wide), 0) % rows
            == lax.broadcasted_iota(jnp.int32, (chunk, wide), 1) % rows
        )
        spread_ref[start : start + chunk] = jnp.where(same_row, piece, 0.0).astype(jnp.bfloat16)

    def stack_one(t, carry):
        stacked = jnp.dot(left_ref[...], window_ref[t], preferred_element_type=jnp.float32)
        stacked = stacked.astype(jnp.bfloat16)
        place = pl.ds(pl.multiple_of(t * rows, rows), rows)
        for o in range(orient):
            for z in range(2):
                begin = (o * 2 + z) * rows
                stacked_ref[o, place, z * quarter : (z + 1) * quarter] = stacked[begin : begin + rows]
        return carry

    lax.fori_loop(0, frames, stack_one, 0, unroll=4)

    for o in range(orient):
        for start in range(0, wide, 256):
            coeff_ref[o, start : start + 256] = jnp.dot(
                stacked_ref[o, start : start + 256], right_ref[o], preferred_element_type=jnp.float32
            ).astype(jnp.bfloat16)

    def phase_one(t, carry):
        place = pl.ds(pl.multiple_of(t * rows, rows), rows)
        refer = pl.ds(pl.multiple_of(ref_frame_ref[segments_ref[t]] * rows, rows), rows)
        for o in range(orient):
            coeff_real = coeff_ref[o, place, 0:quarter].astype(jnp.float32)
            coeff_imag = coeff_ref[o, place, quarter:both].astype(jnp.float32)
            ref_real = coeff_ref[o, refer, 0:quarter].astype(jnp.float32)
            ref_imag = coeff_ref[o, refer, quarter:both].astype(jnp.float32)
            prod_real = coeff_real * ref_real + coeff_imag * ref_imag
            prod_imag = coeff_imag * ref_real - coeff_real * ref_imag
            square = prod_real * prod_real + prod_imag * prod_imag + 1.0
            phase_ref[o, place] = (prod_imag * lax.rsqrt(square)).astype(jnp.bfloat16)
        return carry

    lax.fori_loop(0, frames, phase_one, 0, unroll=2)

    for start in range(0, wide, chunk):
        above = jnp.zeros((chunk, quarter), jnp.float32)
        below = jnp.ones((chunk, quarter), jnp.float32)
        for o in range(orient):
            filtered = jnp.dot(
                spread_ref[start : start + chunk], phase_ref[o], preferred_element_type=jnp.float32
            )
            filtered = filtered.astype(jnp.bfloat16).astype(jnp.float32)
            coeff_real = coeff_ref[o, start : start + chunk, 0:quarter].astype(jnp.float32)
            coeff_imag = coeff_ref[o, start : start + chunk, quarter:both].astype(jnp.float32)
            amplitude = coeff_real * coeff_real + coeff_imag * coeff_imag
            above = above + amplitude * filtered
            below = below + amplitude
        motion = (above / below).astype(out_ref.dtype)
        for i in range(chunk // rows):
            out_ref[start // rows + i] = motion[i * rows : (i + 1) * rows]


def pixel_motion(segments, ref_pick, band_taps, windows, rows, halo):
    frames, _, quarter = windows.shape
    wide = frames * rows
    left = slab_left_table(rows, halo, ORIENT)
    right = make_right_table(quarter, ORIENT)
    smem = pl.BlockSpec(memory_space=pltpu.SMEM)
    vmem = pl.BlockSpec(memory_space=pltpu.VMEM)
    return pl.pallas_call(
        pixel_kernel,
        in_specs=[smem, smem, smem, vmem, vmem, vmem],
        out_specs=vmem,
        out_shape=jax.ShapeDtypeStruct((frames, rows, quarter), jnp.bfloat16),
        scratch_shapes=[
            pltpu.VMEM((ORIENT, wide, 2 * quarter), jnp.bfloat16),
            pltpu.VMEM((ORIENT, wide, 2 * quarter), jnp.bfloat16),
            pltpu.VMEM((ORIENT, wide, quarter), jnp.bfloat16),
            pltpu.VMEM((wide, wide), jnp.bfloat16),
            pltpu.SMEM((NSEG,), jnp.int32),
        ],
        compiler_params=pltpu.CompilerParams(vmem_limit_bytes=VMEM_LIMIT),
        cost_estimate=pl.CostEstimate(
            flops=2 * ORIENT * wide * quarter * (4 * quarter + wide),
            bytes_accessed=2 * frames * quarter * (3 * rows + 2 * halo),
            transcendentals=ORIENT * wide * quarter,
        ),
    )(segments, ref_pick, band_taps.astype(jnp.float32), windows, jnp.asarray(left), jnp.asarray(right))


def slab_body(video_frames, segments, ref_pick, band_taps, slabs):
    frames_here, size, _ = video_frames.shape
    quarter = size // 4
    rows = quarter // slabs
    reduced = reduce_frames(video_frames, slabs, rows, HALO)
    windows = lax.all_to_all(reduced, "frames", split_axis=0, concat_axis=0, tiled=True)
    windows = windows.reshape(slabs * frames_here, rows + 2 * HALO, quarter)
    motion = pixel_motion(segments, ref_pick, band_taps, windows, rows, HALO)
    motion = motion.reshape(slabs, frames_here, rows, quarter)
    motion = lax.all_to_all(motion, "frames", split_axis=0, concat_axis=0, tiled=True)
    motion = jnp.swapaxes(motion, 0, 1).reshape(frames_here, quarter, quarter)
    return motion.astype(jnp.float32)


def spread(x, axis, root):
    mine = lax.axis_index(axis) == root
    return lax.psum(jnp.where(mine, x, jnp.zeros_like(x)), axis)


def traced_down(full_size, quarter):
    position = jnp.arange(quarter, dtype=jnp.float32)[:, None]
    columns = jnp.arange(full_size, dtype=jnp.float32)[None, :]
    offset_grid = columns - 4.0 * position - 1.5
    weight = jnp.exp(-offset_grid * offset_grid / (2.0 * blur_sigma * blur_sigma))
    return (weight / jnp.sum(weight, axis=1, keepdims=True)).astype(jnp.bfloat16)


def gabor_tables(quarter, orient):
    position = jnp.arange(quarter, dtype=jnp.float32)
    offset_grid = position[None, :] - position[:, None]
    envelope = gabor_gain * jnp.exp(-offset_grid * offset_grid / (2.0 * gabor_sigma * gabor_sigma))
    angles = jnp.arange(orient, dtype=jnp.float32) * (math.pi / orient)
    wave_x = wave_number * jnp.cos(angles)
    wave_y = wave_number * jnp.sin(angles)
    phase_y = wave_y[:, None, None] * offset_grid[None]
    left_table = jnp.stack([envelope * jnp.cos(phase_y), envelope * jnp.sin(phase_y)], axis=2)
    left_table = left_table.reshape(orient * quarter * 2, quarter).astype(jnp.bfloat16)
    phase_x = wave_x[:, None, None] * (-offset_grid)[None]
    real_part = envelope * jnp.cos(phase_x)
    imag_part = envelope * jnp.sin(phase_x)
    upper_half = jnp.concatenate([real_part, imag_part], axis=2)
    lower_half = jnp.concatenate([-imag_part, real_part], axis=2)
    right_table = jnp.concatenate([upper_half, lower_half], axis=1).astype(jnp.bfloat16)
    return (left_table, right_table)


def phase_terms(coeffs, per_frame):
    quarter = coeffs.shape[-1] // 2
    coeff_real = coeffs[..., :quarter].astype(jnp.float32)
    coeff_imag = coeffs[..., quarter:].astype(jnp.float32)
    ref_real = per_frame[..., :quarter].astype(jnp.float32)
    ref_imag = per_frame[..., quarter:].astype(jnp.float32)
    prod_real = coeff_real * ref_real + coeff_imag * ref_imag
    prod_imag = coeff_imag * ref_real - coeff_real * ref_imag
    phase_signal = (
        prod_imag / jnp.sqrt(prod_real * prod_real + prod_imag * prod_imag + 1.0)
    ).astype(jnp.bfloat16)
    amplitude = coeff_real * coeff_real + coeff_imag * coeff_imag
    return (phase_signal, amplitude)


def taps_matrix(band_taps, frame_count):
    frame_index = jnp.arange(frame_count, dtype=jnp.int32)
    lag_grid = frame_index[:, None] - frame_index[None, :]
    one_hot = (
        lag_grid[:, :, None] == jnp.arange(band_taps.shape[0], dtype=jnp.int32)[None, None, :]
    ).astype(jnp.float32)
    return jnp.einsum("tsk,k->ts", one_hot, band_taps.astype(jnp.float32)).astype(jnp.bfloat16)


def segment_refs(segments, ref_pick, segment_count):
    numbers = jnp.arange(segment_count, dtype=jnp.int32)
    starts = jnp.sum((segments[None, :] < numbers[:, None]).astype(jnp.int32), axis=1)
    counts = jnp.sum((segments[None, :] == numbers[:, None]).astype(jnp.int32), axis=1)
    return starts + ref_pick % counts


def frame_body(video_frames, segments, ref_pick, band_taps):
    frames_here = video_frames.shape[0]
    down_matrix = traced_down(IMG, QUART)
    left_table, right_table = gabor_tables(QUART, ORIENT)

    def reduce_frames(pictures):
        half_done = jnp.einsum(
            "nia,qa->niq", pictures, down_matrix, preferred_element_type=jnp.float32
        ).astype(jnp.bfloat16)
        return jnp.einsum(
            "qi,nik->nqk", down_matrix, half_done, preferred_element_type=jnp.float32
        ).astype(jnp.bfloat16)

    def filter_frames(reduced):
        stacked = jnp.einsum(
            "ra,nak->nrk", left_table, reduced, preferred_element_type=jnp.float32
        ).astype(jnp.bfloat16)
        stacked = stacked.reshape(reduced.shape[0], ORIENT, QUART, 2 * QUART)
        return jnp.einsum(
            "noya,oab->noyb", stacked, right_table, preferred_element_type=jnp.float32
        ).astype(jnp.bfloat16)

    small_own = reduce_frames(video_frames)
    coeff_own = filter_frames(small_own)
    ref_frames = segment_refs(segments, ref_pick, NSEG)
    gathered = []
    for segment in range(NSEG):
        root_index = ref_frames[segment] // frames_here
        local_index = ref_frames[segment] % frames_here
        payload = lax.dynamic_index_in_dim(video_frames, local_index, 0, keepdims=False)
        gathered.append(spread(payload, "frames", root_index))
    ref_coeff = filter_frames(reduce_frames(jnp.stack(gathered)))
    first_frame = lax.axis_index("frames") * frames_here
    own_ids = lax.dynamic_slice_in_dim(segments, first_frame, frames_here)
    select = (own_ids[:, None] == jnp.arange(NSEG, dtype=jnp.int32)[None, :]).astype(jnp.bfloat16)
    per_frame = jnp.dot(select, ref_coeff.reshape(NSEG, -1), preferred_element_type=jnp.float32)
    per_frame = per_frame.astype(jnp.bfloat16).reshape(coeff_own.shape)
    phase_signal, amplitude = phase_terms(coeff_own, per_frame)
    phase_signal = phase_signal.reshape(frames_here, ORIENT, QUART * QUART)
    pixel_rows = lax.all_to_all(phase_signal, "frames", split_axis=2, concat_axis=0, tiled=True)
    matrix = taps_matrix(band_taps, pixel_rows.shape[0])
    filtered = jnp.einsum(
        "ts,sop->top", matrix, pixel_rows, preferred_element_type=jnp.float32
    ).astype(jnp.bfloat16)
    filtered = lax.all_to_all(filtered, "frames", split_axis=0, concat_axis=2, tiled=True)
    filtered = filtered.reshape(frames_here, ORIENT, QUART, QUART).astype(jnp.float32)
    return jnp.sum(amplitude * filtered, axis=1) / (jnp.sum(amplitude, axis=1) + 1.0)


def solution(mesh):
    in_specs = (P(("groups", "frames"), None, None), P("groups"), P("groups"), P())
    out_specs = P(("groups", "frames"), None, None)
    slabs = mesh.shape["frames"]

    def body(video_frames, segments, ref_pick, band_taps):
        if (video_frames.shape[1] // 4) % (slabs * TILE) == 0:
            return slab_body(video_frames, segments, ref_pick, band_taps, slabs)
        return frame_body(video_frames, segments, ref_pick, band_taps)

    return jax.shard_map(body, mesh=mesh, in_specs=in_specs, out_specs=out_specs, check_vma=False)
```

```python
import functools
import math

import jax
import jax.numpy as jnp
import numpy as np
from jax import lax
from jax.experimental import pallas as pl
from jax.experimental.pallas import tpu as pltpu
from jax.sharding import PartitionSpec as P

IMG = 1024
ORIENT = 4
NSEG = 4
QUART = 256


blur_sigma = 2.0
gabor_sigma = 2.0
wave_number = math.pi / 2.0
gabor_gain = 2.0

HALO = 32
TILE = 16
CORES = 2
MIB = 1024 * 1024


def make_down(full_size, quarter):
    position = np.arange(quarter, dtype=np.float32)[:, None]
    columns = np.arange(full_size, dtype=np.float32)[None, :]
    offset_grid = columns - np.float32(4.0) * position - np.float32(1.5)
    weight = np.exp(-offset_grid * offset_grid / np.float32(2.0 * blur_sigma * blur_sigma))
    return (weight / np.sum(weight, axis=1, keepdims=True)).astype(jnp.bfloat16)


def envelope_of(offset_grid):
    return np.float32(gabor_gain) * np.exp(
        -offset_grid * offset_grid / np.float32(2.0 * gabor_sigma * gabor_sigma)
    )


def waves(orient):
    angles = np.arange(orient, dtype=np.float32) * np.float32(math.pi / orient)
    wave_x = np.float32(wave_number) * np.cos(angles)
    wave_y = np.float32(wave_number) * np.sin(angles)
    return wave_x, wave_y


def slab_left_table(rows, halo, orient):
    offset = (
        np.arange(rows + 2 * halo, dtype=np.float32)[None, :]
        - np.float32(halo)
        - np.arange(rows, dtype=np.float32)[:, None]
    )
    wave_y = waves(orient)[1]
    phase = wave_y[:, None, None] * offset[None]
    envelope = envelope_of(offset)[None]
    table = np.stack([envelope * np.cos(phase), envelope * np.sin(phase)], axis=1)
    return table.reshape(orient * 2 * rows, rows + 2 * halo).astype(jnp.bfloat16)


def make_right_table(quarter, orient):
    position = np.arange(quarter, dtype=np.float32)
    offset = position[:, None] - position[None, :]
    wave_x = waves(orient)[0]
    phase_x = wave_x[:, None, None] * offset[None]
    envelope = envelope_of(offset)[None]
    real_part = envelope * np.cos(phase_x)
    imag_part = envelope * np.sin(phase_x)
    upper_half = np.concatenate([real_part, imag_part], axis=2)
    lower_half = np.concatenate([-imag_part, real_part], axis=2)
    return np.concatenate([upper_half, lower_half], axis=1).astype(jnp.bfloat16)


def reduce_kernel(frame_ref, down_t_ref, down_ref, out_ref, total_ref, padded_ref, *, rows, halo):
    step = pl.program_id(1)
    half = jnp.dot(frame_ref[0], down_t_ref[...], preferred_element_type=jnp.float32)
    part = jnp.dot(down_ref[...], half.astype(jnp.bfloat16), preferred_element_type=jnp.float32)

    @pl.when(step == 0)
    def _():
        total_ref[...] = part

    @pl.when(step > 0)
    def _():
        total_ref[...] += part

    @pl.when(step == pl.num_programs(1) - 1)
    def _():
        quarter = total_ref.shape[0]
        edge = jnp.zeros((halo, quarter), jnp.bfloat16)
        padded_ref[0:halo] = edge
        padded_ref[halo + quarter :] = edge
        padded_ref[halo : halo + quarter] = total_ref[...].astype(jnp.bfloat16)
        for slab in range(out_ref.shape[0]):
            out_ref[slab, 0] = padded_ref[slab * rows : slab * rows + rows + 2 * halo]


def reduce_frames(video_frames, slabs, rows, halo):
    count, size, _ = video_frames.shape
    quarter = slabs * rows
    block = size // 2
    down = make_down(size, quarter)
    window = rows + 2 * halo
    return pl.pallas_call(
        functools.partial(reduce_kernel, rows=rows, halo=halo),
        grid=(count, size // block),
        in_specs=[
            pl.BlockSpec((1, block, size), lambda f, i: (f, i, 0)),
            pl.BlockSpec((size, quarter), lambda f, i: (0, 0)),
            pl.BlockSpec((quarter, block), lambda f, i: (0, i)),
        ],
        out_specs=pl.BlockSpec((slabs, 1, window, quarter), lambda f, i: (0, f, 0, 0)),
        out_shape=jax.ShapeDtypeStruct((slabs, count, window, quarter), jnp.bfloat16),
        scratch_shapes=[
            pltpu.VMEM((quarter, quarter), jnp.float32),
            pltpu.VMEM((quarter + 2 * halo, quarter), jnp.bfloat16),
        ],
        compiler_params=pltpu.CompilerParams(vmem_limit_bytes=24 * MIB),
        cost_estimate=pl.CostEstimate(
            flops=2 * count * size * quarter * (size + quarter),
            bytes_accessed=2 * count * size * size,
            transcendentals=0,
        ),
    )(video_frames, jnp.asarray(down.T.copy()), jnp.asarray(down))


def pixel_kernel(
    place_ref, segments_ref, pick_ref, taps_ref, mine_ref, other_ref, left_ref, right_ref, out_ref,
    stacked_ref, coeff_ref, phase_ref, spread_ref, ref_frame_ref, ref_slot_ref, *, history, frames,
):
    _, frames_here, _, quarter = mine_ref.shape
    chunk, rows, _ = out_ref.shape
    orient = right_ref.shape[0]
    nseg = pick_ref.shape[0]
    taps = taps_ref.shape[0]
    both = 2 * quarter
    timed = history + chunk
    whole = timed == frames
    wide_out, wide_in = chunk * rows, timed * rows
    core, first = place_ref[0], place_ref[1] * chunk - history
    window = pl.ds(pl.multiple_of(core * rows, rows), left_ref.shape[1])

    def count_one(t, totals):
        here = segments_ref[t]
        below = [total + (here < s).astype(jnp.int32) for s, total in enumerate(totals[0])]
        same = [total + (here == s).astype(jnp.int32) for s, total in enumerate(totals[1])]
        return tuple(below), tuple(same)

    zeros = tuple(jnp.int32(0) for _ in range(nseg))
    starts, counts = lax.fori_loop(0, frames, count_one, (zeros, zeros), unroll=8)
    for s in range(nseg):
        frame = starts[s] + lax.rem(pick_ref[s], counts[s])
        ref_frame_ref[s] = frame
        ref_slot_ref[s] = frame if whole else timed + s

    lag = history + lax.broadcasted_iota(jnp.int32, (chunk, timed), 0) - lax.broadcasted_iota(
        jnp.int32, (chunk, timed), 1
    )
    if history:
        real = first + lax.broadcasted_iota(jnp.int32, (chunk, timed), 1) >= 0
        lag = jnp.where(real, lag, -1)
    matrix = jnp.zeros((chunk, timed), jnp.float32)
    for k in range(taps):
        matrix = jnp.where(lag == k, taps_ref[k], matrix)
    repeat_left = (
        lax.broadcasted_iota(jnp.int32, (wide_out, chunk), 0) // rows
        == lax.broadcasted_iota(jnp.int32, (wide_out, chunk), 1)
    ).astype(jnp.bfloat16)
    repeat_right = (
        lax.broadcasted_iota(jnp.int32, (timed, wide_in), 1) // rows
        == lax.broadcasted_iota(jnp.int32, (timed, wide_in), 0)
    ).astype(jnp.bfloat16)
    tall = jnp.dot(repeat_left, matrix.astype(jnp.bfloat16), preferred_element_type=jnp.float32)
    tall = tall.astype(jnp.bfloat16)
    piece = min(128, wide_out)
    for start in range(0, wide_out, piece):
        part = jnp.dot(tall[start : start + piece], repeat_right, preferred_element_type=jnp.float32)
        same_row = (
            lax.broadcasted_iota(jnp.int32, (piece, wide_in), 0) % rows
            == lax.broadcasted_iota(jnp.int32, (piece, wide_in), 1) % rows
        )
        spread_ref[start : start + piece] = jnp.where(same_row, part, 0.0).astype(jnp.bfloat16)

    def stack_one(picture, slot):
        stacked = jnp.dot(left_ref[...], picture, preferred_element_type=jnp.float32)
        stacked = stacked.astype(jnp.bfloat16)
        place = pl.ds(pl.multiple_of(slot * rows, rows), rows)
        for o in range(orient):
            for z in range(2):
                begin = (o * 2 + z) * rows
                stacked_ref[o, place, z * quarter : (z + 1) * quarter] = stacked[begin : begin + rows]

    def stack_chip(i, carry):
        chip = i if whole else jnp.maximum(first // (CORES * frames_here) + i, 0)
        for f in range(frames_here):
            stack_one(mine_ref[chip, f, window], (i * CORES + core) * frames_here + f)
            stack_one(other_ref[chip, f, window], (i * CORES + 1 - core) * frames_here + f)
        return carry

    lax.fori_loop(0, timed // (CORES * frames_here), stack_chip, 0, unroll=2)
    if not whole:
        for s in range(nseg):
            frame = ref_frame_ref[s]
            device, f = frame // frames_here, frame % frames_here
            chip = device // CORES
            own = jnp.full(left_ref.shape[1:] + (quarter,), device % CORES, jnp.int32) == core
            picture = jnp.where(
                own, mine_ref[chip, f, window].astype(jnp.float32), other_ref[chip, f, window].astype(jnp.float32)
            )
            stack_one(picture.astype(jnp.bfloat16), timed + s)

    wide_all = stacked_ref.shape[1]
    for o in range(orient):
        for start in range(0, wide_all, 256):
            stop = min(start + 256, wide_all)
            coeff_ref[o, start:stop] = jnp.dot(
                stacked_ref[o, start:stop], right_ref[o], preferred_element_type=jnp.float32
            ).astype(jnp.bfloat16)

    def phase_one(slot, carry):
        place = pl.ds(pl.multiple_of(slot * rows, rows), rows)
        segment = segments_ref[slot if whole else jnp.maximum(first + slot, 0)]
        refer = pl.ds(pl.multiple_of(ref_slot_ref[segment] * rows, rows), rows)
        for o in range(orient):
            coeff_real = coeff_ref[o, place, 0:quarter].astype(jnp.float32)
            coeff_imag = coeff_ref[o, place, quarter:both].astype(jnp.float32)
            ref_real = coeff_ref[o, refer, 0:quarter].astype(jnp.float32)
            ref_imag = coeff_ref[o, refer, quarter:both].astype(jnp.float32)
            prod_real = coeff_real * ref_real + coeff_imag * ref_imag
            prod_imag = coeff_imag * ref_real - coeff_real * ref_imag
            square = prod_real * prod_real + prod_imag * prod_imag + 1.0
            phase_ref[o, place] = (prod_imag * lax.rsqrt(square)).astype(jnp.bfloat16)
        return carry

    lax.fori_loop(0, timed, phase_one, 0, unroll=2)

    for start in range(0, wide_out, piece):
        here = slice(history * rows + start, history * rows + start + piece)
        above = jnp.zeros((piece, quarter), jnp.float32)
        below = jnp.ones((piece, quarter), jnp.float32)
        for o in range(orient):
            filtered = jnp.dot(
                spread_ref[start : start + piece], phase_ref[o], preferred_element_type=jnp.float32
            )
            filtered = filtered.astype(jnp.bfloat16).astype(jnp.float32)
            coeff_real = coeff_ref[o, here, 0:quarter].astype(jnp.float32)
            coeff_imag = coeff_ref[o, here, quarter:both].astype(jnp.float32)
            amplitude = coeff_real * coeff_real + coeff_imag * coeff_imag
            above = above + amplitude * filtered
            below = below + amplitude
        motion = (above / below).astype(out_ref.dtype)
        for i in range(piece // rows):
            out_ref[start // rows + i] = motion[i * rows : (i + 1) * rows]


def pixel_motion(place, segments, ref_pick, band_taps, mine, other, rows, chunk):
    chips, frames_here, _, quarter = mine.shape
    frames = chips * CORES * frames_here
    history = min(chunk * -(-(band_taps.shape[0] - 1) // chunk), frames - chunk)
    timed = history + chunk
    slots = timed if timed == frames else timed + NSEG
    left = slab_left_table(rows, HALO, ORIENT)
    right = make_right_table(quarter, ORIENT)
    smem = pl.BlockSpec(memory_space=pltpu.SMEM)
    vmem = pl.BlockSpec(memory_space=pltpu.VMEM)
    slot_bytes = ORIENT * rows * 2 * quarter * 2
    limit = 2 * mine.size * 2 + 4 * slots * slot_bytes + 16 * MIB
    return pl.pallas_call(
        functools.partial(pixel_kernel, history=history, frames=frames),
        in_specs=[smem] * 4 + [vmem] * 4,
        out_specs=vmem,
        out_shape=jax.ShapeDtypeStruct((chunk, rows, quarter), jnp.bfloat16),
        scratch_shapes=[
            pltpu.VMEM((ORIENT, slots * rows, 2 * quarter), jnp.bfloat16),
            pltpu.VMEM((ORIENT, slots * rows, 2 * quarter), jnp.bfloat16),
            pltpu.VMEM((ORIENT, timed * rows, quarter), jnp.bfloat16),
            pltpu.VMEM((chunk * rows, timed * rows), jnp.bfloat16),
            pltpu.SMEM((NSEG,), jnp.int32),
            pltpu.SMEM((NSEG,), jnp.int32),
        ],
        compiler_params=pltpu.CompilerParams(vmem_limit_bytes=limit),
        cost_estimate=pl.CostEstimate(
            flops=2 * ORIENT * rows * quarter * (slots * 4 * quarter + chunk * timed * rows),
            bytes_accessed=4 * mine.size + right.size * 2,
            transcendentals=ORIENT * timed * rows * quarter,
        ),
    )(place, segments, ref_pick, band_taps.astype(jnp.float32), mine, other, jnp.asarray(left), jnp.asarray(right))


def body(video_frames, segments, ref_pick, band_taps, *, chunks, slabs):
    frames_here, size, _ = video_frames.shape
    quarter = size // 4
    slab_rows = quarter // slabs
    rows = slab_rows // CORES
    reduced = reduce_frames(video_frames, slabs, slab_rows, HALO)
    mine = lax.all_to_all(reduced, "slab", split_axis=0, concat_axis=0, tiled=True)
    if chunks > 1:
        mine = lax.all_gather(mine, "chunk", axis=0, tiled=True)
    other = lax.ppermute(mine, "core", [(0, 1), (1, 0)])
    place = jnp.stack([lax.axis_index("core"), lax.axis_index("chunk")])
    chunk = slabs * CORES * frames_here
    motion = pixel_motion(place, segments, ref_pick, band_taps, mine, other, rows, chunk)
    motion = motion.reshape(slabs * CORES, frames_here, rows, quarter)
    motion = lax.all_to_all(motion, ("slab", "core"), split_axis=0, concat_axis=0, tiled=True)
    motion = jnp.swapaxes(motion, 0, 1).reshape(frames_here, quarter, quarter)
    return motion.astype(jnp.float32)


def solution(mesh):
    chips = mesh.shape["frames"] // CORES
    slabs = min(chips, QUART // (CORES * TILE))
    chunks = chips // slabs
    names = ("groups", "chunk", "slab", "core")
    cut = jax.sharding.Mesh(mesh.devices.reshape(mesh.shape["groups"], chunks, slabs, CORES), names)
    in_specs = (P(names, None, None), P("groups"), P("groups"), P())
    return jax.shard_map(
        functools.partial(body, chunks=chunks, slabs=slabs),
        mesh=cut, in_specs=in_specs, out_specs=P(names, None, None), check_vma=False,
    )
```

```python
import functools
import math

import jax
import jax.numpy as jnp
import numpy as np
from jax import lax
from jax.experimental import pallas as pl
from jax.experimental.pallas import tpu as pltpu
from jax.sharding import PartitionSpec as P

IMG = 1024
ORIENT = 4
NSEG = 4
QUART = 256


blur_sigma = 2.0
gabor_sigma = 2.0
wave_number = math.pi / 2.0
gabor_gain = 2.0

HALO = 32
TILE = 16
CORES = 2
MIB = 1024 * 1024


def envelope_of(offset_grid):
    return np.float32(gabor_gain) * np.exp(
        -offset_grid * offset_grid / np.float32(2.0 * gabor_sigma * gabor_sigma)
    )


def waves(orient):
    angles = np.arange(orient, dtype=np.float32) * np.float32(math.pi / orient)
    wave_x = np.float32(wave_number) * np.cos(angles)
    wave_y = np.float32(wave_number) * np.sin(angles)
    return wave_x, wave_y


def slab_left_table(rows, halo, orient):
    offset = (
        np.arange(rows + 2 * halo, dtype=np.float32)[None, :]
        - np.float32(halo)
        - np.arange(rows, dtype=np.float32)[:, None]
    )
    wave_y = waves(orient)[1]
    phase = wave_y[:, None, None] * offset[None]
    envelope = envelope_of(offset)[None]
    table = np.stack([envelope * np.cos(phase), envelope * np.sin(phase)], axis=1)
    return table.reshape(orient * 2 * rows, rows + 2 * halo).astype(jnp.bfloat16)


def make_right_table(quarter, orient):
    position = np.arange(quarter, dtype=np.float32)
    offset = position[:, None] - position[None, :]
    wave_x = waves(orient)[0]
    phase_x = wave_x[:, None, None] * offset[None]
    envelope = envelope_of(offset)[None]
    real_part = envelope * np.cos(phase_x)
    imag_part = envelope * np.sin(phase_x)
    upper_half = np.concatenate([real_part, imag_part], axis=2)
    lower_half = np.concatenate([-imag_part, real_part], axis=2)
    return np.concatenate([upper_half, lower_half], axis=1).astype(jnp.bfloat16)


def down_weights(full_size, quarter, axis):
    shape = (full_size, quarter) if axis == 0 else (quarter, full_size)
    position = lax.broadcasted_iota(jnp.int32, shape, 1 - axis).astype(jnp.float32)
    columns = lax.broadcasted_iota(jnp.int32, shape, axis).astype(jnp.float32)
    offset_grid = columns - 4.0 * position - 1.5
    weight = jnp.exp(-offset_grid * offset_grid / (2.0 * blur_sigma * blur_sigma))
    return (weight / jnp.sum(weight, axis=axis, keepdims=True)).astype(jnp.bfloat16)


def reduce_kernel(frames_ref, *refs, shifts, rows, halo, block):
    out_refs = refs[:shifts]
    picture_ref, down_t_ref, down_ref, total_ref, padded_ref, sems = refs[shifts:]
    count, size, _ = picture_ref.shape
    quarter = down_ref.shape[0]

    copies = []
    for f in range(count):
        for i in range(size // block):
            here = pl.ds(i * block, block)
            copy = pltpu.make_async_copy(frames_ref.at[f, here], picture_ref.at[f, here], sems.at[f, i])
            copy.start()
            copies.append(copy)
    down_t_ref[...] = down_weights(size, quarter, 0)
    down_ref[...] = down_weights(size, quarter, 1)
    edge = jnp.zeros((halo, quarter), jnp.bfloat16)
    padded_ref[0:halo] = edge
    padded_ref[halo + quarter :] = edge

    me = lax.axis_index("slab")
    reach = block // 4
    for f in range(count):
        total_ref[...] = jnp.zeros_like(total_ref)
        for i in range(size // block):
            copies[f * (size // block) + i].wait()
            half = jnp.dot(
                picture_ref[f, i * block : (i + 1) * block], down_t_ref[...], preferred_element_type=jnp.float32
            ).astype(jnp.bfloat16)
            near = slice(max(i * reach - TILE, 0), min((i + 1) * reach + TILE, quarter))
            total_ref[near] += jnp.dot(
                down_ref[near, i * block : (i + 1) * block], half, preferred_element_type=jnp.float32
            )
        padded_ref[halo : halo + quarter] = total_ref[...].astype(jnp.bfloat16)
        for shift, out_ref in enumerate(out_refs):
            slab = lax.rem(me + shift, shifts)
            out_ref[f] = padded_ref[pl.ds(pl.multiple_of(slab * rows, rows), rows + 2 * halo)]


def reduce_frames(video_frames, slabs, rows, halo):
    count, size, _ = video_frames.shape
    quarter = slabs * rows
    block = size // 4
    out = jax.ShapeDtypeStruct((count, rows + 2 * halo, quarter), jnp.bfloat16)
    return pl.pallas_call(
        functools.partial(reduce_kernel, shifts=slabs, rows=rows, halo=halo, block=block),
        in_specs=[pl.BlockSpec(memory_space=pltpu.HBM)],
        out_specs=[pl.BlockSpec(memory_space=pltpu.VMEM)] * slabs,
        out_shape=[out] * slabs,
        scratch_shapes=[
            pltpu.VMEM((count, size, size), jnp.bfloat16),
            pltpu.VMEM((size, quarter), jnp.bfloat16),
            pltpu.VMEM((quarter, size), jnp.bfloat16),
            pltpu.VMEM((quarter, quarter), jnp.float32),
            pltpu.VMEM((quarter + 2 * halo, quarter), jnp.bfloat16),
            pltpu.SemaphoreType.DMA((count, size // block)),
        ],
        compiler_params=pltpu.CompilerParams(vmem_limit_bytes=24 * MIB),
        cost_estimate=pl.CostEstimate(
            flops=2 * count * size * quarter * (size + quarter),
            bytes_accessed=2 * count * size * size,
            transcendentals=0,
        ),
    )(video_frames)


def cut_kernel(*refs, rows):
    in_refs, (mine_ref, other_ref) = refs[:-2], refs[-2:]
    slabs, _, window, _ = mine_ref.shape
    me, core = lax.axis_index("slab"), lax.axis_index("core")
    for shift, in_ref in enumerate(in_refs):
        chip = lax.rem(me - shift + slabs, slabs)
        mine_ref[chip] = in_ref[:, pl.ds(pl.multiple_of(core * rows, rows), window)]
        other_ref[chip] = in_ref[:, pl.ds(pl.multiple_of((1 - core) * rows, rows), window)]


def cut_windows(pieces, rows):
    count, window, quarter = pieces[0].shape
    out = jax.ShapeDtypeStruct((len(pieces), count, window - rows, quarter), jnp.bfloat16)
    return pl.pallas_call(
        functools.partial(cut_kernel, rows=rows),
        in_specs=[pl.BlockSpec(memory_space=pltpu.VMEM)] * len(pieces),
        out_specs=[pl.BlockSpec(memory_space=pltpu.VMEM)] * 2,
        out_shape=[out, out],
        compiler_params=pltpu.CompilerParams(vmem_limit_bytes=16 * MIB),
        cost_estimate=pl.CostEstimate(flops=0, bytes_accessed=8 * out.size, transcendentals=0),
    )(*pieces)


def time_kernel(segments_ref, pick_ref, taps_ref, spread_ref, frame_ref, *, history, frames, rows):
    chunk, timed = spread_ref.shape[0] // rows, spread_ref.shape[1] // rows
    nseg = pick_ref.shape[0]
    taps = taps_ref.shape[0]
    wide_out, wide_in = chunk * rows, timed * rows

    def count_one(t, totals):
        here = segments_ref[t]
        below = [total + (here < s).astype(jnp.int32) for s, total in enumerate(totals[0])]
        same = [total + (here == s).astype(jnp.int32) for s, total in enumerate(totals[1])]
        return tuple(below), tuple(same)

    zeros = tuple(jnp.int32(0) for _ in range(nseg))
    starts, counts = lax.fori_loop(0, frames, count_one, (zeros, zeros), unroll=8)
    for s in range(nseg):
        frame_ref[s] = starts[s] + lax.rem(pick_ref[s], counts[s])

    lag = history + lax.broadcasted_iota(jnp.int32, (chunk, timed), 0) - lax.broadcasted_iota(
        jnp.int32, (chunk, timed), 1
    )
    if history:
        first = lax.axis_index("chunk") * chunk - history
        real = first + lax.broadcasted_iota(jnp.int32, (chunk, timed), 1) >= 0
        lag = jnp.where(real, lag, -1)
    matrix = jnp.zeros((chunk, timed), jnp.float32)
    for k in range(taps):
        matrix = jnp.where(lag == k, taps_ref[k], matrix)
    repeat_left = (
        lax.broadcasted_iota(jnp.int32, (wide_out, chunk), 0) // rows
        == lax.broadcasted_iota(jnp.int32, (wide_out, chunk), 1)
    ).astype(jnp.bfloat16)
    repeat_right = (
        lax.broadcasted_iota(jnp.int32, (timed, wide_in), 1) // rows
        == lax.broadcasted_iota(jnp.int32, (timed, wide_in), 0)
    ).astype(jnp.bfloat16)
    tall = jnp.dot(repeat_left, matrix.astype(jnp.bfloat16), preferred_element_type=jnp.float32)
    tall = tall.astype(jnp.bfloat16)
    piece = min(128, wide_out)
    for start in range(0, wide_out, piece):
        part = jnp.dot(tall[start : start + piece], repeat_right, preferred_element_type=jnp.float32)
        same_row = (
            lax.broadcasted_iota(jnp.int32, (piece, wide_in), 0) % rows
            == lax.broadcasted_iota(jnp.int32, (piece, wide_in), 1) % rows
        )
        spread_ref[start : start + piece] = jnp.where(same_row, part, 0.0).astype(jnp.bfloat16)


def time_tables(segments, ref_pick, band_taps, rows, chunk, history):
    frames = segments.shape[0]
    wide_out, wide_in = chunk * rows, (history + chunk) * rows
    smem = pl.BlockSpec(memory_space=pltpu.SMEM)
    return pl.pallas_call(
        functools.partial(time_kernel, history=history, frames=frames, rows=rows),
        in_specs=[smem] * 3,
        out_specs=[pl.BlockSpec(memory_space=pltpu.VMEM), smem],
        out_shape=[
            jax.ShapeDtypeStruct((wide_out, wide_in), jnp.bfloat16),
            jax.ShapeDtypeStruct(ref_pick.shape, jnp.int32),
        ],
        compiler_params=pltpu.CompilerParams(vmem_limit_bytes=16 * MIB),
        cost_estimate=pl.CostEstimate(
            flops=2 * wide_out * wide_in * chunk, bytes_accessed=2 * wide_out * wide_in, transcendentals=0
        ),
    )(segments, ref_pick, band_taps.astype(jnp.float32))


def pixel_kernel(
    segments_ref, ref_frame_ref, spread_ref, mine_ref, other_ref, left_ref, right_ref, out_ref,
    stacked_ref, coeff_ref, phase_ref, *, history, frames,
):
    _, frames_here, _, quarter = mine_ref.shape
    chunk, rows, _ = out_ref.shape
    orient = right_ref.shape[0]
    nseg = ref_frame_ref.shape[0]
    both = 2 * quarter
    timed = history + chunk
    whole = timed == frames
    wide_out = chunk * rows
    core = lax.axis_index("core")
    first = 0 if whole else lax.axis_index("chunk") * chunk - history

    def stack_one(picture, slot):
        stacked = jnp.dot(left_ref[...], picture, preferred_element_type=jnp.float32)
        stacked = stacked.astype(jnp.bfloat16)
        place = pl.ds(pl.multiple_of(slot * rows, rows), rows)
        for o in range(orient):
            for z in range(2):
                begin = (o * 2 + z) * rows
                stacked_ref[o, place, z * quarter : (z + 1) * quarter] = stacked[begin : begin + rows]

    def stack_chip(i, carry):
        chip = i if whole else jnp.maximum(first // (CORES * frames_here) + i, 0)
        for f in range(frames_here):
            stack_one(mine_ref[chip, f], (i * CORES + core) * frames_here + f)
            stack_one(other_ref[chip, f], (i * CORES + 1 - core) * frames_here + f)
        return carry

    lax.fori_loop(0, timed // (CORES * frames_here), stack_chip, 0, unroll=2)
    if not whole:
        for s in range(nseg):
            frame = ref_frame_ref[s]
            device, f = frame // frames_here, frame % frames_here
            chip = device // CORES
            own = jnp.full(left_ref.shape[1:] + (quarter,), device % CORES, jnp.int32) == core
            picture = jnp.where(
                own, mine_ref[chip, f].astype(jnp.float32), other_ref[chip, f].astype(jnp.float32)
            )
            stack_one(picture.astype(jnp.bfloat16), timed + s)

    wide_all = stacked_ref.shape[1]
    for o in range(orient):
        for start in range(0, wide_all, 256):
            stop = min(start + 256, wide_all)
            coeff_ref[o, start:stop] = jnp.dot(
                stacked_ref[o, start:stop], right_ref[o], preferred_element_type=jnp.float32
            ).astype(jnp.bfloat16)

    def phase_one(slot, carry):
        place = pl.ds(pl.multiple_of(slot * rows, rows), rows)
        segment = segments_ref[slot if whole else jnp.maximum(first + slot, 0)]
        refer = pl.ds(pl.multiple_of((ref_frame_ref[segment] if whole else timed + segment) * rows, rows), rows)
        for o in range(orient):
            coeff_real = coeff_ref[o, place, 0:quarter].astype(jnp.float32)
            coeff_imag = coeff_ref[o, place, quarter:both].astype(jnp.float32)
            ref_real = coeff_ref[o, refer, 0:quarter].astype(jnp.float32)
            ref_imag = coeff_ref[o, refer, quarter:both].astype(jnp.float32)
            prod_real = coeff_real * ref_real + coeff_imag * ref_imag
            prod_imag = coeff_imag * ref_real - coeff_real * ref_imag
            square = prod_real * prod_real + prod_imag * prod_imag + 1.0
            phase_ref[o, place] = (prod_imag * lax.rsqrt(square)).astype(jnp.bfloat16)
        return carry

    lax.fori_loop(0, timed, phase_one, 0, unroll=2)

    piece = min(128, wide_out)
    for start in range(0, wide_out, piece):
        here = slice(history * rows + start, history * rows + start + piece)
        above = jnp.zeros((piece, quarter), jnp.float32)
        below = jnp.ones((piece, quarter), jnp.float32)
        for o in range(orient):
            filtered = jnp.dot(
                spread_ref[start : start + piece], phase_ref[o], preferred_element_type=jnp.float32
            )
            filtered = filtered.astype(jnp.bfloat16).astype(jnp.float32)
            coeff_real = coeff_ref[o, here, 0:quarter].astype(jnp.float32)
            coeff_imag = coeff_ref[o, here, quarter:both].astype(jnp.float32)
            amplitude = coeff_real * coeff_real + coeff_imag * coeff_imag
            above = above + amplitude * filtered
            below = below + amplitude
        motion = (above / below).astype(out_ref.dtype)
        for i in range(piece // rows):
            out_ref[start // rows + i] = motion[i * rows : (i + 1) * rows]


def pixel_motion(segments, ref_frames, spread, mine, other, rows, chunk, history):
    chips, frames_here, _, quarter = mine.shape
    frames = chips * CORES * frames_here
    timed = history + chunk
    slots = timed if timed == frames else timed + NSEG
    left = slab_left_table(rows, HALO, ORIENT)
    right = make_right_table(quarter, ORIENT)
    smem = pl.BlockSpec(memory_space=pltpu.SMEM)
    vmem = pl.BlockSpec(memory_space=pltpu.VMEM)
    slot_bytes = ORIENT * rows * 2 * quarter * 2
    limit = 2 * mine.size * 2 + 4 * slots * slot_bytes + 16 * MIB
    return pl.pallas_call(
        functools.partial(pixel_kernel, history=history, frames=frames),
        in_specs=[smem] * 2 + [vmem] * 5,
        out_specs=vmem,
        out_shape=jax.ShapeDtypeStruct((chunk, rows, quarter), jnp.bfloat16),
        scratch_shapes=[
            pltpu.VMEM((ORIENT, slots * rows, 2 * quarter), jnp.bfloat16),
            pltpu.VMEM((ORIENT, slots * rows, 2 * quarter), jnp.bfloat16),
            pltpu.VMEM((ORIENT, timed * rows, quarter), jnp.bfloat16),
        ],
        compiler_params=pltpu.CompilerParams(vmem_limit_bytes=limit),
        cost_estimate=pl.CostEstimate(
            flops=2 * ORIENT * rows * quarter * (slots * 4 * quarter + chunk * timed * rows),
            bytes_accessed=4 * mine.size + right.size * 2,
            transcendentals=ORIENT * timed * rows * quarter,
        ),
    )(segments, ref_frames, spread, mine, other, jnp.asarray(left), jnp.asarray(right))


def body(video_frames, segments, ref_pick, band_taps, *, chunks, slabs):
    frames_here, size, _ = video_frames.shape
    quarter = size // 4
    slab_rows = quarter // slabs
    rows = slab_rows // CORES
    chunk = slabs * CORES * frames_here
    history = min(chunk * -(-(band_taps.shape[0] - 1) // chunk), segments.shape[0] - chunk)
    windows = reduce_frames(video_frames, slabs, slab_rows, HALO)
    pieces = [windows[0]]
    for shift in range(1, slabs):
        ring = [(chip, (chip + shift) % slabs) for chip in range(slabs)]
        pieces.append(lax.ppermute(windows[shift], "slab", ring))
    mine, other = cut_windows(pieces, rows)
    other = lax.ppermute(other, "core", [(0, 1), (1, 0)])
    if chunks > 1:
        mine = lax.all_gather(mine, "chunk", axis=0, tiled=True)
        other = lax.all_gather(other, "chunk", axis=0, tiled=True)
    spread, ref_frames = time_tables(segments, ref_pick, band_taps, rows, chunk, history)
    motion = pixel_motion(segments, ref_frames, spread, mine, other, rows, chunk, history)
    motion = motion.reshape(slabs * CORES, frames_here, rows, quarter)
    motion = lax.all_to_all(motion, ("slab", "core"), split_axis=0, concat_axis=0, tiled=True)
    motion = jnp.swapaxes(motion, 0, 1).reshape(frames_here, quarter, quarter)
    return motion.astype(jnp.float32)


def solution(mesh):
    chips = mesh.shape["frames"] // CORES
    slabs = min(chips, QUART // (CORES * TILE))
    chunks = chips // slabs
    names = ("groups", "chunk", "slab", "core")
    cut = jax.sharding.Mesh(mesh.devices.reshape(mesh.shape["groups"], chunks, slabs, CORES), names)
    in_specs = (P(names, None, None), P("groups"), P("groups"), P())
    return jax.shard_map(
        functools.partial(body, chunks=chunks, slabs=slabs),
        mesh=cut, in_specs=in_specs, out_specs=P(names, None, None), check_vma=False,
    )
```

```python
import functools
import math

import jax
import jax.numpy as jnp
import numpy as np
from jax import lax
from jax.experimental import pallas as pl
from jax.experimental.pallas import tpu as pltpu
from jax.sharding import PartitionSpec as P

IMG = 1024
ORIENT = 4
NSEG = 4
QUART = 256


blur_sigma = 2.0
gabor_sigma = 2.0
wave_number = math.pi / 2.0
gabor_gain = 2.0

HALO = 32
TILE = 16
CORES = 2
MIB = 1024 * 1024


def envelope_of(offset_grid):
    return np.float32(gabor_gain) * np.exp(
        -offset_grid * offset_grid / np.float32(2.0 * gabor_sigma * gabor_sigma)
    )


def waves(orient):
    angles = np.arange(orient, dtype=np.float32) * np.float32(math.pi / orient)
    wave_x = np.float32(wave_number) * np.cos(angles)
    wave_y = np.float32(wave_number) * np.sin(angles)
    return wave_x, wave_y


def slab_left_table(rows, halo, orient):
    offset = (
        np.arange(rows + 2 * halo, dtype=np.float32)[None, :]
        - np.float32(halo)
        - np.arange(rows, dtype=np.float32)[:, None]
    )
    wave_y = waves(orient)[1]
    phase = wave_y[:, None, None] * offset[None]
    envelope = envelope_of(offset)[None]
    table = np.stack([envelope * np.cos(phase), envelope * np.sin(phase)], axis=1)
    return table.reshape(orient * 2 * rows, rows + 2 * halo).astype(jnp.bfloat16)


def make_right_table(quarter, orient):
    position = np.arange(quarter, dtype=np.float32)
    offset = position[:, None] - position[None, :]
    wave_x = waves(orient)[0]
    phase_x = wave_x[:, None, None] * offset[None]
    envelope = envelope_of(offset)[None]
    real_part = envelope * np.cos(phase_x)
    imag_part = envelope * np.sin(phase_x)
    upper_half = np.concatenate([real_part, imag_part], axis=2)
    lower_half = np.concatenate([-imag_part, real_part], axis=2)
    return np.concatenate([upper_half, lower_half], axis=1).astype(jnp.bfloat16)


def down_sums(full_size, quarter):
    position = np.arange(quarter, dtype=np.float32)[:, None]
    columns = np.arange(full_size, dtype=np.float32)[None, :]
    offset_grid = columns - np.float32(4.0) * position - np.float32(1.5)
    weight = np.exp(-offset_grid * offset_grid / np.float32(2.0 * blur_sigma * blur_sigma))
    return np.sum(weight, axis=1)


def down_block(position, column, shape, axis, sums):
    positions = position + lax.broadcasted_iota(jnp.int32, shape, 1 - axis)
    columns = column + lax.broadcasted_iota(jnp.int32, shape, axis)
    offset_grid = columns.astype(jnp.float32) - 4.0 * positions.astype(jnp.float32) - 1.5
    weight = jnp.exp(-offset_grid * offset_grid / (2.0 * blur_sigma * blur_sigma))
    inner = float(sums[len(sums) // 2])
    line = position + lax.broadcasted_iota(jnp.int32, tuple(1 if i == axis else n for i, n in enumerate(shape)), 1 - axis)
    scale = jnp.full(line.shape, 1.0 / inner, jnp.float32)
    for q in range(position, min(position + shape[1 - axis], len(sums))):
        if abs(float(sums[q]) - inner) > 1e-7 * inner:
            scale = jnp.where(line == q, 1.0 / float(sums[q]), scale)
    return (weight * scale).astype(jnp.bfloat16)


def build_down(down_t_ref, down_ref):
    size, quarter = down_t_ref.shape
    sums = down_sums(size, quarter)
    lanes = min(128, quarter)
    down_t_ref[...] = jnp.zeros_like(down_t_ref)
    down_ref[...] = jnp.zeros_like(down_ref)
    for row in range(0, size, 128):
        for lane in range(0, quarter, lanes):
            if 4 * (lane + lanes - 1) + 30 >= row and 4 * lane - 27 <= row + 127:
                down_t_ref[row : row + 128, lane : lane + lanes] = down_block(lane, row, (128, lanes), 0, sums)
    for row in range(0, quarter, 32):
        for lane in range(0, size, 128):
            if 4 * (row + 31) + 30 >= lane and 4 * row - 27 <= lane + 127:
                down_ref[row : row + 32, lane : lane + 128] = down_block(row, lane, (32, 128), 1, sums)


def reduce_kernel(frames_ref, *refs, shifts, rows, halo, block):
    out_refs = refs[:shifts]
    picture_ref, down_t_ref, down_ref, total_ref, padded_ref, sems = refs[shifts:]
    count, size, _ = picture_ref.shape
    quarter = down_ref.shape[0]

    copies = []
    for f in range(count):
        for i in range(size // block):
            here = pl.ds(i * block, block)
            copy = pltpu.make_async_copy(frames_ref.at[f, here], picture_ref.at[f, here], sems.at[f, i])
            copy.start()
            copies.append(copy)
    build_down(down_t_ref, down_ref)
    edge = jnp.zeros((halo, quarter), jnp.bfloat16)
    padded_ref[0:halo] = edge
    padded_ref[halo + quarter :] = edge

    me = lax.axis_index("slab")
    reach = block // 4
    for f in range(count):
        total_ref[...] = jnp.zeros_like(total_ref)
        for i in range(size // block):
            copies[f * (size // block) + i].wait()
            half = jnp.dot(
                picture_ref[f, i * block : (i + 1) * block], down_t_ref[...], preferred_element_type=jnp.float32
            ).astype(jnp.bfloat16)
            near = slice(max(i * reach - TILE, 0), min((i + 1) * reach + TILE, quarter))
            total_ref[near] += jnp.dot(
                down_ref[near, i * block : (i + 1) * block], half, preferred_element_type=jnp.float32
            )
        padded_ref[halo : halo + quarter] = total_ref[...].astype(jnp.bfloat16)
        for shift, out_ref in enumerate(out_refs):
            slab = lax.rem(me + shift, shifts)
            out_ref[f] = padded_ref[pl.ds(pl.multiple_of(slab * rows, rows), rows + 2 * halo)]


def reduce_frames(video_frames, slabs, rows, halo):
    count, size, _ = video_frames.shape
    quarter = slabs * rows
    block = size // 4
    out = jax.ShapeDtypeStruct((count, rows + 2 * halo, quarter), jnp.bfloat16)
    return pl.pallas_call(
        functools.partial(reduce_kernel, shifts=slabs, rows=rows, halo=halo, block=block),
        in_specs=[pl.BlockSpec(memory_space=pltpu.HBM)],
        out_specs=[pl.BlockSpec(memory_space=pltpu.VMEM)] * slabs,
        out_shape=[out] * slabs,
        scratch_shapes=[
            pltpu.VMEM((count, size, size), jnp.bfloat16),
            pltpu.VMEM((size, quarter), jnp.bfloat16),
            pltpu.VMEM((quarter, size), jnp.bfloat16),
            pltpu.VMEM((quarter, quarter), jnp.float32),
            pltpu.VMEM((quarter + 2 * halo, quarter), jnp.bfloat16),
            pltpu.SemaphoreType.DMA((count, size // block)),
        ],
        compiler_params=pltpu.CompilerParams(vmem_limit_bytes=52 * MIB),
        cost_estimate=pl.CostEstimate(
            flops=2 * count * size * quarter * (size + quarter),
            bytes_accessed=2 * count * size * size,
            transcendentals=0,
        ),
    )(video_frames)


def cut_kernel(*refs, rows):
    in_refs, (mine_ref, other_ref) = refs[1:-2], refs[-2:]
    slabs, _, window, _ = mine_ref.shape
    me, core = lax.axis_index("slab"), lax.axis_index("core")
    for shift, in_ref in enumerate(in_refs):
        chip = lax.rem(me - shift + slabs, slabs)
        mine_ref[chip] = in_ref[:, pl.ds(pl.multiple_of(core * rows, rows), window)]
        other_ref[chip] = in_ref[:, pl.ds(pl.multiple_of((1 - core) * rows, rows), window)]


def cut_windows(ref_frames, pieces, rows):
    count, window, quarter = pieces[0].shape
    out = jax.ShapeDtypeStruct((len(pieces), count, window - rows, quarter), jnp.bfloat16)
    return pl.pallas_call(
        functools.partial(cut_kernel, rows=rows),
        in_specs=[pl.BlockSpec(memory_space=pltpu.SMEM)] + [pl.BlockSpec(memory_space=pltpu.VMEM)] * len(pieces),
        out_specs=[pl.BlockSpec(memory_space=pltpu.VMEM)] * 2,
        out_shape=[out, out],
        compiler_params=pltpu.CompilerParams(vmem_limit_bytes=16 * MIB),
        cost_estimate=pl.CostEstimate(flops=0, bytes_accessed=8 * out.size, transcendentals=0),
    )(ref_frames, *pieces)


def time_kernel(segments_ref, pick_ref, taps_ref, spread_ref, frame_ref, *, history, frames, rows):
    chunk, timed = spread_ref.shape[0] // rows, spread_ref.shape[1] // rows
    nseg = pick_ref.shape[0]
    taps = taps_ref.shape[0]
    wide_out, wide_in = chunk * rows, timed * rows

    def count_one(t, totals):
        here = segments_ref[t]
        below = [total + (here < s).astype(jnp.int32) for s, total in enumerate(totals[0])]
        same = [total + (here == s).astype(jnp.int32) for s, total in enumerate(totals[1])]
        return tuple(below), tuple(same)

    zeros = tuple(jnp.int32(0) for _ in range(nseg))
    starts, counts = lax.fori_loop(0, frames, count_one, (zeros, zeros), unroll=8)
    for s in range(nseg):
        frame_ref[s] = starts[s] + lax.rem(pick_ref[s], counts[s])

    lag = history + lax.broadcasted_iota(jnp.int32, (chunk, timed), 0) - lax.broadcasted_iota(
        jnp.int32, (chunk, timed), 1
    )
    if history:
        first = lax.axis_index("chunk") * chunk - history
        real = first + lax.broadcasted_iota(jnp.int32, (chunk, timed), 1) >= 0
        lag = jnp.where(real, lag, -1)
    matrix = jnp.zeros((chunk, timed), jnp.float32)
    for k in range(taps):
        matrix = jnp.where(lag == k, taps_ref[k], matrix)
    repeat_left = (
        lax.broadcasted_iota(jnp.int32, (wide_out, chunk), 0) // rows
        == lax.broadcasted_iota(jnp.int32, (wide_out, chunk), 1)
    ).astype(jnp.bfloat16)
    repeat_right = (
        lax.broadcasted_iota(jnp.int32, (timed, wide_in), 1) // rows
        == lax.broadcasted_iota(jnp.int32, (timed, wide_in), 0)
    ).astype(jnp.bfloat16)
    tall = jnp.dot(repeat_left, matrix.astype(jnp.bfloat16), preferred_element_type=jnp.float32)
    tall = tall.astype(jnp.bfloat16)
    piece = min(128, wide_out)
    for start in range(0, wide_out, piece):
        part = jnp.dot(tall[start : start + piece], repeat_right, preferred_element_type=jnp.float32)
        same_row = (
            lax.broadcasted_iota(jnp.int32, (piece, wide_in), 0) % rows
            == lax.broadcasted_iota(jnp.int32, (piece, wide_in), 1) % rows
        )
        spread_ref[start : start + piece] = jnp.where(same_row, part, 0.0).astype(jnp.bfloat16)


def time_tables(segments, ref_pick, band_taps, rows, chunk, history):
    frames = segments.shape[0]
    wide_out, wide_in = chunk * rows, (history + chunk) * rows
    smem = pl.BlockSpec(memory_space=pltpu.SMEM)
    return pl.pallas_call(
        functools.partial(time_kernel, history=history, frames=frames, rows=rows),
        in_specs=[smem] * 3,
        out_specs=[pl.BlockSpec(memory_space=pltpu.VMEM), smem],
        out_shape=[
            jax.ShapeDtypeStruct((wide_out, wide_in), jnp.bfloat16),
            jax.ShapeDtypeStruct(ref_pick.shape, jnp.int32),
        ],
        compiler_params=pltpu.CompilerParams(vmem_limit_bytes=16 * MIB),
        cost_estimate=pl.CostEstimate(
            flops=2 * wide_out * wide_in * chunk, bytes_accessed=2 * wide_out * wide_in, transcendentals=0
        ),
    )(segments, ref_pick, band_taps.astype(jnp.float32))


def filter_frames(window_refs, left_ref, right_ref, stacked_ref, put):
    rows = left_ref.shape[0] // (2 * right_ref.shape[0])
    orient, both, _ = right_ref.shape
    quarter = both // 2
    for n, window in enumerate(window_refs):
        stacked = jnp.dot(left_ref[...], window[...], preferred_element_type=jnp.float32).astype(jnp.bfloat16)
        for o in range(orient):
            for z in range(2):
                begin = (o * 2 + z) * rows
                stacked_ref[o, n * rows : (n + 1) * rows, z * quarter : (z + 1) * quarter] = stacked[begin : begin + rows]
    many = len(window_refs) * rows
    step = min(256, many)
    pair = 2 * rows
    for o in range(orient):
        for start in range(0, many, step):
            stop = min(start + step, many)
            coeff = jnp.dot(stacked_ref[o, start:stop], right_ref[o], preferred_element_type=jnp.float32)
            coeff = coeff.astype(jnp.bfloat16)
            for place in range(start, stop, pair):
                put(o, place // pair, coeff[place - start : place - start + pair])


def coeff_kernel(window_ref, left_ref, right_ref, coeff_ref, stacked_ref):
    chips, frames_here, window, quarter = window_ref.shape
    rows = left_ref.shape[0] // (2 * right_ref.shape[0])

    def put(o, i, block):
        coeff_ref[o, 2 * i * rows : 2 * (i + 1) * rows] = block

    filter_frames(
        [window_ref.at[chip, f] for chip in range(chips) for f in range(frames_here)], left_ref, right_ref, stacked_ref, put
    )


def own_coeffs(windows, left, right, rows):
    chips, frames_here, _, quarter = windows.shape
    vmem = pl.BlockSpec(memory_space=pltpu.VMEM)
    out = jax.ShapeDtypeStruct((ORIENT, chips * frames_here * rows, 2 * quarter), jnp.bfloat16)
    return pl.pallas_call(
        coeff_kernel,
        in_specs=[vmem] * 3,
        out_specs=vmem,
        out_shape=out,
        scratch_shapes=[pltpu.VMEM(out.shape, jnp.bfloat16)],
        compiler_params=pltpu.CompilerParams(vmem_limit_bytes=8 * out.size + 16 * MIB),
        cost_estimate=pl.CostEstimate(
            flops=8 * out.size * quarter, bytes_accessed=2 * (windows.size + out.size), transcendentals=0
        ),
    )(windows, left, right)


def pixel_kernel(
    segments_ref, ref_frame_ref, spread_ref, mine_ref, other_ref, refer_ref, left_ref, right_ref, out_ref,
    stacked_ref, coeff_ref, phase_ref, *, history, whole,
):
    chips, frames_here, _, quarter = other_ref.shape
    chunk, rows, _ = out_ref.shape
    orient = right_ref.shape[0]
    nseg = ref_frame_ref.shape[0]
    both = 2 * quarter
    timed = history + chunk
    wide_out = chunk * rows
    pair = frames_here * rows
    core = lax.axis_index("core")

    for chip in range(chips):
        place = pl.ds(pl.multiple_of((chip * CORES + core) * pair, pair), pair)
        for o in range(orient):
            coeff_ref[o, place] = mine_ref[o, chip * pair : (chip + 1) * pair]

    def put(o, i, block):
        if i < chips:
            coeff_ref[o, pl.ds(pl.multiple_of((i * CORES + 1 - core) * pair, pair), pair)] = block
        else:
            begin = timed * rows + (i - chips) * pair
            coeff_ref[o, begin : begin + pair] = block

    windows = [other_ref.at[chip, f] for chip in range(chips) for f in range(frames_here)]
    if not whole:
        windows += [refer_ref.at[s] for s in range(nseg)]
    filter_frames(windows, left_ref, right_ref, stacked_ref, put)

    def phase_one(slot, carry):
        place = pl.ds(pl.multiple_of(slot * rows, rows), rows)
        if whole:
            source = ref_frame_ref[segments_ref[slot]]
        else:
            first = lax.axis_index("chunk") * chunk - history
            source = timed + segments_ref[jnp.maximum(first + slot, 0)]
        refer = pl.ds(pl.multiple_of(source * rows, rows), rows)
        for o in range(orient):
            coeff_real = coeff_ref[o, place, 0:quarter].astype(jnp.float32)
            coeff_imag = coeff_ref[o, place, quarter:both].astype(jnp.float32)
            ref_real = coeff_ref[o, refer, 0:quarter].astype(jnp.float32)
            ref_imag = coeff_ref[o, refer, quarter:both].astype(jnp.float32)
            prod_real = coeff_real * ref_real + coeff_imag * ref_imag
            prod_imag = coeff_imag * ref_real - coeff_real * ref_imag
            square = prod_real * prod_real + prod_imag * prod_imag + 1.0
            phase_ref[o, place] = (prod_imag * lax.rsqrt(square)).astype(jnp.bfloat16)
        return carry

    lax.fori_loop(0, timed, phase_one, 0, unroll=2)

    piece = min(128, wide_out)
    for start in range(0, wide_out, piece):
        here = slice(history * rows + start, history * rows + start + piece)
        above = jnp.zeros((piece, quarter), jnp.float32)
        below = jnp.ones((piece, quarter), jnp.float32)
        for o in range(orient):
            filtered = jnp.dot(
                spread_ref[start : start + piece], phase_ref[o], preferred_element_type=jnp.float32
            )
            filtered = filtered.astype(jnp.bfloat16).astype(jnp.float32)
            coeff_real = coeff_ref[o, here, 0:quarter].astype(jnp.float32)
            coeff_imag = coeff_ref[o, here, quarter:both].astype(jnp.float32)
            amplitude = coeff_real * coeff_real + coeff_imag * coeff_imag
            above = above + amplitude * filtered
            below = below + amplitude
        motion = (above / below).astype(out_ref.dtype)
        for i in range(piece // rows):
            out_ref[start // rows + i] = motion[i * rows : (i + 1) * rows]


def pixel_motion(segments, ref_frames, spread, mine, other, refer, left, right, rows, chunk, history):
    chips, frames_here, _, quarter = other.shape
    timed = history + chunk
    whole = refer is None
    slots = timed if whole else timed + NSEG
    smem = pl.BlockSpec(memory_space=pltpu.SMEM)
    vmem = pl.BlockSpec(memory_space=pltpu.VMEM)
    slot_bytes = ORIENT * rows * 2 * quarter * 2
    return pl.pallas_call(
        functools.partial(pixel_kernel, history=history, whole=whole),
        in_specs=[smem] * 2 + [vmem] * 6,
        out_specs=vmem,
        out_shape=jax.ShapeDtypeStruct((chunk, rows, quarter), jnp.bfloat16),
        scratch_shapes=[
            pltpu.VMEM((ORIENT, (slots - timed // 2) * rows, 2 * quarter), jnp.bfloat16),
            pltpu.VMEM((ORIENT, slots * rows, 2 * quarter), jnp.bfloat16),
            pltpu.VMEM((ORIENT, timed * rows, quarter), jnp.bfloat16),
        ],
        compiler_params=pltpu.CompilerParams(vmem_limit_bytes=4 * slots * slot_bytes + 16 * MIB),
        cost_estimate=pl.CostEstimate(
            flops=2 * ORIENT * rows * quarter * (slots * 2 * quarter + chunk * timed * rows),
            bytes_accessed=2 * (other.size + mine.size + right.size),
            transcendentals=ORIENT * timed * rows * quarter,
        ),
    )(segments, ref_frames, spread, mine, other, other if whole else refer, left, right)


def chunk_windows(mine, other, ref_frames, history_chips, chips):
    mine = lax.all_gather(mine, "chunk", axis=0, tiled=True)
    other = lax.all_gather(other, "chunk", axis=0, tiled=True)
    frames_here = mine.shape[1]
    core = lax.axis_index("core")
    device = ref_frames // frames_here
    place = device // CORES * frames_here + ref_frames % frames_here
    own = (device % CORES == core)[:, None, None]
    flat = (-1,) + mine.shape[2:]
    refer = jnp.where(own, mine.reshape(flat)[place], other.reshape(flat)[place])

    def cut(windows):
        before = jnp.zeros((history_chips,) + windows.shape[1:], windows.dtype)
        windows = jnp.concatenate([before, windows])
        return lax.dynamic_slice_in_dim(windows, lax.axis_index("chunk") * chips, history_chips + chips)

    return cut(mine), cut(other), refer


def body(video_frames, segments, ref_pick, band_taps, *, chunks, slabs):
    frames_here, size, _ = video_frames.shape
    quarter = size // 4
    slab_rows = quarter // slabs
    rows = slab_rows // CORES
    chunk = slabs * CORES * frames_here
    history = min(chunk * -(-(band_taps.shape[0] - 1) // chunk), segments.shape[0] - chunk)
    left = jnp.asarray(slab_left_table(rows, HALO, ORIENT))
    right = jnp.asarray(make_right_table(quarter, ORIENT))
    windows = reduce_frames(video_frames, slabs, slab_rows, HALO)
    spread, ref_frames = time_tables(segments, ref_pick, band_taps, rows, chunk, history)
    pieces = [windows[0]] * slabs
    for shift in sorted(range(1, slabs), key=lambda s: abs(s - slabs // 2)):
        ring = [(chip, (chip + shift) % slabs) for chip in range(slabs)]
        pieces[shift] = lax.ppermute(windows[shift], "slab", ring)
    mine, other = cut_windows(ref_frames, pieces, rows)
    other = lax.ppermute(other, "core", [(0, 1), (1, 0)])
    refer = None
    if chunks > 1:
        mine, other, refer = chunk_windows(mine, other, ref_frames, history // (CORES * frames_here), slabs)
    mine = own_coeffs(mine, left, right, rows)
    motion = pixel_motion(segments, ref_frames, spread, mine, other, refer, left, right, rows, chunk, history)
    motion = motion.reshape(slabs * CORES, frames_here, rows, quarter)
    motion = lax.all_to_all(motion, ("slab", "core"), split_axis=0, concat_axis=0, tiled=True)
    motion = jnp.swapaxes(motion, 0, 1).reshape(frames_here, quarter, quarter)
    return motion.astype(jnp.float32)


def solution(mesh):
    chips = mesh.shape["frames"] // CORES
    slabs = min(chips, QUART // (CORES * TILE))
    chunks = chips // slabs
    names = ("groups", "chunk", "slab", "core")
    cut = jax.sharding.Mesh(mesh.devices.reshape(mesh.shape["groups"], chunks, slabs, CORES), names)
    in_specs = (P(names, None, None), P("groups"), P("groups"), P())
    return jax.shard_map(
        functools.partial(body, chunks=chunks, slabs=slabs),
        mesh=cut, in_specs=in_specs, out_specs=P(names, None, None), check_vma=False,
    )
```

```python
import functools
import math

import jax
import jax.numpy as jnp
import numpy as np
from jax import lax
from jax.experimental import pallas as pl
from jax.experimental.pallas import tpu as pltpu
from jax.sharding import PartitionSpec as P

IMG = 1024
ORIENT = 4
NSEG = 4
QUART = 256


blur_sigma = 2.0
gabor_sigma = 2.0
wave_number = math.pi / 2.0
gabor_gain = 2.0

HALO = 32
TILE = 16
CORES = 2
MIB = 1024 * 1024


def envelope_of(offset_grid):
    return np.float32(gabor_gain) * np.exp(
        -offset_grid * offset_grid / np.float32(2.0 * gabor_sigma * gabor_sigma)
    )


def waves(orient):
    angles = np.arange(orient, dtype=np.float32) * np.float32(math.pi / orient)
    wave_x = np.float32(wave_number) * np.cos(angles)
    wave_y = np.float32(wave_number) * np.sin(angles)
    return wave_x, wave_y


def slab_left_table(rows, halo, orient):
    offset = (
        np.arange(rows + 2 * halo, dtype=np.float32)[None, :]
        - np.float32(halo)
        - np.arange(rows, dtype=np.float32)[:, None]
    )
    wave_y = waves(orient)[1]
    phase = wave_y[:, None, None] * offset[None]
    envelope = envelope_of(offset)[None]
    table = np.stack([envelope * np.cos(phase), envelope * np.sin(phase)], axis=1)
    return table.reshape(orient * 2 * rows, rows + 2 * halo).astype(jnp.bfloat16)


def make_right_table(quarter, orient):
    position = np.arange(quarter, dtype=np.float32)
    offset = position[:, None] - position[None, :]
    wave_x = waves(orient)[0]
    phase_x = wave_x[:, None, None] * offset[None]
    envelope = envelope_of(offset)[None]
    real_part = envelope * np.cos(phase_x)
    imag_part = envelope * np.sin(phase_x)
    upper_half = np.concatenate([real_part, imag_part], axis=2)
    lower_half = np.concatenate([-imag_part, real_part], axis=2)
    return np.concatenate([upper_half, lower_half], axis=1).astype(jnp.bfloat16)


def down_sums(full_size, quarter):
    position = np.arange(quarter, dtype=np.float32)[:, None]
    columns = np.arange(full_size, dtype=np.float32)[None, :]
    offset_grid = columns - np.float32(4.0) * position - np.float32(1.5)
    weight = np.exp(-offset_grid * offset_grid / np.float32(2.0 * blur_sigma * blur_sigma))
    return np.sum(weight, axis=1)


def down_block(position, column, shape, axis, sums):
    positions = position + lax.broadcasted_iota(jnp.int32, shape, 1 - axis)
    columns = column + lax.broadcasted_iota(jnp.int32, shape, axis)
    offset_grid = columns.astype(jnp.float32) - 4.0 * positions.astype(jnp.float32) - 1.5
    weight = jnp.exp(-offset_grid * offset_grid / (2.0 * blur_sigma * blur_sigma))
    inner = float(sums[len(sums) // 2])
    line = position + lax.broadcasted_iota(jnp.int32, tuple(1 if i == axis else n for i, n in enumerate(shape)), 1 - axis)
    scale = jnp.full(line.shape, 1.0 / inner, jnp.float32)
    for q in range(position, min(position + shape[1 - axis], len(sums))):
        if abs(float(sums[q]) - inner) > 1e-7 * inner:
            scale = jnp.where(line == q, 1.0 / float(sums[q]), scale)
    return (weight * scale).astype(jnp.bfloat16)


def build_down(down_t_ref, down_ref):
    size, quarter = down_t_ref.shape
    sums = down_sums(size, quarter)
    lanes = min(128, quarter)
    down_t_ref[...] = jnp.zeros_like(down_t_ref)
    down_ref[...] = jnp.zeros_like(down_ref)
    for row in range(0, size, 128):
        for lane in range(0, quarter, lanes):
            if 4 * (lane + lanes - 1) + 30 >= row and 4 * lane - 27 <= row + 127:
                down_t_ref[row : row + 128, lane : lane + lanes] = down_block(lane, row, (128, lanes), 0, sums)
    for row in range(0, quarter, 32):
        for lane in range(0, size, 128):
            if 4 * (row + 31) + 30 >= lane and 4 * row - 27 <= lane + 127:
                down_ref[row : row + 32, lane : lane + 128] = down_block(row, lane, (32, 128), 1, sums)


def reduce_kernel(frames_ref, *refs, shifts, rows, halo, block):
    out_refs = refs[:shifts]
    picture_ref, down_t_ref, down_ref, half_ref, total_ref, padded_ref, sems = refs[shifts:]
    count, size, _ = picture_ref.shape
    quarter = down_ref.shape[0]

    copies = []
    for f in range(count):
        for i in range(size // block):
            here = pl.ds(i * block, block)
            copy = pltpu.make_async_copy(frames_ref.at[f, here], picture_ref.at[f, here], sems.at[f, i])
            copy.start()
            copies.append(copy)
    build_down(down_t_ref, down_ref)
    edge = jnp.zeros((halo, quarter), jnp.bfloat16)
    padded_ref[0:halo] = edge
    padded_ref[halo + quarter :] = edge

    me = lax.axis_index("slab")
    reach = quarter
    for f in range(count):
        total_ref[...] = jnp.zeros_like(total_ref)
        for i in range(size // block):
            copies[f * (size // block) + i].wait()
            half_ref[...] = jnp.dot(
                picture_ref[f, i * block : (i + 1) * block], down_t_ref[...], preferred_element_type=jnp.float32
            ).astype(jnp.bfloat16)
            for row in range(0, block, reach):
                begin = i * block + row
                near = slice(max(begin // 4 - TILE, 0), min((begin + reach) // 4 + TILE, quarter))
                total_ref[near] += jnp.dot(
                    down_ref[near, begin : begin + reach], half_ref[row : row + reach], preferred_element_type=jnp.float32
                )
        padded_ref[halo : halo + quarter] = total_ref[...].astype(jnp.bfloat16)
        for shift, out_ref in enumerate(out_refs):
            slab = lax.bitwise_xor(me, shift)
            out_ref[f] = padded_ref[pl.ds(pl.multiple_of(slab * rows, rows), rows + 2 * halo)]


def reduce_frames(video_frames, slabs, rows, halo):
    count, size, _ = video_frames.shape
    quarter = slabs * rows
    block = size // 2
    out = jax.ShapeDtypeStruct((count, rows + 2 * halo, quarter), jnp.bfloat16)
    return pl.pallas_call(
        functools.partial(reduce_kernel, shifts=slabs, rows=rows, halo=halo, block=block),
        in_specs=[pl.BlockSpec(memory_space=pltpu.HBM)],
        out_specs=[pl.BlockSpec(memory_space=pltpu.VMEM)] * slabs,
        out_shape=[out] * slabs,
        scratch_shapes=[
            pltpu.VMEM((count, size, size), jnp.bfloat16),
            pltpu.VMEM((size, quarter), jnp.bfloat16),
            pltpu.VMEM((quarter, size), jnp.bfloat16),
            pltpu.VMEM((block, quarter), jnp.bfloat16),
            pltpu.VMEM((quarter, quarter), jnp.float32),
            pltpu.VMEM((quarter + 2 * halo, quarter), jnp.bfloat16),
            pltpu.SemaphoreType.DMA((count, size // block)),
        ],
        compiler_params=pltpu.CompilerParams(vmem_limit_bytes=52 * MIB),
        cost_estimate=pl.CostEstimate(
            flops=2 * count * size * quarter * (size + quarter),
            bytes_accessed=2 * count * size * size,
            transcendentals=0,
        ),
    )(video_frames)


def cut_kernel(*refs, rows):
    in_refs, (mine_ref, other_ref) = refs[1:-2], refs[-2:]
    window = mine_ref.shape[2]
    me, core = lax.axis_index("slab"), lax.axis_index("core")
    for shift, in_ref in enumerate(in_refs):
        chip = lax.bitwise_xor(me, shift)
        mine_ref[chip] = in_ref[:, pl.ds(pl.multiple_of(core * rows, rows), window)]
        other_ref[chip] = in_ref[:, pl.ds(pl.multiple_of((1 - core) * rows, rows), window)]


def cut_windows(ref_frames, pieces, rows):
    count, window, quarter = pieces[0].shape
    out = jax.ShapeDtypeStruct((len(pieces), count, window - rows, quarter), jnp.bfloat16)
    return pl.pallas_call(
        functools.partial(cut_kernel, rows=rows),
        in_specs=[pl.BlockSpec(memory_space=pltpu.SMEM)] + [pl.BlockSpec(memory_space=pltpu.VMEM)] * len(pieces),
        out_specs=[pl.BlockSpec(memory_space=pltpu.VMEM)] * 2,
        out_shape=[out, out],
        compiler_params=pltpu.CompilerParams(vmem_limit_bytes=16 * MIB),
        cost_estimate=pl.CostEstimate(flops=0, bytes_accessed=8 * out.size, transcendentals=0),
    )(ref_frames, *pieces)


def time_kernel(segments_ref, pick_ref, taps_ref, spread_ref, frame_ref, *, history, frames, rows):
    chunk, timed = spread_ref.shape[0] // rows, spread_ref.shape[1] // rows
    nseg = pick_ref.shape[0]
    taps = taps_ref.shape[0]
    wide_out, wide_in = chunk * rows, timed * rows

    def count_one(t, totals):
        here = segments_ref[t]
        below = [total + (here < s).astype(jnp.int32) for s, total in enumerate(totals[0])]
        same = [total + (here == s).astype(jnp.int32) for s, total in enumerate(totals[1])]
        return tuple(below), tuple(same)

    zeros = tuple(jnp.int32(0) for _ in range(nseg))
    starts, counts = lax.fori_loop(0, frames, count_one, (zeros, zeros), unroll=8)
    for s in range(nseg):
        frame_ref[s] = starts[s] + lax.rem(pick_ref[s], counts[s])

    lag = history + lax.broadcasted_iota(jnp.int32, (chunk, timed), 0) - lax.broadcasted_iota(
        jnp.int32, (chunk, timed), 1
    )
    if history:
        first = lax.axis_index("chunk") * chunk - history
        real = first + lax.broadcasted_iota(jnp.int32, (chunk, timed), 1) >= 0
        lag = jnp.where(real, lag, -1)
    matrix = jnp.zeros((chunk, timed), jnp.float32)
    for k in range(taps):
        matrix = jnp.where(lag == k, taps_ref[k], matrix)
    repeat_left = (
        lax.broadcasted_iota(jnp.int32, (wide_out, chunk), 0) // rows
        == lax.broadcasted_iota(jnp.int32, (wide_out, chunk), 1)
    ).astype(jnp.bfloat16)
    repeat_right = (
        lax.broadcasted_iota(jnp.int32, (timed, wide_in), 1) // rows
        == lax.broadcasted_iota(jnp.int32, (timed, wide_in), 0)
    ).astype(jnp.bfloat16)
    tall = jnp.dot(repeat_left, matrix.astype(jnp.bfloat16), preferred_element_type=jnp.float32)
    tall = tall.astype(jnp.bfloat16)
    piece = min(128, wide_out)
    for start in range(0, wide_out, piece):
        part = jnp.dot(tall[start : start + piece], repeat_right, preferred_element_type=jnp.float32)
        same_row = (
            lax.broadcasted_iota(jnp.int32, (piece, wide_in), 0) % rows
            == lax.broadcasted_iota(jnp.int32, (piece, wide_in), 1) % rows
        )
        spread_ref[start : start + piece] = jnp.where(same_row, part, 0.0).astype(jnp.bfloat16)


def time_tables(segments, ref_pick, band_taps, rows, chunk, history):
    frames = segments.shape[0]
    wide_out, wide_in = chunk * rows, (history + chunk) * rows
    smem = pl.BlockSpec(memory_space=pltpu.SMEM)
    return pl.pallas_call(
        functools.partial(time_kernel, history=history, frames=frames, rows=rows),
        in_specs=[smem] * 3,
        out_specs=[pl.BlockSpec(memory_space=pltpu.VMEM), smem],
        out_shape=[
            jax.ShapeDtypeStruct((wide_out, wide_in), jnp.bfloat16),
            jax.ShapeDtypeStruct(ref_pick.shape, jnp.int32),
        ],
        compiler_params=pltpu.CompilerParams(vmem_limit_bytes=16 * MIB),
        cost_estimate=pl.CostEstimate(
            flops=2 * wide_out * wide_in * chunk, bytes_accessed=2 * wide_out * wide_in, transcendentals=0
        ),
    )(segments, ref_pick, band_taps.astype(jnp.float32))


def filter_frames(window_refs, left_ref, right_ref, stacked_ref, put):
    rows = left_ref.shape[0] // (2 * right_ref.shape[0])
    orient, both, _ = right_ref.shape
    quarter = both // 2
    for n, window in enumerate(window_refs):
        stacked = jnp.dot(left_ref[...], window[...], preferred_element_type=jnp.float32).astype(jnp.bfloat16)
        for o in range(orient):
            for z in range(2):
                begin = (o * 2 + z) * rows
                stacked_ref[o, n * rows : (n + 1) * rows, z * quarter : (z + 1) * quarter] = stacked[begin : begin + rows]
    many = len(window_refs) * rows
    step = min(256, many)
    pair = 2 * rows
    for o in range(orient):
        for start in range(0, many, step):
            stop = min(start + step, many)
            coeff = jnp.dot(stacked_ref[o, start:stop], right_ref[o], preferred_element_type=jnp.float32)
            coeff = coeff.astype(jnp.bfloat16)
            for place in range(start, stop, pair):
                put(o, place // pair, coeff[place - start : place - start + pair])


def coeff_kernel(window_ref, left_ref, right_ref, coeff_ref, stacked_ref):
    chips, frames_here, window, quarter = window_ref.shape
    rows = left_ref.shape[0] // (2 * right_ref.shape[0])

    def put(o, i, block):
        coeff_ref[o, 2 * i * rows : 2 * (i + 1) * rows] = block

    filter_frames(
        [window_ref.at[chip, f] for chip in range(chips) for f in range(frames_here)], left_ref, right_ref, stacked_ref, put
    )


def own_coeffs(windows, left, right, rows):
    chips, frames_here, _, quarter = windows.shape
    vmem = pl.BlockSpec(memory_space=pltpu.VMEM)
    out = jax.ShapeDtypeStruct((ORIENT, chips * frames_here * rows, 2 * quarter), jnp.bfloat16)
    return pl.pallas_call(
        coeff_kernel,
        in_specs=[vmem] * 3,
        out_specs=vmem,
        out_shape=out,
        scratch_shapes=[pltpu.VMEM(out.shape, jnp.bfloat16)],
        compiler_params=pltpu.CompilerParams(vmem_limit_bytes=8 * out.size + 16 * MIB),
        cost_estimate=pl.CostEstimate(
            flops=8 * out.size * quarter, bytes_accessed=2 * (windows.size + out.size), transcendentals=0
        ),
    )(windows, left, right)


def pixel_kernel(
    segments_ref, ref_frame_ref, spread_ref, mine_ref, other_ref, refer_ref, left_ref, right_ref, out_ref,
    stacked_ref, coeff_ref, phase_ref, *, history, whole,
):
    chips, frames_here, _, quarter = other_ref.shape
    chunk, rows, _ = out_ref.shape
    orient = right_ref.shape[0]
    nseg = ref_frame_ref.shape[0]
    both = 2 * quarter
    timed = history + chunk
    wide_out = chunk * rows
    pair = frames_here * rows
    core = lax.axis_index("core")

    for chip in range(chips):
        place = pl.ds(pl.multiple_of((chip * CORES + core) * pair, pair), pair)
        for o in range(orient):
            coeff_ref[o, place] = mine_ref[o, chip * pair : (chip + 1) * pair]

    def put(o, i, block):
        if i < chips:
            coeff_ref[o, pl.ds(pl.multiple_of((i * CORES + 1 - core) * pair, pair), pair)] = block
        else:
            begin = timed * rows + (i - chips) * pair
            coeff_ref[o, begin : begin + pair] = block

    windows = [other_ref.at[chip, f] for chip in range(chips) for f in range(frames_here)]
    if not whole:
        windows += [refer_ref.at[s] for s in range(nseg)]
    filter_frames(windows, left_ref, right_ref, stacked_ref, put)

    def phase_one(slot, carry):
        place = pl.ds(pl.multiple_of(slot * rows, rows), rows)
        if whole:
            source = ref_frame_ref[segments_ref[slot]]
        else:
            first = lax.axis_index("chunk") * chunk - history
            source = timed + segments_ref[jnp.maximum(first + slot, 0)]
        refer = pl.ds(pl.multiple_of(source * rows, rows), rows)
        for o in range(orient):
            coeff_real = coeff_ref[o, place, 0:quarter].astype(jnp.float32)
            coeff_imag = coeff_ref[o, place, quarter:both].astype(jnp.float32)
            ref_real = coeff_ref[o, refer, 0:quarter].astype(jnp.float32)
            ref_imag = coeff_ref[o, refer, quarter:both].astype(jnp.float32)
            prod_real = coeff_real * ref_real + coeff_imag * ref_imag
            prod_imag = coeff_imag * ref_real - coeff_real * ref_imag
            square = prod_real * prod_real + prod_imag * prod_imag + 1.0
            phase_ref[o, place] = (prod_imag * lax.rsqrt(square)).astype(jnp.bfloat16)
        return carry

    lax.fori_loop(0, timed, phase_one, 0, unroll=2)

    piece = min(128, wide_out)
    for start in range(0, wide_out, piece):
        here = slice(history * rows + start, history * rows + start + piece)
        above = jnp.zeros((piece, quarter), jnp.float32)
        below = jnp.ones((piece, quarter), jnp.float32)
        for o in range(orient):
            filtered = jnp.dot(
                spread_ref[start : start + piece], phase_ref[o], preferred_element_type=jnp.float32
            )
            filtered = filtered.astype(jnp.bfloat16).astype(jnp.float32)
            coeff_real = coeff_ref[o, here, 0:quarter].astype(jnp.float32)
            coeff_imag = coeff_ref[o, here, quarter:both].astype(jnp.float32)
            amplitude = coeff_real * coeff_real + coeff_imag * coeff_imag
            above = above + amplitude * filtered
            below = below + amplitude
        motion = (above / below).astype(out_ref.dtype)
        for i in range(piece // rows):
            out_ref[start // rows + i] = motion[i * rows : (i + 1) * rows]


def pixel_motion(segments, ref_frames, spread, mine, other, refer, left, right, rows, chunk, history):
    chips, frames_here, _, quarter = other.shape
    timed = history + chunk
    whole = refer is None
    slots = timed if whole else timed + NSEG
    smem = pl.BlockSpec(memory_space=pltpu.SMEM)
    vmem = pl.BlockSpec(memory_space=pltpu.VMEM)
    slot_bytes = ORIENT * rows * 2 * quarter * 2
    return pl.pallas_call(
        functools.partial(pixel_kernel, history=history, whole=whole),
        in_specs=[smem] * 2 + [vmem] * 6,
        out_specs=vmem,
        out_shape=jax.ShapeDtypeStruct((chunk, rows, quarter), jnp.bfloat16),
        scratch_shapes=[
            pltpu.VMEM((ORIENT, (slots - timed // 2) * rows, 2 * quarter), jnp.bfloat16),
            pltpu.VMEM((ORIENT, slots * rows, 2 * quarter), jnp.bfloat16),
            pltpu.VMEM((ORIENT, timed * rows, quarter), jnp.bfloat16),
        ],
        compiler_params=pltpu.CompilerParams(vmem_limit_bytes=4 * slots * slot_bytes + 16 * MIB),
        cost_estimate=pl.CostEstimate(
            flops=2 * ORIENT * rows * quarter * (slots * 2 * quarter + chunk * timed * rows),
            bytes_accessed=2 * (other.size + mine.size + right.size),
            transcendentals=ORIENT * timed * rows * quarter,
        ),
    )(segments, ref_frames, spread, mine, other, other if whole else refer, left, right)


def chunk_windows(mine, other, ref_frames, history_chips, chips):
    mine = lax.all_gather(mine, "chunk", axis=0, tiled=True)
    other = lax.all_gather(other, "chunk", axis=0, tiled=True)
    frames_here = mine.shape[1]
    core = lax.axis_index("core")
    device = ref_frames // frames_here
    place = device // CORES * frames_here + ref_frames % frames_here
    own = (device % CORES == core)[:, None, None]
    flat = (-1,) + mine.shape[2:]
    refer = jnp.where(own, mine.reshape(flat)[place], other.reshape(flat)[place])

    def cut(windows):
        before = jnp.zeros((history_chips,) + windows.shape[1:], windows.dtype)
        windows = jnp.concatenate([before, windows])
        return lax.dynamic_slice_in_dim(windows, lax.axis_index("chunk") * chips, history_chips + chips)

    return cut(mine), cut(other), refer


def body(video_frames, segments, ref_pick, band_taps, *, chunks, slabs):
    frames_here, size, _ = video_frames.shape
    quarter = size // 4
    slab_rows = quarter // slabs
    rows = slab_rows // CORES
    chunk = slabs * CORES * frames_here
    history = min(chunk * -(-(band_taps.shape[0] - 1) // chunk), segments.shape[0] - chunk)
    left = jnp.asarray(slab_left_table(rows, HALO, ORIENT))
    right = jnp.asarray(make_right_table(quarter, ORIENT))
    windows = reduce_frames(video_frames, slabs, slab_rows, HALO)
    spread, ref_frames = time_tables(segments, ref_pick, band_taps, rows, chunk, history)
    pieces = [windows[0]] * slabs
    order = [k for k in (1,) if k < slabs // 2] + list(range(slabs // 2, slabs)) + list(range(2, slabs // 2))
    for k in order:
        pieces[k] = lax.ppermute(windows[k], "slab", [(chip, chip ^ k) for chip in range(slabs)])
    mine, other = cut_windows(ref_frames, pieces, rows)
    other = lax.ppermute(other, "core", [(0, 1), (1, 0)])
    refer = None
    if chunks > 1:
        mine, other, refer = chunk_windows(mine, other, ref_frames, history // (CORES * frames_here), slabs)
    mine = own_coeffs(mine, left, right, rows)
    motion = pixel_motion(segments, ref_frames, spread, mine, other, refer, left, right, rows, chunk, history)
    motion = motion.reshape(slabs * CORES, frames_here, rows, quarter)
    motion = lax.all_to_all(motion, ("slab", "core"), split_axis=0, concat_axis=0, tiled=True)
    motion = jnp.swapaxes(motion, 0, 1).reshape(frames_here, quarter, quarter)
    return motion.astype(jnp.float32)


def solution(mesh):
    chips = mesh.shape["frames"] // CORES
    slabs = min(chips, QUART // (CORES * TILE))
    chunks = chips // slabs
    names = ("groups", "chunk", "slab", "core")
    cut = jax.sharding.Mesh(mesh.devices.reshape(mesh.shape["groups"], chunks, slabs, CORES), names)
    in_specs = (P(names, None, None), P("groups"), P("groups"), P())
    return jax.shard_map(
        functools.partial(body, chunks=chunks, slabs=slabs),
        mesh=cut, in_specs=in_specs, out_specs=P(names, None, None), check_vma=False,
    )
```

```python
import functools
import itertools
import math

import jax
import jax.numpy as jnp
import numpy as np
from jax import lax
from jax.experimental import pallas as pl
from jax.experimental.pallas import tpu as pltpu
from jax.sharding import PartitionSpec as P

IMG = 1024
ORIENT = 4
NSEG = 4
QUART = 256


blur_sigma = 2.0
gabor_sigma = 2.0
wave_number = math.pi / 2.0
gabor_gain = 2.0

HALO = 32
TILE = 16
CORES = 2
MIB = 1024 * 1024


def envelope_of(offset_grid):
    return np.float32(gabor_gain) * np.exp(
        -offset_grid * offset_grid / np.float32(2.0 * gabor_sigma * gabor_sigma)
    )


def waves(orient):
    angles = np.arange(orient, dtype=np.float32) * np.float32(math.pi / orient)
    wave_x = np.float32(wave_number) * np.cos(angles)
    wave_y = np.float32(wave_number) * np.sin(angles)
    return wave_x, wave_y


def slab_left_table(rows, halo, orient):
    offset = (
        np.arange(rows + 2 * halo, dtype=np.float32)[None, :]
        - np.float32(halo)
        - np.arange(rows, dtype=np.float32)[:, None]
    )
    wave_y = waves(orient)[1]
    phase = wave_y[:, None, None] * offset[None]
    envelope = envelope_of(offset)[None]
    table = np.stack([envelope * np.cos(phase), envelope * np.sin(phase)], axis=1)
    return table.reshape(orient * 2 * rows, rows + 2 * halo).astype(jnp.bfloat16)


def make_right_table(quarter, orient):
    position = np.arange(quarter, dtype=np.float32)
    offset = position[:, None] - position[None, :]
    wave_x = waves(orient)[0]
    phase_x = wave_x[:, None, None] * offset[None]
    envelope = envelope_of(offset)[None]
    real_part = envelope * np.cos(phase_x)
    imag_part = envelope * np.sin(phase_x)
    upper_half = np.concatenate([real_part, imag_part], axis=2)
    lower_half = np.concatenate([-imag_part, real_part], axis=2)
    return np.concatenate([upper_half, lower_half], axis=1).astype(jnp.bfloat16)


def down_sums(full_size, quarter):
    position = np.arange(quarter, dtype=np.float32)[:, None]
    columns = np.arange(full_size, dtype=np.float32)[None, :]
    offset_grid = columns - np.float32(4.0) * position - np.float32(1.5)
    weight = np.exp(-offset_grid * offset_grid / np.float32(2.0 * blur_sigma * blur_sigma))
    return np.sum(weight, axis=1)


def down_block(position, column, shape, axis, sums):
    positions = position + lax.broadcasted_iota(jnp.int32, shape, 1 - axis)
    columns = column + lax.broadcasted_iota(jnp.int32, shape, axis)
    offset_grid = columns.astype(jnp.float32) - 4.0 * positions.astype(jnp.float32) - 1.5
    weight = jnp.exp(-offset_grid * offset_grid / (2.0 * blur_sigma * blur_sigma))
    inner = float(sums[len(sums) // 2])
    line = position + lax.broadcasted_iota(jnp.int32, tuple(1 if i == axis else n for i, n in enumerate(shape)), 1 - axis)
    scale = jnp.full(line.shape, 1.0 / inner, jnp.float32)
    for q in range(position, min(position + shape[1 - axis], len(sums))):
        if abs(float(sums[q]) - inner) > 1e-7 * inner:
            scale = jnp.where(line == q, 1.0 / float(sums[q]), scale)
    return (weight * scale).astype(jnp.bfloat16)


def build_down(down_t_ref, down_ref):
    size, quarter = down_t_ref.shape
    sums = down_sums(size, quarter)
    lanes = min(128, quarter)
    down_t_ref[...] = jnp.zeros_like(down_t_ref)
    down_ref[...] = jnp.zeros_like(down_ref)
    for row in range(0, size, 128):
        for lane in range(0, quarter, lanes):
            if 4 * (lane + lanes - 1) + 30 >= row and 4 * lane - 27 <= row + 127:
                down_t_ref[row : row + 128, lane : lane + lanes] = down_block(lane, row, (128, lanes), 0, sums)
    for row in range(0, quarter, 32):
        for lane in range(0, size, 128):
            if 4 * (row + 31) + 30 >= lane and 4 * row - 27 <= lane + 127:
                down_ref[row : row + 32, lane : lane + 128] = down_block(row, lane, (32, 128), 1, sums)


def reduce_kernel(frames_ref, *refs, shifts, rows, halo, block):
    out_refs = refs[:shifts]
    picture_ref, down_t_ref, down_ref, half_ref, total_ref, padded_ref, sems = refs[shifts:]
    count, size, _ = picture_ref.shape
    quarter = down_ref.shape[0]

    copies = []
    for f in range(count):
        for i in range(size // block):
            here = pl.ds(i * block, block)
            copy = pltpu.make_async_copy(frames_ref.at[f, here], picture_ref.at[f, here], sems.at[f, i])
            copy.start()
            copies.append(copy)
    build_down(down_t_ref, down_ref)
    edge = jnp.zeros((halo, quarter), jnp.bfloat16)
    padded_ref[0:halo] = edge
    padded_ref[halo + quarter :] = edge

    me = lax.axis_index("slab")
    reach = quarter
    for f in range(count):
        total_ref[...] = jnp.zeros_like(total_ref)
        for i in range(size // block):
            copies[f * (size // block) + i].wait()
            half_ref[...] = jnp.dot(
                picture_ref[f, i * block : (i + 1) * block], down_t_ref[...], preferred_element_type=jnp.float32
            ).astype(jnp.bfloat16)
            for row in range(0, block, reach):
                begin = i * block + row
                near = slice(max(begin // 4 - TILE, 0), min((begin + reach) // 4 + TILE, quarter))
                total_ref[near] += jnp.dot(
                    down_ref[near, begin : begin + reach], half_ref[row : row + reach], preferred_element_type=jnp.float32
                )
        padded_ref[halo : halo + quarter] = total_ref[...].astype(jnp.bfloat16)
        for shift, out_ref in enumerate(out_refs):
            slab = lax.bitwise_xor(me, shift)
            out_ref[f] = padded_ref[pl.ds(pl.multiple_of(slab * rows, rows), rows + 2 * halo)]


def reduce_frames(video_frames, slabs, rows, halo):
    count, size, _ = video_frames.shape
    quarter = slabs * rows
    block = size // 2
    out = jax.ShapeDtypeStruct((count, rows + 2 * halo, quarter), jnp.bfloat16)
    return pl.pallas_call(
        functools.partial(reduce_kernel, shifts=slabs, rows=rows, halo=halo, block=block),
        in_specs=[pl.BlockSpec(memory_space=pltpu.HBM)],
        out_specs=[pl.BlockSpec(memory_space=pltpu.VMEM)] * slabs,
        out_shape=[out] * slabs,
        scratch_shapes=[
            pltpu.VMEM((count, size, size), jnp.bfloat16),
            pltpu.VMEM((size, quarter), jnp.bfloat16),
            pltpu.VMEM((quarter, size), jnp.bfloat16),
            pltpu.VMEM((block, quarter), jnp.bfloat16),
            pltpu.VMEM((quarter, quarter), jnp.float32),
            pltpu.VMEM((quarter + 2 * halo, quarter), jnp.bfloat16),
            pltpu.SemaphoreType.DMA((count, size // block)),
        ],
        compiler_params=pltpu.CompilerParams(vmem_limit_bytes=52 * MIB),
        cost_estimate=pl.CostEstimate(
            flops=2 * count * size * quarter * (size + quarter),
            bytes_accessed=2 * count * size * size,
            transcendentals=0,
        ),
    )(video_frames)


def cut_kernel(*refs, rows):
    in_refs, (mine_ref, other_ref) = refs[1:-2], refs[-2:]
    window = mine_ref.shape[2]
    me, core = lax.axis_index("slab"), lax.axis_index("core")
    for shift, in_ref in enumerate(in_refs):
        chip = lax.bitwise_xor(me, shift)
        mine_ref[chip] = in_ref[:, pl.ds(pl.multiple_of(core * rows, rows), window)]
        other_ref[chip] = in_ref[:, pl.ds(pl.multiple_of((1 - core) * rows, rows), window)]


def cut_windows(ref_frames, pieces, rows):
    count, window, quarter = pieces[0].shape
    out = jax.ShapeDtypeStruct((len(pieces), count, window - rows, quarter), jnp.bfloat16)
    return pl.pallas_call(
        functools.partial(cut_kernel, rows=rows),
        in_specs=[pl.BlockSpec(memory_space=pltpu.SMEM)] + [pl.BlockSpec(memory_space=pltpu.VMEM)] * len(pieces),
        out_specs=[pl.BlockSpec(memory_space=pltpu.VMEM)] * 2,
        out_shape=[out, out],
        compiler_params=pltpu.CompilerParams(vmem_limit_bytes=16 * MIB),
        cost_estimate=pl.CostEstimate(flops=0, bytes_accessed=8 * out.size, transcendentals=0),
    )(ref_frames, *pieces)


def time_kernel(segments_ref, pick_ref, taps_ref, spread_ref, frame_ref, *, history, frames, rows):
    chunk, timed = spread_ref.shape[0] // rows, spread_ref.shape[1] // rows
    nseg = pick_ref.shape[0]
    taps = taps_ref.shape[0]
    wide_out, wide_in = chunk * rows, timed * rows

    def count_one(t, totals):
        here = segments_ref[t]
        below = [total + (here < s).astype(jnp.int32) for s, total in enumerate(totals[0])]
        same = [total + (here == s).astype(jnp.int32) for s, total in enumerate(totals[1])]
        return tuple(below), tuple(same)

    zeros = tuple(jnp.int32(0) for _ in range(nseg))
    starts, counts = lax.fori_loop(0, frames, count_one, (zeros, zeros), unroll=8)
    for s in range(nseg):
        frame_ref[s] = starts[s] + lax.rem(pick_ref[s], counts[s])

    lag = history + lax.broadcasted_iota(jnp.int32, (chunk, timed), 0) - lax.broadcasted_iota(
        jnp.int32, (chunk, timed), 1
    )
    if history:
        first = lax.axis_index("chunk") * chunk - history
        real = first + lax.broadcasted_iota(jnp.int32, (chunk, timed), 1) >= 0
        lag = jnp.where(real, lag, -1)
    matrix = jnp.zeros((chunk, timed), jnp.float32)
    for k in range(taps):
        matrix = jnp.where(lag == k, taps_ref[k], matrix)
    repeat_left = (
        lax.broadcasted_iota(jnp.int32, (wide_out, chunk), 0) // rows
        == lax.broadcasted_iota(jnp.int32, (wide_out, chunk), 1)
    ).astype(jnp.bfloat16)
    repeat_right = (
        lax.broadcasted_iota(jnp.int32, (timed, wide_in), 1) // rows
        == lax.broadcasted_iota(jnp.int32, (timed, wide_in), 0)
    ).astype(jnp.bfloat16)
    tall = jnp.dot(repeat_left, matrix.astype(jnp.bfloat16), preferred_element_type=jnp.float32)
    tall = tall.astype(jnp.bfloat16)
    piece = min(128, wide_out)
    for start in range(0, wide_out, piece):
        part = jnp.dot(tall[start : start + piece], repeat_right, preferred_element_type=jnp.float32)
        same_row = (
            lax.broadcasted_iota(jnp.int32, (piece, wide_in), 0) % rows
            == lax.broadcasted_iota(jnp.int32, (piece, wide_in), 1) % rows
        )
        spread_ref[start : start + piece] = jnp.where(same_row, part, 0.0).astype(jnp.bfloat16)


def time_tables(segments, ref_pick, band_taps, rows, chunk, history):
    frames = segments.shape[0]
    wide_out, wide_in = chunk * rows, (history + chunk) * rows
    smem = pl.BlockSpec(memory_space=pltpu.SMEM)
    return pl.pallas_call(
        functools.partial(time_kernel, history=history, frames=frames, rows=rows),
        in_specs=[smem] * 3,
        out_specs=[pl.BlockSpec(memory_space=pltpu.VMEM), smem],
        out_shape=[
            jax.ShapeDtypeStruct((wide_out, wide_in), jnp.bfloat16),
            jax.ShapeDtypeStruct(ref_pick.shape, jnp.int32),
        ],
        compiler_params=pltpu.CompilerParams(vmem_limit_bytes=16 * MIB),
        cost_estimate=pl.CostEstimate(
            flops=2 * wide_out * wide_in * chunk, bytes_accessed=2 * wide_out * wide_in, transcendentals=0
        ),
    )(segments, ref_pick, band_taps.astype(jnp.float32))


def filter_frames(window_refs, left_ref, right_ref, stacked_ref, put):
    rows = left_ref.shape[0] // (2 * right_ref.shape[0])
    orient, both, _ = right_ref.shape
    quarter = both // 2
    for n, window in enumerate(window_refs):
        stacked = jnp.dot(left_ref[...], window[...], preferred_element_type=jnp.float32).astype(jnp.bfloat16)
        for o in range(orient):
            for z in range(2):
                begin = (o * 2 + z) * rows
                stacked_ref[o, n * rows : (n + 1) * rows, z * quarter : (z + 1) * quarter] = stacked[begin : begin + rows]
    many = len(window_refs) * rows
    step = min(256, many)
    pair = 2 * rows
    for o in range(orient):
        for start in range(0, many, step):
            stop = min(start + step, many)
            coeff = jnp.dot(stacked_ref[o, start:stop], right_ref[o], preferred_element_type=jnp.float32)
            coeff = coeff.astype(jnp.bfloat16)
            for place in range(start, stop, pair):
                put(o, place // pair, coeff[place - start : place - start + pair])


def coeff_kernel(window_ref, left_ref, right_ref, coeff_ref, stacked_ref):
    chips, frames_here, window, quarter = window_ref.shape
    rows = left_ref.shape[0] // (2 * right_ref.shape[0])

    def put(o, i, block):
        coeff_ref[o, 2 * i * rows : 2 * (i + 1) * rows] = block

    filter_frames(
        [window_ref.at[chip, f] for chip in range(chips) for f in range(frames_here)], left_ref, right_ref, stacked_ref, put
    )


def own_coeffs(windows, left, right, rows):
    chips, frames_here, _, quarter = windows.shape
    vmem = pl.BlockSpec(memory_space=pltpu.VMEM)
    out = jax.ShapeDtypeStruct((ORIENT, chips * frames_here * rows, 2 * quarter), jnp.bfloat16)
    return pl.pallas_call(
        coeff_kernel,
        in_specs=[vmem] * 3,
        out_specs=vmem,
        out_shape=out,
        scratch_shapes=[pltpu.VMEM(out.shape, jnp.bfloat16)],
        compiler_params=pltpu.CompilerParams(vmem_limit_bytes=8 * out.size + 16 * MIB),
        cost_estimate=pl.CostEstimate(
            flops=8 * out.size * quarter, bytes_accessed=2 * (windows.size + out.size), transcendentals=0
        ),
    )(windows, left, right)


def pixel_kernel(
    segments_ref, ref_frame_ref, spread_ref, mine_ref, other_ref, refer_ref, left_ref, right_ref, out_ref,
    stacked_ref, coeff_ref, phase_ref, *, history, whole,
):
    chips, frames_here, _, quarter = other_ref.shape
    chunk, rows, _ = out_ref.shape
    orient = right_ref.shape[0]
    nseg = ref_frame_ref.shape[0]
    both = 2 * quarter
    timed = history + chunk
    wide_out = chunk * rows
    pair = frames_here * rows
    core = lax.axis_index("core")

    for chip in range(chips):
        place = pl.ds(pl.multiple_of((chip * CORES + core) * pair, pair), pair)
        for o in range(orient):
            coeff_ref[o, place] = mine_ref[o, chip * pair : (chip + 1) * pair]

    def put(o, i, block):
        if i < chips:
            coeff_ref[o, pl.ds(pl.multiple_of((i * CORES + 1 - core) * pair, pair), pair)] = block
        else:
            begin = timed * rows + (i - chips) * pair
            coeff_ref[o, begin : begin + pair] = block

    windows = [other_ref.at[chip, f] for chip in range(chips) for f in range(frames_here)]
    if not whole:
        windows += [refer_ref.at[s] for s in range(nseg)]
    filter_frames(windows, left_ref, right_ref, stacked_ref, put)

    def phase_one(slot, carry):
        place = pl.ds(pl.multiple_of(slot * rows, rows), rows)
        if whole:
            source = ref_frame_ref[segments_ref[slot]]
        else:
            first = lax.axis_index("chunk") * chunk - history
            source = timed + segments_ref[jnp.maximum(first + slot, 0)]
        refer = pl.ds(pl.multiple_of(source * rows, rows), rows)
        for o in range(orient):
            coeff_real = coeff_ref[o, place, 0:quarter].astype(jnp.float32)
            coeff_imag = coeff_ref[o, place, quarter:both].astype(jnp.float32)
            ref_real = coeff_ref[o, refer, 0:quarter].astype(jnp.float32)
            ref_imag = coeff_ref[o, refer, quarter:both].astype(jnp.float32)
            prod_real = coeff_real * ref_real + coeff_imag * ref_imag
            prod_imag = coeff_imag * ref_real - coeff_real * ref_imag
            square = prod_real * prod_real + prod_imag * prod_imag + 1.0
            phase_ref[o, place] = (prod_imag * lax.rsqrt(square)).astype(jnp.bfloat16)
        return carry

    lax.fori_loop(0, timed, phase_one, 0, unroll=2)

    piece = min(128, wide_out)
    for start in range(0, wide_out, piece):
        here = slice(history * rows + start, history * rows + start + piece)
        above = jnp.zeros((piece, quarter), jnp.float32)
        below = jnp.ones((piece, quarter), jnp.float32)
        for o in range(orient):
            filtered = jnp.dot(
                spread_ref[start : start + piece], phase_ref[o], preferred_element_type=jnp.float32
            )
            filtered = filtered.astype(jnp.bfloat16).astype(jnp.float32)
            coeff_real = coeff_ref[o, here, 0:quarter].astype(jnp.float32)
            coeff_imag = coeff_ref[o, here, quarter:both].astype(jnp.float32)
            amplitude = coeff_real * coeff_real + coeff_imag * coeff_imag
            above = above + amplitude * filtered
            below = below + amplitude
        motion = (above / below).astype(out_ref.dtype)
        for i in range(piece // rows):
            out_ref[start // rows + i] = motion[i * rows : (i + 1) * rows]


def pixel_motion(segments, ref_frames, spread, mine, other, refer, left, right, rows, chunk, history):
    chips, frames_here, _, quarter = other.shape
    timed = history + chunk
    whole = refer is None
    slots = timed if whole else timed + NSEG
    smem = pl.BlockSpec(memory_space=pltpu.SMEM)
    vmem = pl.BlockSpec(memory_space=pltpu.VMEM)
    slot_bytes = ORIENT * rows * 2 * quarter * 2
    return pl.pallas_call(
        functools.partial(pixel_kernel, history=history, whole=whole),
        in_specs=[smem] * 2 + [vmem] * 6,
        out_specs=vmem,
        out_shape=jax.ShapeDtypeStruct((chunk, rows, quarter), jnp.bfloat16),
        scratch_shapes=[
            pltpu.VMEM((ORIENT, (slots - timed // 2) * rows, 2 * quarter), jnp.bfloat16),
            pltpu.VMEM((ORIENT, slots * rows, 2 * quarter), jnp.bfloat16),
            pltpu.VMEM((ORIENT, timed * rows, quarter), jnp.bfloat16),
        ],
        compiler_params=pltpu.CompilerParams(vmem_limit_bytes=4 * slots * slot_bytes + 16 * MIB),
        cost_estimate=pl.CostEstimate(
            flops=2 * ORIENT * rows * quarter * (slots * 2 * quarter + chunk * timed * rows),
            bytes_accessed=2 * (other.size + mine.size + right.size),
            transcendentals=ORIENT * timed * rows * quarter,
        ),
    )(segments, ref_frames, spread, mine, other, other if whole else refer, left, right)


def chunk_windows(mine, other, ref_frames, history_chips, chips):
    mine = lax.all_gather(mine, "chunk", axis=0, tiled=True)
    other = lax.all_gather(other, "chunk", axis=0, tiled=True)
    frames_here = mine.shape[1]
    core = lax.axis_index("core")
    device = ref_frames // frames_here
    place = device // CORES * frames_here + ref_frames % frames_here
    own = (device % CORES == core)[:, None, None]
    flat = (-1,) + mine.shape[2:]
    refer = jnp.where(own, mine.reshape(flat)[place], other.reshape(flat)[place])

    def cut(windows):
        before = jnp.zeros((history_chips,) + windows.shape[1:], windows.dtype)
        windows = jnp.concatenate([before, windows])
        return lax.dynamic_slice_in_dim(windows, lax.axis_index("chunk") * chips, history_chips + chips)

    return cut(mine), cut(other), refer


def body(video_frames, segments, ref_pick, band_taps, *, chunks, slabs):
    frames_here, size, _ = video_frames.shape
    quarter = size // 4
    slab_rows = quarter // slabs
    rows = slab_rows // CORES
    chunk = slabs * CORES * frames_here
    history = min(chunk * -(-(band_taps.shape[0] - 1) // chunk), segments.shape[0] - chunk)
    left = jnp.asarray(slab_left_table(rows, HALO, ORIENT))
    right = jnp.asarray(make_right_table(quarter, ORIENT))
    windows = reduce_frames(video_frames, slabs, slab_rows, HALO)
    spread, ref_frames = time_tables(segments, ref_pick, band_taps, rows, chunk, history)
    pieces = [windows[0]] * slabs
    near = list(range(2, slabs // 2)) + [k for k in (1,) if k < slabs // 2]
    far = sorted(range(slabs // 2, slabs), key=lambda k: k % 2)
    order = [k for pair in itertools.zip_longest(near, far) for k in pair if k is not None]
    for k in order:
        pieces[k] = lax.ppermute(windows[k], "slab", [(chip, chip ^ k) for chip in range(slabs)])
    mine, other = cut_windows(ref_frames, pieces, rows)
    other = lax.ppermute(other, "core", [(0, 1), (1, 0)])
    refer = None
    if chunks > 1:
        mine, other, refer = chunk_windows(mine, other, ref_frames, history // (CORES * frames_here), slabs)
    mine = own_coeffs(mine, left, right, rows)
    motion = pixel_motion(segments, ref_frames, spread, mine, other, refer, left, right, rows, chunk, history)
    motion = motion.reshape(slabs * CORES, frames_here, rows, quarter)
    motion = lax.all_to_all(motion, ("slab", "core"), split_axis=0, concat_axis=0, tiled=True)
    motion = jnp.swapaxes(motion, 0, 1).reshape(frames_here, quarter, quarter)
    return motion.astype(jnp.float32)


def solution(mesh):
    chips = mesh.shape["frames"] // CORES
    slabs = min(chips, QUART // (CORES * TILE))
    chunks = chips // slabs
    names = ("groups", "chunk", "slab", "core")
    cut = jax.sharding.Mesh(mesh.devices.reshape(mesh.shape["groups"], chunks, slabs, CORES), names)
    in_specs = (P(names, None, None), P("groups"), P("groups"), P())
    return jax.shard_map(
        functools.partial(body, chunks=chunks, slabs=slabs),
        mesh=cut, in_specs=in_specs, out_specs=P(names, None, None), check_vma=False,
    )
```

```python
import functools
import itertools
import math

import jax
import jax.numpy as jnp
import numpy as np
from jax import lax
from jax.experimental import pallas as pl
from jax.experimental.pallas import tpu as pltpu
from jax.sharding import PartitionSpec as P

IMG = 1024
ORIENT = 4
NSEG = 4
QUART = 256


blur_sigma = 2.0
gabor_sigma = 2.0
wave_number = math.pi / 2.0
gabor_gain = 2.0

HALO = 32
TILE = 16
CORES = 2
MIB = 1024 * 1024


def envelope_of(offset_grid):
    return np.float32(gabor_gain) * np.exp(
        -offset_grid * offset_grid / np.float32(2.0 * gabor_sigma * gabor_sigma)
    )


def waves(orient):
    angles = np.arange(orient, dtype=np.float32) * np.float32(math.pi / orient)
    wave_x = np.float32(wave_number) * np.cos(angles)
    wave_y = np.float32(wave_number) * np.sin(angles)
    return wave_x, wave_y


def slab_left_table(rows, halo, orient):
    offset = (
        np.arange(rows + 2 * halo, dtype=np.float32)[None, :]
        - np.float32(halo)
        - np.arange(rows, dtype=np.float32)[:, None]
    )
    wave_y = waves(orient)[1]
    phase = wave_y[:, None, None] * offset[None]
    envelope = envelope_of(offset)[None]
    table = np.stack([envelope * np.cos(phase), envelope * np.sin(phase)], axis=1)
    return table.reshape(orient * 2 * rows, rows + 2 * halo).astype(jnp.bfloat16)


def make_right_table(quarter, orient):
    position = np.arange(quarter, dtype=np.float32)
    offset = position[:, None] - position[None, :]
    wave_x = waves(orient)[0]
    phase_x = wave_x[:, None, None] * offset[None]
    envelope = envelope_of(offset)[None]
    real_part = envelope * np.cos(phase_x)
    imag_part = envelope * np.sin(phase_x)
    upper_half = np.concatenate([real_part, imag_part], axis=2)
    lower_half = np.concatenate([-imag_part, real_part], axis=2)
    return np.concatenate([upper_half, lower_half], axis=1).astype(jnp.bfloat16)


def down_sums(full_size, quarter):
    position = np.arange(quarter, dtype=np.float32)[:, None]
    columns = np.arange(full_size, dtype=np.float32)[None, :]
    offset_grid = columns - np.float32(4.0) * position - np.float32(1.5)
    weight = np.exp(-offset_grid * offset_grid / np.float32(2.0 * blur_sigma * blur_sigma))
    return np.sum(weight, axis=1)


def down_block(position, column, shape, axis, sums):
    positions = position + lax.broadcasted_iota(jnp.int32, shape, 1 - axis)
    columns = column + lax.broadcasted_iota(jnp.int32, shape, axis)
    offset_grid = columns.astype(jnp.float32) - 4.0 * positions.astype(jnp.float32) - 1.5
    weight = jnp.exp(-offset_grid * offset_grid / (2.0 * blur_sigma * blur_sigma))
    inner = float(sums[len(sums) // 2])
    line = position + lax.broadcasted_iota(jnp.int32, tuple(1 if i == axis else n for i, n in enumerate(shape)), 1 - axis)
    scale = jnp.full(line.shape, 1.0 / inner, jnp.float32)
    for q in range(position, min(position + shape[1 - axis], len(sums))):
        if abs(float(sums[q]) - inner) > 1e-7 * inner:
            scale = jnp.where(line == q, 1.0 / float(sums[q]), scale)
    return (weight * scale).astype(jnp.bfloat16)


def build_down(down_t_ref, down_ref):
    size, quarter = down_t_ref.shape
    sums = down_sums(size, quarter)
    lanes = min(128, quarter)
    down_t_ref[...] = jnp.zeros_like(down_t_ref)
    down_ref[...] = jnp.zeros_like(down_ref)
    for row in range(0, size, 128):
        for lane in range(0, quarter, lanes):
            if 4 * (lane + lanes - 1) + 30 >= row and 4 * lane - 27 <= row + 127:
                down_t_ref[row : row + 128, lane : lane + lanes] = down_block(lane, row, (128, lanes), 0, sums)
    for row in range(0, quarter, 32):
        for lane in range(0, size, 128):
            if 4 * (row + 31) + 30 >= lane and 4 * row - 27 <= lane + 127:
                down_ref[row : row + 32, lane : lane + 128] = down_block(row, lane, (32, 128), 1, sums)


def reduce_kernel(frames_ref, *refs, order, rows, halo, block):
    out_refs = refs[: len(order)]
    picture_ref, down_t_ref, down_ref, half_ref, total_ref, padded_ref, sems = refs[len(order) :]
    count, size, _ = picture_ref.shape
    quarter = down_ref.shape[0]

    copies = []
    for f in range(count):
        for i in range(size // block):
            here = pl.ds(i * block, block)
            copy = pltpu.make_async_copy(frames_ref.at[f, here], picture_ref.at[f, here], sems.at[f, i])
            copy.start()
            copies.append(copy)
    build_down(down_t_ref, down_ref)
    edge = jnp.zeros((halo, quarter), jnp.bfloat16)
    padded_ref[0:halo] = edge
    padded_ref[halo + quarter :] = edge

    me = lax.axis_index("slab")
    reach = quarter
    for f in range(count):
        total_ref[...] = jnp.zeros_like(total_ref)
        for i in range(size // block):
            copies[f * (size // block) + i].wait()
            half_ref[...] = jnp.dot(
                picture_ref[f, i * block : (i + 1) * block], down_t_ref[...], preferred_element_type=jnp.float32
            ).astype(jnp.bfloat16)
            for row in range(0, block, reach):
                begin = i * block + row
                near = slice(max(begin // 4 - TILE, 0), min((begin + reach) // 4 + TILE, quarter))
                total_ref[near] += jnp.dot(
                    down_ref[near, begin : begin + reach], half_ref[row : row + reach], preferred_element_type=jnp.float32
                )
        padded_ref[halo : halo + quarter] = total_ref[...].astype(jnp.bfloat16)
        for k, out_ref in zip(order, out_refs):
            slab = lax.bitwise_xor(me, k)
            out_ref[f] = padded_ref[pl.ds(pl.multiple_of(slab * rows, rows), rows + 2 * halo)]


def reduce_frames(video_frames, order, rows, halo):
    count, size, _ = video_frames.shape
    slabs = len(order)
    quarter = slabs * rows
    block = size // 2
    out = jax.ShapeDtypeStruct((count, rows + 2 * halo, quarter), jnp.bfloat16)
    return pl.pallas_call(
        functools.partial(reduce_kernel, order=order, rows=rows, halo=halo, block=block),
        in_specs=[pl.BlockSpec(memory_space=pltpu.HBM)],
        out_specs=[pl.BlockSpec(memory_space=pltpu.VMEM)] * slabs,
        out_shape=[out] * slabs,
        scratch_shapes=[
            pltpu.VMEM((count, size, size), jnp.bfloat16),
            pltpu.VMEM((size, quarter), jnp.bfloat16),
            pltpu.VMEM((quarter, size), jnp.bfloat16),
            pltpu.VMEM((block, quarter), jnp.bfloat16),
            pltpu.VMEM((quarter, quarter), jnp.float32),
            pltpu.VMEM((quarter + 2 * halo, quarter), jnp.bfloat16),
            pltpu.SemaphoreType.DMA((count, size // block)),
        ],
        compiler_params=pltpu.CompilerParams(vmem_limit_bytes=52 * MIB),
        cost_estimate=pl.CostEstimate(
            flops=2 * count * size * quarter * (size + quarter),
            bytes_accessed=2 * count * size * size,
            transcendentals=0,
        ),
    )(video_frames)


def exchange_order(slabs):
    far = sorted(range(slabs // 2, slabs), key=lambda k: k % 2)
    near = list(range(2, slabs // 2))
    turns = [k for pair in itertools.zip_longest(far, near) for k in pair if k is not None]
    return [0] + turns + [k for k in (1,) if k < slabs // 2]


def cut_kernel(*refs, order, rows):
    in_refs, (mine_ref, other_ref) = refs[1:-2], refs[-2:]
    window = mine_ref.shape[2]
    me, core = lax.axis_index("slab"), lax.axis_index("core")
    for k, in_ref in zip(order, in_refs):
        chip = lax.bitwise_xor(me, k)
        mine_ref[chip] = in_ref[:, pl.ds(pl.multiple_of(core * rows, rows), window)]
        other_ref[chip] = in_ref[:, pl.ds(pl.multiple_of((1 - core) * rows, rows), window)]


def cut_windows(ref_frames, pieces, order, rows):
    count, window, quarter = pieces[0].shape
    out = jax.ShapeDtypeStruct((len(pieces), count, window - rows, quarter), jnp.bfloat16)
    return pl.pallas_call(
        functools.partial(cut_kernel, order=order, rows=rows),
        in_specs=[pl.BlockSpec(memory_space=pltpu.SMEM)] + [pl.BlockSpec(memory_space=pltpu.VMEM)] * len(pieces),
        out_specs=[pl.BlockSpec(memory_space=pltpu.VMEM)] * 2,
        out_shape=[out, out],
        compiler_params=pltpu.CompilerParams(vmem_limit_bytes=16 * MIB),
        cost_estimate=pl.CostEstimate(flops=0, bytes_accessed=8 * out.size, transcendentals=0),
    )(ref_frames, *pieces)


def time_kernel(segments_ref, pick_ref, taps_ref, spread_ref, frame_ref, *, history, frames, rows):
    chunk, timed = spread_ref.shape[0] // rows, spread_ref.shape[1] // rows
    nseg = pick_ref.shape[0]
    taps = taps_ref.shape[0]
    wide_out, wide_in = chunk * rows, timed * rows

    def count_one(t, totals):
        here = segments_ref[t]
        below = [total + (here < s).astype(jnp.int32) for s, total in enumerate(totals[0])]
        same = [total + (here == s).astype(jnp.int32) for s, total in enumerate(totals[1])]
        return tuple(below), tuple(same)

    zeros = tuple(jnp.int32(0) for _ in range(nseg))
    starts, counts = lax.fori_loop(0, frames, count_one, (zeros, zeros), unroll=8)
    for s in range(nseg):
        frame_ref[s] = starts[s] + lax.rem(pick_ref[s], counts[s])

    lag = history + lax.broadcasted_iota(jnp.int32, (chunk, timed), 0) - lax.broadcasted_iota(
        jnp.int32, (chunk, timed), 1
    )
    if history:
        first = lax.axis_index("chunk") * chunk - history
        real = first + lax.broadcasted_iota(jnp.int32, (chunk, timed), 1) >= 0
        lag = jnp.where(real, lag, -1)
    matrix = jnp.zeros((chunk, timed), jnp.float32)
    for k in range(taps):
        matrix = jnp.where(lag == k, taps_ref[k], matrix)
    repeat_left = (
        lax.broadcasted_iota(jnp.int32, (wide_out, chunk), 0) // rows
        == lax.broadcasted_iota(jnp.int32, (wide_out, chunk), 1)
    ).astype(jnp.bfloat16)
    repeat_right = (
        lax.broadcasted_iota(jnp.int32, (timed, wide_in), 1) // rows
        == lax.broadcasted_iota(jnp.int32, (timed, wide_in), 0)
    ).astype(jnp.bfloat16)
    tall = jnp.dot(repeat_left, matrix.astype(jnp.bfloat16), preferred_element_type=jnp.float32)
    tall = tall.astype(jnp.bfloat16)
    piece = min(128, wide_out)
    for start in range(0, wide_out, piece):
        part = jnp.dot(tall[start : start + piece], repeat_right, preferred_element_type=jnp.float32)
        same_row = (
            lax.broadcasted_iota(jnp.int32, (piece, wide_in), 0) % rows
            == lax.broadcasted_iota(jnp.int32, (piece, wide_in), 1) % rows
        )
        spread_ref[start : start + piece] = jnp.where(same_row, part, 0.0).astype(jnp.bfloat16)


def time_tables(segments, ref_pick, band_taps, rows, chunk, history):
    frames = segments.shape[0]
    wide_out, wide_in = chunk * rows, (history + chunk) * rows
    smem = pl.BlockSpec(memory_space=pltpu.SMEM)
    return pl.pallas_call(
        functools.partial(time_kernel, history=history, frames=frames, rows=rows),
        in_specs=[smem] * 3,
        out_specs=[pl.BlockSpec(memory_space=pltpu.VMEM), smem],
        out_shape=[
            jax.ShapeDtypeStruct((wide_out, wide_in), jnp.bfloat16),
            jax.ShapeDtypeStruct(ref_pick.shape, jnp.int32),
        ],
        compiler_params=pltpu.CompilerParams(vmem_limit_bytes=16 * MIB),
        cost_estimate=pl.CostEstimate(
            flops=2 * wide_out * wide_in * chunk, bytes_accessed=2 * wide_out * wide_in, transcendentals=0
        ),
    )(segments, ref_pick, band_taps.astype(jnp.float32))


def filter_frames(window_refs, left_ref, right_ref, stacked_ref, put):
    rows = left_ref.shape[0] // (2 * right_ref.shape[0])
    orient, both, _ = right_ref.shape
    quarter = both // 2
    for n, window in enumerate(window_refs):
        stacked = jnp.dot(left_ref[...], window[...], preferred_element_type=jnp.float32).astype(jnp.bfloat16)
        for o in range(orient):
            for z in range(2):
                begin = (o * 2 + z) * rows
                stacked_ref[o, n * rows : (n + 1) * rows, z * quarter : (z + 1) * quarter] = stacked[begin : begin + rows]
    many = len(window_refs) * rows
    step = min(256, many)
    pair = 2 * rows
    for o in range(orient):
        for start in range(0, many, step):
            stop = min(start + step, many)
            coeff = jnp.dot(stacked_ref[o, start:stop], right_ref[o], preferred_element_type=jnp.float32)
            coeff = coeff.astype(jnp.bfloat16)
            for place in range(start, stop, pair):
                put(o, place // pair, coeff[place - start : place - start + pair])


def coeff_kernel(window_ref, left_ref, right_ref, coeff_ref, stacked_ref):
    chips, frames_here, window, quarter = window_ref.shape
    rows = left_ref.shape[0] // (2 * right_ref.shape[0])

    def put(o, i, block):
        coeff_ref[o, 2 * i * rows : 2 * (i + 1) * rows] = block

    filter_frames(
        [window_ref.at[chip, f] for chip in range(chips) for f in range(frames_here)], left_ref, right_ref, stacked_ref, put
    )


def own_coeffs(windows, left, right, rows):
    chips, frames_here, _, quarter = windows.shape
    vmem = pl.BlockSpec(memory_space=pltpu.VMEM)
    out = jax.ShapeDtypeStruct((ORIENT, chips * frames_here * rows, 2 * quarter), jnp.bfloat16)
    return pl.pallas_call(
        coeff_kernel,
        in_specs=[vmem] * 3,
        out_specs=vmem,
        out_shape=out,
        scratch_shapes=[pltpu.VMEM(out.shape, jnp.bfloat16)],
        compiler_params=pltpu.CompilerParams(vmem_limit_bytes=8 * out.size + 16 * MIB),
        cost_estimate=pl.CostEstimate(
            flops=8 * out.size * quarter, bytes_accessed=2 * (windows.size + out.size), transcendentals=0
        ),
    )(windows, left, right)


def pixel_kernel(
    segments_ref, ref_frame_ref, spread_ref, mine_ref, other_ref, refer_ref, left_ref, right_ref, out_ref,
    stacked_ref, coeff_ref, phase_ref, *, history, whole,
):
    chips, frames_here, _, quarter = other_ref.shape
    chunk, rows, _ = out_ref.shape
    orient = right_ref.shape[0]
    nseg = ref_frame_ref.shape[0]
    both = 2 * quarter
    timed = history + chunk
    wide_out = chunk * rows
    pair = frames_here * rows
    core = lax.axis_index("core")

    for chip in range(chips):
        place = pl.ds(pl.multiple_of((chip * CORES + core) * pair, pair), pair)
        for o in range(orient):
            coeff_ref[o, place] = mine_ref[o, chip * pair : (chip + 1) * pair]

    def put(o, i, block):
        if i < chips:
            coeff_ref[o, pl.ds(pl.multiple_of((i * CORES + 1 - core) * pair, pair), pair)] = block
        else:
            begin = timed * rows + (i - chips) * pair
            coeff_ref[o, begin : begin + pair] = block

    windows = [other_ref.at[chip, f] for chip in range(chips) for f in range(frames_here)]
    if not whole:
        windows += [refer_ref.at[s] for s in range(nseg)]
    filter_frames(windows, left_ref, right_ref, stacked_ref, put)

    def phase_one(slot, carry):
        place = pl.ds(pl.multiple_of(slot * rows, rows), rows)
        if whole:
            source = ref_frame_ref[segments_ref[slot]]
        else:
            first = lax.axis_index("chunk") * chunk - history
            source = timed + segments_ref[jnp.maximum(first + slot, 0)]
        refer = pl.ds(pl.multiple_of(source * rows, rows), rows)
        for o in range(orient):
            coeff_real = coeff_ref[o, place, 0:quarter].astype(jnp.float32)
            coeff_imag = coeff_ref[o, place, quarter:both].astype(jnp.float32)
            ref_real = coeff_ref[o, refer, 0:quarter].astype(jnp.float32)
            ref_imag = coeff_ref[o, refer, quarter:both].astype(jnp.float32)
            prod_real = coeff_real * ref_real + coeff_imag * ref_imag
            prod_imag = coeff_imag * ref_real - coeff_real * ref_imag
            square = prod_real * prod_real + prod_imag * prod_imag + 1.0
            phase_ref[o, place] = (prod_imag * lax.rsqrt(square)).astype(jnp.bfloat16)
        return carry

    lax.fori_loop(0, timed, phase_one, 0, unroll=2)

    piece = min(128, wide_out)
    for start in range(0, wide_out, piece):
        here = slice(history * rows + start, history * rows + start + piece)
        above = jnp.zeros((piece, quarter), jnp.float32)
        below = jnp.ones((piece, quarter), jnp.float32)
        for o in range(orient):
            filtered = jnp.dot(
                spread_ref[start : start + piece], phase_ref[o], preferred_element_type=jnp.float32
            )
            filtered = filtered.astype(jnp.bfloat16).astype(jnp.float32)
            coeff_real = coeff_ref[o, here, 0:quarter].astype(jnp.float32)
            coeff_imag = coeff_ref[o, here, quarter:both].astype(jnp.float32)
            amplitude = coeff_real * coeff_real + coeff_imag * coeff_imag
            above = above + amplitude * filtered
            below = below + amplitude
        motion = (above / below).astype(out_ref.dtype)
        for i in range(piece // rows):
            out_ref[start // rows + i] = motion[i * rows : (i + 1) * rows]


def pixel_motion(segments, ref_frames, spread, mine, other, refer, left, right, rows, chunk, history):
    chips, frames_here, _, quarter = other.shape
    timed = history + chunk
    whole = refer is None
    slots = timed if whole else timed + NSEG
    smem = pl.BlockSpec(memory_space=pltpu.SMEM)
    vmem = pl.BlockSpec(memory_space=pltpu.VMEM)
    slot_bytes = ORIENT * rows * 2 * quarter * 2
    return pl.pallas_call(
        functools.partial(pixel_kernel, history=history, whole=whole),
        in_specs=[smem] * 2 + [vmem] * 6,
        out_specs=vmem,
        out_shape=jax.ShapeDtypeStruct((chunk, rows, quarter), jnp.bfloat16),
        scratch_shapes=[
            pltpu.VMEM((ORIENT, (slots - timed // 2) * rows, 2 * quarter), jnp.bfloat16),
            pltpu.VMEM((ORIENT, slots * rows, 2 * quarter), jnp.bfloat16),
            pltpu.VMEM((ORIENT, timed * rows, quarter), jnp.bfloat16),
        ],
        compiler_params=pltpu.CompilerParams(vmem_limit_bytes=4 * slots * slot_bytes + 16 * MIB),
        cost_estimate=pl.CostEstimate(
            flops=2 * ORIENT * rows * quarter * (slots * 2 * quarter + chunk * timed * rows),
            bytes_accessed=2 * (other.size + mine.size + right.size),
            transcendentals=ORIENT * timed * rows * quarter,
        ),
    )(segments, ref_frames, spread, mine, other, other if whole else refer, left, right)


def chunk_windows(mine, other, ref_frames, history_chips, chips):
    mine = lax.all_gather(mine, "chunk", axis=0, tiled=True)
    other = lax.all_gather(other, "chunk", axis=0, tiled=True)
    frames_here = mine.shape[1]
    core = lax.axis_index("core")
    device = ref_frames // frames_here
    place = device // CORES * frames_here + ref_frames % frames_here
    own = (device % CORES == core)[:, None, None]
    flat = (-1,) + mine.shape[2:]
    refer = jnp.where(own, mine.reshape(flat)[place], other.reshape(flat)[place])

    def cut(windows):
        before = jnp.zeros((history_chips,) + windows.shape[1:], windows.dtype)
        windows = jnp.concatenate([before, windows])
        return lax.dynamic_slice_in_dim(windows, lax.axis_index("chunk") * chips, history_chips + chips)

    return cut(mine), cut(other), refer


def body(video_frames, segments, ref_pick, band_taps, *, chunks, slabs):
    frames_here, size, _ = video_frames.shape
    quarter = size // 4
    slab_rows = quarter // slabs
    rows = slab_rows // CORES
    chunk = slabs * CORES * frames_here
    history = min(chunk * -(-(band_taps.shape[0] - 1) // chunk), segments.shape[0] - chunk)
    left = jnp.asarray(slab_left_table(rows, HALO, ORIENT))
    right = jnp.asarray(make_right_table(quarter, ORIENT))
    order = exchange_order(slabs)
    windows = reduce_frames(video_frames, order, slab_rows, HALO)
    spread, ref_frames = time_tables(segments, ref_pick, band_taps, rows, chunk, history)
    pieces = [windows[0]]
    for k, window in zip(order[1:], windows[1:]):
        pieces.append(lax.ppermute(window, "slab", [(chip, chip ^ k) for chip in range(slabs)]))
    mine, other = cut_windows(ref_frames, pieces, order, rows)
    other = lax.ppermute(other, "core", [(0, 1), (1, 0)])
    refer = None
    if chunks > 1:
        mine, other, refer = chunk_windows(mine, other, ref_frames, history // (CORES * frames_here), slabs)
    mine = own_coeffs(mine, left, right, rows)
    motion = pixel_motion(segments, ref_frames, spread, mine, other, refer, left, right, rows, chunk, history)
    motion = motion.reshape(slabs * CORES, frames_here, rows, quarter)
    motion = lax.all_to_all(motion, ("slab", "core"), split_axis=0, concat_axis=0, tiled=True)
    motion = jnp.swapaxes(motion, 0, 1).reshape(frames_here, quarter, quarter)
    return motion.astype(jnp.float32)


def solution(mesh):
    chips = mesh.shape["frames"] // CORES
    slabs = min(chips, QUART // (CORES * TILE))
    chunks = chips // slabs
    names = ("groups", "chunk", "slab", "core")
    cut = jax.sharding.Mesh(mesh.devices.reshape(mesh.shape["groups"], chunks, slabs, CORES), names)
    in_specs = (P(names, None, None), P("groups"), P("groups"), P())
    return jax.shard_map(
        functools.partial(body, chunks=chunks, slabs=slabs),
        mesh=cut, in_specs=in_specs, out_specs=P(names, None, None), check_vma=False,
    )
```

```python
import functools
import itertools
import math

import jax
import jax.numpy as jnp
import numpy as np
from jax import lax
from jax.experimental import pallas as pl
from jax.experimental.pallas import tpu as pltpu
from jax.sharding import PartitionSpec as P

IMG = 1024
ORIENT = 4
NSEG = 4
QUART = 256


blur_sigma = 2.0
gabor_sigma = 2.0
wave_number = math.pi / 2.0
gabor_gain = 2.0

HALO = 32
TILE = 16
CORES = 2
PAIR = 2
MIB = 1024 * 1024


def envelope_of(offset_grid):
    return np.float32(gabor_gain) * np.exp(
        -offset_grid * offset_grid / np.float32(2.0 * gabor_sigma * gabor_sigma)
    )


def waves(orient):
    angles = np.arange(orient, dtype=np.float32) * np.float32(math.pi / orient)
    wave_x = np.float32(wave_number) * np.cos(angles)
    wave_y = np.float32(wave_number) * np.sin(angles)
    return wave_x, wave_y


def slab_left_table(rows, halo, orient):
    offset = (
        np.arange(rows + 2 * halo, dtype=np.float32)[None, :]
        - np.float32(halo)
        - np.arange(rows, dtype=np.float32)[:, None]
    )
    wave_y = waves(orient)[1]
    phase = wave_y[:, None, None] * offset[None]
    envelope = envelope_of(offset)[None]
    table = np.stack([envelope * np.cos(phase), envelope * np.sin(phase)], axis=1)
    return table.reshape(orient * 2 * rows, rows + 2 * halo).astype(jnp.bfloat16)


def make_right_table(quarter, orient):
    position = np.arange(quarter, dtype=np.float32)
    offset = position[:, None] - position[None, :]
    wave_x = waves(orient)[0]
    phase_x = wave_x[:, None, None] * offset[None]
    envelope = envelope_of(offset)[None]
    real_part = envelope * np.cos(phase_x)
    imag_part = envelope * np.sin(phase_x)
    upper_half = np.concatenate([real_part, imag_part], axis=2)
    lower_half = np.concatenate([-imag_part, real_part], axis=2)
    return np.concatenate([upper_half, lower_half], axis=1).astype(jnp.bfloat16)


def down_sums(full_size, quarter):
    position = np.arange(quarter, dtype=np.float32)[:, None]
    columns = np.arange(full_size, dtype=np.float32)[None, :]
    offset_grid = columns - np.float32(4.0) * position - np.float32(1.5)
    weight = np.exp(-offset_grid * offset_grid / np.float32(2.0 * blur_sigma * blur_sigma))
    return np.sum(weight, axis=1)


def down_block(position, column, shape, axis, sums):
    positions = position + lax.broadcasted_iota(jnp.int32, shape, 1 - axis)
    columns = column + lax.broadcasted_iota(jnp.int32, shape, axis)
    offset_grid = columns.astype(jnp.float32) - 4.0 * positions.astype(jnp.float32) - 1.5
    weight = jnp.exp(-offset_grid * offset_grid / (2.0 * blur_sigma * blur_sigma))
    inner = float(sums[len(sums) // 2])
    line = position + lax.broadcasted_iota(jnp.int32, tuple(1 if i == axis else n for i, n in enumerate(shape)), 1 - axis)
    scale = jnp.full(line.shape, 1.0 / inner, jnp.float32)
    for q in range(position, min(position + shape[1 - axis], len(sums))):
        if abs(float(sums[q]) - inner) > 1e-7 * inner:
            scale = jnp.where(line == q, 1.0 / float(sums[q]), scale)
    return (weight * scale).astype(jnp.bfloat16)


def build_down(down_t_ref, down_ref):
    size, quarter = down_t_ref.shape
    sums = down_sums(size, quarter)
    lanes = min(128, quarter)
    down_t_ref[...] = jnp.zeros_like(down_t_ref)
    down_ref[...] = jnp.zeros_like(down_ref)
    for row in range(0, size, 128):
        for lane in range(0, quarter, lanes):
            if 4 * (lane + lanes - 1) + 30 >= row and 4 * lane - 27 <= row + 127:
                down_t_ref[row : row + 128, lane : lane + lanes] = down_block(lane, row, (128, lanes), 0, sums)
    for row in range(0, quarter, 32):
        for lane in range(0, size, 128):
            if 4 * (row + 31) + 30 >= lane and 4 * row - 27 <= lane + 127:
                down_ref[row : row + 32, lane : lane + 128] = down_block(row, lane, (32, 128), 1, sums)


def reduce_kernel(frames_ref, *refs, order, rows, halo, block):
    out_refs = refs[: len(order)]
    picture_ref, down_t_ref, down_ref, half_ref, total_ref, padded_ref, sems = refs[len(order) :]
    count, size, _ = picture_ref.shape
    quarter = down_ref.shape[0]

    copies = []
    for f in range(count):
        for i in range(size // block):
            here = pl.ds(i * block, block)
            copy = pltpu.make_async_copy(frames_ref.at[f, here], picture_ref.at[f, here], sems.at[f, i])
            copy.start()
            copies.append(copy)
    build_down(down_t_ref, down_ref)
    edge = jnp.zeros((halo, quarter), jnp.bfloat16)
    padded_ref[0:halo] = edge
    padded_ref[halo + quarter :] = edge

    me = lax.axis_index("slab")
    reach = quarter
    for f in range(count):
        total_ref[...] = jnp.zeros_like(total_ref)
        for i in range(size // block):
            copies[f * (size // block) + i].wait()
            half_ref[...] = jnp.dot(
                picture_ref[f, i * block : (i + 1) * block], down_t_ref[...], preferred_element_type=jnp.float32
            ).astype(jnp.bfloat16)
            for row in range(0, block, reach):
                begin = i * block + row
                near = slice(max(begin // 4 - TILE, 0), min((begin + reach) // 4 + TILE, quarter))
                total_ref[near] += jnp.dot(
                    down_ref[near, begin : begin + reach], half_ref[row : row + reach], preferred_element_type=jnp.float32
                )
        padded_ref[halo : halo + quarter] = total_ref[...].astype(jnp.bfloat16)
        for k, out_ref in zip(order, out_refs):
            pair = lax.bitwise_xor(me // PAIR, k)
            out_ref[f] = padded_ref[pl.ds(pl.multiple_of(pair * rows, rows), rows + 2 * halo)]


def reduce_frames(video_frames, order, rows, halo):
    count, size, _ = video_frames.shape
    quarter = len(order) * rows
    block = size // 2
    out = jax.ShapeDtypeStruct((count, rows + 2 * halo, quarter), jnp.bfloat16)
    return pl.pallas_call(
        functools.partial(reduce_kernel, order=order, rows=rows, halo=halo, block=block),
        in_specs=[pl.BlockSpec(memory_space=pltpu.HBM)],
        out_specs=[pl.BlockSpec(memory_space=pltpu.VMEM)] * len(order),
        out_shape=[out] * len(order),
        scratch_shapes=[
            pltpu.VMEM((count, size, size), jnp.bfloat16),
            pltpu.VMEM((size, quarter), jnp.bfloat16),
            pltpu.VMEM((quarter, size), jnp.bfloat16),
            pltpu.VMEM((block, quarter), jnp.bfloat16),
            pltpu.VMEM((quarter, quarter), jnp.float32),
            pltpu.VMEM((quarter + 2 * halo, quarter), jnp.bfloat16),
            pltpu.SemaphoreType.DMA((count, size // block)),
        ],
        compiler_params=pltpu.CompilerParams(vmem_limit_bytes=52 * MIB),
        cost_estimate=pl.CostEstimate(
            flops=2 * count * size * quarter * (size + quarter),
            bytes_accessed=2 * count * size * size,
            transcendentals=0,
        ),
    )(video_frames)


def exchange_order(pairs):
    far, near = range(pairs // 2, pairs), range(1, pairs // 2)
    return [0] + [k for turn in itertools.zip_longest(far, near) for k in turn if k is not None]


def cut_kernel(*refs, order, rows):
    in_refs, (mine_ref, other_ref) = refs[1:-2], refs[-2:]
    window = mine_ref.shape[2]
    me, core = lax.axis_index("slab"), lax.axis_index("core")
    first = lax.rem(me, PAIR) * CORES
    for n, in_ref in enumerate(in_refs):
        chip = lax.bitwise_xor(me, PAIR * order[n // PAIR] + n % PAIR)
        mine_ref[chip] = in_ref[:, pl.ds(pl.multiple_of((first + core) * rows, rows), window)]
        other_ref[chip] = in_ref[:, pl.ds(pl.multiple_of((first + 1 - core) * rows, rows), window)]


def cut_windows(ref_frames, pieces, order, rows):
    count, window, quarter = pieces[0].shape
    window -= (PAIR * CORES - 1) * rows
    out = jax.ShapeDtypeStruct((len(pieces), count, window, quarter), jnp.bfloat16)
    return pl.pallas_call(
        functools.partial(cut_kernel, order=order, rows=rows),
        in_specs=[pl.BlockSpec(memory_space=pltpu.SMEM)] + [pl.BlockSpec(memory_space=pltpu.VMEM)] * len(pieces),
        out_specs=[pl.BlockSpec(memory_space=pltpu.VMEM)] * 2,
        out_shape=[out, out],
        compiler_params=pltpu.CompilerParams(vmem_limit_bytes=16 * MIB),
        cost_estimate=pl.CostEstimate(flops=0, bytes_accessed=8 * out.size, transcendentals=0),
    )(ref_frames, *pieces)


def time_kernel(segments_ref, pick_ref, taps_ref, spread_ref, frame_ref, *, history, frames, rows):
    chunk, timed = spread_ref.shape[0] // rows, spread_ref.shape[1] // rows
    nseg = pick_ref.shape[0]
    taps = taps_ref.shape[0]
    wide_out, wide_in = chunk * rows, timed * rows

    def count_one(t, totals):
        here = segments_ref[t]
        below = [total + (here < s).astype(jnp.int32) for s, total in enumerate(totals[0])]
        same = [total + (here == s).astype(jnp.int32) for s, total in enumerate(totals[1])]
        return tuple(below), tuple(same)

    zeros = tuple(jnp.int32(0) for _ in range(nseg))
    starts, counts = lax.fori_loop(0, frames, count_one, (zeros, zeros), unroll=8)
    for s in range(nseg):
        frame_ref[s] = starts[s] + lax.rem(pick_ref[s], counts[s])

    lag = history + lax.broadcasted_iota(jnp.int32, (chunk, timed), 0) - lax.broadcasted_iota(
        jnp.int32, (chunk, timed), 1
    )
    if history:
        first = lax.axis_index("chunk") * chunk - history
        real = first + lax.broadcasted_iota(jnp.int32, (chunk, timed), 1) >= 0
        lag = jnp.where(real, lag, -1)
    matrix = jnp.zeros((chunk, timed), jnp.float32)
    for k in range(taps):
        matrix = jnp.where(lag == k, taps_ref[k], matrix)
    repeat_left = (
        lax.broadcasted_iota(jnp.int32, (wide_out, chunk), 0) // rows
        == lax.broadcasted_iota(jnp.int32, (wide_out, chunk), 1)
    ).astype(jnp.bfloat16)
    repeat_right = (
        lax.broadcasted_iota(jnp.int32, (timed, wide_in), 1) // rows
        == lax.broadcasted_iota(jnp.int32, (timed, wide_in), 0)
    ).astype(jnp.bfloat16)
    tall = jnp.dot(repeat_left, matrix.astype(jnp.bfloat16), preferred_element_type=jnp.float32)
    tall = tall.astype(jnp.bfloat16)
    piece = min(128, wide_out)
    for start in range(0, wide_out, piece):
        part = jnp.dot(tall[start : start + piece], repeat_right, preferred_element_type=jnp.float32)
        same_row = (
            lax.broadcasted_iota(jnp.int32, (piece, wide_in), 0) % rows
            == lax.broadcasted_iota(jnp.int32, (piece, wide_in), 1) % rows
        )
        spread_ref[start : start + piece] = jnp.where(same_row, part, 0.0).astype(jnp.bfloat16)


def time_tables(segments, ref_pick, band_taps, rows, chunk, history):
    frames = segments.shape[0]
    wide_out, wide_in = chunk * rows, (history + chunk) * rows
    smem = pl.BlockSpec(memory_space=pltpu.SMEM)
    return pl.pallas_call(
        functools.partial(time_kernel, history=history, frames=frames, rows=rows),
        in_specs=[smem] * 3,
        out_specs=[pl.BlockSpec(memory_space=pltpu.VMEM), smem],
        out_shape=[
            jax.ShapeDtypeStruct((wide_out, wide_in), jnp.bfloat16),
            jax.ShapeDtypeStruct(ref_pick.shape, jnp.int32),
        ],
        compiler_params=pltpu.CompilerParams(vmem_limit_bytes=16 * MIB),
        cost_estimate=pl.CostEstimate(
            flops=2 * wide_out * wide_in * chunk, bytes_accessed=2 * wide_out * wide_in, transcendentals=0
        ),
    )(segments, ref_pick, band_taps.astype(jnp.float32))


def filter_frames(window_refs, left_ref, right_ref, stacked_ref, put):
    rows = left_ref.shape[0] // (2 * right_ref.shape[0])
    orient, both, _ = right_ref.shape
    quarter = both // 2
    for n, window in enumerate(window_refs):
        stacked = jnp.dot(left_ref[...], window[...], preferred_element_type=jnp.float32).astype(jnp.bfloat16)
        for o in range(orient):
            for z in range(2):
                begin = (o * 2 + z) * rows
                stacked_ref[o, n * rows : (n + 1) * rows, z * quarter : (z + 1) * quarter] = stacked[begin : begin + rows]
    many = len(window_refs) * rows
    step = min(256, many)
    pair = 2 * rows
    for o in range(orient):
        for start in range(0, many, step):
            stop = min(start + step, many)
            coeff = jnp.dot(stacked_ref[o, start:stop], right_ref[o], preferred_element_type=jnp.float32)
            coeff = coeff.astype(jnp.bfloat16)
            for place in range(start, stop, pair):
                put(o, place // pair, coeff[place - start : place - start + pair])


def coeff_kernel(window_ref, left_ref, right_ref, coeff_ref, stacked_ref):
    chips, frames_here, window, quarter = window_ref.shape
    rows = left_ref.shape[0] // (2 * right_ref.shape[0])

    def put(o, i, block):
        coeff_ref[o, 2 * i * rows : 2 * (i + 1) * rows] = block

    filter_frames(
        [window_ref.at[chip, f] for chip in range(chips) for f in range(frames_here)], left_ref, right_ref, stacked_ref, put
    )


def own_coeffs(windows, left, right, rows):
    chips, frames_here, _, quarter = windows.shape
    vmem = pl.BlockSpec(memory_space=pltpu.VMEM)
    out = jax.ShapeDtypeStruct((ORIENT, chips * frames_here * rows, 2 * quarter), jnp.bfloat16)
    return pl.pallas_call(
        coeff_kernel,
        in_specs=[vmem] * 3,
        out_specs=vmem,
        out_shape=out,
        scratch_shapes=[pltpu.VMEM(out.shape, jnp.bfloat16)],
        compiler_params=pltpu.CompilerParams(vmem_limit_bytes=8 * out.size + 16 * MIB),
        cost_estimate=pl.CostEstimate(
            flops=8 * out.size * quarter, bytes_accessed=2 * (windows.size + out.size), transcendentals=0
        ),
    )(windows, left, right)


def pixel_kernel(
    segments_ref, ref_frame_ref, spread_ref, mine_ref, other_ref, refer_ref, left_ref, right_ref, out_ref,
    stacked_ref, coeff_ref, phase_ref, *, history, whole,
):
    chips, frames_here, _, quarter = other_ref.shape
    chunk, rows, _ = out_ref.shape
    orient = right_ref.shape[0]
    nseg = ref_frame_ref.shape[0]
    both = 2 * quarter
    timed = history + chunk
    wide_out = chunk * rows
    pair = frames_here * rows
    core = lax.axis_index("core")

    for chip in range(chips):
        place = pl.ds(pl.multiple_of((chip * CORES + core) * pair, pair), pair)
        for o in range(orient):
            coeff_ref[o, place] = mine_ref[o, chip * pair : (chip + 1) * pair]

    def put(o, i, block):
        if i < chips:
            coeff_ref[o, pl.ds(pl.multiple_of((i * CORES + 1 - core) * pair, pair), pair)] = block
        else:
            begin = timed * rows + (i - chips) * pair
            coeff_ref[o, begin : begin + pair] = block

    windows = [other_ref.at[chip, f] for chip in range(chips) for f in range(frames_here)]
    if not whole:
        windows += [refer_ref.at[s] for s in range(nseg)]
    filter_frames(windows, left_ref, right_ref, stacked_ref, put)

    def phase_one(slot, carry):
        place = pl.ds(pl.multiple_of(slot * rows, rows), rows)
        if whole:
            source = ref_frame_ref[segments_ref[slot]]
        else:
            first = lax.axis_index("chunk") * chunk - history
            source = timed + segments_ref[jnp.maximum(first + slot, 0)]
        refer = pl.ds(pl.multiple_of(source * rows, rows), rows)
        for o in range(orient):
            coeff_real = coeff_ref[o, place, 0:quarter].astype(jnp.float32)
            coeff_imag = coeff_ref[o, place, quarter:both].astype(jnp.float32)
            ref_real = coeff_ref[o, refer, 0:quarter].astype(jnp.float32)
            ref_imag = coeff_ref[o, refer, quarter:both].astype(jnp.float32)
            prod_real = coeff_real * ref_real + coeff_imag * ref_imag
            prod_imag = coeff_imag * ref_real - coeff_real * ref_imag
            square = prod_real * prod_real + prod_imag * prod_imag + 1.0
            phase_ref[o, place] = (prod_imag * lax.rsqrt(square)).astype(jnp.bfloat16)
        return carry

    lax.fori_loop(0, timed, phase_one, 0, unroll=2)

    piece = min(128, wide_out)
    for start in range(0, wide_out, piece):
        here = slice(history * rows + start, history * rows + start + piece)
        above = jnp.zeros((piece, quarter), jnp.float32)
        below = jnp.ones((piece, quarter), jnp.float32)
        for o in range(orient):
            filtered = jnp.dot(
                spread_ref[start : start + piece], phase_ref[o], preferred_element_type=jnp.float32
            )
            filtered = filtered.astype(jnp.bfloat16).astype(jnp.float32)
            coeff_real = coeff_ref[o, here, 0:quarter].astype(jnp.float32)
            coeff_imag = coeff_ref[o, here, quarter:both].astype(jnp.float32)
            amplitude = coeff_real * coeff_real + coeff_imag * coeff_imag
            above = above + amplitude * filtered
            below = below + amplitude
        motion = (above / below).astype(out_ref.dtype)
        for i in range(piece // rows):
            out_ref[start // rows + i] = motion[i * rows : (i + 1) * rows]


def pixel_motion(segments, ref_frames, spread, mine, other, refer, left, right, rows, chunk, history):
    chips, frames_here, _, quarter = other.shape
    timed = history + chunk
    whole = refer is None
    slots = timed if whole else timed + NSEG
    smem = pl.BlockSpec(memory_space=pltpu.SMEM)
    vmem = pl.BlockSpec(memory_space=pltpu.VMEM)
    slot_bytes = ORIENT * rows * 2 * quarter * 2
    return pl.pallas_call(
        functools.partial(pixel_kernel, history=history, whole=whole),
        in_specs=[smem] * 2 + [vmem] * 6,
        out_specs=vmem,
        out_shape=jax.ShapeDtypeStruct((chunk, rows, quarter), jnp.bfloat16),
        scratch_shapes=[
            pltpu.VMEM((ORIENT, (slots - timed // 2) * rows, 2 * quarter), jnp.bfloat16),
            pltpu.VMEM((ORIENT, slots * rows, 2 * quarter), jnp.bfloat16),
            pltpu.VMEM((ORIENT, timed * rows, quarter), jnp.bfloat16),
        ],
        compiler_params=pltpu.CompilerParams(vmem_limit_bytes=4 * slots * slot_bytes + 16 * MIB),
        cost_estimate=pl.CostEstimate(
            flops=2 * ORIENT * rows * quarter * (slots * 2 * quarter + chunk * timed * rows),
            bytes_accessed=2 * (other.size + mine.size + right.size),
            transcendentals=ORIENT * timed * rows * quarter,
        ),
    )(segments, ref_frames, spread, mine, other, other if whole else refer, left, right)


def chunk_windows(mine, other, ref_frames, history_chips, chips):
    mine = lax.all_gather(mine, "chunk", axis=0, tiled=True)
    other = lax.all_gather(other, "chunk", axis=0, tiled=True)
    frames_here = mine.shape[1]
    core = lax.axis_index("core")
    device = ref_frames // frames_here
    place = device // CORES * frames_here + ref_frames % frames_here
    own = (device % CORES == core)[:, None, None]
    flat = (-1,) + mine.shape[2:]
    refer = jnp.where(own, mine.reshape(flat)[place], other.reshape(flat)[place])

    def cut(windows):
        before = jnp.zeros((history_chips,) + windows.shape[1:], windows.dtype)
        windows = jnp.concatenate([before, windows])
        return lax.dynamic_slice_in_dim(windows, lax.axis_index("chunk") * chips, history_chips + chips)

    return cut(mine), cut(other), refer


def body(video_frames, segments, ref_pick, band_taps, *, chunks, slabs):
    frames_here, size, _ = video_frames.shape
    quarter = size // 4
    slab_rows = quarter // slabs
    rows = slab_rows // CORES
    chunk = slabs * CORES * frames_here
    history = min(chunk * -(-(band_taps.shape[0] - 1) // chunk), segments.shape[0] - chunk)
    left = jnp.asarray(slab_left_table(rows, HALO, ORIENT))
    right = jnp.asarray(make_right_table(quarter, ORIENT))
    order = exchange_order(slabs // PAIR)
    windows = reduce_frames(video_frames, order, PAIR * slab_rows, HALO)
    spread, ref_frames = time_tables(segments, ref_pick, band_taps, rows, chunk, history)
    pieces = []
    for k, window in zip(order, windows):
        if k:
            window = lax.ppermute(window, "slab", [(chip, chip ^ (PAIR * k)) for chip in range(slabs)])
        pieces += [window, lax.ppermute(window, "slab", [(chip, chip ^ 1) for chip in range(slabs)])]
    mine, other = cut_windows(ref_frames, pieces, order, rows)
    other = lax.ppermute(other, "core", [(0, 1), (1, 0)])
    refer = None
    if chunks > 1:
        mine, other, refer = chunk_windows(mine, other, ref_frames, history // (CORES * frames_here), slabs)
    mine = own_coeffs(mine, left, right, rows)
    motion = pixel_motion(segments, ref_frames, spread, mine, other, refer, left, right, rows, chunk, history)
    motion = motion.reshape(slabs * CORES, frames_here, rows, quarter)
    motion = lax.all_to_all(motion, ("slab", "core"), split_axis=0, concat_axis=0, tiled=True)
    motion = jnp.swapaxes(motion, 0, 1).reshape(frames_here, quarter, quarter)
    return motion.astype(jnp.float32)


def solution(mesh):
    chips = mesh.shape["frames"] // CORES
    slabs = min(chips, QUART // (CORES * TILE))
    chunks = chips // slabs
    names = ("groups", "chunk", "slab", "core")
    cut = jax.sharding.Mesh(mesh.devices.reshape(mesh.shape["groups"], chunks, slabs, CORES), names)
    in_specs = (P(names, None, None), P("groups"), P("groups"), P())
    return jax.shard_map(
        functools.partial(body, chunks=chunks, slabs=slabs),
        mesh=cut, in_specs=in_specs, out_specs=P(names, None, None), check_vma=False,
    )
```

```python
import functools
import itertools
import math

import jax
import jax.numpy as jnp
import numpy as np
from jax import lax
from jax.experimental import pallas as pl
from jax.experimental.pallas import tpu as pltpu
from jax.sharding import PartitionSpec as P

IMG = 1024
ORIENT = 4
NSEG = 4
QUART = 256


blur_sigma = 2.0
gabor_sigma = 2.0
wave_number = math.pi / 2.0
gabor_gain = 2.0

HALO = 32
TILE = 16
DOWN = 2
SHARE = 2
CORES = 2
MIB = 1024 * 1024


def envelope_of(offset_grid):
    return np.float32(gabor_gain) * np.exp(
        -offset_grid * offset_grid / np.float32(2.0 * gabor_sigma * gabor_sigma)
    )


def waves(orient):
    angles = np.arange(orient, dtype=np.float32) * np.float32(math.pi / orient)
    wave_x = np.float32(wave_number) * np.cos(angles)
    wave_y = np.float32(wave_number) * np.sin(angles)
    return wave_x, wave_y


def slab_left_table(rows, halo, orient):
    offset = (
        np.arange(rows + 2 * halo, dtype=np.float32)[None, :]
        - np.float32(halo)
        - np.arange(rows, dtype=np.float32)[:, None]
    )
    wave_y = waves(orient)[1]
    phase = wave_y[:, None, None] * offset[None]
    envelope = envelope_of(offset)[None]
    table = np.stack([envelope * np.cos(phase), envelope * np.sin(phase)], axis=1)
    return table.reshape(orient * 2 * rows, rows + 2 * halo).astype(jnp.bfloat16)


def make_right_table(columns, halo, orient):
    window = columns + 2 * halo
    offset = (
        np.arange(window, dtype=np.float32)[:, None] - np.float32(halo) - np.arange(columns, dtype=np.float32)[None, :]
    )
    wave_x = waves(orient)[0]
    phase_x = wave_x[:, None, None] * offset[None]
    envelope = envelope_of(offset)[None]
    real_part = envelope * np.cos(phase_x)
    imag_part = envelope * np.sin(phase_x)
    table = np.zeros((orient // SHARE, SHARE, 2, window, 2, SHARE, columns), np.float32)
    for o in range(orient):
        group, i = divmod(o, SHARE)
        table[group, i, 0, :, 0, i] = real_part[o]
        table[group, i, 0, :, 1, i] = imag_part[o]
        table[group, i, 1, :, 0, i] = -imag_part[o]
        table[group, i, 1, :, 1, i] = real_part[o]
    return table.reshape(orient // SHARE, SHARE * 2 * window, 2 * SHARE * columns).astype(jnp.bfloat16)


def down_sums(full_size, quarter):
    position = np.arange(quarter, dtype=np.float32)[:, None]
    columns = np.arange(full_size, dtype=np.float32)[None, :]
    offset_grid = columns - np.float32(4.0) * position - np.float32(1.5)
    weight = np.exp(-offset_grid * offset_grid / np.float32(2.0 * blur_sigma * blur_sigma))
    return np.sum(weight, axis=1)


def down_block(position, column, shape, axis, sums):
    positions = position + lax.broadcasted_iota(jnp.int32, shape, 1 - axis)
    columns = column + lax.broadcasted_iota(jnp.int32, shape, axis)
    offset_grid = columns.astype(jnp.float32) - 4.0 * positions.astype(jnp.float32) - 1.5
    weight = jnp.exp(-offset_grid * offset_grid / (2.0 * blur_sigma * blur_sigma))
    inner = float(sums[len(sums) // 2])
    line = position + lax.broadcasted_iota(jnp.int32, tuple(1 if i == axis else n for i, n in enumerate(shape)), 1 - axis)
    scale = jnp.full(line.shape, 1.0 / inner, jnp.float32)
    for q in range(position, min(position + shape[1 - axis], len(sums))):
        if abs(float(sums[q]) - inner) > 1e-7 * inner:
            scale = jnp.where(line == q, 1.0 / float(sums[q]), scale)
    return (weight * scale).astype(jnp.bfloat16)


def build_down(down_t_ref, down_ref):
    size, quarter = down_t_ref.shape
    sums = down_sums(size, quarter)
    lanes = min(128, quarter)
    down_t_ref[...] = jnp.zeros_like(down_t_ref)
    down_ref[...] = jnp.zeros_like(down_ref)
    for row in range(0, size, 128):
        for lane in range(0, quarter, lanes):
            if 4 * (lane + lanes - 1) + 30 >= row and 4 * lane - 27 <= row + 127:
                down_t_ref[row : row + 128, lane : lane + lanes] = down_block(lane, row, (128, lanes), 0, sums)
    for row in range(0, quarter, 32):
        for lane in range(0, size, 128):
            if 4 * (row + 31) + 30 >= lane and 4 * row - 27 <= lane + 127:
                down_ref[row : row + 32, lane : lane + 128] = down_block(row, lane, (32, 128), 1, sums)


def reduce_kernel(frames_ref, *refs, order, halo, block):
    out_refs = refs[: len(order)]
    picture_ref, down_t_ref, down_ref, half_ref, total_ref, strip_ref, sems = refs[len(order) :]
    count, size, _ = picture_ref.shape
    quarter = down_ref.shape[0]
    strips, _, lanes = strip_ref.shape
    columns = lanes - 2 * halo
    window = out_refs[0].shape[1]

    copies = []
    for f in range(count):
        for i in range(size // block):
            here = pl.ds(i * block, block)
            copy = pltpu.make_async_copy(frames_ref.at[f, here], picture_ref.at[f, here], sems.at[f, i])
            copy.start()
            copies.append(copy)
    build_down(down_t_ref, down_ref)

    me = lax.axis_index("slab")
    reach = quarter
    for f in range(count):
        total_ref[...] = jnp.zeros_like(total_ref)
        for i in range(size // block):
            copies[f * (size // block) + i].wait()
            half_ref[...] = jnp.dot(
                picture_ref[f, i * block : (i + 1) * block], down_t_ref[...], preferred_element_type=jnp.float32
            ).astype(jnp.bfloat16)
            for row in range(0, block, reach):
                begin = i * block + row
                near = slice(max(begin // 4 - TILE, 0), min((begin + reach) // 4 + TILE, quarter))
                total_ref[near] += jnp.dot(
                    down_ref[near, begin : begin + reach], half_ref[row : row + reach], preferred_element_type=jnp.float32
                )
        for strip in range(strips):
            begin = strip * columns - halo
            moved = pltpu.roll(total_ref[...], (-begin) % quarter, 1)[:, 0:lanes]
            column = begin + lax.broadcasted_iota(jnp.int32, (quarter, lanes), 1)
            inside = (column >= 0) & (column < quarter)
            strip_ref[strip] = jnp.where(inside, moved, 0.0).astype(jnp.bfloat16)
        for k, out_ref in zip(order, out_refs):
            slab = lax.bitwise_xor(me, k)
            begin = pl.multiple_of(lax.rem(slab, DOWN) * (quarter - window), TILE)
            out_ref[f] = strip_ref[slab // DOWN, pl.ds(begin, window)]


def reduce_frames(video_frames, order, halo):
    count, size, _ = video_frames.shape
    quarter = size // 4
    strips = len(order) // DOWN
    lanes = quarter // strips + 2 * halo
    block = size // 2
    out = jax.ShapeDtypeStruct((count, quarter // DOWN + halo, lanes), jnp.bfloat16)
    return pl.pallas_call(
        functools.partial(reduce_kernel, order=order, halo=halo, block=block),
        in_specs=[pl.BlockSpec(memory_space=pltpu.HBM)],
        out_specs=[pl.BlockSpec(memory_space=pltpu.VMEM)] * len(order),
        out_shape=[out] * len(order),
        scratch_shapes=[
            pltpu.VMEM((count, size, size), jnp.bfloat16),
            pltpu.VMEM((size, quarter), jnp.bfloat16),
            pltpu.VMEM((quarter, size), jnp.bfloat16),
            pltpu.VMEM((block, quarter), jnp.bfloat16),
            pltpu.VMEM((quarter, quarter), jnp.float32),
            pltpu.VMEM((strips, quarter, lanes), jnp.bfloat16),
            pltpu.SemaphoreType.DMA((count, size // block)),
        ],
        compiler_params=pltpu.CompilerParams(vmem_limit_bytes=52 * MIB),
        cost_estimate=pl.CostEstimate(
            flops=2 * count * size * quarter * (size + quarter),
            bytes_accessed=2 * count * size * size,
            transcendentals=0,
        ),
    )(video_frames)


def exchange_order(slabs):
    far = sorted(range(slabs // 2, slabs), key=lambda k: k % 2)
    near = list(range(2, slabs // 2))
    turns = [k for pair in itertools.zip_longest(far, near) for k in pair if k is not None]
    return [0] + turns + [k for k in (1,) if k < slabs // 2]


def cut_kernel(*refs, order, halo):
    in_refs, (mine_ref, other_ref), padded_ref = refs[1:-3], refs[-3:-1], refs[-1]
    count, window, lanes = in_refs[0].shape
    height = mine_ref.shape[1]
    rows = height - 2 * halo
    me, core = lax.axis_index("slab"), lax.axis_index("core")
    edge = jnp.zeros((halo, count * lanes), jnp.bfloat16)
    padded_ref[0:halo] = edge
    padded_ref[halo + window :] = edge
    above = lax.rem(me, DOWN) * halo
    for k, in_ref in zip(order, in_refs):
        chip = lax.bitwise_xor(me, k)
        for f in range(count):
            padded_ref[halo : halo + window, f * lanes : (f + 1) * lanes] = in_ref[f]
        for out_ref, number in ((mine_ref, core), (other_ref, 1 - core)):
            out_ref[chip] = padded_ref[pl.ds(pl.multiple_of(above + number * rows, TILE), height)]


def cut_windows(ref_frames, pieces, order, halo):
    count, window, lanes = pieces[0].shape
    height = (window - halo) // CORES + 2 * halo
    out = jax.ShapeDtypeStruct((len(pieces), height, count * lanes), jnp.bfloat16)
    return pl.pallas_call(
        functools.partial(cut_kernel, order=order, halo=halo),
        in_specs=[pl.BlockSpec(memory_space=pltpu.SMEM)] + [pl.BlockSpec(memory_space=pltpu.VMEM)] * len(pieces),
        out_specs=[pl.BlockSpec(memory_space=pltpu.VMEM)] * 2,
        out_shape=[out, out],
        scratch_shapes=[pltpu.VMEM((window + 2 * halo, count * lanes), jnp.bfloat16)],
        compiler_params=pltpu.CompilerParams(vmem_limit_bytes=16 * MIB),
        cost_estimate=pl.CostEstimate(flops=0, bytes_accessed=8 * out.size, transcendentals=0),
    )(ref_frames, *pieces)


def time_kernel(segments_ref, pick_ref, taps_ref, spread_ref, frame_ref, *, history, frames, rows):
    chunk, timed = spread_ref.shape[0] // rows, spread_ref.shape[1] // rows
    nseg = pick_ref.shape[0]
    taps = taps_ref.shape[0]
    wide_out, wide_in = chunk * rows, timed * rows

    def count_one(t, totals):
        here = segments_ref[t]
        below = [total + (here < s).astype(jnp.int32) for s, total in enumerate(totals[0])]
        same = [total + (here == s).astype(jnp.int32) for s, total in enumerate(totals[1])]
        return tuple(below), tuple(same)

    zeros = tuple(jnp.int32(0) for _ in range(nseg))
    starts, counts = lax.fori_loop(0, frames, count_one, (zeros, zeros), unroll=8)
    for s in range(nseg):
        frame_ref[s] = starts[s] + lax.rem(pick_ref[s], counts[s])

    lag = history + lax.broadcasted_iota(jnp.int32, (chunk, timed), 0) - lax.broadcasted_iota(
        jnp.int32, (chunk, timed), 1
    )
    if history:
        first = lax.axis_index("chunk") * chunk - history
        real = first + lax.broadcasted_iota(jnp.int32, (chunk, timed), 1) >= 0
        lag = jnp.where(real, lag, -1)
    matrix = jnp.zeros((chunk, timed), jnp.float32)
    for k in range(taps):
        matrix = jnp.where(lag == k, taps_ref[k], matrix)
    repeat_left = (
        lax.broadcasted_iota(jnp.int32, (wide_out, chunk), 0) // rows
        == lax.broadcasted_iota(jnp.int32, (wide_out, chunk), 1)
    ).astype(jnp.bfloat16)
    repeat_right = (
        lax.broadcasted_iota(jnp.int32, (timed, wide_in), 1) // rows
        == lax.broadcasted_iota(jnp.int32, (timed, wide_in), 0)
    ).astype(jnp.bfloat16)
    tall = jnp.dot(repeat_left, matrix.astype(jnp.bfloat16), preferred_element_type=jnp.float32)
    tall = tall.astype(jnp.bfloat16)
    piece = min(128, wide_out)
    for start in range(0, wide_out, piece):
        part = jnp.dot(tall[start : start + piece], repeat_right, preferred_element_type=jnp.float32)
        same_row = (
            lax.broadcasted_iota(jnp.int32, (piece, wide_in), 0) % rows
            == lax.broadcasted_iota(jnp.int32, (piece, wide_in), 1) % rows
        )
        spread_ref[start : start + piece] = jnp.where(same_row, part, 0.0).astype(jnp.bfloat16)


def time_tables(segments, ref_pick, band_taps, rows, chunk, history):
    frames = segments.shape[0]
    wide_out, wide_in = chunk * rows, (history + chunk) * rows
    smem = pl.BlockSpec(memory_space=pltpu.SMEM)
    return pl.pallas_call(
        functools.partial(time_kernel, history=history, frames=frames, rows=rows),
        in_specs=[smem] * 3,
        out_specs=[pl.BlockSpec(memory_space=pltpu.VMEM), smem],
        out_shape=[
            jax.ShapeDtypeStruct((wide_out, wide_in), jnp.bfloat16),
            jax.ShapeDtypeStruct(ref_pick.shape, jnp.int32),
        ],
        compiler_params=pltpu.CompilerParams(vmem_limit_bytes=16 * MIB),
        cost_estimate=pl.CostEstimate(
            flops=2 * wide_out * wide_in * chunk, bytes_accessed=2 * wide_out * wide_in, transcendentals=0
        ),
    )(segments, ref_pick, band_taps.astype(jnp.float32))


def filter_frames(window_refs, left_ref, right_ref, stacked_ref, put):
    groups, deep, _ = right_ref.shape
    lanes = deep // (2 * SHARE)
    rows = left_ref.shape[0] // (2 * SHARE * groups)
    bands = rows // TILE
    pair = window_refs[0].shape[1] // lanes
    many = len(window_refs) * pair * TILE
    for n, window in enumerate(window_refs):
        stacked = jnp.dot(left_ref[...], window[...], preferred_element_type=jnp.float32).astype(jnp.bfloat16)
        for oz in range(2 * SHARE * groups):
            group, place = divmod(oz, 2 * SHARE)
            for band in range(bands):
                begin = oz * rows + band * TILE
                for f in range(pair):
                    row = band * many + (n * pair + f) * TILE
                    stacked_ref[group, row : row + TILE, place * lanes : (place + 1) * lanes] = stacked[
                        begin : begin + TILE, f * lanes : (f + 1) * lanes
                    ]
    step = min(256, many)
    block = pair * TILE
    for group in range(groups):
        for band in range(bands):
            for start in range(0, many, step):
                stop = min(start + step, many)
                coeff = jnp.dot(
                    stacked_ref[group, band * many + start : band * many + stop],
                    right_ref[group],
                    preferred_element_type=jnp.float32,
                ).astype(jnp.bfloat16)
                for place in range(start, stop, block):
                    put(group, band, place // block, coeff[place - start : place - start + block])


def coeff_kernel(window_ref, left_ref, right_ref, coeff_ref, stacked_ref):
    chips = window_ref.shape[0]
    block = coeff_ref.shape[2] // chips

    def put(group, band, i, values):
        coeff_ref[group, band, i * block : (i + 1) * block] = values

    filter_frames([window_ref.at[chip] for chip in range(chips)], left_ref, right_ref, stacked_ref, put)


def own_coeffs(windows, left, right, rows, frames_here):
    groups, deep, wide = right.shape
    vmem = pl.BlockSpec(memory_space=pltpu.VMEM)
    many = windows.shape[0] * frames_here * TILE
    out = jax.ShapeDtypeStruct((groups, rows // TILE, many, wide), jnp.bfloat16)
    return pl.pallas_call(
        coeff_kernel,
        in_specs=[vmem] * 3,
        out_specs=vmem,
        out_shape=out,
        scratch_shapes=[pltpu.VMEM((groups, rows // TILE * many, deep), jnp.bfloat16)],
        compiler_params=pltpu.CompilerParams(vmem_limit_bytes=8 * out.size + 16 * MIB),
        cost_estimate=pl.CostEstimate(
            flops=4 * out.size * deep, bytes_accessed=2 * (windows.size + out.size), transcendentals=0
        ),
    )(windows, left, right)


def pixel_kernel(
    segments_ref, ref_frame_ref, spread_ref, mine_ref, other_ref, refer_ref, left_ref, right_ref, out_ref,
    stacked_ref, coeff_ref, phase_ref, *, history, whole,
):
    chips = other_ref.shape[0]
    groups, bands, _, wide = coeff_ref.shape
    half = wide // 2
    block = mine_ref.shape[2] // chips
    pair = block // TILE
    chunk = out_ref.shape[0] * pair
    timed = history + chunk
    core = lax.axis_index("core")

    for chip in range(chips):
        place = pl.ds(pl.multiple_of((chip * CORES + core) * block, block), block)
        for group in range(groups):
            for band in range(bands):
                coeff_ref[group, band, place] = mine_ref[group, band, chip * block : (chip + 1) * block]

    def put(group, band, i, values):
        if i < chips:
            place = pl.ds(pl.multiple_of((i * CORES + 1 - core) * block, block), block)
        else:
            place = slice(timed * TILE + (i - chips) * block, timed * TILE + (i - chips + 1) * block)
        coeff_ref[group, band, place] = values

    windows = [other_ref.at[chip] for chip in range(chips)]
    if not whole:
        windows += [refer_ref.at[i] for i in range(refer_ref.shape[0])]
    filter_frames(windows, left_ref, right_ref, stacked_ref, put)

    def phase_one(slot, carry):
        place = pl.ds(pl.multiple_of(slot * TILE, TILE), TILE)
        if whole:
            source = ref_frame_ref[segments_ref[slot]]
        else:
            first = lax.axis_index("chunk") * chunk - history
            source = timed + segments_ref[jnp.maximum(first + slot, 0)]
        refer = pl.ds(pl.multiple_of(source * TILE, TILE), TILE)
        for group in range(groups):
            for band in range(bands):
                coeff_real = coeff_ref[group, band, place, 0:half].astype(jnp.float32)
                coeff_imag = coeff_ref[group, band, place, half:wide].astype(jnp.float32)
                ref_real = coeff_ref[group, band, refer, 0:half].astype(jnp.float32)
                ref_imag = coeff_ref[group, band, refer, half:wide].astype(jnp.float32)
                prod_real = coeff_real * ref_real + coeff_imag * ref_imag
                prod_imag = coeff_imag * ref_real - coeff_real * ref_imag
                square = prod_real * prod_real + prod_imag * prod_imag + 1.0
                phase = (prod_imag * lax.rsqrt(square)).astype(jnp.bfloat16)
                phase_ref[band, place, group * half : (group + 1) * half] = phase
        return carry

    lax.fori_loop(0, timed, phase_one, 0, unroll=2)

    piece = min(128, chunk * TILE)
    columns = half // SHARE
    left_half = lax.broadcasted_iota(jnp.int32, (TILE, half), 1) < columns
    for band in range(bands):
        for start in range(0, chunk * TILE, piece):
            here = slice(history * TILE + start, history * TILE + start + piece)
            filtered = jnp.dot(spread_ref[start : start + piece], phase_ref[band], preferred_element_type=jnp.float32)
            filtered = filtered.astype(jnp.bfloat16).astype(jnp.float32)
            above = jnp.zeros((piece, half), jnp.float32)
            below = jnp.zeros((piece, half), jnp.float32)
            for group in range(groups):
                coeff_real = coeff_ref[group, band, here, 0:half].astype(jnp.float32)
                coeff_imag = coeff_ref[group, band, here, half:wide].astype(jnp.float32)
                amplitude = coeff_real * coeff_real + coeff_imag * coeff_imag
                above = above + amplitude * filtered[:, group * half : (group + 1) * half]
                below = below + amplitude
            above = above + pltpu.roll(above, columns, 1)
            below = below + pltpu.roll(below, columns, 1)
            motion = above / (below + 1.0)
            for i in range(piece // block):
                first, second = motion[i * block : i * block + TILE], motion[i * block + TILE : (i + 1) * block]
                both = jnp.where(left_half, first, second).astype(out_ref.dtype)
                out_ref[start // block + i, band * TILE : (band + 1) * TILE] = both


def pixel_motion(segments, ref_frames, spread, mine, other, refer, left, right, chunk, history):
    chips = other.shape[0]
    groups, bands, many, wide = mine.shape
    deep = right.shape[1]
    timed = history + chunk
    whole = refer is None
    slots = timed if whole else timed + NSEG
    pair = many // chips // TILE
    smem = pl.BlockSpec(memory_space=pltpu.SMEM)
    vmem = pl.BlockSpec(memory_space=pltpu.VMEM)
    return pl.pallas_call(
        functools.partial(pixel_kernel, history=history, whole=whole),
        in_specs=[smem] * 2 + [vmem] * 6,
        out_specs=vmem,
        out_shape=jax.ShapeDtypeStruct((chunk // pair, bands * TILE, wide // 2), jnp.bfloat16),
        scratch_shapes=[
            pltpu.VMEM((groups, bands * (slots - timed // 2) * TILE, deep), jnp.bfloat16),
            pltpu.VMEM((groups, bands, slots * TILE, wide), jnp.bfloat16),
            pltpu.VMEM((bands, timed * TILE, groups * wide // 2), jnp.bfloat16),
        ],
        compiler_params=pltpu.CompilerParams(vmem_limit_bytes=8 * groups * bands * slots * TILE * wide + 16 * MIB),
        cost_estimate=pl.CostEstimate(
            flops=2 * groups * bands * TILE * wide * (slots * deep + chunk * timed * TILE // 2),
            bytes_accessed=2 * (other.size + mine.size + right.size),
            transcendentals=groups * bands * TILE * timed * wide // 2,
        ),
    )(segments, ref_frames, spread, mine, other, other if whole else refer, left, right)


def join_kernel(tiles_ref, out_ref):
    count, quarter, _ = out_ref.shape
    devices, rows, lanes = tiles_ref.shape
    columns = lanes // count
    strips = quarter // columns
    left = lax.broadcasted_iota(jnp.int32, (rows, lanes), 1) < columns
    for strip in range(0, strips, 2):
        for i in range(devices // strips):
            one = tiles_ref[strip * devices // strips + i].astype(jnp.float32)
            two = tiles_ref[(strip + 1) * devices // strips + i].astype(jnp.float32)
            here = slice(strip * columns, (strip + 2) * columns)
            out_ref[0, i * rows : (i + 1) * rows, here] = jnp.where(left, one, pltpu.roll(two, columns, 1))
            out_ref[1, i * rows : (i + 1) * rows, here] = jnp.where(left, pltpu.roll(one, columns, 1), two)


def join_tiles(tiles, quarter):
    vmem = pl.BlockSpec(memory_space=pltpu.VMEM)
    return pl.pallas_call(
        join_kernel,
        in_specs=[vmem],
        out_specs=vmem,
        out_shape=jax.ShapeDtypeStruct((2, quarter, quarter), jnp.float32),
        compiler_params=pltpu.CompilerParams(vmem_limit_bytes=16 * MIB),
        cost_estimate=pl.CostEstimate(flops=tiles.size, bytes_accessed=6 * tiles.size, transcendentals=0),
    )(tiles)


def chunk_windows(mine, other, ref_frames, frames_here, history_chips, chips):
    mine = lax.all_gather(mine, "chunk", axis=0, tiled=True)
    other = lax.all_gather(other, "chunk", axis=0, tiled=True)
    height = mine.shape[1]
    core = lax.axis_index("core")
    device, f = ref_frames // frames_here, ref_frames % frames_here
    own = (device % CORES == core)[:, None, None]

    def pick(windows):
        return windows.reshape(windows.shape[0], height, frames_here, -1)[device // CORES, :, f]

    refer = jnp.where(own, pick(mine), pick(other))
    refer = refer.reshape(NSEG // frames_here, frames_here, height, -1)
    refer = jnp.swapaxes(refer, 1, 2).reshape(NSEG // frames_here, height, -1)

    def cut(windows):
        before = jnp.zeros((history_chips,) + windows.shape[1:], windows.dtype)
        windows = jnp.concatenate([before, windows])
        return lax.dynamic_slice_in_dim(windows, lax.axis_index("chunk") * chips, history_chips + chips)

    return cut(mine), cut(other), refer


def body(video_frames, segments, ref_pick, band_taps, *, chunks, slabs):
    frames_here, size, _ = video_frames.shape
    quarter = size // 4
    rows = quarter // (DOWN * CORES)
    columns = quarter * DOWN // slabs
    chunk = slabs * CORES * frames_here
    history = min(chunk * -(-(band_taps.shape[0] - 1) // chunk), segments.shape[0] - chunk)
    left = jnp.asarray(slab_left_table(rows, HALO, ORIENT))
    right = jnp.asarray(make_right_table(columns, HALO, ORIENT))
    order = exchange_order(slabs)
    windows = reduce_frames(video_frames, order, HALO)
    spread, ref_frames = time_tables(segments, ref_pick, band_taps, TILE, chunk, history)
    pieces = [windows[0]]
    for k, window in zip(order[1:], windows[1:]):
        pieces.append(lax.ppermute(window, "slab", [(chip, chip ^ k) for chip in range(slabs)]))
    mine, other = cut_windows(ref_frames, pieces, order, HALO)
    other = lax.ppermute(other, "core", [(0, 1), (1, 0)])
    refer = None
    if chunks > 1:
        history_chips = history // (CORES * frames_here)
        mine, other, refer = chunk_windows(mine, other, ref_frames, frames_here, history_chips, slabs)
    mine = own_coeffs(mine, left, right, rows, frames_here)
    motion = pixel_motion(segments, ref_frames, spread, mine, other, refer, left, right, chunk, history)
    motion = lax.all_to_all(motion, ("slab", "core"), split_axis=0, concat_axis=0, tiled=True)
    return join_tiles(motion, quarter)


def solution(mesh):
    chips = mesh.shape["frames"] // CORES
    slabs = min(chips, QUART * DOWN // (2 * HALO))
    chunks = chips // slabs
    names = ("groups", "chunk", "slab", "core")
    cut = jax.sharding.Mesh(mesh.devices.reshape(mesh.shape["groups"], chunks, slabs, CORES), names)
    in_specs = (P(names, None, None), P("groups"), P("groups"), P())
    return jax.shard_map(
        functools.partial(body, chunks=chunks, slabs=slabs),
        mesh=cut, in_specs=in_specs, out_specs=P(names, None, None), check_vma=False,
    )
```

```python
import functools
import math

import jax
import jax.numpy as jnp
import numpy as np
from jax import lax
from jax.experimental import pallas as pl
from jax.experimental.pallas import tpu as pltpu
from jax.sharding import PartitionSpec as P

IMG = 1024
ORIENT = 4
NSEG = 4
QUART = 256


blur_sigma = 2.0
gabor_sigma = 2.0
wave_number = math.pi / 2.0
gabor_gain = 2.0

HALO = 32
TILE = 16
CORES = 2
MIB = 1024 * 1024


def envelope_of(offset_grid):
    return np.float32(gabor_gain) * np.exp(
        -offset_grid * offset_grid / np.float32(2.0 * gabor_sigma * gabor_sigma)
    )


def waves(orient):
    angles = np.arange(orient, dtype=np.float32) * np.float32(math.pi / orient)
    wave_x = np.float32(wave_number) * np.cos(angles)
    wave_y = np.float32(wave_number) * np.sin(angles)
    return wave_x, wave_y


def slab_left_table(rows, halo, orient):
    offset = (
        np.arange(rows + 2 * halo, dtype=np.float32)[None, :]
        - np.float32(halo)
        - np.arange(rows, dtype=np.float32)[:, None]
    )
    wave_y = waves(orient)[1]
    phase = wave_y[:, None, None] * offset[None]
    envelope = envelope_of(offset)[None]
    table = np.stack([envelope * np.cos(phase), envelope * np.sin(phase)], axis=1)
    return table.reshape(orient * 2 * rows, rows + 2 * halo).astype(jnp.bfloat16)


def make_right_table(quarter, orient):
    position = np.arange(quarter, dtype=np.float32)
    offset = position[:, None] - position[None, :]
    wave_x = waves(orient)[0]
    phase_x = wave_x[:, None, None] * offset[None]
    envelope = envelope_of(offset)[None]
    real_part = envelope * np.cos(phase_x)
    imag_part = envelope * np.sin(phase_x)
    upper_half = np.concatenate([real_part, imag_part], axis=2)
    lower_half = np.concatenate([-imag_part, real_part], axis=2)
    return np.concatenate([upper_half, lower_half], axis=1).astype(jnp.bfloat16)


def down_sums(full_size, quarter):
    position = np.arange(quarter, dtype=np.float32)[:, None]
    columns = np.arange(full_size, dtype=np.float32)[None, :]
    offset_grid = columns - np.float32(4.0) * position - np.float32(1.5)
    weight = np.exp(-offset_grid * offset_grid / np.float32(2.0 * blur_sigma * blur_sigma))
    return np.sum(weight, axis=1)


def down_block(position, column, shape, axis, sums):
    positions = position + lax.broadcasted_iota(jnp.int32, shape, 1 - axis)
    columns = column + lax.broadcasted_iota(jnp.int32, shape, axis)
    offset_grid = columns.astype(jnp.float32) - 4.0 * positions.astype(jnp.float32) - 1.5
    weight = jnp.exp(-offset_grid * offset_grid / (2.0 * blur_sigma * blur_sigma))
    inner = float(sums[len(sums) // 2])
    line = position + lax.broadcasted_iota(jnp.int32, tuple(1 if i == axis else n for i, n in enumerate(shape)), 1 - axis)
    scale = jnp.full(line.shape, 1.0 / inner, jnp.float32)
    for q in range(position, min(position + shape[1 - axis], len(sums))):
        if abs(float(sums[q]) - inner) > 1e-7 * inner:
            scale = jnp.where(line == q, 1.0 / float(sums[q]), scale)
    return (weight * scale).astype(jnp.bfloat16)


def build_down(down_t_ref, down_ref):
    size, quarter = down_t_ref.shape
    sums = down_sums(size, quarter)
    lanes = min(128, quarter)
    down_t_ref[...] = jnp.zeros_like(down_t_ref)
    down_ref[...] = jnp.zeros_like(down_ref)
    for row in range(0, size, 128):
        for lane in range(0, quarter, lanes):
            if 4 * (lane + lanes - 1) + 30 >= row and 4 * lane - 27 <= row + 127:
                down_t_ref[row : row + 128, lane : lane + lanes] = down_block(lane, row, (128, lanes), 0, sums)
    for row in range(0, quarter, 32):
        for lane in range(0, size, 128):
            if 4 * (row + 31) + 30 >= lane and 4 * row - 27 <= lane + 127:
                down_ref[row : row + 32, lane : lane + 128] = down_block(row, lane, (32, 128), 1, sums)


def reduce_kernel(frames_ref, *refs, near, rows, halo, block):
    out_refs = refs[: 1 + len(near)]
    picture_ref, down_t_ref, down_ref, half_ref, total_ref, padded_ref, sems = refs[1 + len(near) :]
    count, size, _ = picture_ref.shape
    quarter = down_ref.shape[0]

    copies = []
    for f in range(count):
        for i in range(size // block):
            here = pl.ds(i * block, block)
            copy = pltpu.make_async_copy(frames_ref.at[f, here], picture_ref.at[f, here], sems.at[f, i])
            copy.start()
            copies.append(copy)
    build_down(down_t_ref, down_ref)
    edge = jnp.zeros((halo, quarter), jnp.bfloat16)
    padded_ref[0:halo] = edge
    padded_ref[halo + quarter :] = edge

    me = lax.axis_index("slab")
    reach = quarter
    for f in range(count):
        total_ref[...] = jnp.zeros_like(total_ref)
        for i in range(size // block):
            copies[f * (size // block) + i].wait()
            half_ref[...] = jnp.dot(
                picture_ref[f, i * block : (i + 1) * block], down_t_ref[...], preferred_element_type=jnp.float32
            ).astype(jnp.bfloat16)
            for row in range(0, block, reach):
                begin = i * block + row
                touched = slice(max(begin // 4 - TILE, 0), min((begin + reach) // 4 + TILE, quarter))
                total_ref[touched] += jnp.dot(
                    down_ref[touched, begin : begin + reach], half_ref[row : row + reach], preferred_element_type=jnp.float32
                )
        padded_ref[halo : halo + quarter] = total_ref[...].astype(jnp.bfloat16)
        for k, out_ref in zip(near, out_refs[1:]):
            slab = lax.bitwise_xor(me, k)
            out_ref[f] = padded_ref[pl.ds(pl.multiple_of(slab * rows, rows), rows + 2 * halo)]
        across = out_refs[0].shape[1]
        begin = jnp.where(me < len(near), quarter - across, 0)
        out_refs[0][f] = padded_ref[pl.ds(pl.multiple_of(halo + begin, TILE), across)]


def reduce_frames(video_frames, near, rows, halo):
    count, size, _ = video_frames.shape
    quarter = 2 * len(near) * rows
    block = size // 2
    out = jax.ShapeDtypeStruct((count, rows + 2 * halo, quarter), jnp.bfloat16)
    across = jax.ShapeDtypeStruct((count, quarter // 2 + halo, quarter), jnp.bfloat16)
    return pl.pallas_call(
        functools.partial(reduce_kernel, near=near, rows=rows, halo=halo, block=block),
        in_specs=[pl.BlockSpec(memory_space=pltpu.HBM)],
        out_specs=[pl.BlockSpec(memory_space=pltpu.VMEM)] * (1 + len(near)),
        out_shape=[across] + [out] * len(near),
        scratch_shapes=[
            pltpu.VMEM((count, size, size), jnp.bfloat16),
            pltpu.VMEM((size, quarter), jnp.bfloat16),
            pltpu.VMEM((quarter, size), jnp.bfloat16),
            pltpu.VMEM((block, quarter), jnp.bfloat16),
            pltpu.VMEM((quarter, quarter), jnp.float32),
            pltpu.VMEM((quarter + 2 * halo, quarter), jnp.bfloat16),
            pltpu.SemaphoreType.DMA((count, size // block)),
        ],
        compiler_params=pltpu.CompilerParams(vmem_limit_bytes=52 * MIB),
        cost_estimate=pl.CostEstimate(
            flops=2 * count * size * quarter * (size + quarter),
            bytes_accessed=2 * count * size * size,
            transcendentals=0,
        ),
    )(video_frames)


def pass_kernel(rows_ref, *refs, near, rows, halo):
    out_refs, padded_ref = refs[:-1], refs[-1]
    count, across, quarter = rows_ref.shape
    me = lax.axis_index("slab")
    edge = jnp.zeros((halo, quarter), jnp.bfloat16)
    above = jnp.where(me < len(near), 0, halo)
    for f in range(count):
        padded_ref[f, 0:halo] = edge
        padded_ref[f, halo + across :] = edge
        padded_ref[f, halo : halo + across] = rows_ref[f]
        for k, out_ref in zip(near, out_refs):
            place = lax.rem(lax.bitwise_xor(me, k), len(near)) * rows + above
            out_ref[f] = padded_ref[f, pl.ds(pl.multiple_of(place, TILE), rows + 2 * halo)]


def pass_on(across, near, rows, halo):
    count, height, quarter = across.shape
    vmem = pl.BlockSpec(memory_space=pltpu.VMEM)
    out = jax.ShapeDtypeStruct((count, rows + 2 * halo, quarter), jnp.bfloat16)
    return pl.pallas_call(
        functools.partial(pass_kernel, near=near, rows=rows, halo=halo),
        in_specs=[vmem],
        out_specs=[vmem] * len(near),
        out_shape=[out] * len(near),
        scratch_shapes=[pltpu.VMEM((count, height + 2 * halo, quarter), jnp.bfloat16)],
        compiler_params=pltpu.CompilerParams(vmem_limit_bytes=16 * MIB),
        cost_estimate=pl.CostEstimate(flops=0, bytes_accessed=4 * len(near) * out.size, transcendentals=0),
    )(across)


def cut_kernel(*refs, near, rows):
    in_refs, (mine_ref, other_ref) = refs[: len(near)], refs[-2:]
    window = mine_ref.shape[2]
    me, core = lax.axis_index("slab"), lax.axis_index("core")
    for k, in_ref in zip(near, in_refs):
        chip = lax.rem(lax.bitwise_xor(me, k), len(near))
        mine_ref[chip] = in_ref[:, pl.ds(pl.multiple_of(core * rows, rows), window)]
        other_ref[chip] = in_ref[:, pl.ds(pl.multiple_of((1 - core) * rows, rows), window)]


def cut_windows(pieces, near, rows, after):
    count, window, quarter = pieces[0].shape
    out = jax.ShapeDtypeStruct((len(pieces), count, window - rows, quarter), jnp.bfloat16)
    return pl.pallas_call(
        functools.partial(cut_kernel, near=near, rows=rows),
        in_specs=[pl.BlockSpec(memory_space=pltpu.VMEM)] * len(pieces) + [pl.BlockSpec(memory_space=pl.ANY)] * len(after),
        out_specs=[pl.BlockSpec(memory_space=pltpu.VMEM)] * 2,
        out_shape=[out, out],
        compiler_params=pltpu.CompilerParams(vmem_limit_bytes=16 * MIB),
        cost_estimate=pl.CostEstimate(flops=0, bytes_accessed=8 * out.size, transcendentals=0),
    )(*pieces, *after)


def time_kernel(segments_ref, pick_ref, taps_ref, spread_ref, frame_ref, *, history, frames, rows):
    chunk, timed = spread_ref.shape[0] // rows, spread_ref.shape[1] // rows
    nseg = pick_ref.shape[0]
    taps = taps_ref.shape[0]
    wide_out, wide_in = chunk * rows, timed * rows

    def count_one(t, totals):
        here = segments_ref[t]
        below = [total + (here < s).astype(jnp.int32) for s, total in enumerate(totals[0])]
        same = [total + (here == s).astype(jnp.int32) for s, total in enumerate(totals[1])]
        return tuple(below), tuple(same)

    zeros = tuple(jnp.int32(0) for _ in range(nseg))
    starts, counts = lax.fori_loop(0, frames, count_one, (zeros, zeros), unroll=8)
    for s in range(nseg):
        frame_ref[s] = starts[s] + lax.rem(pick_ref[s], counts[s])

    lag = history + lax.broadcasted_iota(jnp.int32, (chunk, timed), 0) - lax.broadcasted_iota(
        jnp.int32, (chunk, timed), 1
    )
    if history:
        first = lax.axis_index("chunk") * chunk - history
        real = first + lax.broadcasted_iota(jnp.int32, (chunk, timed), 1) >= 0
        lag = jnp.where(real, lag, -1)
    matrix = jnp.zeros((chunk, timed), jnp.float32)
    for k in range(taps):
        matrix = jnp.where(lag == k, taps_ref[k], matrix)
    repeat_left = (
        lax.broadcasted_iota(jnp.int32, (wide_out, chunk), 0) // rows
        == lax.broadcasted_iota(jnp.int32, (wide_out, chunk), 1)
    ).astype(jnp.bfloat16)
    repeat_right = (
        lax.broadcasted_iota(jnp.int32, (timed, wide_in), 1) // rows
        == lax.broadcasted_iota(jnp.int32, (timed, wide_in), 0)
    ).astype(jnp.bfloat16)
    tall = jnp.dot(repeat_left, matrix.astype(jnp.bfloat16), preferred_element_type=jnp.float32)
    tall = tall.astype(jnp.bfloat16)
    piece = min(128, wide_out)
    for start in range(0, wide_out, piece):
        part = jnp.dot(tall[start : start + piece], repeat_right, preferred_element_type=jnp.float32)
        same_row = (
            lax.broadcasted_iota(jnp.int32, (piece, wide_in), 0) % rows
            == lax.broadcasted_iota(jnp.int32, (piece, wide_in), 1) % rows
        )
        spread_ref[start : start + piece] = jnp.where(same_row, part, 0.0).astype(jnp.bfloat16)


def time_tables(segments, ref_pick, band_taps, rows, chunk, history):
    frames = segments.shape[0]
    wide_out, wide_in = chunk * rows, (history + chunk) * rows
    smem = pl.BlockSpec(memory_space=pltpu.SMEM)
    return pl.pallas_call(
        functools.partial(time_kernel, history=history, frames=frames, rows=rows),
        in_specs=[smem] * 3,
        out_specs=[pl.BlockSpec(memory_space=pltpu.VMEM), smem],
        out_shape=[
            jax.ShapeDtypeStruct((wide_out, wide_in), jnp.bfloat16),
            jax.ShapeDtypeStruct(ref_pick.shape, jnp.int32),
        ],
        compiler_params=pltpu.CompilerParams(vmem_limit_bytes=16 * MIB),
        cost_estimate=pl.CostEstimate(
            flops=2 * wide_out * wide_in * chunk, bytes_accessed=2 * wide_out * wide_in, transcendentals=0
        ),
    )(segments, ref_pick, band_taps.astype(jnp.float32))


def filter_frames(window_refs, left_ref, right_ref, stacked_ref, put):
    rows = left_ref.shape[0] // (2 * right_ref.shape[0])
    orient, both, _ = right_ref.shape
    quarter = both // 2
    for n, window in enumerate(window_refs):
        stacked = jnp.dot(left_ref[...], window[...], preferred_element_type=jnp.float32).astype(jnp.bfloat16)
        for o in range(orient):
            for z in range(2):
                begin = (o * 2 + z) * rows
                stacked_ref[o, n * rows : (n + 1) * rows, z * quarter : (z + 1) * quarter] = stacked[begin : begin + rows]
    many = len(window_refs) * rows
    step = min(256, many)
    pair = 2 * rows
    for o in range(orient):
        for start in range(0, many, step):
            stop = min(start + step, many)
            coeff = jnp.dot(stacked_ref[o, start:stop], right_ref[o], preferred_element_type=jnp.float32)
            coeff = coeff.astype(jnp.bfloat16)
            for place in range(start, stop, pair):
                put(o, place // pair, coeff[place - start : place - start + pair])


def coeff_kernel(window_ref, left_ref, right_ref, coeff_ref, stacked_ref):
    chips, frames_here, window, quarter = window_ref.shape
    rows = left_ref.shape[0] // (2 * right_ref.shape[0])

    def put(o, i, block):
        coeff_ref[o, 2 * i * rows : 2 * (i + 1) * rows] = block

    filter_frames(
        [window_ref.at[chip, f] for chip in range(chips) for f in range(frames_here)], left_ref, right_ref, stacked_ref, put
    )


def own_coeffs(windows, left, right, rows):
    chips, frames_here, _, quarter = windows.shape
    vmem = pl.BlockSpec(memory_space=pltpu.VMEM)
    out = jax.ShapeDtypeStruct((ORIENT, chips * frames_here * rows, 2 * quarter), jnp.bfloat16)
    return pl.pallas_call(
        coeff_kernel,
        in_specs=[vmem] * 3,
        out_specs=vmem,
        out_shape=out,
        scratch_shapes=[pltpu.VMEM(out.shape, jnp.bfloat16)],
        compiler_params=pltpu.CompilerParams(vmem_limit_bytes=8 * out.size + 16 * MIB),
        cost_estimate=pl.CostEstimate(
            flops=8 * out.size * quarter, bytes_accessed=2 * (windows.size + out.size), transcendentals=0
        ),
    )(windows, left, right)


def pixel_kernel(
    segments_ref, ref_frame_ref, spread_ref, other_ref, refer_ref, left_ref, right_ref, *refs, places, history, whole
):
    ready_refs, (out_ref, stacked_ref, coeff_ref, phase_ref) = refs[:-4], refs[-4:]
    chips, frames_here, _, quarter = other_ref.shape
    chunk, rows, _ = out_ref.shape
    orient = right_ref.shape[0]
    nseg = ref_frame_ref.shape[0]
    both = 2 * quarter
    timed = history + chunk
    wide_out = chunk * rows
    pair = frames_here * rows
    core = lax.axis_index("core")

    def place_of(half, twin, chip):
        upper = 0 if half is None else lax.rem(lax.axis_index("slab") // chips + half, 2) * chips
        return pl.ds(pl.multiple_of(((upper + chip) * CORES + lax.rem(core + twin, CORES)) * pair, pair), pair)

    for ready_ref, (half, twin) in zip(ready_refs, places):
        for chip in range(ready_ref.shape[1] // pair):
            for o in range(orient):
                coeff_ref[o, place_of(half, twin, chip)] = ready_ref[o, chip * pair : (chip + 1) * pair]

    def put(o, i, block):
        if i < chips:
            coeff_ref[o, place_of(*places[-1], i)] = block
        else:
            begin = timed * rows + (i - chips) * pair
            coeff_ref[o, begin : begin + pair] = block

    windows = [other_ref.at[chip, f] for chip in range(chips) for f in range(frames_here)]
    if not whole:
        windows += [refer_ref.at[s] for s in range(nseg)]
    filter_frames(windows, left_ref, right_ref, stacked_ref, put)

    def phase_one(slot, carry):
        place = pl.ds(pl.multiple_of(slot * rows, rows), rows)
        if whole:
            source = ref_frame_ref[segments_ref[slot]]
        else:
            first = lax.axis_index("chunk") * chunk - history
            source = timed + segments_ref[jnp.maximum(first + slot, 0)]
        refer = pl.ds(pl.multiple_of(source * rows, rows), rows)
        for o in range(orient):
            coeff_real = coeff_ref[o, place, 0:quarter].astype(jnp.float32)
            coeff_imag = coeff_ref[o, place, quarter:both].astype(jnp.float32)
            ref_real = coeff_ref[o, refer, 0:quarter].astype(jnp.float32)
            ref_imag = coeff_ref[o, refer, quarter:both].astype(jnp.float32)
            prod_real = coeff_real * ref_real + coeff_imag * ref_imag
            prod_imag = coeff_imag * ref_real - coeff_real * ref_imag
            square = prod_real * prod_real + prod_imag * prod_imag + 1.0
            phase_ref[o, place] = (prod_imag * lax.rsqrt(square)).astype(jnp.bfloat16)
        return carry

    lax.fori_loop(0, timed, phase_one, 0, unroll=2)

    piece = min(128, wide_out)
    for start in range(0, wide_out, piece):
        here = slice(history * rows + start, history * rows + start + piece)
        above = jnp.zeros((piece, quarter), jnp.float32)
        below = jnp.ones((piece, quarter), jnp.float32)
        for o in range(orient):
            filtered = jnp.dot(
                spread_ref[start : start + piece], phase_ref[o], preferred_element_type=jnp.float32
            )
            filtered = filtered.astype(jnp.bfloat16).astype(jnp.float32)
            coeff_real = coeff_ref[o, here, 0:quarter].astype(jnp.float32)
            coeff_imag = coeff_ref[o, here, quarter:both].astype(jnp.float32)
            amplitude = coeff_real * coeff_real + coeff_imag * coeff_imag
            above = above + amplitude * filtered
            below = below + amplitude
        motion = (above / below).astype(out_ref.dtype)
        for i in range(piece // rows):
            out_ref[start // rows + i] = motion[i * rows : (i + 1) * rows]


def pixel_motion(segments, ref_frames, spread, ready, other, refer, left, right, places, rows, chunk, history):
    chips, frames_here, _, quarter = other.shape
    timed = history + chunk
    whole = refer is None
    slots = timed if whole else timed + NSEG
    smem = pl.BlockSpec(memory_space=pltpu.SMEM)
    vmem = pl.BlockSpec(memory_space=pltpu.VMEM)
    slot_bytes = ORIENT * rows * 2 * quarter * 2
    return pl.pallas_call(
        functools.partial(pixel_kernel, places=places, history=history, whole=whole),
        in_specs=[smem] * 2 + [vmem] * (5 + len(ready)),
        out_specs=vmem,
        out_shape=jax.ShapeDtypeStruct((chunk, rows, quarter), jnp.bfloat16),
        scratch_shapes=[
            pltpu.VMEM((ORIENT, (slots - timed + chips * frames_here) * rows, 2 * quarter), jnp.bfloat16),
            pltpu.VMEM((ORIENT, slots * rows, 2 * quarter), jnp.bfloat16),
            pltpu.VMEM((ORIENT, timed * rows, quarter), jnp.bfloat16),
        ],
        compiler_params=pltpu.CompilerParams(vmem_limit_bytes=4 * slots * slot_bytes + 16 * MIB),
        cost_estimate=pl.CostEstimate(
            flops=2 * ORIENT * rows * quarter * (slots * 2 * quarter + chunk * timed * rows),
            bytes_accessed=2 * (other.size + sum(one.size for one in ready) + right.size),
            transcendentals=ORIENT * timed * rows * quarter,
        ),
    )(segments, ref_frames, spread, other, other if whole else refer, left, right, *ready)


def chunk_windows(mine, other, ref_frames, history_chips, chips):
    mine = lax.all_gather(mine, "chunk", axis=0, tiled=True)
    other = lax.all_gather(other, "chunk", axis=0, tiled=True)
    frames_here = mine.shape[1]
    core = lax.axis_index("core")
    device = ref_frames // frames_here
    place = device // CORES * frames_here + ref_frames % frames_here
    own = (device % CORES == core)[:, None, None]
    flat = (-1,) + mine.shape[2:]
    refer = jnp.where(own, mine.reshape(flat)[place], other.reshape(flat)[place])

    def cut(windows):
        before = jnp.zeros((history_chips,) + windows.shape[1:], windows.dtype)
        windows = jnp.concatenate([before, windows])
        return lax.dynamic_slice_in_dim(windows, lax.axis_index("chunk") * chips, history_chips + chips)

    return cut(mine), cut(other), refer


def body(video_frames, segments, ref_pick, band_taps, *, chunks, slabs):
    frames_here, size, _ = video_frames.shape
    quarter = size // 4
    slab_rows = quarter // slabs
    rows = slab_rows // CORES
    chunk = slabs * CORES * frames_here
    history = min(chunk * -(-(band_taps.shape[0] - 1) // chunk), segments.shape[0] - chunk)
    left = jnp.asarray(slab_left_table(rows, HALO, ORIENT))
    right = jnp.asarray(make_right_table(quarter, ORIENT))
    half = slabs // 2
    near = [k for k in range(half) if k > 1] + [k for k in range(half) if k < 2][::-1]

    def exchange(array, k):
        return lax.ppermute(array, "slab", [(chip, chip ^ k) for chip in range(slabs)]) if k else array

    def swap(array):
        return lax.ppermute(array, "core", [(0, 1), (1, 0)])

    across, *windows = reduce_frames(video_frames, near, slab_rows, HALO)
    spread, ref_frames = time_tables(segments, ref_pick, band_taps, rows, chunk, history)
    across = exchange(across, half)
    windows = [exchange(window, k) for k, window in zip(near, windows)]
    passed = [exchange(window, k) for k, window in zip(near, pass_on(across, near, slab_rows, HALO))]
    mine, other = cut_windows(windows, near, rows, [spread])
    if chunks > 1:
        far_mine, far_other = cut_windows(passed, near, rows, [])
        lower = lax.axis_index("slab") >= half
        mine, other = [
            jnp.where(lower, jnp.concatenate([far, one]), jnp.concatenate([one, far]))
            for one, far in ((mine, far_mine), (other, far_other))
        ]
        mine, other, refer = chunk_windows(mine, swap(other), ref_frames, history // (CORES * frames_here), slabs)
        ready = [own_coeffs(mine, left, right, rows)]
        places = [(None, 0), (None, 1)]
    else:
        ready = [own_coeffs(one, left, right, rows) for one in (mine, swap(other))]
        mine, other = cut_windows(passed, near, rows, ready[:1])
        other, refer = swap(other), None
        ready.append(own_coeffs(mine, left, right, rows))
        places = [(0, 0), (0, 1), (1, 0), (1, 1)]
    motion = pixel_motion(segments, ref_frames, spread, ready, other, refer, left, right, places, rows, chunk, history)
    motion = motion.reshape(slabs * CORES, frames_here, rows, quarter)
    motion = lax.all_to_all(motion, ("slab", "core"), split_axis=0, concat_axis=0, tiled=True)
    motion = jnp.swapaxes(motion, 0, 1).reshape(frames_here, quarter, quarter)
    return motion.astype(jnp.float32)


def solution(mesh):
    chips = mesh.shape["frames"] // CORES
    slabs = min(chips, QUART // (CORES * TILE))
    chunks = chips // slabs
    names = ("groups", "chunk", "slab", "core")
    cut = jax.sharding.Mesh(mesh.devices.reshape(mesh.shape["groups"], chunks, slabs, CORES), names)
    in_specs = (P(names, None, None), P("groups"), P("groups"), P())
    return jax.shard_map(
        functools.partial(body, chunks=chunks, slabs=slabs),
        mesh=cut, in_specs=in_specs, out_specs=P(names, None, None), check_vma=False,
    )
```

```python
import functools
import math

import jax
import jax.numpy as jnp
import numpy as np
from jax import lax
from jax.experimental import pallas as pl
from jax.experimental.pallas import tpu as pltpu
from jax.sharding import PartitionSpec as P

IMG = 1024
ORIENT = 4
NSEG = 4
QUART = 256


blur_sigma = 2.0
gabor_sigma = 2.0
wave_number = math.pi / 2.0
gabor_gain = 2.0

HALO = 32
TILE = 16
CORES = 2
MIB = 1024 * 1024


def envelope_of(offset_grid):
    return np.float32(gabor_gain) * np.exp(
        -offset_grid * offset_grid / np.float32(2.0 * gabor_sigma * gabor_sigma)
    )


def waves(orient):
    angles = np.arange(orient, dtype=np.float32) * np.float32(math.pi / orient)
    wave_x = np.float32(wave_number) * np.cos(angles)
    wave_y = np.float32(wave_number) * np.sin(angles)
    return wave_x, wave_y


def slab_left_table(rows, halo, orient):
    offset = (
        np.arange(rows + 2 * halo, dtype=np.float32)[None, :]
        - np.float32(halo)
        - np.arange(rows, dtype=np.float32)[:, None]
    )
    wave_y = waves(orient)[1]
    phase = wave_y[:, None, None] * offset[None]
    envelope = envelope_of(offset)[None]
    table = np.stack([envelope * np.cos(phase), envelope * np.sin(phase)], axis=1)
    return table.reshape(orient * 2 * rows, rows + 2 * halo).astype(jnp.bfloat16)


def make_right_table(quarter, orient):
    position = np.arange(quarter, dtype=np.float32)
    offset = position[:, None] - position[None, :]
    wave_x = waves(orient)[0]
    phase_x = wave_x[:, None, None] * offset[None]
    envelope = envelope_of(offset)[None]
    real_part = envelope * np.cos(phase_x)
    imag_part = envelope * np.sin(phase_x)
    upper_half = np.concatenate([real_part, imag_part], axis=2)
    lower_half = np.concatenate([-imag_part, real_part], axis=2)
    return np.concatenate([upper_half, lower_half], axis=1).astype(jnp.bfloat16)


def down_sums(full_size, quarter):
    position = np.arange(quarter, dtype=np.float32)[:, None]
    columns = np.arange(full_size, dtype=np.float32)[None, :]
    offset_grid = columns - np.float32(4.0) * position - np.float32(1.5)
    weight = np.exp(-offset_grid * offset_grid / np.float32(2.0 * blur_sigma * blur_sigma))
    return np.sum(weight, axis=1)


def down_block(position, column, shape, axis, sums):
    positions = position + lax.broadcasted_iota(jnp.int32, shape, 1 - axis)
    columns = column + lax.broadcasted_iota(jnp.int32, shape, axis)
    offset_grid = columns.astype(jnp.float32) - 4.0 * positions.astype(jnp.float32) - 1.5
    weight = jnp.exp(-offset_grid * offset_grid / (2.0 * blur_sigma * blur_sigma))
    inner = float(sums[len(sums) // 2])
    line = position + lax.broadcasted_iota(jnp.int32, tuple(1 if i == axis else n for i, n in enumerate(shape)), 1 - axis)
    scale = jnp.full(line.shape, 1.0 / inner, jnp.float32)
    for q in range(position, min(position + shape[1 - axis], len(sums))):
        if abs(float(sums[q]) - inner) > 1e-7 * inner:
            scale = jnp.where(line == q, 1.0 / float(sums[q]), scale)
    return (weight * scale).astype(jnp.bfloat16)


def build_down(down_t_ref, down_ref):
    size, quarter = down_t_ref.shape
    sums = down_sums(size, quarter)
    lanes = min(128, quarter)
    down_t_ref[...] = jnp.zeros_like(down_t_ref)
    down_ref[...] = jnp.zeros_like(down_ref)
    for row in range(0, size, 128):
        for lane in range(0, quarter, lanes):
            if 4 * (lane + lanes - 1) + 30 >= row and 4 * lane - 27 <= row + 127:
                down_t_ref[row : row + 128, lane : lane + lanes] = down_block(lane, row, (128, lanes), 0, sums)
    for row in range(0, quarter, 32):
        for lane in range(0, size, 128):
            if 4 * (row + 31) + 30 >= lane and 4 * row - 27 <= lane + 127:
                down_ref[row : row + 32, lane : lane + 128] = down_block(row, lane, (32, 128), 1, sums)


def reduce_kernel(frames_ref, *refs, near, rows, halo, block):
    out_refs = refs[: 1 + len(near)]
    picture_ref, down_t_ref, down_ref, half_ref, total_ref, padded_ref, sems = refs[1 + len(near) :]
    count, size, _ = picture_ref.shape
    quarter = down_ref.shape[0]

    copies = []
    for f in range(count):
        for i in range(size // block):
            here = pl.ds(i * block, block)
            copy = pltpu.make_async_copy(frames_ref.at[f, here], picture_ref.at[f, here], sems.at[f, i])
            copy.start()
            copies.append(copy)
    build_down(down_t_ref, down_ref)
    edge = jnp.zeros((halo, quarter), jnp.bfloat16)
    padded_ref[0:halo] = edge
    padded_ref[halo + quarter :] = edge

    me = lax.axis_index("slab")
    reach = quarter
    for f in range(count):
        total_ref[...] = jnp.zeros_like(total_ref)
        for i in range(size // block):
            copies[f * (size // block) + i].wait()
            half_ref[...] = jnp.dot(
                picture_ref[f, i * block : (i + 1) * block], down_t_ref[...], preferred_element_type=jnp.float32
            ).astype(jnp.bfloat16)
            for row in range(0, block, reach):
                begin = i * block + row
                touched = slice(max(begin // 4 - TILE, 0), min((begin + reach) // 4 + TILE, quarter))
                total_ref[touched] += jnp.dot(
                    down_ref[touched, begin : begin + reach], half_ref[row : row + reach], preferred_element_type=jnp.float32
                )
        padded_ref[halo : halo + quarter] = total_ref[...].astype(jnp.bfloat16)
        for k, out_ref in zip(near, out_refs[1:]):
            slab = lax.bitwise_xor(me, k)
            out_ref[f] = padded_ref[pl.ds(pl.multiple_of(slab * rows, rows), rows + 2 * halo)]
        across = out_refs[0].shape[1]
        begin = jnp.where(me < len(near), quarter - across, 0)
        out_refs[0][f] = padded_ref[pl.ds(pl.multiple_of(halo + begin, TILE), across)]


def reduce_frames(video_frames, near, rows, halo):
    count, size, _ = video_frames.shape
    quarter = 2 * len(near) * rows
    block = size // 2
    out = jax.ShapeDtypeStruct((count, rows + 2 * halo, quarter), jnp.bfloat16)
    across = jax.ShapeDtypeStruct((count, quarter // 2 + halo, quarter), jnp.bfloat16)
    return pl.pallas_call(
        functools.partial(reduce_kernel, near=near, rows=rows, halo=halo, block=block),
        in_specs=[pl.BlockSpec(memory_space=pltpu.HBM)],
        out_specs=[pl.BlockSpec(memory_space=pltpu.VMEM)] * (1 + len(near)),
        out_shape=[across] + [out] * len(near),
        scratch_shapes=[
            pltpu.VMEM((count, size, size), jnp.bfloat16),
            pltpu.VMEM((size, quarter), jnp.bfloat16),
            pltpu.VMEM((quarter, size), jnp.bfloat16),
            pltpu.VMEM((block, quarter), jnp.bfloat16),
            pltpu.VMEM((quarter, quarter), jnp.float32),
            pltpu.VMEM((quarter + 2 * halo, quarter), jnp.bfloat16),
            pltpu.SemaphoreType.DMA((count, size // block)),
        ],
        compiler_params=pltpu.CompilerParams(vmem_limit_bytes=52 * MIB),
        cost_estimate=pl.CostEstimate(
            flops=2 * count * size * quarter * (size + quarter),
            bytes_accessed=2 * count * size * size,
            transcendentals=0,
        ),
    )(video_frames)


def pass_kernel(rows_ref, *refs, near, rows, halo):
    out_refs, padded_ref = refs[:-1], refs[-1]
    count, across, quarter = rows_ref.shape
    me = lax.axis_index("slab")
    edge = jnp.zeros((halo, quarter), jnp.bfloat16)
    above = jnp.where(me < len(near), 0, halo)
    for f in range(count):
        padded_ref[f, 0:halo] = edge
        padded_ref[f, halo + across :] = edge
        padded_ref[f, halo : halo + across] = rows_ref[f]
        for k, out_ref in zip(near, out_refs):
            place = lax.rem(lax.bitwise_xor(me, k), len(near)) * rows + above
            out_ref[f] = padded_ref[f, pl.ds(pl.multiple_of(place, TILE), rows + 2 * halo)]


def pass_on(across, near, rows, halo):
    count, height, quarter = across.shape
    vmem = pl.BlockSpec(memory_space=pltpu.VMEM)
    out = jax.ShapeDtypeStruct((count, rows + 2 * halo, quarter), jnp.bfloat16)
    return pl.pallas_call(
        functools.partial(pass_kernel, near=near, rows=rows, halo=halo),
        in_specs=[vmem],
        out_specs=[vmem] * len(near),
        out_shape=[out] * len(near),
        scratch_shapes=[pltpu.VMEM((count, height + 2 * halo, quarter), jnp.bfloat16)],
        compiler_params=pltpu.CompilerParams(vmem_limit_bytes=16 * MIB),
        cost_estimate=pl.CostEstimate(flops=0, bytes_accessed=4 * len(near) * out.size, transcendentals=0),
    )(across)


def cut_kernel(*refs, near, rows):
    in_refs, (mine_ref, other_ref) = refs[: len(near)], refs[-2:]
    window = mine_ref.shape[2]
    me, core = lax.axis_index("slab"), lax.axis_index("core")
    for k, in_ref in zip(near, in_refs):
        chip = lax.rem(lax.bitwise_xor(me, k), len(near))
        mine_ref[chip] = in_ref[:, pl.ds(pl.multiple_of(core * rows, rows), window)]
        other_ref[chip] = in_ref[:, pl.ds(pl.multiple_of((1 - core) * rows, rows), window)]


def cut_windows(pieces, near, rows, after):
    count, window, quarter = pieces[0].shape
    out = jax.ShapeDtypeStruct((len(pieces), count, window - rows, quarter), jnp.bfloat16)
    return pl.pallas_call(
        functools.partial(cut_kernel, near=near, rows=rows),
        in_specs=[pl.BlockSpec(memory_space=pltpu.VMEM)] * len(pieces) + [pl.BlockSpec(memory_space=pl.ANY)] * len(after),
        out_specs=[pl.BlockSpec(memory_space=pltpu.VMEM)] * 2,
        out_shape=[out, out],
        compiler_params=pltpu.CompilerParams(vmem_limit_bytes=16 * MIB),
        cost_estimate=pl.CostEstimate(flops=0, bytes_accessed=8 * out.size, transcendentals=0),
    )(*pieces, *after)


def time_kernel(segments_ref, pick_ref, taps_ref, spread_ref, frame_ref, *, history, frames, rows):
    chunk, timed = spread_ref.shape[0] // rows, spread_ref.shape[1] // rows
    nseg = pick_ref.shape[0]
    taps = taps_ref.shape[0]
    wide_out, wide_in = chunk * rows, timed * rows

    def count_one(t, totals):
        here = segments_ref[t]
        below = [total + (here < s).astype(jnp.int32) for s, total in enumerate(totals[0])]
        same = [total + (here == s).astype(jnp.int32) for s, total in enumerate(totals[1])]
        return tuple(below), tuple(same)

    zeros = tuple(jnp.int32(0) for _ in range(nseg))
    starts, counts = lax.fori_loop(0, frames, count_one, (zeros, zeros), unroll=8)
    for s in range(nseg):
        frame_ref[s] = starts[s] + lax.rem(pick_ref[s], counts[s])

    lag = history + lax.broadcasted_iota(jnp.int32, (chunk, timed), 0) - lax.broadcasted_iota(
        jnp.int32, (chunk, timed), 1
    )
    if history:
        first = lax.axis_index("chunk") * chunk - history
        real = first + lax.broadcasted_iota(jnp.int32, (chunk, timed), 1) >= 0
        lag = jnp.where(real, lag, -1)
    matrix = jnp.zeros((chunk, timed), jnp.float32)
    for k in range(taps):
        matrix = jnp.where(lag == k, taps_ref[k], matrix)
    repeat_left = (
        lax.broadcasted_iota(jnp.int32, (wide_out, chunk), 0) // rows
        == lax.broadcasted_iota(jnp.int32, (wide_out, chunk), 1)
    ).astype(jnp.bfloat16)
    repeat_right = (
        lax.broadcasted_iota(jnp.int32, (timed, wide_in), 1) // rows
        == lax.broadcasted_iota(jnp.int32, (timed, wide_in), 0)
    ).astype(jnp.bfloat16)
    tall = jnp.dot(repeat_left, matrix.astype(jnp.bfloat16), preferred_element_type=jnp.float32)
    tall = tall.astype(jnp.bfloat16)
    piece = min(128, wide_out)
    for start in range(0, wide_out, piece):
        part = jnp.dot(tall[start : start + piece], repeat_right, preferred_element_type=jnp.float32)
        same_row = (
            lax.broadcasted_iota(jnp.int32, (piece, wide_in), 0) % rows
            == lax.broadcasted_iota(jnp.int32, (piece, wide_in), 1) % rows
        )
        spread_ref[start : start + piece] = jnp.where(same_row, part, 0.0).astype(jnp.bfloat16)


def time_tables(segments, ref_pick, band_taps, rows, chunk, history):
    frames = segments.shape[0]
    wide_out, wide_in = chunk * rows, (history + chunk) * rows
    smem = pl.BlockSpec(memory_space=pltpu.SMEM)
    return pl.pallas_call(
        functools.partial(time_kernel, history=history, frames=frames, rows=rows),
        in_specs=[smem] * 3,
        out_specs=[pl.BlockSpec(memory_space=pltpu.VMEM), smem],
        out_shape=[
            jax.ShapeDtypeStruct((wide_out, wide_in), jnp.bfloat16),
            jax.ShapeDtypeStruct(ref_pick.shape, jnp.int32),
        ],
        compiler_params=pltpu.CompilerParams(vmem_limit_bytes=16 * MIB),
        cost_estimate=pl.CostEstimate(
            flops=2 * wide_out * wide_in * chunk, bytes_accessed=2 * wide_out * wide_in, transcendentals=0
        ),
    )(segments, ref_pick, band_taps.astype(jnp.float32))


def filter_frames(window_refs, left_ref, right_ref, stacked_ref, put):
    rows = left_ref.shape[0] // (2 * right_ref.shape[0])
    orient, both, _ = right_ref.shape
    quarter = both // 2
    for n, window in enumerate(window_refs):
        stacked = jnp.dot(left_ref[...], window[...], preferred_element_type=jnp.float32).astype(jnp.bfloat16)
        for o in range(orient):
            for z in range(2):
                begin = (o * 2 + z) * rows
                stacked_ref[o, n * rows : (n + 1) * rows, z * quarter : (z + 1) * quarter] = stacked[begin : begin + rows]
    many = len(window_refs) * rows
    step = min(256, many)
    pair = 2 * rows
    for o in range(orient):
        for start in range(0, many, step):
            stop = min(start + step, many)
            coeff = jnp.dot(stacked_ref[o, start:stop], right_ref[o], preferred_element_type=jnp.float32)
            coeff = coeff.astype(jnp.bfloat16)
            for place in range(start, stop, pair):
                put(o, place // pair, coeff[place - start : place - start + pair])


def coeff_kernel(window_ref, left_ref, right_ref, coeff_ref, stacked_ref):
    chips, frames_here, window, quarter = window_ref.shape
    rows = left_ref.shape[0] // (2 * right_ref.shape[0])

    def put(o, i, block):
        coeff_ref[o, 2 * i * rows : 2 * (i + 1) * rows] = block

    filter_frames(
        [window_ref.at[chip, f] for chip in range(chips) for f in range(frames_here)], left_ref, right_ref, stacked_ref, put
    )


def own_coeffs(windows, left, right, rows):
    chips, frames_here, _, quarter = windows.shape
    vmem = pl.BlockSpec(memory_space=pltpu.VMEM)
    out = jax.ShapeDtypeStruct((ORIENT, chips * frames_here * rows, 2 * quarter), jnp.bfloat16)
    return pl.pallas_call(
        coeff_kernel,
        in_specs=[vmem] * 3,
        out_specs=vmem,
        out_shape=out,
        scratch_shapes=[pltpu.VMEM(out.shape, jnp.bfloat16)],
        compiler_params=pltpu.CompilerParams(vmem_limit_bytes=8 * out.size + 16 * MIB),
        cost_estimate=pl.CostEstimate(
            flops=8 * out.size * quarter, bytes_accessed=2 * (windows.size + out.size), transcendentals=0
        ),
    )(windows, left, right)


def pixel_kernel(
    segments_ref, ref_frame_ref, spread_ref, other_ref, refer_ref, left_ref, right_ref, *refs, places, history, whole
):
    ready_refs, (out_ref, stacked_ref, coeff_ref, phase_ref) = refs[:-4], refs[-4:]
    chips, frames_here, _, quarter = other_ref.shape
    chunk, rows, _ = out_ref.shape
    orient = right_ref.shape[0]
    nseg = ref_frame_ref.shape[0]
    both = 2 * quarter
    timed = history + chunk
    wide_out = chunk * rows
    pair = frames_here * rows
    core = lax.axis_index("core")

    def place_of(half, twin, chip):
        upper = 0 if half is None else lax.rem(lax.axis_index("slab") // chips + half, 2) * chips
        return pl.ds(pl.multiple_of(((upper + chip) * CORES + lax.rem(core + twin, CORES)) * pair, pair), pair)

    for ready_ref, (half, twin) in zip(ready_refs, places):
        for chip in range(ready_ref.shape[1] // pair):
            for o in range(orient):
                coeff_ref[o, place_of(half, twin, chip)] = ready_ref[o, chip * pair : (chip + 1) * pair]

    def put(o, i, block):
        if i < chips:
            coeff_ref[o, place_of(*places[-1], i)] = block
        else:
            begin = timed * rows + (i - chips) * pair
            coeff_ref[o, begin : begin + pair] = block

    windows = [other_ref.at[chip, f] for chip in range(chips) for f in range(frames_here)]
    if not whole:
        windows += [refer_ref.at[s] for s in range(nseg)]
    filter_frames(windows, left_ref, right_ref, stacked_ref, put)

    def phase_one(slot, carry):
        place = pl.ds(pl.multiple_of(slot * rows, rows), rows)
        if whole:
            source = ref_frame_ref[segments_ref[slot]]
        else:
            first = lax.axis_index("chunk") * chunk - history
            source = timed + segments_ref[jnp.maximum(first + slot, 0)]
        refer = pl.ds(pl.multiple_of(source * rows, rows), rows)
        for o in range(orient):
            coeff_real = coeff_ref[o, place, 0:quarter].astype(jnp.float32)
            coeff_imag = coeff_ref[o, place, quarter:both].astype(jnp.float32)
            ref_real = coeff_ref[o, refer, 0:quarter].astype(jnp.float32)
            ref_imag = coeff_ref[o, refer, quarter:both].astype(jnp.float32)
            prod_real = coeff_real * ref_real + coeff_imag * ref_imag
            prod_imag = coeff_imag * ref_real - coeff_real * ref_imag
            square = prod_real * prod_real + prod_imag * prod_imag + 1.0
            phase_ref[o, place] = (prod_imag * lax.rsqrt(square)).astype(jnp.bfloat16)
        return carry

    lax.fori_loop(0, timed, phase_one, 0, unroll=2)

    piece = min(128, wide_out)
    for start in range(0, wide_out, piece):
        here = slice(history * rows + start, history * rows + start + piece)
        above = jnp.zeros((piece, quarter), jnp.float32)
        below = jnp.ones((piece, quarter), jnp.float32)
        for o in range(orient):
            filtered = jnp.dot(
                spread_ref[start : start + piece], phase_ref[o], preferred_element_type=jnp.float32
            )
            filtered = filtered.astype(jnp.bfloat16).astype(jnp.float32)
            coeff_real = coeff_ref[o, here, 0:quarter].astype(jnp.float32)
            coeff_imag = coeff_ref[o, here, quarter:both].astype(jnp.float32)
            amplitude = coeff_real * coeff_real + coeff_imag * coeff_imag
            above = above + amplitude * filtered
            below = below + amplitude
        motion = (above / below).astype(out_ref.dtype)
        for i in range(piece // rows):
            out_ref[start // rows + i] = motion[i * rows : (i + 1) * rows]


def pixel_motion(segments, ref_frames, spread, ready, other, refer, left, right, places, rows, chunk, history):
    chips, frames_here, _, quarter = other.shape
    timed = history + chunk
    whole = refer is None
    slots = timed if whole else timed + NSEG
    smem = pl.BlockSpec(memory_space=pltpu.SMEM)
    vmem = pl.BlockSpec(memory_space=pltpu.VMEM)
    slot_bytes = ORIENT * rows * 2 * quarter * 2
    return pl.pallas_call(
        functools.partial(pixel_kernel, places=places, history=history, whole=whole),
        in_specs=[smem] * 2 + [vmem] * (5 + len(ready)),
        out_specs=vmem,
        out_shape=jax.ShapeDtypeStruct((chunk, rows, quarter), jnp.bfloat16),
        scratch_shapes=[
            pltpu.VMEM((ORIENT, (slots - timed + chips * frames_here) * rows, 2 * quarter), jnp.bfloat16),
            pltpu.VMEM((ORIENT, slots * rows, 2 * quarter), jnp.bfloat16),
            pltpu.VMEM((ORIENT, timed * rows, quarter), jnp.bfloat16),
        ],
        compiler_params=pltpu.CompilerParams(vmem_limit_bytes=4 * slots * slot_bytes + 16 * MIB),
        cost_estimate=pl.CostEstimate(
            flops=2 * ORIENT * rows * quarter * (slots * 2 * quarter + chunk * timed * rows),
            bytes_accessed=2 * (other.size + sum(one.size for one in ready) + right.size),
            transcendentals=ORIENT * timed * rows * quarter,
        ),
    )(segments, ref_frames, spread, other, other if whole else refer, left, right, *ready)


def chunk_windows(mine, other, ref_frames, history_chips, chips):
    mine = lax.all_gather(mine, "chunk", axis=0, tiled=True)
    other = lax.all_gather(other, "chunk", axis=0, tiled=True)
    frames_here = mine.shape[1]
    core = lax.axis_index("core")
    device = ref_frames // frames_here
    place = device // CORES * frames_here + ref_frames % frames_here
    own = (device % CORES == core)[:, None, None]
    flat = (-1,) + mine.shape[2:]
    refer = jnp.where(own, mine.reshape(flat)[place], other.reshape(flat)[place])

    def cut(windows):
        before = jnp.zeros((history_chips,) + windows.shape[1:], windows.dtype)
        windows = jnp.concatenate([before, windows])
        return lax.dynamic_slice_in_dim(windows, lax.axis_index("chunk") * chips, history_chips + chips)

    return cut(mine), cut(other), refer


def body(video_frames, segments, ref_pick, band_taps, *, chunks, slabs):
    frames_here, size, _ = video_frames.shape
    quarter = size // 4
    slab_rows = quarter // slabs
    rows = slab_rows // CORES
    chunk = slabs * CORES * frames_here
    history = min(chunk * -(-(band_taps.shape[0] - 1) // chunk), segments.shape[0] - chunk)
    left = jnp.asarray(slab_left_table(rows, HALO, ORIENT))
    right = jnp.asarray(make_right_table(quarter, ORIENT))
    half = slabs // 2
    near = [k for k in range(half) if k > 1] + [k for k in range(half) if k < 2][::-1]

    def exchange(array, k):
        return lax.ppermute(array, "slab", [(chip, chip ^ k) for chip in range(slabs)]) if k else array

    def swap(array):
        return lax.ppermute(array, "core", [(0, 1), (1, 0)])

    across, *windows = reduce_frames(video_frames, near, slab_rows, HALO)
    spread, ref_frames = time_tables(segments, ref_pick, band_taps, rows, chunk, history)
    across = exchange(across, half)
    windows, spread = lax.optimization_barrier((windows, spread))
    windows = [exchange(window, k) for k, window in zip(near, windows)]
    passed = [exchange(window, k) for k, window in zip(near, pass_on(across, near, slab_rows, HALO))]
    mine, other = cut_windows(windows, near, rows, [spread])
    if chunks > 1:
        far_mine, far_other = cut_windows(passed, near, rows, [])
        lower = lax.axis_index("slab") >= half
        mine, other = [
            jnp.where(lower, jnp.concatenate([far, one]), jnp.concatenate([one, far]))
            for one, far in ((mine, far_mine), (other, far_other))
        ]
        mine, other, refer = chunk_windows(mine, swap(other), ref_frames, history // (CORES * frames_here), slabs)
        ready = [own_coeffs(mine, left, right, rows)]
        places = [(None, 0), (None, 1)]
    else:
        ready = [own_coeffs(one, left, right, rows) for one in (mine, swap(other))]
        mine, other = cut_windows(passed, near, rows, ready[:1])
        other, refer = swap(other), None
        ready.append(own_coeffs(mine, left, right, rows))
        places = [(0, 0), (0, 1), (1, 0), (1, 1)]
    motion = pixel_motion(segments, ref_frames, spread, ready, other, refer, left, right, places, rows, chunk, history)
    motion = motion.reshape(slabs * CORES, frames_here, rows, quarter)
    motion = lax.all_to_all(motion, ("slab", "core"), split_axis=0, concat_axis=0, tiled=True)
    motion = jnp.swapaxes(motion, 0, 1).reshape(frames_here, quarter, quarter)
    return motion.astype(jnp.float32)


def solution(mesh):
    chips = mesh.shape["frames"] // CORES
    slabs = min(chips, QUART // (CORES * TILE))
    chunks = chips // slabs
    names = ("groups", "chunk", "slab", "core")
    cut = jax.sharding.Mesh(mesh.devices.reshape(mesh.shape["groups"], chunks, slabs, CORES), names)
    in_specs = (P(names, None, None), P("groups"), P("groups"), P())
    return jax.shard_map(
        functools.partial(body, chunks=chunks, slabs=slabs),
        mesh=cut, in_specs=in_specs, out_specs=P(names, None, None), check_vma=False,
    )
```

```python
import functools
import math

import jax
import jax.numpy as jnp
import numpy as np
from jax import lax
from jax.experimental import pallas as pl
from jax.experimental.pallas import tpu as pltpu
from jax.sharding import PartitionSpec as P

IMG = 1024
ORIENT = 4
NSEG = 4
QUART = 256


blur_sigma = 2.0
gabor_sigma = 2.0
wave_number = math.pi / 2.0
gabor_gain = 2.0

HALO = 32
TILE = 16
DOWN = 2
SHARE = 2
CORES = 2
MIB = 1024 * 1024


def envelope_of(offset_grid):
    return np.float32(gabor_gain) * np.exp(
        -offset_grid * offset_grid / np.float32(2.0 * gabor_sigma * gabor_sigma)
    )


def waves(orient):
    angles = np.arange(orient, dtype=np.float32) * np.float32(math.pi / orient)
    wave_x = np.float32(wave_number) * np.cos(angles)
    wave_y = np.float32(wave_number) * np.sin(angles)
    return wave_x, wave_y


def slab_left_table(rows, halo, orient):
    offset = (
        np.arange(rows + 2 * halo, dtype=np.float32)[None, :]
        - np.float32(halo)
        - np.arange(rows, dtype=np.float32)[:, None]
    )
    wave_y = waves(orient)[1]
    phase = wave_y[:, None, None] * offset[None]
    envelope = envelope_of(offset)[None]
    table = np.stack([envelope * np.cos(phase), envelope * np.sin(phase)], axis=1)
    return table.reshape(orient * 2 * rows, rows + 2 * halo).astype(jnp.bfloat16)


def make_right_table(columns, halo, orient):
    window = columns + 2 * halo
    offset = (
        np.arange(window, dtype=np.float32)[:, None] - np.float32(halo) - np.arange(columns, dtype=np.float32)[None, :]
    )
    wave_x = waves(orient)[0]
    phase_x = wave_x[:, None, None] * offset[None]
    envelope = envelope_of(offset)[None]
    real_part = envelope * np.cos(phase_x)
    imag_part = envelope * np.sin(phase_x)
    table = np.zeros((orient // SHARE, SHARE, 2, window, 2, SHARE, columns), np.float32)
    for o in range(orient):
        group, i = divmod(o, SHARE)
        table[group, i, 0, :, 0, i] = real_part[o]
        table[group, i, 0, :, 1, i] = imag_part[o]
        table[group, i, 1, :, 0, i] = -imag_part[o]
        table[group, i, 1, :, 1, i] = real_part[o]
    return table.reshape(orient // SHARE, SHARE * 2 * window, 2 * SHARE * columns).astype(jnp.bfloat16)


def down_sums(full_size, quarter):
    position = np.arange(quarter, dtype=np.float32)[:, None]
    columns = np.arange(full_size, dtype=np.float32)[None, :]
    offset_grid = columns - np.float32(4.0) * position - np.float32(1.5)
    weight = np.exp(-offset_grid * offset_grid / np.float32(2.0 * blur_sigma * blur_sigma))
    return np.sum(weight, axis=1)


def down_block(position, column, shape, axis, sums):
    positions = position + lax.broadcasted_iota(jnp.int32, shape, 1 - axis)
    columns = column + lax.broadcasted_iota(jnp.int32, shape, axis)
    offset_grid = columns.astype(jnp.float32) - 4.0 * positions.astype(jnp.float32) - 1.5
    weight = jnp.exp(-offset_grid * offset_grid / (2.0 * blur_sigma * blur_sigma))
    inner = float(sums[len(sums) // 2])
    line = position + lax.broadcasted_iota(jnp.int32, tuple(1 if i == axis else n for i, n in enumerate(shape)), 1 - axis)
    scale = jnp.full(line.shape, 1.0 / inner, jnp.float32)
    for q in range(position, min(position + shape[1 - axis], len(sums))):
        if abs(float(sums[q]) - inner) > 1e-7 * inner:
            scale = jnp.where(line == q, 1.0 / float(sums[q]), scale)
    return (weight * scale).astype(jnp.bfloat16)


def build_down(down_t_ref, down_ref):
    size, quarter = down_t_ref.shape
    sums = down_sums(size, quarter)
    lanes = min(128, quarter)
    down_t_ref[...] = jnp.zeros_like(down_t_ref)
    down_ref[...] = jnp.zeros_like(down_ref)
    for row in range(0, size, 128):
        for lane in range(0, quarter, lanes):
            if 4 * (lane + lanes - 1) + 30 >= row and 4 * lane - 27 <= row + 127:
                down_t_ref[row : row + 128, lane : lane + lanes] = down_block(lane, row, (128, lanes), 0, sums)
    for row in range(0, quarter, 32):
        for lane in range(0, size, 128):
            if 4 * (row + 31) + 30 >= lane and 4 * row - 27 <= lane + 127:
                down_ref[row : row + 32, lane : lane + 128] = down_block(row, lane, (32, 128), 1, sums)


def reduce_kernel(frames_ref, *refs, order, halo, block):
    out_refs = refs[: len(order)]
    picture_ref, down_t_ref, down_ref, half_ref, total_ref, strip_ref, sems = refs[len(order) :]
    count, size, _ = picture_ref.shape
    quarter = down_ref.shape[0]
    strips, _, lanes = strip_ref.shape
    columns = lanes - 2 * halo
    window = out_refs[0].shape[1]

    copies = []
    for f in range(count):
        for i in range(size // block):
            here = pl.ds(i * block, block)
            copy = pltpu.make_async_copy(frames_ref.at[f, here], picture_ref.at[f, here], sems.at[f, i])
            copy.start()
            copies.append(copy)
    build_down(down_t_ref, down_ref)

    me = lax.axis_index("slab")
    reach = quarter
    for f in range(count):
        total_ref[...] = jnp.zeros_like(total_ref)
        for i in range(size // block):
            copies[f * (size // block) + i].wait()
            half_ref[...] = jnp.dot(
                picture_ref[f, i * block : (i + 1) * block], down_t_ref[...], preferred_element_type=jnp.float32
            ).astype(jnp.bfloat16)
            for row in range(0, block, reach):
                begin = i * block + row
                near = slice(max(begin // 4 - TILE, 0), min((begin + reach) // 4 + TILE, quarter))
                total_ref[near] += jnp.dot(
                    down_ref[near, begin : begin + reach], half_ref[row : row + reach], preferred_element_type=jnp.float32
                )
        for strip in range(strips):
            begin = strip * columns - halo
            moved = pltpu.roll(total_ref[...], (-begin) % quarter, 1)[:, 0:lanes]
            column = begin + lax.broadcasted_iota(jnp.int32, (quarter, lanes), 1)
            inside = (column >= 0) & (column < quarter)
            strip_ref[strip] = jnp.where(inside, moved, 0.0).astype(jnp.bfloat16)
        for k, out_ref in zip(order, out_refs):
            slab = lax.bitwise_xor(me, k)
            begin = pl.multiple_of(lax.rem(slab, DOWN) * (quarter - window), TILE)
            out_ref[f] = strip_ref[slab // DOWN, pl.ds(begin, window)]


def reduce_frames(video_frames, order, halo):
    count, size, _ = video_frames.shape
    quarter = size // 4
    strips = len(order) // DOWN
    lanes = quarter // strips + 2 * halo
    block = size // 2
    out = jax.ShapeDtypeStruct((count, quarter // DOWN + halo, lanes), jnp.bfloat16)
    return pl.pallas_call(
        functools.partial(reduce_kernel, order=order, halo=halo, block=block),
        in_specs=[pl.BlockSpec(memory_space=pltpu.HBM)],
        out_specs=[pl.BlockSpec(memory_space=pltpu.VMEM)] * len(order),
        out_shape=[out] * len(order),
        scratch_shapes=[
            pltpu.VMEM((count, size, size), jnp.bfloat16),
            pltpu.VMEM((size, quarter), jnp.bfloat16),
            pltpu.VMEM((quarter, size), jnp.bfloat16),
            pltpu.VMEM((block, quarter), jnp.bfloat16),
            pltpu.VMEM((quarter, quarter), jnp.float32),
            pltpu.VMEM((strips, quarter, lanes), jnp.bfloat16),
            pltpu.SemaphoreType.DMA((count, size // block)),
        ],
        compiler_params=pltpu.CompilerParams(vmem_limit_bytes=52 * MIB),
        cost_estimate=pl.CostEstimate(
            flops=2 * count * size * quarter * (size + quarter),
            bytes_accessed=2 * count * size * size,
            transcendentals=0,
        ),
    )(video_frames)


def exchange_order(slabs):
    far = sorted(range(slabs // 2, slabs), key=lambda k: k % 2)
    near = list(range(2, slabs // 2))
    if near and len(far) > 2:
        turns = near[:1] + far[:2] + near[1:] + far[2:]
    else:
        turns = near + far
    return [0] + turns + [k for k in (1,) if k < slabs // 2]


def cut_kernel(*refs, order, halo):
    in_refs, (mine_ref, other_ref), padded_ref = refs[1:-3], refs[-3:-1], refs[-1]
    count, window, lanes = in_refs[0].shape
    height = mine_ref.shape[1]
    rows = height - 2 * halo
    me, core = lax.axis_index("slab"), lax.axis_index("core")
    edge = jnp.zeros((halo, count * lanes), jnp.bfloat16)
    padded_ref[0:halo] = edge
    padded_ref[halo + window :] = edge
    above = lax.rem(me, DOWN) * halo
    for k, in_ref in zip(order, in_refs):
        chip = lax.bitwise_xor(me, k)
        for f in range(count):
            padded_ref[halo : halo + window, f * lanes : (f + 1) * lanes] = in_ref[f]
        for out_ref, number in ((mine_ref, core), (other_ref, 1 - core)):
            out_ref[chip] = padded_ref[pl.ds(pl.multiple_of(above + number * rows, TILE), height)]


def cut_windows(ref_frames, pieces, order, halo):
    count, window, lanes = pieces[0].shape
    height = (window - halo) // CORES + 2 * halo
    out = jax.ShapeDtypeStruct((len(pieces), height, count * lanes), jnp.bfloat16)
    return pl.pallas_call(
        functools.partial(cut_kernel, order=order, halo=halo),
        in_specs=[pl.BlockSpec(memory_space=pltpu.SMEM)] + [pl.BlockSpec(memory_space=pltpu.VMEM)] * len(pieces),
        out_specs=[pl.BlockSpec(memory_space=pltpu.VMEM)] * 2,
        out_shape=[out, out],
        scratch_shapes=[pltpu.VMEM((window + 2 * halo, count * lanes), jnp.bfloat16)],
        compiler_params=pltpu.CompilerParams(vmem_limit_bytes=16 * MIB),
        cost_estimate=pl.CostEstimate(flops=0, bytes_accessed=8 * out.size, transcendentals=0),
    )(ref_frames, *pieces)


def time_kernel(segments_ref, pick_ref, taps_ref, spread_ref, frame_ref, *, history, frames, rows):
    chunk, timed = spread_ref.shape[0] // rows, spread_ref.shape[1] // rows
    nseg = pick_ref.shape[0]
    taps = taps_ref.shape[0]
    wide_out, wide_in = chunk * rows, timed * rows

    def count_one(t, totals):
        here = segments_ref[t]
        below = [total + (here < s).astype(jnp.int32) for s, total in enumerate(totals[0])]
        same = [total + (here == s).astype(jnp.int32) for s, total in enumerate(totals[1])]
        return tuple(below), tuple(same)

    zeros = tuple(jnp.int32(0) for _ in range(nseg))
    starts, counts = lax.fori_loop(0, frames, count_one, (zeros, zeros), unroll=8)
    for s in range(nseg):
        frame_ref[s] = starts[s] + lax.rem(pick_ref[s], counts[s])

    lag = history + lax.broadcasted_iota(jnp.int32, (chunk, timed), 0) - lax.broadcasted_iota(
        jnp.int32, (chunk, timed), 1
    )
    if history:
        first = lax.axis_index("chunk") * chunk - history
        real = first + lax.broadcasted_iota(jnp.int32, (chunk, timed), 1) >= 0
        lag = jnp.where(real, lag, -1)
    matrix = jnp.zeros((chunk, timed), jnp.float32)
    for k in range(taps):
        matrix = jnp.where(lag == k, taps_ref[k], matrix)
    repeat_left = (
        lax.broadcasted_iota(jnp.int32, (wide_out, chunk), 0) // rows
        == lax.broadcasted_iota(jnp.int32, (wide_out, chunk), 1)
    ).astype(jnp.bfloat16)
    repeat_right = (
        lax.broadcasted_iota(jnp.int32, (timed, wide_in), 1) // rows
        == lax.broadcasted_iota(jnp.int32, (timed, wide_in), 0)
    ).astype(jnp.bfloat16)
    tall = jnp.dot(repeat_left, matrix.astype(jnp.bfloat16), preferred_element_type=jnp.float32)
    tall = tall.astype(jnp.bfloat16)
    piece = min(128, wide_out)
    for start in range(0, wide_out, piece):
        part = jnp.dot(tall[start : start + piece], repeat_right, preferred_element_type=jnp.float32)
        same_row = (
            lax.broadcasted_iota(jnp.int32, (piece, wide_in), 0) % rows
            == lax.broadcasted_iota(jnp.int32, (piece, wide_in), 1) % rows
        )
        spread_ref[start : start + piece] = jnp.where(same_row, part, 0.0).astype(jnp.bfloat16)


def time_tables(segments, ref_pick, band_taps, rows, chunk, history):
    frames = segments.shape[0]
    wide_out, wide_in = chunk * rows, (history + chunk) * rows
    smem = pl.BlockSpec(memory_space=pltpu.SMEM)
    return pl.pallas_call(
        functools.partial(time_kernel, history=history, frames=frames, rows=rows),
        in_specs=[smem] * 3,
        out_specs=[pl.BlockSpec(memory_space=pltpu.VMEM), smem],
        out_shape=[
            jax.ShapeDtypeStruct((wide_out, wide_in), jnp.bfloat16),
            jax.ShapeDtypeStruct(ref_pick.shape, jnp.int32),
        ],
        compiler_params=pltpu.CompilerParams(vmem_limit_bytes=16 * MIB),
        cost_estimate=pl.CostEstimate(
            flops=2 * wide_out * wide_in * chunk, bytes_accessed=2 * wide_out * wide_in, transcendentals=0
        ),
    )(segments, ref_pick, band_taps.astype(jnp.float32))


def filter_frames(window_refs, left_ref, right_ref, stacked_ref, put):
    groups, deep, _ = right_ref.shape
    lanes = deep // (2 * SHARE)
    rows = left_ref.shape[0] // (2 * SHARE * groups)
    bands = rows // TILE
    pair = window_refs[0].shape[1] // lanes
    many = len(window_refs) * pair * TILE
    for n, window in enumerate(window_refs):
        stacked = jnp.dot(left_ref[...], window[...], preferred_element_type=jnp.float32).astype(jnp.bfloat16)
        for oz in range(2 * SHARE * groups):
            group, place = divmod(oz, 2 * SHARE)
            for band in range(bands):
                begin = oz * rows + band * TILE
                for f in range(pair):
                    row = band * many + (n * pair + f) * TILE
                    stacked_ref[group, row : row + TILE, place * lanes : (place + 1) * lanes] = stacked[
                        begin : begin + TILE, f * lanes : (f + 1) * lanes
                    ]
    step = min(256, many)
    block = pair * TILE
    for group in range(groups):
        for band in range(bands):
            for start in range(0, many, step):
                stop = min(start + step, many)
                coeff = jnp.dot(
                    stacked_ref[group, band * many + start : band * many + stop],
                    right_ref[group],
                    preferred_element_type=jnp.float32,
                ).astype(jnp.bfloat16)
                for place in range(start, stop, block):
                    put(group, band, place // block, coeff[place - start : place - start + block])


def coeff_kernel(window_ref, left_ref, right_ref, coeff_ref, stacked_ref):
    chips = window_ref.shape[0]
    block = coeff_ref.shape[2] // chips

    def put(group, band, i, values):
        coeff_ref[group, band, i * block : (i + 1) * block] = values

    filter_frames([window_ref.at[chip] for chip in range(chips)], left_ref, right_ref, stacked_ref, put)


def own_coeffs(windows, left, right, rows, frames_here):
    groups, deep, wide = right.shape
    vmem = pl.BlockSpec(memory_space=pltpu.VMEM)
    many = windows.shape[0] * frames_here * TILE
    out = jax.ShapeDtypeStruct((groups, rows // TILE, many, wide), jnp.bfloat16)
    return pl.pallas_call(
        coeff_kernel,
        in_specs=[vmem] * 3,
        out_specs=vmem,
        out_shape=out,
        scratch_shapes=[pltpu.VMEM((groups, rows // TILE * many, deep), jnp.bfloat16)],
        compiler_params=pltpu.CompilerParams(vmem_limit_bytes=8 * out.size + 16 * MIB),
        cost_estimate=pl.CostEstimate(
            flops=4 * out.size * deep, bytes_accessed=2 * (windows.size + out.size), transcendentals=0
        ),
    )(windows, left, right)


def pixel_kernel(
    segments_ref, ref_frame_ref, spread_ref, mine_ref, other_ref, refer_ref, left_ref, right_ref, *refs,
    order, history, whole,
):
    out_refs, (stacked_ref, coeff_ref, phase_ref, out_ref) = refs[:-4], refs[-4:]
    chips = other_ref.shape[0]
    groups, bands, _, wide = coeff_ref.shape
    half = wide // 2
    block = mine_ref.shape[2] // chips
    pair = block // TILE
    chunk = out_ref.shape[0] * pair
    timed = history + chunk
    core = lax.axis_index("core")

    for chip in range(chips):
        place = pl.ds(pl.multiple_of((chip * CORES + core) * block, block), block)
        for group in range(groups):
            for band in range(bands):
                coeff_ref[group, band, place] = mine_ref[group, band, chip * block : (chip + 1) * block]

    def put(group, band, i, values):
        if i < chips:
            place = pl.ds(pl.multiple_of((i * CORES + 1 - core) * block, block), block)
        else:
            place = slice(timed * TILE + (i - chips) * block, timed * TILE + (i - chips + 1) * block)
        coeff_ref[group, band, place] = values

    windows = [other_ref.at[chip] for chip in range(chips)]
    if not whole:
        windows += [refer_ref.at[i] for i in range(refer_ref.shape[0])]
    filter_frames(windows, left_ref, right_ref, stacked_ref, put)

    def phase_one(slot, carry):
        place = pl.ds(pl.multiple_of(slot * TILE, TILE), TILE)
        if whole:
            source = ref_frame_ref[segments_ref[slot]]
        else:
            first = lax.axis_index("chunk") * chunk - history
            source = timed + segments_ref[jnp.maximum(first + slot, 0)]
        refer = pl.ds(pl.multiple_of(source * TILE, TILE), TILE)
        for group in range(groups):
            for band in range(bands):
                coeff_real = coeff_ref[group, band, place, 0:half].astype(jnp.float32)
                coeff_imag = coeff_ref[group, band, place, half:wide].astype(jnp.float32)
                ref_real = coeff_ref[group, band, refer, 0:half].astype(jnp.float32)
                ref_imag = coeff_ref[group, band, refer, half:wide].astype(jnp.float32)
                prod_real = coeff_real * ref_real + coeff_imag * ref_imag
                prod_imag = coeff_imag * ref_real - coeff_real * ref_imag
                square = prod_real * prod_real + prod_imag * prod_imag + 1.0
                phase = (prod_imag * lax.rsqrt(square)).astype(jnp.bfloat16)
                phase_ref[band, place, group * half : (group + 1) * half] = phase
        return carry

    lax.fori_loop(0, timed, phase_one, 0, unroll=2)

    piece = min(128, chunk * TILE)
    columns = half // SHARE
    left_half = lax.broadcasted_iota(jnp.int32, (TILE, half), 1) < columns
    for band in range(bands):
        for start in range(0, chunk * TILE, piece):
            here = slice(history * TILE + start, history * TILE + start + piece)
            filtered = jnp.dot(spread_ref[start : start + piece], phase_ref[band], preferred_element_type=jnp.float32)
            filtered = filtered.astype(jnp.bfloat16).astype(jnp.float32)
            above = jnp.zeros((piece, half), jnp.float32)
            below = jnp.zeros((piece, half), jnp.float32)
            for group in range(groups):
                coeff_real = coeff_ref[group, band, here, 0:half].astype(jnp.float32)
                coeff_imag = coeff_ref[group, band, here, half:wide].astype(jnp.float32)
                amplitude = coeff_real * coeff_real + coeff_imag * coeff_imag
                above = above + amplitude * filtered[:, group * half : (group + 1) * half]
                below = below + amplitude
            above = above + pltpu.roll(above, columns, 1)
            below = below + pltpu.roll(below, columns, 1)
            motion = above / (below + 1.0)
            for i in range(piece // block):
                first, second = motion[i * block : i * block + TILE], motion[i * block + TILE : (i + 1) * block]
                both = jnp.where(left_half, first, second).astype(out_ref.dtype)
                out_ref[start // block + i, band * TILE : (band + 1) * TILE] = both
    me = lax.axis_index("slab")
    for k, chip_ref in zip(order, out_refs):
        chip_ref[...] = out_ref[pl.ds(lax.bitwise_xor(me, k) * CORES, CORES)]


def pixel_motion(segments, ref_frames, spread, mine, other, refer, left, right, order, chunk, history):
    chips = other.shape[0]
    groups, bands, many, wide = mine.shape
    deep = right.shape[1]
    timed = history + chunk
    whole = refer is None
    slots = timed if whole else timed + NSEG
    pair = many // chips // TILE
    smem = pl.BlockSpec(memory_space=pltpu.SMEM)
    vmem = pl.BlockSpec(memory_space=pltpu.VMEM)
    return pl.pallas_call(
        functools.partial(pixel_kernel, order=order, history=history, whole=whole),
        in_specs=[smem] * 2 + [vmem] * 6,
        out_specs=[vmem] * len(order),
        out_shape=[jax.ShapeDtypeStruct((CORES, bands * TILE, wide // 2), jnp.bfloat16)] * len(order),
        scratch_shapes=[
            pltpu.VMEM((groups, bands * (slots - timed // 2) * TILE, deep), jnp.bfloat16),
            pltpu.VMEM((groups, bands, slots * TILE, wide), jnp.bfloat16),
            pltpu.VMEM((bands, timed * TILE, groups * wide // 2), jnp.bfloat16),
            pltpu.VMEM((chunk // pair, bands * TILE, wide // 2), jnp.bfloat16),
        ],
        compiler_params=pltpu.CompilerParams(vmem_limit_bytes=8 * groups * bands * slots * TILE * wide + 16 * MIB),
        cost_estimate=pl.CostEstimate(
            flops=2 * groups * bands * TILE * wide * (slots * deep + chunk * timed * TILE // 2),
            bytes_accessed=2 * (other.size + mine.size + right.size),
            transcendentals=groups * bands * TILE * timed * wide // 2,
        ),
    )(segments, ref_frames, spread, mine, other, other if whole else refer, left, right)


def sort_kernel(*refs, order):
    me, core = lax.axis_index("slab"), lax.axis_index("core")
    for k, in_ref in zip(order, refs):
        refs[-1][lax.bitwise_xor(me, k)] = in_ref[1 - core]


def sort_tiles(tiles, order):
    vmem = pl.BlockSpec(memory_space=pltpu.VMEM)
    out = jax.ShapeDtypeStruct((len(tiles),) + tiles[0].shape[1:], jnp.bfloat16)
    return pl.pallas_call(
        functools.partial(sort_kernel, order=order),
        in_specs=[vmem] * len(tiles),
        out_specs=vmem,
        out_shape=out,
        compiler_params=pltpu.CompilerParams(vmem_limit_bytes=16 * MIB),
        cost_estimate=pl.CostEstimate(flops=0, bytes_accessed=4 * out.size, transcendentals=0),
    )(*tiles)


def join_kernel(*refs, order):
    in_refs, (swapped_ref, out_ref, tiles_ref) = refs[:-3], refs[-3:]
    me, core = lax.axis_index("slab"), lax.axis_index("core")
    for k, in_ref in zip(order, in_refs):
        tiles_ref[lax.bitwise_xor(me, k) * CORES + core] = in_ref[core]
    for chip in range(len(order)):
        tiles_ref[chip * CORES + 1 - core] = swapped_ref[chip]
    count, quarter, _ = out_ref.shape
    devices, rows, lanes = tiles_ref.shape
    columns = lanes // count
    strips = quarter // columns
    left = lax.broadcasted_iota(jnp.int32, (rows, lanes), 1) < columns
    for strip in range(0, strips, 2):
        for i in range(devices // strips):
            one = tiles_ref[strip * devices // strips + i].astype(jnp.float32)
            two = tiles_ref[(strip + 1) * devices // strips + i].astype(jnp.float32)
            here = slice(strip * columns, (strip + 2) * columns)
            out_ref[0, i * rows : (i + 1) * rows, here] = jnp.where(left, one, pltpu.roll(two, columns, 1))
            out_ref[1, i * rows : (i + 1) * rows, here] = jnp.where(left, pltpu.roll(one, columns, 1), two)


def join_tiles(tiles, swapped, order, quarter):
    vmem = pl.BlockSpec(memory_space=pltpu.VMEM)
    return pl.pallas_call(
        functools.partial(join_kernel, order=order),
        in_specs=[vmem] * (len(tiles) + 1),
        out_specs=vmem,
        out_shape=jax.ShapeDtypeStruct((2, quarter, quarter), jnp.float32),
        scratch_shapes=[pltpu.VMEM((CORES * len(tiles),) + tiles[0].shape[1:], jnp.bfloat16)],
        compiler_params=pltpu.CompilerParams(vmem_limit_bytes=16 * MIB),
        cost_estimate=pl.CostEstimate(flops=swapped.size, bytes_accessed=12 * swapped.size, transcendentals=0),
    )(*tiles, swapped)


def chunk_windows(mine, other, ref_frames, frames_here, history_chips, chips):
    mine = lax.all_gather(mine, "chunk", axis=0, tiled=True)
    other = lax.all_gather(other, "chunk", axis=0, tiled=True)
    height = mine.shape[1]
    core = lax.axis_index("core")
    device, f = ref_frames // frames_here, ref_frames % frames_here
    own = (device % CORES == core)[:, None, None]

    def pick(windows):
        return windows.reshape(windows.shape[0], height, frames_here, -1)[device // CORES, :, f]

    refer = jnp.where(own, pick(mine), pick(other))
    refer = refer.reshape(NSEG // frames_here, frames_here, height, -1)
    refer = jnp.swapaxes(refer, 1, 2).reshape(NSEG // frames_here, height, -1)

    def cut(windows):
        before = jnp.zeros((history_chips,) + windows.shape[1:], windows.dtype)
        windows = jnp.concatenate([before, windows])
        return lax.dynamic_slice_in_dim(windows, lax.axis_index("chunk") * chips, history_chips + chips)

    return cut(mine), cut(other), refer


def body(video_frames, segments, ref_pick, band_taps, *, chunks, slabs):
    frames_here, size, _ = video_frames.shape
    quarter = size // 4
    rows = quarter // (DOWN * CORES)
    columns = quarter * DOWN // slabs
    chunk = slabs * CORES * frames_here
    history = min(chunk * -(-(band_taps.shape[0] - 1) // chunk), segments.shape[0] - chunk)
    left = jnp.asarray(slab_left_table(rows, HALO, ORIENT))
    right = jnp.asarray(make_right_table(columns, HALO, ORIENT))
    order = exchange_order(slabs)

    def exchange(array, k):
        return lax.ppermute(array, "slab", [(chip, chip ^ k) for chip in range(slabs)]) if k else array

    def swap(array):
        return lax.ppermute(array, "core", [(0, 1), (1, 0)])

    windows = reduce_frames(video_frames, order, HALO)
    spread, ref_frames = time_tables(segments, ref_pick, band_taps, TILE, chunk, history)
    pieces = [exchange(window, k) for k, window in zip(order, windows)]
    mine, other = cut_windows(ref_frames, pieces, order, HALO)
    other, refer = swap(other), None
    if chunks > 1:
        history_chips = history // (CORES * frames_here)
        mine, other, refer = chunk_windows(mine, other, ref_frames, frames_here, history_chips, slabs)
    mine = own_coeffs(mine, left, right, rows, frames_here)
    motion = pixel_motion(segments, ref_frames, spread, mine, other, refer, left, right, order, chunk, history)
    tiles = [exchange(tile, k) for k, tile in zip(order, motion)]
    return join_tiles(tiles, swap(sort_tiles(tiles, order)), order, quarter)


def solution(mesh):
    chips = mesh.shape["frames"] // CORES
    slabs = min(chips, QUART * DOWN // (2 * HALO))
    chunks = chips // slabs
    names = ("groups", "chunk", "slab", "core")
    cut = jax.sharding.Mesh(mesh.devices.reshape(mesh.shape["groups"], chunks, slabs, CORES), names)
    in_specs = (P(names, None, None), P("groups"), P("groups"), P())
    return jax.shard_map(
        functools.partial(body, chunks=chunks, slabs=slabs),
        mesh=cut, in_specs=in_specs, out_specs=P(names, None, None), check_vma=False,
    )
```

```python
import functools
import math

import jax
import jax.numpy as jnp
import numpy as np
from jax import lax
from jax.experimental import pallas as pl
from jax.experimental.pallas import tpu as pltpu
from jax.sharding import PartitionSpec as P

IMG = 1024
ORIENT = 4
NSEG = 4
QUART = 256


blur_sigma = 2.0
gabor_sigma = 2.0
wave_number = math.pi / 2.0
gabor_gain = 2.0

HALO = 32
TILE = 16
DOWN = 2
SHARE = 2
CORES = 2
MIB = 1024 * 1024


def envelope_of(offset_grid):
    return np.float32(gabor_gain) * np.exp(
        -offset_grid * offset_grid / np.float32(2.0 * gabor_sigma * gabor_sigma)
    )


def waves(orient):
    angles = np.arange(orient, dtype=np.float32) * np.float32(math.pi / orient)
    wave_x = np.float32(wave_number) * np.cos(angles)
    wave_y = np.float32(wave_number) * np.sin(angles)
    return wave_x, wave_y


def slab_left_table(rows, halo, orient):
    offset = (
        np.arange(rows + 2 * halo, dtype=np.float32)[None, :]
        - np.float32(halo)
        - np.arange(rows, dtype=np.float32)[:, None]
    )
    wave_y = waves(orient)[1]
    phase = wave_y[:, None, None] * offset[None]
    envelope = envelope_of(offset)[None]
    table = np.stack([envelope * np.cos(phase), envelope * np.sin(phase)], axis=1)
    return table.reshape(orient * 2 * rows, rows + 2 * halo).astype(jnp.bfloat16)


def make_right_table(columns, halo, orient):
    window = columns + 2 * halo
    offset = (
        np.arange(window, dtype=np.float32)[:, None] - np.float32(halo) - np.arange(columns, dtype=np.float32)[None, :]
    )
    wave_x = waves(orient)[0]
    phase_x = wave_x[:, None, None] * offset[None]
    envelope = envelope_of(offset)[None]
    real_part = envelope * np.cos(phase_x)
    imag_part = envelope * np.sin(phase_x)
    table = np.zeros((orient // SHARE, SHARE, 2, window, 2, SHARE, columns), np.float32)
    for o in range(orient):
        group, i = divmod(o, SHARE)
        table[group, i, 0, :, 0, i] = real_part[o]
        table[group, i, 0, :, 1, i] = imag_part[o]
        table[group, i, 1, :, 0, i] = -imag_part[o]
        table[group, i, 1, :, 1, i] = real_part[o]
    return table.reshape(orient // SHARE, SHARE * 2 * window, 2 * SHARE * columns).astype(jnp.bfloat16)


def down_sums(full_size, quarter):
    position = np.arange(quarter, dtype=np.float32)[:, None]
    columns = np.arange(full_size, dtype=np.float32)[None, :]
    offset_grid = columns - np.float32(4.0) * position - np.float32(1.5)
    weight = np.exp(-offset_grid * offset_grid / np.float32(2.0 * blur_sigma * blur_sigma))
    return np.sum(weight, axis=1)


def down_block(position, column, shape, axis, sums):
    positions = position + lax.broadcasted_iota(jnp.int32, shape, 1 - axis)
    columns = column + lax.broadcasted_iota(jnp.int32, shape, axis)
    offset_grid = columns.astype(jnp.float32) - 4.0 * positions.astype(jnp.float32) - 1.5
    weight = jnp.exp(-offset_grid * offset_grid / (2.0 * blur_sigma * blur_sigma))
    inner = float(sums[len(sums) // 2])
    line = position + lax.broadcasted_iota(jnp.int32, tuple(1 if i == axis else n for i, n in enumerate(shape)), 1 - axis)
    scale = jnp.full(line.shape, 1.0 / inner, jnp.float32)
    for q in range(position, min(position + shape[1 - axis], len(sums))):
        if abs(float(sums[q]) - inner) > 1e-7 * inner:
            scale = jnp.where(line == q, 1.0 / float(sums[q]), scale)
    return (weight * scale).astype(jnp.bfloat16)


def build_down(down_t_ref, down_ref):
    size, quarter = down_t_ref.shape
    sums = down_sums(size, quarter)
    lanes = min(128, quarter)
    down_t_ref[...] = jnp.zeros_like(down_t_ref)
    down_ref[...] = jnp.zeros_like(down_ref)
    for row in range(0, size, 128):
        for lane in range(0, quarter, lanes):
            if 4 * (lane + lanes - 1) + 30 >= row and 4 * lane - 27 <= row + 127:
                down_t_ref[row : row + 128, lane : lane + lanes] = down_block(lane, row, (128, lanes), 0, sums)
    for row in range(0, quarter, 32):
        for lane in range(0, size, 128):
            if 4 * (row + 31) + 30 >= lane and 4 * row - 27 <= lane + 127:
                down_ref[row : row + 32, lane : lane + 128] = down_block(row, lane, (32, 128), 1, sums)


def reduce_kernel(frames_ref, *refs, order, halo, block):
    out_refs = refs[: len(order)]
    picture_ref, down_t_ref, down_ref, half_ref, total_ref, strip_ref, sems = refs[len(order) :]
    count, size, _ = picture_ref.shape
    quarter = down_ref.shape[0]
    strips, _, lanes = strip_ref.shape
    columns = lanes - 2 * halo
    window = out_refs[0].shape[1]

    copies = []
    for f in range(count):
        for i in range(size // block):
            here = pl.ds(i * block, block)
            copy = pltpu.make_async_copy(frames_ref.at[f, here], picture_ref.at[f, here], sems.at[f, i])
            copy.start()
            copies.append(copy)
    build_down(down_t_ref, down_ref)

    me = lax.axis_index("slab")
    reach = quarter
    for f in range(count):
        total_ref[...] = jnp.zeros_like(total_ref)
        for i in range(size // block):
            copies[f * (size // block) + i].wait()
            half_ref[...] = jnp.dot(
                picture_ref[f, i * block : (i + 1) * block], down_t_ref[...], preferred_element_type=jnp.float32
            ).astype(jnp.bfloat16)
            for row in range(0, block, reach):
                begin = i * block + row
                near = slice(max(begin // 4 - TILE, 0), min((begin + reach) // 4 + TILE, quarter))
                total_ref[near] += jnp.dot(
                    down_ref[near, begin : begin + reach], half_ref[row : row + reach], preferred_element_type=jnp.float32
                )
        for strip in range(strips):
            begin = strip * columns - halo
            moved = pltpu.roll(total_ref[...], (-begin) % quarter, 1)[:, 0:lanes]
            column = begin + lax.broadcasted_iota(jnp.int32, (quarter, lanes), 1)
            inside = (column >= 0) & (column < quarter)
            strip_ref[strip] = jnp.where(inside, moved, 0.0).astype(jnp.bfloat16)
        for k, out_ref in zip(order, out_refs):
            slab = lax.bitwise_xor(me, k)
            begin = pl.multiple_of(lax.rem(slab, DOWN) * (quarter - window), TILE)
            out_ref[f] = strip_ref[slab // DOWN, pl.ds(begin, window)]


def reduce_frames(video_frames, order, halo):
    count, size, _ = video_frames.shape
    quarter = size // 4
    strips = len(order) // DOWN
    lanes = quarter // strips + 2 * halo
    block = size // 2
    out = jax.ShapeDtypeStruct((count, quarter // DOWN + halo, lanes), jnp.bfloat16)
    return pl.pallas_call(
        functools.partial(reduce_kernel, order=order, halo=halo, block=block),
        in_specs=[pl.BlockSpec(memory_space=pltpu.HBM)],
        out_specs=[pl.BlockSpec(memory_space=pltpu.VMEM)] * len(order),
        out_shape=[out] * len(order),
        scratch_shapes=[
            pltpu.VMEM((count, size, size), jnp.bfloat16),
            pltpu.VMEM((size, quarter), jnp.bfloat16),
            pltpu.VMEM((quarter, size), jnp.bfloat16),
            pltpu.VMEM((block, quarter), jnp.bfloat16),
            pltpu.VMEM((quarter, quarter), jnp.float32),
            pltpu.VMEM((strips, quarter, lanes), jnp.bfloat16),
            pltpu.SemaphoreType.DMA((count, size // block)),
        ],
        compiler_params=pltpu.CompilerParams(vmem_limit_bytes=52 * MIB),
        cost_estimate=pl.CostEstimate(
            flops=2 * count * size * quarter * (size + quarter),
            bytes_accessed=2 * count * size * size,
            transcendentals=0,
        ),
    )(video_frames)


def exchange_order(slabs):
    far = sorted(range(slabs // 2, slabs), key=lambda k: k % 2)
    near = list(range(2, slabs // 2)) + [k for k in (1,) if k < slabs // 2]
    return [0] + far[: len(far) // 2] + near[:1] + far[len(far) // 2 :] + near[1:]


def cut_kernel(*refs, many, halo):
    in_refs, (mine_ref, other_ref), padded_ref = refs[:many], refs[-3:-1], refs[-1]
    count, window, lanes = in_refs[0].shape
    height = mine_ref.shape[1]
    rows = height - 2 * halo
    me, core = lax.axis_index("slab"), lax.axis_index("core")
    edge = jnp.zeros((halo, count * lanes), jnp.bfloat16)
    padded_ref[0:halo] = edge
    padded_ref[halo + window :] = edge
    above = lax.rem(me, DOWN) * halo
    for n, in_ref in enumerate(in_refs):
        for f in range(count):
            padded_ref[halo : halo + window, f * lanes : (f + 1) * lanes] = in_ref[f]
        for out_ref, number in ((mine_ref, core), (other_ref, 1 - core)):
            out_ref[n] = padded_ref[pl.ds(pl.multiple_of(above + number * rows, TILE), height)]


def cut_windows(pieces, halo, after):
    count, window, lanes = pieces[0].shape
    height = (window - halo) // CORES + 2 * halo
    out = jax.ShapeDtypeStruct((len(pieces), height, count * lanes), jnp.bfloat16)
    return pl.pallas_call(
        functools.partial(cut_kernel, many=len(pieces), halo=halo),
        in_specs=[pl.BlockSpec(memory_space=pltpu.VMEM)] * len(pieces) + [pl.BlockSpec(memory_space=pl.ANY)] * len(after),
        out_specs=[pl.BlockSpec(memory_space=pltpu.VMEM)] * 2,
        out_shape=[out, out],
        scratch_shapes=[pltpu.VMEM((window + 2 * halo, count * lanes), jnp.bfloat16)],
        compiler_params=pltpu.CompilerParams(vmem_limit_bytes=16 * MIB),
        cost_estimate=pl.CostEstimate(flops=0, bytes_accessed=8 * out.size, transcendentals=0),
    )(*pieces, *after)


def time_kernel(segments_ref, pick_ref, taps_ref, spread_ref, frame_ref, *, history, frames, rows):
    chunk, timed = spread_ref.shape[0] // rows, spread_ref.shape[1] // rows
    nseg = pick_ref.shape[0]
    taps = taps_ref.shape[0]
    wide_out, wide_in = chunk * rows, timed * rows

    def count_one(t, totals):
        here = segments_ref[t]
        below = [total + (here < s).astype(jnp.int32) for s, total in enumerate(totals[0])]
        same = [total + (here == s).astype(jnp.int32) for s, total in enumerate(totals[1])]
        return tuple(below), tuple(same)

    zeros = tuple(jnp.int32(0) for _ in range(nseg))
    starts, counts = lax.fori_loop(0, frames, count_one, (zeros, zeros), unroll=8)
    for s in range(nseg):
        frame_ref[s] = starts[s] + lax.rem(pick_ref[s], counts[s])

    lag = history + lax.broadcasted_iota(jnp.int32, (chunk, timed), 0) - lax.broadcasted_iota(
        jnp.int32, (chunk, timed), 1
    )
    if history:
        first = lax.axis_index("chunk") * chunk - history
        real = first + lax.broadcasted_iota(jnp.int32, (chunk, timed), 1) >= 0
        lag = jnp.where(real, lag, -1)
    matrix = jnp.zeros((chunk, timed), jnp.float32)
    for k in range(taps):
        matrix = jnp.where(lag == k, taps_ref[k], matrix)
    repeat_left = (
        lax.broadcasted_iota(jnp.int32, (wide_out, chunk), 0) // rows
        == lax.broadcasted_iota(jnp.int32, (wide_out, chunk), 1)
    ).astype(jnp.bfloat16)
    repeat_right = (
        lax.broadcasted_iota(jnp.int32, (timed, wide_in), 1) // rows
        == lax.broadcasted_iota(jnp.int32, (timed, wide_in), 0)
    ).astype(jnp.bfloat16)
    tall = jnp.dot(repeat_left, matrix.astype(jnp.bfloat16), preferred_element_type=jnp.float32)
    tall = tall.astype(jnp.bfloat16)
    piece = min(128, wide_out)
    for start in range(0, wide_out, piece):
        part = jnp.dot(tall[start : start + piece], repeat_right, preferred_element_type=jnp.float32)
        same_row = (
            lax.broadcasted_iota(jnp.int32, (piece, wide_in), 0) % rows
            == lax.broadcasted_iota(jnp.int32, (piece, wide_in), 1) % rows
        )
        spread_ref[start : start + piece] = jnp.where(same_row, part, 0.0).astype(jnp.bfloat16)


def time_tables(segments, ref_pick, band_taps, rows, chunk, history):
    frames = segments.shape[0]
    wide_out, wide_in = chunk * rows, (history + chunk) * rows
    smem = pl.BlockSpec(memory_space=pltpu.SMEM)
    return pl.pallas_call(
        functools.partial(time_kernel, history=history, frames=frames, rows=rows),
        in_specs=[smem] * 3,
        out_specs=[pl.BlockSpec(memory_space=pltpu.VMEM), smem],
        out_shape=[
            jax.ShapeDtypeStruct((wide_out, wide_in), jnp.bfloat16),
            jax.ShapeDtypeStruct(ref_pick.shape, jnp.int32),
        ],
        compiler_params=pltpu.CompilerParams(vmem_limit_bytes=16 * MIB),
        cost_estimate=pl.CostEstimate(
            flops=2 * wide_out * wide_in * chunk, bytes_accessed=2 * wide_out * wide_in, transcendentals=0
        ),
    )(segments, ref_pick, band_taps.astype(jnp.float32))


def filter_frames(window_refs, left_ref, right_ref, stacked_ref, put):
    groups, deep, _ = right_ref.shape
    lanes = deep // (2 * SHARE)
    rows = left_ref.shape[0] // (2 * SHARE * groups)
    bands = rows // TILE
    pair = window_refs[0].shape[1] // lanes
    many = len(window_refs) * pair * TILE
    for n, window in enumerate(window_refs):
        stacked = jnp.dot(left_ref[...], window[...], preferred_element_type=jnp.float32).astype(jnp.bfloat16)
        for oz in range(2 * SHARE * groups):
            group, place = divmod(oz, 2 * SHARE)
            for band in range(bands):
                begin = oz * rows + band * TILE
                for f in range(pair):
                    row = band * many + (n * pair + f) * TILE
                    stacked_ref[group, row : row + TILE, place * lanes : (place + 1) * lanes] = stacked[
                        begin : begin + TILE, f * lanes : (f + 1) * lanes
                    ]
    block = pair * TILE
    total = bands * many
    step = min(512, total)
    for group in range(groups):
        for start in range(0, total, step):
            stop = min(start + step, total)
            coeff = jnp.dot(
                stacked_ref[group, start:stop], right_ref[group], preferred_element_type=jnp.float32
            ).astype(jnp.bfloat16)
            for place in range(start, stop, block):
                band, row = divmod(place, many)
                put(group, band, row // block, coeff[place - start : place - start + block])


def coeff_kernel(window_ref, left_ref, right_ref, coeff_ref, stacked_ref):
    chips = window_ref.shape[0]
    block = coeff_ref.shape[2] // chips

    def put(group, band, i, values):
        coeff_ref[group, band, i * block : (i + 1) * block] = values

    filter_frames([window_ref.at[chip] for chip in range(chips)], left_ref, right_ref, stacked_ref, put)


def own_coeffs(windows, left, right, rows, frames_here):
    groups, deep, wide = right.shape
    vmem = pl.BlockSpec(memory_space=pltpu.VMEM)
    many = windows.shape[0] * frames_here * TILE
    out = jax.ShapeDtypeStruct((groups, rows // TILE, many, wide), jnp.bfloat16)
    return pl.pallas_call(
        coeff_kernel,
        in_specs=[vmem] * 3,
        out_specs=vmem,
        out_shape=out,
        scratch_shapes=[pltpu.VMEM((groups, rows // TILE * many, deep), jnp.bfloat16)],
        compiler_params=pltpu.CompilerParams(vmem_limit_bytes=8 * out.size + 16 * MIB),
        cost_estimate=pl.CostEstimate(
            flops=4 * out.size * deep, bytes_accessed=2 * (windows.size + out.size), transcendentals=0
        ),
    )(windows, left, right)


def pixel_kernel(
    segments_ref, ref_frame_ref, spread_ref, other_ref, refer_ref, left_ref, right_ref, *refs, places, history, whole
):
    ready_refs, (out_ref, stacked_ref, coeff_ref, phase_ref, filtered_ref) = refs[:-5], refs[-5:]
    chips = other_ref.shape[0]
    groups, bands, _, wide = coeff_ref.shape
    half = wide // 2
    pair = other_ref.shape[2] // (right_ref.shape[1] // (2 * SHARE))
    block = pair * TILE
    chunk = out_ref.shape[0] * pair
    timed = history + chunk
    core = lax.axis_index("core")

    def place_of(exchanges, twin, n):
        chip = n if exchanges is None else lax.bitwise_xor(lax.axis_index("slab"), exchanges[n])
        return pl.ds(pl.multiple_of((chip * CORES + lax.rem(core + twin, CORES)) * block, block), block)

    for ready_ref, (exchanges, twin) in zip(ready_refs, places):
        for n in range(ready_ref.shape[2] // block):
            for group in range(groups):
                for band in range(bands):
                    coeff_ref[group, band, place_of(exchanges, twin, n)] = ready_ref[group, band, n * block : (n + 1) * block]

    def put(group, band, i, values):
        if i < chips:
            place = place_of(*places[-1], i)
        else:
            place = slice(timed * TILE + (i - chips) * block, timed * TILE + (i - chips + 1) * block)
        coeff_ref[group, band, place] = values

    windows = [other_ref.at[chip] for chip in range(chips)]
    if not whole:
        windows += [refer_ref.at[i] for i in range(refer_ref.shape[0])]
    filter_frames(windows, left_ref, right_ref, stacked_ref, put)

    def phase_one(slot, carry):
        place = pl.ds(pl.multiple_of(slot * TILE, TILE), TILE)
        if whole:
            source = ref_frame_ref[segments_ref[slot]]
        else:
            first = lax.axis_index("chunk") * chunk - history
            source = timed + segments_ref[jnp.maximum(first + slot, 0)]
        refer = pl.ds(pl.multiple_of(source * TILE, TILE), TILE)
        for group in range(groups):
            for band in range(bands):
                coeff_real = coeff_ref[group, band, place, 0:half].astype(jnp.float32)
                coeff_imag = coeff_ref[group, band, place, half:wide].astype(jnp.float32)
                ref_real = coeff_ref[group, band, refer, 0:half].astype(jnp.float32)
                ref_imag = coeff_ref[group, band, refer, half:wide].astype(jnp.float32)
                prod_real = coeff_real * ref_real + coeff_imag * ref_imag
                prod_imag = coeff_imag * ref_real - coeff_real * ref_imag
                square = prod_real * prod_real + prod_imag * prod_imag + 1.0
                phase = (prod_imag * lax.rsqrt(square)).astype(jnp.bfloat16)
                phase_ref[band, place, group * half : (group + 1) * half] = phase
        return carry

    lax.fori_loop(0, timed, phase_one, 0, unroll=2)

    piece = min(128, chunk * TILE)
    columns = half // SHARE
    left_half = lax.broadcasted_iota(jnp.int32, (TILE, half), 1) < columns
    step = min(256, chunk * TILE)
    for band in range(bands):
        for start in range(0, chunk * TILE, step):
            stop = start + step
            filtered_ref[start:stop] = jnp.dot(
                spread_ref[start:stop, : history * TILE + stop],
                phase_ref[band, : history * TILE + stop],
                preferred_element_type=jnp.float32,
            ).astype(jnp.bfloat16)
        for start in range(0, chunk * TILE, piece):
            here = slice(history * TILE + start, history * TILE + start + piece)
            filtered = filtered_ref[start : start + piece].astype(jnp.float32)
            above = jnp.zeros((piece, half), jnp.float32)
            below = jnp.zeros((piece, half), jnp.float32)
            for group in range(groups):
                coeff_real = coeff_ref[group, band, here, 0:half].astype(jnp.float32)
                coeff_imag = coeff_ref[group, band, here, half:wide].astype(jnp.float32)
                amplitude = coeff_real * coeff_real + coeff_imag * coeff_imag
                above = above + amplitude * filtered[:, group * half : (group + 1) * half]
                below = below + amplitude
            above = above + pltpu.roll(above, columns, 1)
            below = below + pltpu.roll(below, columns, 1)
            motion = above / (below + 1.0)
            for i in range(piece // block):
                first, second = motion[i * block : i * block + TILE], motion[i * block + TILE : (i + 1) * block]
                both = jnp.where(left_half, first, second).astype(out_ref.dtype)
                out_ref[start // block + i, band * TILE : (band + 1) * TILE] = both


def pixel_motion(segments, ref_frames, spread, ready, other, refer, left, right, places, chunk, history):
    groups, bands, _, wide = ready[0].shape
    deep = right.shape[1]
    timed = history + chunk
    whole = refer is None
    slots = timed if whole else timed + NSEG
    pair = other.shape[2] // (deep // (2 * SHARE))
    fresh = other.shape[0] * pair + slots - timed
    smem = pl.BlockSpec(memory_space=pltpu.SMEM)
    vmem = pl.BlockSpec(memory_space=pltpu.VMEM)
    return pl.pallas_call(
        functools.partial(pixel_kernel, places=places, history=history, whole=whole),
        in_specs=[smem] * 2 + [vmem] * (5 + len(ready)),
        out_specs=vmem,
        out_shape=jax.ShapeDtypeStruct((chunk // pair, bands * TILE, wide // 2), jnp.bfloat16),
        scratch_shapes=[
            pltpu.VMEM((groups, bands * fresh * TILE, deep), jnp.bfloat16),
            pltpu.VMEM((groups, bands, slots * TILE, wide), jnp.bfloat16),
            pltpu.VMEM((bands, timed * TILE, groups * wide // 2), jnp.bfloat16),
            pltpu.VMEM((chunk * TILE, groups * wide // 2), jnp.bfloat16),
        ],
        compiler_params=pltpu.CompilerParams(vmem_limit_bytes=8 * groups * bands * slots * TILE * wide + 16 * MIB),
        cost_estimate=pl.CostEstimate(
            flops=2 * groups * bands * TILE * wide * (fresh * deep + chunk * timed * TILE // 2),
            bytes_accessed=2 * (other.size + sum(one.size for one in ready) + right.size),
            transcendentals=groups * bands * TILE * timed * wide // 2,
        ),
    )(segments, ref_frames, spread, other, other if whole else refer, left, right, *ready)


def join_kernel(tiles_ref, out_ref):
    count, quarter, _ = out_ref.shape
    devices, rows, lanes = tiles_ref.shape
    columns = lanes // count
    strips = quarter // columns
    left = lax.broadcasted_iota(jnp.int32, (rows, lanes), 1) < columns
    for strip in range(0, strips, 2):
        for i in range(devices // strips):
            one = tiles_ref[strip * devices // strips + i].astype(jnp.float32)
            two = tiles_ref[(strip + 1) * devices // strips + i].astype(jnp.float32)
            here = slice(strip * columns, (strip + 2) * columns)
            out_ref[0, i * rows : (i + 1) * rows, here] = jnp.where(left, one, pltpu.roll(two, columns, 1))
            out_ref[1, i * rows : (i + 1) * rows, here] = jnp.where(left, pltpu.roll(one, columns, 1), two)


def join_tiles(tiles, quarter):
    vmem = pl.BlockSpec(memory_space=pltpu.VMEM)
    return pl.pallas_call(
        join_kernel,
        in_specs=[vmem],
        out_specs=vmem,
        out_shape=jax.ShapeDtypeStruct((2, quarter, quarter), jnp.float32),
        compiler_params=pltpu.CompilerParams(vmem_limit_bytes=16 * MIB),
        cost_estimate=pl.CostEstimate(flops=tiles.size, bytes_accessed=6 * tiles.size, transcendentals=0),
    )(tiles)


def chunk_windows(mine, other, ref_frames, frames_here, history_chips, chips):
    mine = lax.all_gather(mine, "chunk", axis=0, tiled=True)
    other = lax.all_gather(other, "chunk", axis=0, tiled=True)
    height = mine.shape[1]
    core = lax.axis_index("core")
    device, f = ref_frames // frames_here, ref_frames % frames_here
    own = (device % CORES == core)[:, None, None]

    def pick(windows):
        return windows.reshape(windows.shape[0], height, frames_here, -1)[device // CORES, :, f]

    refer = jnp.where(own, pick(mine), pick(other))
    refer = refer.reshape(NSEG // frames_here, frames_here, height, -1)
    refer = jnp.swapaxes(refer, 1, 2).reshape(NSEG // frames_here, height, -1)

    def cut(windows):
        before = jnp.zeros((history_chips,) + windows.shape[1:], windows.dtype)
        windows = jnp.concatenate([before, windows])
        return lax.dynamic_slice_in_dim(windows, lax.axis_index("chunk") * chips, history_chips + chips)

    return cut(mine), cut(other), refer


def body(video_frames, segments, ref_pick, band_taps, *, chunks, slabs):
    frames_here, size, _ = video_frames.shape
    quarter = size // 4
    rows = quarter // (DOWN * CORES)
    columns = quarter * DOWN // slabs
    chunk = slabs * CORES * frames_here
    history = min(chunk * -(-(band_taps.shape[0] - 1) // chunk), segments.shape[0] - chunk)
    left = jnp.asarray(slab_left_table(rows, HALO, ORIENT))
    right = jnp.asarray(make_right_table(columns, HALO, ORIENT))
    order = exchange_order(slabs)

    def exchange(array, k):
        return lax.ppermute(array, "slab", [(chip, chip ^ k) for chip in range(slabs)]) if k else array

    def swap(array):
        return lax.ppermute(array, "core", [(0, 1), (1, 0)])

    windows = reduce_frames(video_frames, order, HALO)
    spread, ref_frames = time_tables(segments, ref_pick, band_taps, TILE, chunk, history)
    pieces = [exchange(window, k) for k, window in zip(order, windows)]
    if chunks > 1:
        mine, other = cut_windows(pieces, HALO, [])
        by_chip = jnp.asarray(np.argsort(order))[lax.axis_index("slab") ^ jnp.arange(slabs)]
        mine, other = mine[by_chip], swap(other)[by_chip]
        history_chips = history // (CORES * frames_here)
        mine, other, refer = chunk_windows(mine, other, ref_frames, frames_here, history_chips, slabs)
        ready = [own_coeffs(mine, left, right, rows, frames_here)]
        places = [(None, 0), (None, 1)]
    else:
        first = slabs // 2
        mine, other = cut_windows(pieces[:first], HALO, [spread])
        ready = [own_coeffs(one, left, right, rows, frames_here) for one in (mine, swap(other))]
        mine, other = cut_windows(pieces[first:], HALO, ready[:1])
        other, refer = swap(other), None
        ready.append(own_coeffs(mine, left, right, rows, frames_here))
        places = [(exchanges, twin) for exchanges in (order[:first], order[first:]) for twin in range(CORES)]
    motion = pixel_motion(segments, ref_frames, spread, ready, other, refer, left, right, places, chunk, history)
    motion = lax.all_to_all(motion, ("slab", "core"), split_axis=0, concat_axis=0, tiled=True)
    return join_tiles(motion, quarter)


def solution(mesh):
    chips = mesh.shape["frames"] // CORES
    slabs = min(chips, QUART * DOWN // (2 * HALO))
    chunks = chips // slabs
    names = ("groups", "chunk", "slab", "core")
    cut = jax.sharding.Mesh(mesh.devices.reshape(mesh.shape["groups"], chunks, slabs, CORES), names)
    in_specs = (P(names, None, None), P("groups"), P("groups"), P())
    return jax.shard_map(
        functools.partial(body, chunks=chunks, slabs=slabs),
        mesh=cut, in_specs=in_specs, out_specs=P(names, None, None), check_vma=False,
    )
```

```python
import functools
import math

import jax
import jax.numpy as jnp
import numpy as np
from jax import lax
from jax.experimental import pallas as pl
from jax.experimental.pallas import tpu as pltpu
from jax.sharding import PartitionSpec as P

IMG = 1024
ORIENT = 4
NSEG = 4
QUART = 256


blur_sigma = 2.0
gabor_sigma = 2.0
wave_number = math.pi / 2.0
gabor_gain = 2.0

HALO = 32
TILE = 16
DOWN = 2
SHARE = 2
CORES = 2
MIB = 1024 * 1024


def envelope_of(offset_grid):
    return np.float32(gabor_gain) * np.exp(
        -offset_grid * offset_grid / np.float32(2.0 * gabor_sigma * gabor_sigma)
    )


def waves(orient):
    angles = np.arange(orient, dtype=np.float32) * np.float32(math.pi / orient)
    wave_x = np.float32(wave_number) * np.cos(angles)
    wave_y = np.float32(wave_number) * np.sin(angles)
    return wave_x, wave_y


def slab_left_table(rows, halo, orient):
    offset = (
        np.arange(rows + 2 * halo, dtype=np.float32)[None, :]
        - np.float32(halo)
        - np.arange(rows, dtype=np.float32)[:, None]
    )
    wave_y = waves(orient)[1]
    phase = wave_y[:, None, None] * offset[None]
    envelope = envelope_of(offset)[None]
    table = np.stack([envelope * np.cos(phase), envelope * np.sin(phase)], axis=1)
    return table.reshape(orient * 2 * rows, rows + 2 * halo).astype(jnp.bfloat16)


def make_right_table(columns, halo, orient):
    window = columns + 2 * halo
    offset = (
        np.arange(window, dtype=np.float32)[:, None] - np.float32(halo) - np.arange(columns, dtype=np.float32)[None, :]
    )
    wave_x = waves(orient)[0]
    phase_x = wave_x[:, None, None] * offset[None]
    envelope = envelope_of(offset)[None]
    real_part = envelope * np.cos(phase_x)
    imag_part = envelope * np.sin(phase_x)
    table = np.zeros((orient // SHARE, SHARE, 2, window, 2, SHARE, columns), np.float32)
    for o in range(orient):
        group, i = divmod(o, SHARE)
        table[group, i, 0, :, 0, i] = real_part[o]
        table[group, i, 0, :, 1, i] = imag_part[o]
        table[group, i, 1, :, 0, i] = -imag_part[o]
        table[group, i, 1, :, 1, i] = real_part[o]
    return table.reshape(orient // SHARE, SHARE * 2 * window, 2 * SHARE * columns).astype(jnp.bfloat16)


def down_sums(full_size, quarter):
    position = np.arange(quarter, dtype=np.float32)[:, None]
    columns = np.arange(full_size, dtype=np.float32)[None, :]
    offset_grid = columns - np.float32(4.0) * position - np.float32(1.5)
    weight = np.exp(-offset_grid * offset_grid / np.float32(2.0 * blur_sigma * blur_sigma))
    return np.sum(weight, axis=1)


def down_block(position, column, shape, axis, sums):
    positions = position + lax.broadcasted_iota(jnp.int32, shape, 1 - axis)
    columns = column + lax.broadcasted_iota(jnp.int32, shape, axis)
    offset_grid = columns.astype(jnp.float32) - 4.0 * positions.astype(jnp.float32) - 1.5
    weight = jnp.exp(-offset_grid * offset_grid / (2.0 * blur_sigma * blur_sigma))
    inner = float(sums[len(sums) // 2])
    line = position + lax.broadcasted_iota(jnp.int32, tuple(1 if i == axis else n for i, n in enumerate(shape)), 1 - axis)
    scale = jnp.full(line.shape, 1.0 / inner, jnp.float32)
    for q in range(position, min(position + shape[1 - axis], len(sums))):
        if abs(float(sums[q]) - inner) > 1e-7 * inner:
            scale = jnp.where(line == q, 1.0 / float(sums[q]), scale)
    return (weight * scale).astype(jnp.bfloat16)


def build_down(table_ref, axis):
    size, quarter = table_ref.shape[axis], table_ref.shape[1 - axis]
    sums = down_sums(size, quarter)
    table_ref[...] = jnp.zeros_like(table_ref)
    tall, wide = (128, 32)[axis], min(128, table_ref.shape[1])
    for row in range(0, table_ref.shape[0], tall):
        for lane in range(0, table_ref.shape[1], wide):
            position, column = (row, lane) if axis else (lane, row)
            positions, columns = (tall, wide) if axis else (wide, tall)
            if 4 * (position + positions - 1) + 30 >= column and 4 * position - 27 <= column + columns - 1:
                block = down_block(position, column, (tall, wide), axis, sums)
                table_ref[row : row + tall, lane : lane + wide] = block


def reduce_kernel(frames_ref, *refs, order, halo, block):
    out_refs = refs[: len(order)]
    picture_ref, down_t_ref, down_ref, half_ref, total_ref, strip_ref, sems = refs[len(order) :]
    count, size, _ = picture_ref.shape
    quarter = down_ref.shape[0]
    strips, _, lanes = strip_ref.shape
    columns = lanes - 2 * halo
    window = out_refs[0].shape[1]

    copies = []
    for f in range(count):
        for i in range(size // block):
            here = pl.ds(i * block, block)
            copy = pltpu.make_async_copy(frames_ref.at[f, here], picture_ref.at[f, here], sems.at[f, i])
            copy.start()
            copies.append(copy)
    build_down(down_t_ref, 0)

    me = lax.axis_index("slab")
    reach = quarter
    for f in range(count):
        total_ref[...] = jnp.zeros_like(total_ref)
        for i in range(size // block):
            copies[f * (size // block) + i].wait()
            half_ref[...] = jnp.dot(
                picture_ref[f, i * block : (i + 1) * block], down_t_ref[...], preferred_element_type=jnp.float32
            ).astype(jnp.bfloat16)
            if f == i == 0:
                build_down(down_ref, 1)
            for row in range(0, block, reach):
                begin = i * block + row
                near = slice(max(begin // 4 - TILE, 0), min((begin + reach) // 4 + TILE, quarter))
                total_ref[near] += jnp.dot(
                    down_ref[near, begin : begin + reach], half_ref[row : row + reach], preferred_element_type=jnp.float32
                )
        for strip in range(strips):
            begin = strip * columns - halo
            moved = pltpu.roll(total_ref[...], (-begin) % quarter, 1)[:, 0:lanes]
            column = begin + lax.broadcasted_iota(jnp.int32, (quarter, lanes), 1)
            inside = (column >= 0) & (column < quarter)
            strip_ref[strip] = jnp.where(inside, moved, 0.0).astype(jnp.bfloat16)
        for k, out_ref in zip(order, out_refs):
            slab = lax.bitwise_xor(me, k)
            begin = pl.multiple_of(lax.rem(slab, DOWN) * (quarter - window), TILE)
            out_ref[f] = strip_ref[slab // DOWN, pl.ds(begin, window)]


def reduce_frames(video_frames, order, halo):
    count, size, _ = video_frames.shape
    quarter = size // 4
    strips = len(order) // DOWN
    lanes = quarter // strips + 2 * halo
    block = size // 2
    out = jax.ShapeDtypeStruct((count, quarter // DOWN + halo, lanes), jnp.bfloat16)
    return pl.pallas_call(
        functools.partial(reduce_kernel, order=order, halo=halo, block=block),
        in_specs=[pl.BlockSpec(memory_space=pltpu.HBM)],
        out_specs=[pl.BlockSpec(memory_space=pltpu.VMEM)] * len(order),
        out_shape=[out] * len(order),
        scratch_shapes=[
            pltpu.VMEM((count, size, size), jnp.bfloat16),
            pltpu.VMEM((size, quarter), jnp.bfloat16),
            pltpu.VMEM((quarter, size), jnp.bfloat16),
            pltpu.VMEM((block, quarter), jnp.bfloat16),
            pltpu.VMEM((quarter, quarter), jnp.float32),
            pltpu.VMEM((strips, quarter, lanes), jnp.bfloat16),
            pltpu.SemaphoreType.DMA((count, size // block)),
        ],
        compiler_params=pltpu.CompilerParams(vmem_limit_bytes=52 * MIB),
        cost_estimate=pl.CostEstimate(
            flops=2 * count * size * quarter * (size + quarter),
            bytes_accessed=2 * count * size * size,
            transcendentals=0,
        ),
    )(video_frames)


def exchange_order(slabs):
    far = sorted(range(slabs // 2, slabs), key=lambda k: k % 2)
    near = list(range(2, slabs // 2))
    turns = [k for pair in zip(far, near) for k in pair]
    return [0] + turns + far[len(near) :] + [k for k in (1,) if k < slabs // 2]


def cut_kernel(*refs, many, halo):
    in_refs, (mine_ref, other_ref), padded_ref = refs[:many], refs[-3:-1], refs[-1]
    count, window, lanes = in_refs[0].shape
    height = mine_ref.shape[1]
    rows = height - 2 * halo
    me, core = lax.axis_index("slab"), lax.axis_index("core")
    edge = jnp.zeros((halo, count * lanes), jnp.bfloat16)
    padded_ref[0:halo] = edge
    padded_ref[halo + window :] = edge
    above = lax.rem(me, DOWN) * halo
    for n, in_ref in enumerate(in_refs):
        for f in range(count):
            padded_ref[halo : halo + window, f * lanes : (f + 1) * lanes] = in_ref[f]
        for out_ref, number in ((mine_ref, core), (other_ref, 1 - core)):
            out_ref[n] = padded_ref[pl.ds(pl.multiple_of(above + number * rows, TILE), height)]


def cut_windows(pieces, halo, after):
    count, window, lanes = pieces[0].shape
    height = (window - halo) // CORES + 2 * halo
    out = jax.ShapeDtypeStruct((len(pieces), height, count * lanes), jnp.bfloat16)
    return pl.pallas_call(
        functools.partial(cut_kernel, many=len(pieces), halo=halo),
        in_specs=[pl.BlockSpec(memory_space=pltpu.VMEM)] * len(pieces) + [pl.BlockSpec(memory_space=pl.ANY)] * len(after),
        out_specs=[pl.BlockSpec(memory_space=pltpu.VMEM)] * 2,
        out_shape=[out, out],
        scratch_shapes=[pltpu.VMEM((window + 2 * halo, count * lanes), jnp.bfloat16)],
        compiler_params=pltpu.CompilerParams(vmem_limit_bytes=16 * MIB),
        cost_estimate=pl.CostEstimate(flops=0, bytes_accessed=8 * out.size, transcendentals=0),
    )(*pieces, *after)


def time_kernel(segments_ref, pick_ref, taps_ref, spread_ref, frame_ref, *, history, frames, rows):
    chunk, timed = spread_ref.shape[0] // rows, spread_ref.shape[1] // rows
    nseg = pick_ref.shape[0]
    taps = taps_ref.shape[0]
    wide_out, wide_in = chunk * rows, timed * rows

    def count_one(t, totals):
        here = segments_ref[t]
        below = [total + (here < s).astype(jnp.int32) for s, total in enumerate(totals[0])]
        same = [total + (here == s).astype(jnp.int32) for s, total in enumerate(totals[1])]
        return tuple(below), tuple(same)

    zeros = tuple(jnp.int32(0) for _ in range(nseg))
    starts, counts = lax.fori_loop(0, frames, count_one, (zeros, zeros), unroll=8)
    for s in range(nseg):
        frame_ref[s] = starts[s] + lax.rem(pick_ref[s], counts[s])

    lag = history + lax.broadcasted_iota(jnp.int32, (chunk, timed), 0) - lax.broadcasted_iota(
        jnp.int32, (chunk, timed), 1
    )
    if history:
        first = lax.axis_index("chunk") * chunk - history
        real = first + lax.broadcasted_iota(jnp.int32, (chunk, timed), 1) >= 0
        lag = jnp.where(real, lag, -1)
    matrix = jnp.zeros((chunk, timed), jnp.float32)
    for k in range(taps):
        matrix = jnp.where(lag == k, taps_ref[k], matrix)
    repeat_left = (
        lax.broadcasted_iota(jnp.int32, (wide_out, chunk), 0) // rows
        == lax.broadcasted_iota(jnp.int32, (wide_out, chunk), 1)
    ).astype(jnp.bfloat16)
    repeat_right = (
        lax.broadcasted_iota(jnp.int32, (timed, wide_in), 1) // rows
        == lax.broadcasted_iota(jnp.int32, (timed, wide_in), 0)
    ).astype(jnp.bfloat16)
    tall = jnp.dot(repeat_left, matrix.astype(jnp.bfloat16), preferred_element_type=jnp.float32)
    tall = tall.astype(jnp.bfloat16)
    piece = min(128, wide_out)
    for start in range(0, wide_out, piece):
        part = jnp.dot(tall[start : start + piece], repeat_right, preferred_element_type=jnp.float32)
        same_row = (
            lax.broadcasted_iota(jnp.int32, (piece, wide_in), 0) % rows
            == lax.broadcasted_iota(jnp.int32, (piece, wide_in), 1) % rows
        )
        spread_ref[start : start + piece] = jnp.where(same_row, part, 0.0).astype(jnp.bfloat16)


def time_tables(segments, ref_pick, band_taps, rows, chunk, history):
    frames = segments.shape[0]
    wide_out, wide_in = chunk * rows, (history + chunk) * rows
    smem = pl.BlockSpec(memory_space=pltpu.SMEM)
    return pl.pallas_call(
        functools.partial(time_kernel, history=history, frames=frames, rows=rows),
        in_specs=[smem] * 3,
        out_specs=[pl.BlockSpec(memory_space=pltpu.VMEM), smem],
        out_shape=[
            jax.ShapeDtypeStruct((wide_out, wide_in), jnp.bfloat16),
            jax.ShapeDtypeStruct(ref_pick.shape, jnp.int32),
        ],
        compiler_params=pltpu.CompilerParams(vmem_limit_bytes=16 * MIB),
        cost_estimate=pl.CostEstimate(
            flops=2 * wide_out * wide_in * chunk, bytes_accessed=2 * wide_out * wide_in, transcendentals=0
        ),
    )(segments, ref_pick, band_taps.astype(jnp.float32))


def filter_frames(window_refs, left_ref, right_ref, stacked_ref, put):
    groups, deep, _ = right_ref.shape
    lanes = deep // (2 * SHARE)
    rows = left_ref.shape[0] // (2 * SHARE * groups)
    bands = rows // TILE
    pair = window_refs[0].shape[1] // lanes
    many = len(window_refs) * pair * TILE
    for n, window in enumerate(window_refs):
        stacked = jnp.dot(left_ref[...], window[...], preferred_element_type=jnp.float32).astype(jnp.bfloat16)
        for oz in range(2 * SHARE * groups):
            group, place = divmod(oz, 2 * SHARE)
            for band in range(bands):
                begin = oz * rows + band * TILE
                for f in range(pair):
                    row = band * many + (n * pair + f) * TILE
                    stacked_ref[group, row : row + TILE, place * lanes : (place + 1) * lanes] = stacked[
                        begin : begin + TILE, f * lanes : (f + 1) * lanes
                    ]
    block = pair * TILE
    total = bands * many
    step = min(512, total)
    for group in range(groups):
        for start in range(0, total, step):
            stop = min(start + step, total)
            coeff = jnp.dot(
                stacked_ref[group, start:stop], right_ref[group], preferred_element_type=jnp.float32
            ).astype(jnp.bfloat16)
            for place in range(start, stop, block):
                band, row = divmod(place, many)
                put(group, band, row // block, coeff[place - start : place - start + block])


def coeff_kernel(window_ref, left_ref, right_ref, coeff_ref, stacked_ref):
    chips = window_ref.shape[0]
    block = coeff_ref.shape[2] // chips

    def put(group, band, i, values):
        coeff_ref[group, band, i * block : (i + 1) * block] = values

    filter_frames([window_ref.at[chip] for chip in range(chips)], left_ref, right_ref, stacked_ref, put)


def own_coeffs(windows, left, right, rows, frames_here):
    groups, deep, wide = right.shape
    vmem = pl.BlockSpec(memory_space=pltpu.VMEM)
    many = windows.shape[0] * frames_here * TILE
    out = jax.ShapeDtypeStruct((groups, rows // TILE, many, wide), jnp.bfloat16)
    return pl.pallas_call(
        coeff_kernel,
        in_specs=[vmem] * 3,
        out_specs=vmem,
        out_shape=out,
        scratch_shapes=[pltpu.VMEM((groups, rows // TILE * many, deep), jnp.bfloat16)],
        compiler_params=pltpu.CompilerParams(vmem_limit_bytes=8 * out.size + 16 * MIB),
        cost_estimate=pl.CostEstimate(
            flops=4 * out.size * deep, bytes_accessed=2 * (windows.size + out.size), transcendentals=0
        ),
    )(windows, left, right)


def pixel_kernel(
    segments_ref, ref_frame_ref, spread_ref, other_ref, refer_ref, left_ref, right_ref, *refs, places, history, whole
):
    ready_refs, (out_ref, stacked_ref, coeff_ref, phase_ref, filtered_ref) = refs[:-5], refs[-5:]
    chips = other_ref.shape[0]
    groups, bands, _, wide = coeff_ref.shape
    half = wide // 2
    pair = other_ref.shape[2] // (right_ref.shape[1] // (2 * SHARE))
    block = pair * TILE
    chunk = out_ref.shape[0] * pair
    timed = history + chunk
    core = lax.axis_index("core")

    def place_of(exchanges, twin, n):
        chip = n if exchanges is None else lax.bitwise_xor(lax.axis_index("slab"), exchanges[n])
        return pl.ds(pl.multiple_of((chip * CORES + lax.rem(core + twin, CORES)) * block, block), block)

    for ready_ref, (exchanges, twin) in zip(ready_refs, places):
        for n in range(ready_ref.shape[2] // block):
            for group in range(groups):
                for band in range(bands):
                    coeff_ref[group, band, place_of(exchanges, twin, n)] = ready_ref[group, band, n * block : (n + 1) * block]

    def put(group, band, i, values):
        if i < chips:
            place = place_of(*places[-1], i)
        else:
            place = slice(timed * TILE + (i - chips) * block, timed * TILE + (i - chips + 1) * block)
        coeff_ref[group, band, place] = values

    windows = [other_ref.at[chip] for chip in range(chips)]
    if not whole:
        windows += [refer_ref.at[i] for i in range(refer_ref.shape[0])]
    filter_frames(windows, left_ref, right_ref, stacked_ref, put)

    def phase_one(slot, carry):
        place = pl.ds(pl.multiple_of(slot * TILE, TILE), TILE)
        if whole:
            source = ref_frame_ref[segments_ref[slot]]
        else:
            first = lax.axis_index("chunk") * chunk - history
            source = timed + segments_ref[jnp.maximum(first + slot, 0)]
        refer = pl.ds(pl.multiple_of(source * TILE, TILE), TILE)
        for group in range(groups):
            for band in range(bands):
                coeff_real = coeff_ref[group, band, place, 0:half].astype(jnp.float32)
                coeff_imag = coeff_ref[group, band, place, half:wide].astype(jnp.float32)
                ref_real = coeff_ref[group, band, refer, 0:half].astype(jnp.float32)
                ref_imag = coeff_ref[group, band, refer, half:wide].astype(jnp.float32)
                prod_real = coeff_real * ref_real + coeff_imag * ref_imag
                prod_imag = coeff_imag * ref_real - coeff_real * ref_imag
                square = prod_real * prod_real + prod_imag * prod_imag + 1.0
                phase = (prod_imag * lax.rsqrt(square)).astype(jnp.bfloat16)
                phase_ref[band, place, group * half : (group + 1) * half] = phase
        return carry

    lax.fori_loop(0, timed, phase_one, 0, unroll=2)

    piece = min(128, chunk * TILE)
    columns = half // SHARE
    left_half = lax.broadcasted_iota(jnp.int32, (TILE, half), 1) < columns
    step = min(256, chunk * TILE)
    for band in range(bands):
        for start in range(0, chunk * TILE, step):
            stop = start + step
            filtered_ref[start:stop] = jnp.dot(
                spread_ref[start:stop, : history * TILE + stop],
                phase_ref[band, : history * TILE + stop],
                preferred_element_type=jnp.float32,
            ).astype(jnp.bfloat16)
        for start in range(0, chunk * TILE, piece):
            here = slice(history * TILE + start, history * TILE + start + piece)
            filtered = filtered_ref[start : start + piece].astype(jnp.float32)
            above = jnp.zeros((piece, half), jnp.float32)
            below = jnp.zeros((piece, half), jnp.float32)
            for group in range(groups):
                coeff_real = coeff_ref[group, band, here, 0:half].astype(jnp.float32)
                coeff_imag = coeff_ref[group, band, here, half:wide].astype(jnp.float32)
                amplitude = coeff_real * coeff_real + coeff_imag * coeff_imag
                above = above + amplitude * filtered[:, group * half : (group + 1) * half]
                below = below + amplitude
            for i in range(piece // block):
                sums = []
                for value in (above, below):
                    one, two = value[i * block : i * block + TILE], value[i * block + TILE : (i + 1) * block]
                    sums.append(jnp.where(left_half, one, two) + pltpu.roll(jnp.where(left_half, two, one), columns, 1))
                both = (sums[0] / (sums[1] + 1.0)).astype(out_ref.dtype)
                out_ref[start // block + i, band * TILE : (band + 1) * TILE] = both


def pixel_motion(segments, ref_frames, spread, ready, other, refer, left, right, places, chunk, history):
    groups, bands, _, wide = ready[0].shape
    deep = right.shape[1]
    timed = history + chunk
    whole = refer is None
    slots = timed if whole else timed + NSEG
    pair = other.shape[2] // (deep // (2 * SHARE))
    fresh = other.shape[0] * pair + slots - timed
    smem = pl.BlockSpec(memory_space=pltpu.SMEM)
    vmem = pl.BlockSpec(memory_space=pltpu.VMEM)
    return pl.pallas_call(
        functools.partial(pixel_kernel, places=places, history=history, whole=whole),
        in_specs=[smem] * 2 + [vmem] * (5 + len(ready)),
        out_specs=vmem,
        out_shape=jax.ShapeDtypeStruct((chunk // pair, bands * TILE, wide // 2), jnp.bfloat16),
        scratch_shapes=[
            pltpu.VMEM((groups, bands * fresh * TILE, deep), jnp.bfloat16),
            pltpu.VMEM((groups, bands, slots * TILE, wide), jnp.bfloat16),
            pltpu.VMEM((bands, timed * TILE, groups * wide // 2), jnp.bfloat16),
            pltpu.VMEM((chunk * TILE, groups * wide // 2), jnp.bfloat16),
        ],
        compiler_params=pltpu.CompilerParams(vmem_limit_bytes=8 * groups * bands * slots * TILE * wide + 16 * MIB),
        cost_estimate=pl.CostEstimate(
            flops=2 * groups * bands * TILE * wide * (fresh * deep + chunk * timed * TILE // 2),
            bytes_accessed=2 * (other.size + sum(one.size for one in ready) + right.size),
            transcendentals=groups * bands * TILE * timed * wide // 2,
        ),
    )(segments, ref_frames, spread, other, other if whole else refer, left, right, *ready)


def join_kernel(tiles_ref, out_ref):
    count, quarter, _ = out_ref.shape
    devices, rows, lanes = tiles_ref.shape
    columns = lanes // count
    strips = quarter // columns
    left = lax.broadcasted_iota(jnp.int32, (rows, lanes), 1) < columns
    for strip in range(0, strips, 2):
        for i in range(devices // strips):
            one = tiles_ref[strip * devices // strips + i].astype(jnp.float32)
            two = tiles_ref[(strip + 1) * devices // strips + i].astype(jnp.float32)
            here = slice(strip * columns, (strip + 2) * columns)
            out_ref[0, i * rows : (i + 1) * rows, here] = jnp.where(left, one, pltpu.roll(two, columns, 1))
            out_ref[1, i * rows : (i + 1) * rows, here] = jnp.where(left, pltpu.roll(one, columns, 1), two)


def join_tiles(tiles, quarter):
    vmem = pl.BlockSpec(memory_space=pltpu.VMEM)
    return pl.pallas_call(
        join_kernel,
        in_specs=[vmem],
        out_specs=vmem,
        out_shape=jax.ShapeDtypeStruct((2, quarter, quarter), jnp.float32),
        compiler_params=pltpu.CompilerParams(vmem_limit_bytes=16 * MIB),
        cost_estimate=pl.CostEstimate(flops=tiles.size, bytes_accessed=6 * tiles.size, transcendentals=0),
    )(tiles)


def chunk_windows(mine, other, ref_frames, frames_here, history_chips, chips):
    mine = lax.all_gather(mine, "chunk", axis=0, tiled=True)
    other = lax.all_gather(other, "chunk", axis=0, tiled=True)
    height = mine.shape[1]
    core = lax.axis_index("core")
    device, f = ref_frames // frames_here, ref_frames % frames_here
    own = (device % CORES == core)[:, None, None]

    def pick(windows):
        return windows.reshape(windows.shape[0], height, frames_here, -1)[device // CORES, :, f]

    refer = jnp.where(own, pick(mine), pick(other))
    refer = refer.reshape(NSEG // frames_here, frames_here, height, -1)
    refer = jnp.swapaxes(refer, 1, 2).reshape(NSEG // frames_here, height, -1)

    def cut(windows):
        before = jnp.zeros((history_chips,) + windows.shape[1:], windows.dtype)
        windows = jnp.concatenate([before, windows])
        return lax.dynamic_slice_in_dim(windows, lax.axis_index("chunk") * chips, history_chips + chips)

    return cut(mine), cut(other), refer


def body(video_frames, segments, ref_pick, band_taps, *, chunks, slabs):
    frames_here, size, _ = video_frames.shape
    quarter = size // 4
    rows = quarter // (DOWN * CORES)
    columns = quarter * DOWN // slabs
    chunk = slabs * CORES * frames_here
    history = min(chunk * -(-(band_taps.shape[0] - 1) // chunk), segments.shape[0] - chunk)
    left = jnp.asarray(slab_left_table(rows, HALO, ORIENT))
    right = jnp.asarray(make_right_table(columns, HALO, ORIENT))
    order = exchange_order(slabs)

    def exchange(array, k):
        return lax.ppermute(array, "slab", [(chip, chip ^ k) for chip in range(slabs)]) if k else array

    def swap(array):
        return lax.ppermute(array, "core", [(0, 1), (1, 0)])

    windows = reduce_frames(video_frames, order, HALO)
    spread, ref_frames = time_tables(segments, ref_pick, band_taps, TILE, chunk, history)
    pieces = [exchange(window, k) for k, window in zip(order, windows)]
    if chunks > 1:
        mine, other = cut_windows(pieces, HALO, [])
        by_chip = jnp.asarray(np.argsort(order))[lax.axis_index("slab") ^ jnp.arange(slabs)]
        mine, other = mine[by_chip], swap(other)[by_chip]
        history_chips = history // (CORES * frames_here)
        mine, other, refer = chunk_windows(mine, other, ref_frames, frames_here, history_chips, slabs)
        ready = [own_coeffs(mine, left, right, rows, frames_here)]
        places = [(None, 0), (None, 1)]
    else:
        first = slabs // 2
        mine, other = cut_windows(pieces[:first], HALO, [spread])
        ready = [own_coeffs(one, left, right, rows, frames_here) for one in (mine, swap(other))]
        mine, other = cut_windows(pieces[first:], HALO, ready[:1])
        other, refer = swap(other), None
        ready.append(own_coeffs(mine, left, right, rows, frames_here))
        places = [(exchanges, twin) for exchanges in (order[:first], order[first:]) for twin in range(CORES)]
    motion = pixel_motion(segments, ref_frames, spread, ready, other, refer, left, right, places, chunk, history)
    motion = lax.all_to_all(motion, ("slab", "core"), split_axis=0, concat_axis=0, tiled=True)
    return join_tiles(motion, quarter)


def solution(mesh):
    chips = mesh.shape["frames"] // CORES
    slabs = min(chips, QUART * DOWN // (2 * HALO))
    chunks = chips // slabs
    names = ("groups", "chunk", "slab", "core")
    cut = jax.sharding.Mesh(mesh.devices.reshape(mesh.shape["groups"], chunks, slabs, CORES), names)
    in_specs = (P(names, None, None), P("groups"), P("groups"), P())
    return jax.shard_map(
        functools.partial(body, chunks=chunks, slabs=slabs),
        mesh=cut, in_specs=in_specs, out_specs=P(names, None, None), check_vma=False,
    )
```

```python
import functools
import math

import jax
import jax.numpy as jnp
import numpy as np
from jax import lax
from jax.experimental import pallas as pl
from jax.experimental.pallas import tpu as pltpu
from jax.sharding import PartitionSpec as P

IMG = 1024
ORIENT = 4
NSEG = 4
QUART = 256


blur_sigma = 2.0
gabor_sigma = 2.0
wave_number = math.pi / 2.0
gabor_gain = 2.0

HALO = 32
TILE = 16
DOWN = 2
SHARE = 2
CORES = 2
MIB = 1024 * 1024


def envelope_of(offset_grid):
    return np.float32(gabor_gain) * np.exp(
        -offset_grid * offset_grid / np.float32(2.0 * gabor_sigma * gabor_sigma)
    )


def waves(orient):
    angles = np.arange(orient, dtype=np.float32) * np.float32(math.pi / orient)
    wave_x = np.float32(wave_number) * np.cos(angles)
    wave_y = np.float32(wave_number) * np.sin(angles)
    return wave_x, wave_y


def slab_left_table(rows, halo, orient):
    offset = (
        np.arange(rows + 2 * halo, dtype=np.float32)[None, :]
        - np.float32(halo)
        - np.arange(rows, dtype=np.float32)[:, None]
    )
    wave_y = waves(orient)[1]
    phase = wave_y[:, None, None] * offset[None]
    envelope = envelope_of(offset)[None]
    table = np.stack([envelope * np.cos(phase), envelope * np.sin(phase)], axis=1)
    return table.reshape(orient * 2 * rows, rows + 2 * halo).astype(jnp.bfloat16)


def make_right_table(columns, halo, orient):
    window = columns + 2 * halo
    offset = (
        np.arange(window, dtype=np.float32)[:, None] - np.float32(halo) - np.arange(columns, dtype=np.float32)[None, :]
    )
    wave_x = waves(orient)[0]
    phase_x = wave_x[:, None, None] * offset[None]
    envelope = envelope_of(offset)[None]
    real_part = envelope * np.cos(phase_x)
    imag_part = envelope * np.sin(phase_x)
    table = np.zeros((orient // SHARE, SHARE, 2, window, 2, SHARE, columns), np.float32)
    for o in range(orient):
        group, i = divmod(o, SHARE)
        table[group, i, 0, :, 0, i] = real_part[o]
        table[group, i, 0, :, 1, i] = imag_part[o]
        table[group, i, 1, :, 0, i] = -imag_part[o]
        table[group, i, 1, :, 1, i] = real_part[o]
    return table.reshape(orient // SHARE, SHARE * 2 * window, 2 * SHARE * columns).astype(jnp.bfloat16)


def down_sums(full_size, quarter):
    position = np.arange(quarter, dtype=np.float32)[:, None]
    columns = np.arange(full_size, dtype=np.float32)[None, :]
    offset_grid = columns - np.float32(4.0) * position - np.float32(1.5)
    weight = np.exp(-offset_grid * offset_grid / np.float32(2.0 * blur_sigma * blur_sigma))
    return np.sum(weight, axis=1)


def down_block(position, column, shape, axis, sums):
    positions = position + lax.broadcasted_iota(jnp.int32, shape, 1 - axis)
    columns = column + lax.broadcasted_iota(jnp.int32, shape, axis)
    offset_grid = columns.astype(jnp.float32) - 4.0 * positions.astype(jnp.float32) - 1.5
    weight = jnp.exp(-offset_grid * offset_grid / (2.0 * blur_sigma * blur_sigma))
    inner = float(sums[len(sums) // 2])
    line = position + lax.broadcasted_iota(jnp.int32, tuple(1 if i == axis else n for i, n in enumerate(shape)), 1 - axis)
    scale = jnp.full(line.shape, 1.0 / inner, jnp.float32)
    for q in range(position, min(position + shape[1 - axis], len(sums))):
        if abs(float(sums[q]) - inner) > 1e-7 * inner:
            scale = jnp.where(line == q, 1.0 / float(sums[q]), scale)
    return (weight * scale).astype(jnp.bfloat16)


def build_down(table_ref, axis):
    size, quarter = table_ref.shape[axis], table_ref.shape[1 - axis]
    sums = down_sums(size, quarter)
    table_ref[...] = jnp.zeros_like(table_ref)
    tall, wide = (128, 32)[axis], min(128, table_ref.shape[1])
    for row in range(0, table_ref.shape[0], tall):
        for lane in range(0, table_ref.shape[1], wide):
            position, column = (row, lane) if axis else (lane, row)
            positions, columns = (tall, wide) if axis else (wide, tall)
            if 4 * (position + positions - 1) + 30 >= column and 4 * position - 27 <= column + columns - 1:
                block = down_block(position, column, (tall, wide), axis, sums)
                table_ref[row : row + tall, lane : lane + wide] = block


def reduce_kernel(frames_ref, *refs, order, halo, block):
    out_refs = refs[: len(order)]
    picture_ref, down_t_ref, down_ref, half_ref, total_ref, strip_ref, sems = refs[len(order) :]
    count, size, _ = picture_ref.shape
    quarter = down_ref.shape[0]
    strips, _, lanes = strip_ref.shape
    columns = lanes - 2 * halo
    window = out_refs[0].shape[1]

    copies = []
    for f in range(count):
        for i in range(size // block):
            here = pl.ds(i * block, block)
            copies.append(pltpu.make_async_copy(frames_ref.at[f, here], picture_ref.at[f, here], sems.at[f, i]))
    copies[0].start()
    build_down(down_t_ref, 0)
    copies[1].start()

    me = lax.axis_index("slab")
    reach = quarter
    for f in range(count):
        total_ref[...] = jnp.zeros_like(total_ref)
        for i in range(size // block):
            turn = f * (size // block) + i
            copies[turn].wait()
            if turn + 2 < len(copies):
                copies[turn + 2].start()
            half_ref[...] = jnp.dot(
                picture_ref[f, i * block : (i + 1) * block], down_t_ref[...], preferred_element_type=jnp.float32
            ).astype(jnp.bfloat16)
            if f == i == 0:
                build_down(down_ref, 1)
            for row in range(0, block, reach):
                begin = i * block + row
                near = slice(max(begin // 4 - TILE, 0), min((begin + reach) // 4 + TILE, quarter))
                total_ref[near] += jnp.dot(
                    down_ref[near, begin : begin + reach], half_ref[row : row + reach], preferred_element_type=jnp.float32
                )
        for strip in range(strips):
            begin = strip * columns - halo
            moved = pltpu.roll(total_ref[...], (-begin) % quarter, 1)[:, 0:lanes]
            column = begin + lax.broadcasted_iota(jnp.int32, (quarter, lanes), 1)
            inside = (column >= 0) & (column < quarter)
            strip_ref[strip] = jnp.where(inside, moved, 0.0).astype(jnp.bfloat16)
        for k, out_ref in zip(order, out_refs):
            slab = lax.bitwise_xor(me, k)
            begin = pl.multiple_of(lax.rem(slab, DOWN) * (quarter - window), TILE)
            out_ref[f] = strip_ref[slab // DOWN, pl.ds(begin, window)]


def reduce_frames(video_frames, order, halo):
    count, size, _ = video_frames.shape
    quarter = size // 4
    strips = len(order) // DOWN
    lanes = quarter // strips + 2 * halo
    block = size // 2
    out = jax.ShapeDtypeStruct((count, quarter // DOWN + halo, lanes), jnp.bfloat16)
    return pl.pallas_call(
        functools.partial(reduce_kernel, order=order, halo=halo, block=block),
        in_specs=[pl.BlockSpec(memory_space=pltpu.HBM)],
        out_specs=[pl.BlockSpec(memory_space=pltpu.VMEM)] * len(order),
        out_shape=[out] * len(order),
        scratch_shapes=[
            pltpu.VMEM((count, size, size), jnp.bfloat16),
            pltpu.VMEM((size, quarter), jnp.bfloat16),
            pltpu.VMEM((quarter, size), jnp.bfloat16),
            pltpu.VMEM((block, quarter), jnp.bfloat16),
            pltpu.VMEM((quarter, quarter), jnp.float32),
            pltpu.VMEM((strips, quarter, lanes), jnp.bfloat16),
            pltpu.SemaphoreType.DMA((count, size // block)),
        ],
        compiler_params=pltpu.CompilerParams(vmem_limit_bytes=52 * MIB),
        cost_estimate=pl.CostEstimate(
            flops=2 * count * size * quarter * (size + quarter),
            bytes_accessed=2 * count * size * size,
            transcendentals=0,
        ),
    )(video_frames)


def exchange_order(slabs):
    far = sorted(range(slabs // 2, slabs), key=lambda k: k % 2)
    near = list(range(2, slabs // 2))
    turns = [k for pair in zip(far, near) for k in pair]
    return [0] + turns + far[len(near) :] + [k for k in (1,) if k < slabs // 2]


def cut_kernel(*refs, many, halo):
    in_refs, (mine_ref, other_ref), padded_ref = refs[:many], refs[-3:-1], refs[-1]
    count, window, lanes = in_refs[0].shape
    height = mine_ref.shape[1]
    rows = height - 2 * halo
    me, core = lax.axis_index("slab"), lax.axis_index("core")
    edge = jnp.zeros((halo, count * lanes), jnp.bfloat16)
    padded_ref[0:halo] = edge
    padded_ref[halo + window :] = edge
    above = lax.rem(me, DOWN) * halo
    for n, in_ref in enumerate(in_refs):
        for f in range(count):
            padded_ref[halo : halo + window, f * lanes : (f + 1) * lanes] = in_ref[f]
        for out_ref, number in ((mine_ref, core), (other_ref, 1 - core)):
            out_ref[n] = padded_ref[pl.ds(pl.multiple_of(above + number * rows, TILE), height)]


def cut_windows(pieces, halo, after):
    count, window, lanes = pieces[0].shape
    height = (window - halo) // CORES + 2 * halo
    out = jax.ShapeDtypeStruct((len(pieces), height, count * lanes), jnp.bfloat16)
    return pl.pallas_call(
        functools.partial(cut_kernel, many=len(pieces), halo=halo),
        in_specs=[pl.BlockSpec(memory_space=pltpu.VMEM)] * len(pieces) + [pl.BlockSpec(memory_space=pl.ANY)] * len(after),
        out_specs=[pl.BlockSpec(memory_space=pltpu.VMEM)] * 2,
        out_shape=[out, out],
        scratch_shapes=[pltpu.VMEM((window + 2 * halo, count * lanes), jnp.bfloat16)],
        compiler_params=pltpu.CompilerParams(vmem_limit_bytes=16 * MIB),
        cost_estimate=pl.CostEstimate(flops=0, bytes_accessed=8 * out.size, transcendentals=0),
    )(*pieces, *after)


def time_kernel(segments_ref, pick_ref, taps_ref, spread_ref, frame_ref, *, history, frames, rows):
    chunk, timed = spread_ref.shape[0] // rows, spread_ref.shape[1] // rows
    nseg = pick_ref.shape[0]
    taps = taps_ref.shape[0]
    wide_out, wide_in = chunk * rows, timed * rows

    def count_one(t, totals):
        here = segments_ref[t]
        below = [total + (here < s).astype(jnp.int32) for s, total in enumerate(totals[0])]
        same = [total + (here == s).astype(jnp.int32) for s, total in enumerate(totals[1])]
        return tuple(below), tuple(same)

    zeros = tuple(jnp.int32(0) for _ in range(nseg))
    starts, counts = lax.fori_loop(0, frames, count_one, (zeros, zeros), unroll=8)
    for s in range(nseg):
        frame_ref[s] = starts[s] + lax.rem(pick_ref[s], counts[s])

    lag = history + lax.broadcasted_iota(jnp.int32, (chunk, timed), 0) - lax.broadcasted_iota(
        jnp.int32, (chunk, timed), 1
    )
    if history:
        first = lax.axis_index("chunk") * chunk - history
        real = first + lax.broadcasted_iota(jnp.int32, (chunk, timed), 1) >= 0
        lag = jnp.where(real, lag, -1)
    matrix = jnp.zeros((chunk, timed), jnp.float32)
    for k in range(taps):
        matrix = jnp.where(lag == k, taps_ref[k], matrix)
    repeat_left = (
        lax.broadcasted_iota(jnp.int32, (wide_out, chunk), 0) // rows
        == lax.broadcasted_iota(jnp.int32, (wide_out, chunk), 1)
    ).astype(jnp.bfloat16)
    repeat_right = (
        lax.broadcasted_iota(jnp.int32, (timed, wide_in), 1) // rows
        == lax.broadcasted_iota(jnp.int32, (timed, wide_in), 0)
    ).astype(jnp.bfloat16)
    tall = jnp.dot(repeat_left, matrix.astype(jnp.bfloat16), preferred_element_type=jnp.float32)
    tall = tall.astype(jnp.bfloat16)
    piece = min(128, wide_out)
    for start in range(0, wide_out, piece):
        part = jnp.dot(tall[start : start + piece], repeat_right, preferred_element_type=jnp.float32)
        same_row = (
            lax.broadcasted_iota(jnp.int32, (piece, wide_in), 0) % rows
            == lax.broadcasted_iota(jnp.int32, (piece, wide_in), 1) % rows
        )
        spread_ref[start : start + piece] = jnp.where(same_row, part, 0.0).astype(jnp.bfloat16)


def time_tables(segments, ref_pick, band_taps, rows, chunk, history):
    frames = segments.shape[0]
    wide_out, wide_in = chunk * rows, (history + chunk) * rows
    smem = pl.BlockSpec(memory_space=pltpu.SMEM)
    return pl.pallas_call(
        functools.partial(time_kernel, history=history, frames=frames, rows=rows),
        in_specs=[smem] * 3,
        out_specs=[pl.BlockSpec(memory_space=pltpu.VMEM), smem],
        out_shape=[
            jax.ShapeDtypeStruct((wide_out, wide_in), jnp.bfloat16),
            jax.ShapeDtypeStruct(ref_pick.shape, jnp.int32),
        ],
        compiler_params=pltpu.CompilerParams(vmem_limit_bytes=16 * MIB),
        cost_estimate=pl.CostEstimate(
            flops=2 * wide_out * wide_in * chunk, bytes_accessed=2 * wide_out * wide_in, transcendentals=0
        ),
    )(segments, ref_pick, band_taps.astype(jnp.float32))


def filter_frames(window_refs, left_ref, right_ref, stacked_ref, put):
    groups, deep, _ = right_ref.shape
    lanes = deep // (2 * SHARE)
    rows = left_ref.shape[0] // (2 * SHARE * groups)
    bands = rows // TILE
    pair = window_refs[0].shape[1] // lanes
    many = len(window_refs) * pair * TILE
    for n, window in enumerate(window_refs):
        stacked = jnp.dot(left_ref[...], window[...], preferred_element_type=jnp.float32).astype(jnp.bfloat16)
        for oz in range(2 * SHARE * groups):
            group, place = divmod(oz, 2 * SHARE)
            for band in range(bands):
                begin = oz * rows + band * TILE
                for f in range(pair):
                    row = band * many + (n * pair + f) * TILE
                    stacked_ref[group, row : row + TILE, place * lanes : (place + 1) * lanes] = stacked[
                        begin : begin + TILE, f * lanes : (f + 1) * lanes
                    ]
    block = pair * TILE
    total = bands * many
    step = min(512, total)
    for group in range(groups):
        for start in range(0, total, step):
            stop = min(start + step, total)
            coeff = jnp.dot(
                stacked_ref[group, start:stop], right_ref[group], preferred_element_type=jnp.float32
            ).astype(jnp.bfloat16)
            for place in range(start, stop, block):
                band, row = divmod(place, many)
                put(group, band, row // block, coeff[place - start : place - start + block])


def coeff_kernel(window_ref, left_ref, right_ref, coeff_ref, stacked_ref):
    chips = window_ref.shape[0]
    block = coeff_ref.shape[2] // chips

    def put(group, band, i, values):
        coeff_ref[group, band, i * block : (i + 1) * block] = values

    filter_frames([window_ref.at[chip] for chip in range(chips)], left_ref, right_ref, stacked_ref, put)


def own_coeffs(windows, left, right, rows, frames_here):
    groups, deep, wide = right.shape
    vmem = pl.BlockSpec(memory_space=pltpu.VMEM)
    many = windows.shape[0] * frames_here * TILE
    out = jax.ShapeDtypeStruct((groups, rows // TILE, many, wide), jnp.bfloat16)
    return pl.pallas_call(
        coeff_kernel,
        in_specs=[vmem] * 3,
        out_specs=vmem,
        out_shape=out,
        scratch_shapes=[pltpu.VMEM((groups, rows // TILE * many, deep), jnp.bfloat16)],
        compiler_params=pltpu.CompilerParams(vmem_limit_bytes=8 * out.size + 16 * MIB),
        cost_estimate=pl.CostEstimate(
            flops=4 * out.size * deep, bytes_accessed=2 * (windows.size + out.size), transcendentals=0
        ),
    )(windows, left, right)


def pixel_kernel(
    segments_ref, ref_frame_ref, spread_ref, other_ref, refer_ref, left_ref, right_ref, *refs, places, history, whole
):
    ready_refs, (out_ref, stacked_ref, coeff_ref, phase_ref, filtered_ref) = refs[:-5], refs[-5:]
    chips = other_ref.shape[0]
    groups, bands, _, wide = coeff_ref.shape
    half = wide // 2
    pair = other_ref.shape[2] // (right_ref.shape[1] // (2 * SHARE))
    block = pair * TILE
    chunk = out_ref.shape[0] * pair
    timed = history + chunk
    core = lax.axis_index("core")

    def place_of(exchanges, twin, n):
        chip = n if exchanges is None else lax.bitwise_xor(lax.axis_index("slab"), exchanges[n])
        return pl.ds(pl.multiple_of((chip * CORES + lax.rem(core + twin, CORES)) * block, block), block)

    for ready_ref, (exchanges, twin) in zip(ready_refs, places):
        for n in range(ready_ref.shape[2] // block):
            for group in range(groups):
                for band in range(bands):
                    coeff_ref[group, band, place_of(exchanges, twin, n)] = ready_ref[group, band, n * block : (n + 1) * block]

    def put(group, band, i, values):
        if i < chips:
            place = place_of(*places[-1], i)
        else:
            place = slice(timed * TILE + (i - chips) * block, timed * TILE + (i - chips + 1) * block)
        coeff_ref[group, band, place] = values

    windows = [other_ref.at[chip] for chip in range(chips)]
    if not whole:
        windows += [refer_ref.at[i] for i in range(refer_ref.shape[0])]
    filter_frames(windows, left_ref, right_ref, stacked_ref, put)

    if whole:
        sources = [ref_frame_ref[segments_ref[slot]] for slot in range(timed)]
    else:
        first = lax.axis_index("chunk") * chunk - history
        sources = [timed + segments_ref[jnp.maximum(first + slot, 0)] for slot in range(timed)]
    piece = min(128, chunk * TILE)
    step = min(256, chunk * TILE)
    columns = half // SHARE
    left_half = lax.broadcasted_iota(jnp.int32, (TILE, half), 1) < columns
    for band in range(bands):
        for slot, source in enumerate(sources):
            place = slice(slot * TILE, (slot + 1) * TILE)
            refer = pl.ds(pl.multiple_of(source * TILE, TILE), TILE)
            for group in range(groups):
                coeff_real = coeff_ref[group, band, place, 0:half].astype(jnp.float32)
                coeff_imag = coeff_ref[group, band, place, half:wide].astype(jnp.float32)
                ref_real = coeff_ref[group, band, refer, 0:half].astype(jnp.float32)
                ref_imag = coeff_ref[group, band, refer, half:wide].astype(jnp.float32)
                prod_real = coeff_real * ref_real + coeff_imag * ref_imag
                prod_imag = coeff_imag * ref_real - coeff_real * ref_imag
                square = prod_real * prod_real + prod_imag * prod_imag + 1.0
                phase = (prod_imag * lax.rsqrt(square)).astype(jnp.bfloat16)
                phase_ref[band, place, group * half : (group + 1) * half] = phase

        for start in range(0, chunk * TILE, step):
            stop = start + step
            filtered_ref[band, start:stop] = jnp.dot(
                spread_ref[start:stop, : history * TILE + stop],
                phase_ref[band, : history * TILE + stop],
                preferred_element_type=jnp.float32,
            ).astype(jnp.bfloat16)
        for start in range(0, chunk * TILE, piece):
            here = slice(history * TILE + start, history * TILE + start + piece)
            filtered = filtered_ref[band, start : start + piece].astype(jnp.float32)
            above = jnp.zeros((piece, half), jnp.float32)
            below = jnp.zeros((piece, half), jnp.float32)
            for group in range(groups):
                coeff_real = coeff_ref[group, band, here, 0:half].astype(jnp.float32)
                coeff_imag = coeff_ref[group, band, here, half:wide].astype(jnp.float32)
                amplitude = coeff_real * coeff_real + coeff_imag * coeff_imag
                above = above + amplitude * filtered[:, group * half : (group + 1) * half]
                below = below + amplitude
            for i in range(piece // block):
                sums = []
                for value in (above, below):
                    one, two = value[i * block : i * block + TILE], value[i * block + TILE : (i + 1) * block]
                    sums.append(jnp.where(left_half, one, two) + pltpu.roll(jnp.where(left_half, two, one), columns, 1))
                both = (sums[0] / (sums[1] + 1.0)).astype(out_ref.dtype)
                out_ref[start // block + i, band * TILE : (band + 1) * TILE] = both


def pixel_motion(segments, ref_frames, spread, ready, other, refer, left, right, places, chunk, history):
    groups, bands, _, wide = ready[0].shape
    deep = right.shape[1]
    timed = history + chunk
    whole = refer is None
    slots = timed if whole else timed + NSEG
    pair = other.shape[2] // (deep // (2 * SHARE))
    fresh = other.shape[0] * pair + slots - timed
    smem = pl.BlockSpec(memory_space=pltpu.SMEM)
    vmem = pl.BlockSpec(memory_space=pltpu.VMEM)
    return pl.pallas_call(
        functools.partial(pixel_kernel, places=places, history=history, whole=whole),
        in_specs=[smem] * 2 + [vmem] * (5 + len(ready)),
        out_specs=vmem,
        out_shape=jax.ShapeDtypeStruct((chunk // pair, bands * TILE, wide // 2), jnp.bfloat16),
        scratch_shapes=[
            pltpu.VMEM((groups, bands * fresh * TILE, deep), jnp.bfloat16),
            pltpu.VMEM((groups, bands, slots * TILE, wide), jnp.bfloat16),
            pltpu.VMEM((bands, timed * TILE, groups * wide // 2), jnp.bfloat16),
            pltpu.VMEM((bands, chunk * TILE, groups * wide // 2), jnp.bfloat16),
        ],
        compiler_params=pltpu.CompilerParams(vmem_limit_bytes=8 * groups * bands * slots * TILE * wide + 16 * MIB),
        cost_estimate=pl.CostEstimate(
            flops=2 * groups * bands * TILE * wide * (fresh * deep + chunk * timed * TILE // 2),
            bytes_accessed=2 * (other.size + sum(one.size for one in ready) + right.size),
            transcendentals=groups * bands * TILE * timed * wide // 2,
        ),
    )(segments, ref_frames, spread, other, other if whole else refer, left, right, *ready)


def join_kernel(tiles_ref, out_ref):
    count, quarter, _ = out_ref.shape
    devices, rows, lanes = tiles_ref.shape
    columns = lanes // count
    strips = quarter // columns
    left = lax.broadcasted_iota(jnp.int32, (rows, lanes), 1) < columns
    for strip in range(0, strips, 2):
        for i in range(devices // strips):
            one = tiles_ref[strip * devices // strips + i].astype(jnp.float32)
            two = tiles_ref[(strip + 1) * devices // strips + i].astype(jnp.float32)
            here = slice(strip * columns, (strip + 2) * columns)
            out_ref[0, i * rows : (i + 1) * rows, here] = jnp.where(left, one, pltpu.roll(two, columns, 1))
            out_ref[1, i * rows : (i + 1) * rows, here] = jnp.where(left, pltpu.roll(one, columns, 1), two)


def join_tiles(tiles, quarter):
    vmem = pl.BlockSpec(memory_space=pltpu.VMEM)
    return pl.pallas_call(
        join_kernel,
        in_specs=[vmem],
        out_specs=vmem,
        out_shape=jax.ShapeDtypeStruct((2, quarter, quarter), jnp.float32),
        compiler_params=pltpu.CompilerParams(vmem_limit_bytes=16 * MIB),
        cost_estimate=pl.CostEstimate(flops=tiles.size, bytes_accessed=6 * tiles.size, transcendentals=0),
    )(tiles)


def chunk_windows(mine, other, ref_frames, frames_here, history_chips, chips):
    mine = lax.all_gather(mine, "chunk", axis=0, tiled=True)
    other = lax.all_gather(other, "chunk", axis=0, tiled=True)
    height = mine.shape[1]
    core = lax.axis_index("core")
    device, f = ref_frames // frames_here, ref_frames % frames_here
    own = (device % CORES == core)[:, None, None]

    def pick(windows):
        return windows.reshape(windows.shape[0], height, frames_here, -1)[device // CORES, :, f]

    refer = jnp.where(own, pick(mine), pick(other))
    refer = refer.reshape(NSEG // frames_here, frames_here, height, -1)
    refer = jnp.swapaxes(refer, 1, 2).reshape(NSEG // frames_here, height, -1)

    def cut(windows):
        before = jnp.zeros((history_chips,) + windows.shape[1:], windows.dtype)
        windows = jnp.concatenate([before, windows])
        return lax.dynamic_slice_in_dim(windows, lax.axis_index("chunk") * chips, history_chips + chips)

    return cut(mine), cut(other), refer


def body(video_frames, segments, ref_pick, band_taps, *, chunks, slabs):
    frames_here, size, _ = video_frames.shape
    quarter = size // 4
    rows = quarter // (DOWN * CORES)
    columns = quarter * DOWN // slabs
    chunk = slabs * CORES * frames_here
    history = min(chunk * -(-(band_taps.shape[0] - 1) // chunk), segments.shape[0] - chunk)
    left = jnp.asarray(slab_left_table(rows, HALO, ORIENT))
    right = jnp.asarray(make_right_table(columns, HALO, ORIENT))
    order = exchange_order(slabs)

    def exchange(array, k):
        return lax.ppermute(array, "slab", [(chip, chip ^ k) for chip in range(slabs)]) if k else array

    def swap(array):
        return lax.ppermute(array, "core", [(0, 1), (1, 0)])

    windows = reduce_frames(video_frames, order, HALO)
    spread, ref_frames = time_tables(segments, ref_pick, band_taps, TILE, chunk, history)
    pieces = [exchange(window, k) for k, window in zip(order, windows)]
    if chunks > 1:
        mine, other = cut_windows(pieces, HALO, [])
        by_chip = jnp.asarray(np.argsort(order))[lax.axis_index("slab") ^ jnp.arange(slabs)]
        mine, other = mine[by_chip], swap(other)[by_chip]
        history_chips = history // (CORES * frames_here)
        mine, other, refer = chunk_windows(mine, other, ref_frames, frames_here, history_chips, slabs)
        ready = [own_coeffs(mine, left, right, rows, frames_here)]
        places = [(None, 0), (None, 1)]
    else:
        first = slabs // 2
        mine, other = cut_windows(pieces[:first], HALO, [spread])
        ready = [own_coeffs(one, left, right, rows, frames_here) for one in (mine, swap(other))]
        mine, other = cut_windows(pieces[first:], HALO, ready[:1])
        other, refer = swap(other), None
        ready.append(own_coeffs(mine, left, right, rows, frames_here))
        places = [(exchanges, twin) for exchanges in (order[:first], order[first:]) for twin in range(CORES)]
    motion = pixel_motion(segments, ref_frames, spread, ready, other, refer, left, right, places, chunk, history)
    motion = lax.all_to_all(motion, ("slab", "core"), split_axis=0, concat_axis=0, tiled=True)
    return join_tiles(motion, quarter)


def solution(mesh):
    chips = mesh.shape["frames"] // CORES
    slabs = min(chips, QUART * DOWN // (2 * HALO))
    chunks = chips // slabs
    names = ("groups", "chunk", "slab", "core")
    cut = jax.sharding.Mesh(mesh.devices.reshape(mesh.shape["groups"], chunks, slabs, CORES), names)
    in_specs = (P(names, None, None), P("groups"), P("groups"), P())
    return jax.shard_map(
        functools.partial(body, chunks=chunks, slabs=slabs),
        mesh=cut, in_specs=in_specs, out_specs=P(names, None, None), check_vma=False,
    )
```

```python
import functools
import math

import jax
import jax.numpy as jnp
import numpy as np
from jax import lax
from jax.experimental import pallas as pl
from jax.experimental.pallas import tpu as pltpu
from jax.sharding import PartitionSpec as P

IMG = 1024
ORIENT = 4
NSEG = 4
QUART = 256


blur_sigma = 2.0
gabor_sigma = 2.0
wave_number = math.pi / 2.0
gabor_gain = 2.0

HALO = 32
TILE = 16
DOWN = 2
SHARE = 2
CORES = 2
MIB = 1024 * 1024


def envelope_of(offset_grid):
    return np.float32(gabor_gain) * np.exp(
        -offset_grid * offset_grid / np.float32(2.0 * gabor_sigma * gabor_sigma)
    )


def waves(orient):
    angles = np.arange(orient, dtype=np.float32) * np.float32(math.pi / orient)
    wave_x = np.float32(wave_number) * np.cos(angles)
    wave_y = np.float32(wave_number) * np.sin(angles)
    return wave_x, wave_y


def slab_left_table(rows, halo, orient):
    offset = (
        np.arange(rows + 2 * halo, dtype=np.float32)[None, :]
        - np.float32(halo)
        - np.arange(rows, dtype=np.float32)[:, None]
    )
    wave_y = waves(orient)[1]
    phase = wave_y[:, None, None] * offset[None]
    envelope = envelope_of(offset)[None]
    table = np.stack([envelope * np.cos(phase), envelope * np.sin(phase)], axis=1)
    return table.reshape(orient * 2 * rows, rows + 2 * halo).astype(jnp.bfloat16)


def make_right_table(columns, halo, orient):
    window = columns + 2 * halo
    offset = (
        np.arange(window, dtype=np.float32)[:, None] - np.float32(halo) - np.arange(columns, dtype=np.float32)[None, :]
    )
    wave_x = waves(orient)[0]
    phase_x = wave_x[:, None, None] * offset[None]
    envelope = envelope_of(offset)[None]
    real_part = envelope * np.cos(phase_x)
    imag_part = envelope * np.sin(phase_x)
    table = np.zeros((orient // SHARE, SHARE, 2, window, 2, SHARE, columns), np.float32)
    for o in range(orient):
        group, i = divmod(o, SHARE)
        table[group, i, 0, :, 0, i] = real_part[o]
        table[group, i, 0, :, 1, i] = imag_part[o]
        table[group, i, 1, :, 0, i] = -imag_part[o]
        table[group, i, 1, :, 1, i] = real_part[o]
    return table.reshape(orient // SHARE, SHARE * 2 * window, 2 * SHARE * columns).astype(jnp.bfloat16)


def down_sums(full_size, quarter):
    position = np.arange(quarter, dtype=np.float32)[:, None]
    columns = np.arange(full_size, dtype=np.float32)[None, :]
    offset_grid = columns - np.float32(4.0) * position - np.float32(1.5)
    weight = np.exp(-offset_grid * offset_grid / np.float32(2.0 * blur_sigma * blur_sigma))
    return np.sum(weight, axis=1)


def down_block(position, column, shape, axis, sums):
    positions = position + lax.broadcasted_iota(jnp.int32, shape, 1 - axis)
    columns = column + lax.broadcasted_iota(jnp.int32, shape, axis)
    offset_grid = columns.astype(jnp.float32) - 4.0 * positions.astype(jnp.float32) - 1.5
    weight = jnp.exp(-offset_grid * offset_grid / (2.0 * blur_sigma * blur_sigma))
    inner = float(sums[len(sums) // 2])
    line = position + lax.broadcasted_iota(jnp.int32, tuple(1 if i == axis else n for i, n in enumerate(shape)), 1 - axis)
    scale = jnp.full(line.shape, 1.0 / inner, jnp.float32)
    for q in range(position, min(position + shape[1 - axis], len(sums))):
        if abs(float(sums[q]) - inner) > 1e-7 * inner:
            scale = jnp.where(line == q, 1.0 / float(sums[q]), scale)
    return (weight * scale).astype(jnp.bfloat16)


def build_down(table_ref, axis):
    size, quarter = table_ref.shape[axis], table_ref.shape[1 - axis]
    sums = down_sums(size, quarter)
    table_ref[...] = jnp.zeros_like(table_ref)
    tall, wide = (128, 32)[axis], min(128, table_ref.shape[1])
    for row in range(0, table_ref.shape[0], tall):
        for lane in range(0, table_ref.shape[1], wide):
            position, column = (row, lane) if axis else (lane, row)
            positions, columns = (tall, wide) if axis else (wide, tall)
            if 4 * (position + positions - 1) + 30 >= column and 4 * position - 27 <= column + columns - 1:
                block = down_block(position, column, (tall, wide), axis, sums)
                table_ref[row : row + tall, lane : lane + wide] = block


def reduce_kernel(frames_ref, *refs, far, near, halo, block):
    out_refs = refs[: len(far + near)]
    picture_ref, down_t_ref, down_ref, half_ref, total_ref, strip_ref, sems = refs[len(far + near) :]
    count, size, _ = picture_ref.shape
    quarter = down_ref.shape[0]
    strips, _, lanes = strip_ref.shape
    columns = lanes - 2 * halo
    window = out_refs[-1].shape[1]

    copies = []
    for f in range(count):
        for i in range(size // block):
            here = pl.ds(i * block, block)
            copy = pltpu.make_async_copy(frames_ref.at[f, here], picture_ref.at[f, here], sems.at[f, i])
            copy.start()
            copies.append(copy)
    build_down(down_t_ref, 0)

    me = lax.axis_index("slab")
    reach = quarter
    for f in range(count):
        total_ref[...] = jnp.zeros_like(total_ref)
        for i in range(size // block):
            copies[f * (size // block) + i].wait()
            half_ref[...] = jnp.dot(
                picture_ref[f, i * block : (i + 1) * block], down_t_ref[...], preferred_element_type=jnp.float32
            ).astype(jnp.bfloat16)
            if f == i == 0:
                build_down(down_ref, 1)
            for row in range(0, block, reach):
                begin = i * block + row
                touched = slice(max(begin // 4 - TILE, 0), min((begin + reach) // 4 + TILE, quarter))
                total_ref[touched] += jnp.dot(
                    down_ref[touched, begin : begin + reach], half_ref[row : row + reach], preferred_element_type=jnp.float32
                )
        for strip in range(strips):
            begin = strip * columns - halo
            moved = pltpu.roll(total_ref[...], (-begin) % quarter, 1)[:, 0:lanes]
            column = begin + lax.broadcasted_iota(jnp.int32, (quarter, lanes), 1)
            inside = (column >= 0) & (column < quarter)
            strip_ref[strip] = jnp.where(inside, moved, 0.0).astype(jnp.bfloat16)
        for k, out_ref in zip(far + near, out_refs):
            slab = lax.bitwise_xor(me, k)
            if k in far:
                out_ref[f] = strip_ref[slab // DOWN]
            else:
                begin = pl.multiple_of(lax.rem(slab, DOWN) * (quarter - window), TILE)
                out_ref[f] = strip_ref[slab // DOWN, pl.ds(begin, window)]


def reduce_frames(video_frames, far, near, slabs, halo):
    count, size, _ = video_frames.shape
    quarter = size // 4
    strips = slabs // DOWN
    lanes = quarter // strips + 2 * halo
    block = size // 2
    out = [jax.ShapeDtypeStruct((count, quarter, lanes), jnp.bfloat16)] * len(far)
    out += [jax.ShapeDtypeStruct((count, quarter // DOWN + halo, lanes), jnp.bfloat16)] * len(near)
    return pl.pallas_call(
        functools.partial(reduce_kernel, far=far, near=near, halo=halo, block=block),
        in_specs=[pl.BlockSpec(memory_space=pltpu.HBM)],
        out_specs=[pl.BlockSpec(memory_space=pltpu.VMEM)] * len(out),
        out_shape=out,
        scratch_shapes=[
            pltpu.VMEM((count, size, size), jnp.bfloat16),
            pltpu.VMEM((size, quarter), jnp.bfloat16),
            pltpu.VMEM((quarter, size), jnp.bfloat16),
            pltpu.VMEM((block, quarter), jnp.bfloat16),
            pltpu.VMEM((quarter, quarter), jnp.float32),
            pltpu.VMEM((strips, quarter, lanes), jnp.bfloat16),
            pltpu.SemaphoreType.DMA((count, size // block)),
        ],
        compiler_params=pltpu.CompilerParams(vmem_limit_bytes=52 * MIB),
        cost_estimate=pl.CostEstimate(
            flops=2 * count * size * quarter * (size + quarter),
            bytes_accessed=2 * count * size * size,
            transcendentals=0,
        ),
    )(video_frames)


def pass_kernel(strip_ref, own_ref, next_ref):
    count, window, _ = own_ref.shape
    down = lax.rem(lax.axis_index("slab"), DOWN)
    spare = strip_ref.shape[1] - window
    for f in range(count):
        own_ref[f] = strip_ref[f, pl.ds(pl.multiple_of(down * spare, TILE), window)]
        next_ref[f] = strip_ref[f, pl.ds(pl.multiple_of((1 - down) * spare, TILE), window)]


def pass_on(strip, halo):
    count, quarter, lanes = strip.shape
    vmem = pl.BlockSpec(memory_space=pltpu.VMEM)
    out = jax.ShapeDtypeStruct((count, quarter // DOWN + halo, lanes), jnp.bfloat16)
    return pl.pallas_call(
        pass_kernel,
        in_specs=[vmem],
        out_specs=[vmem] * 2,
        out_shape=[out] * 2,
        compiler_params=pltpu.CompilerParams(vmem_limit_bytes=16 * MIB),
        cost_estimate=pl.CostEstimate(flops=0, bytes_accessed=8 * out.size, transcendentals=0),
    )(strip)


def cut_kernel(*refs, many, halo):
    in_refs, (mine_ref, other_ref), padded_ref = refs[:many], refs[-3:-1], refs[-1]
    count, window, lanes = in_refs[0].shape
    height = mine_ref.shape[1]
    rows = height - 2 * halo
    me, core = lax.axis_index("slab"), lax.axis_index("core")
    edge = jnp.zeros((halo, count * lanes), jnp.bfloat16)
    padded_ref[0:halo] = edge
    padded_ref[halo + window :] = edge
    above = lax.rem(me, DOWN) * halo
    for n, in_ref in enumerate(in_refs):
        for f in range(count):
            padded_ref[halo : halo + window, f * lanes : (f + 1) * lanes] = in_ref[f]
        for out_ref, number in ((mine_ref, core), (other_ref, 1 - core)):
            out_ref[n] = padded_ref[pl.ds(pl.multiple_of(above + number * rows, TILE), height)]


def cut_windows(pieces, halo, after):
    count, window, lanes = pieces[0].shape
    height = (window - halo) // CORES + 2 * halo
    out = jax.ShapeDtypeStruct((len(pieces), height, count * lanes), jnp.bfloat16)
    return pl.pallas_call(
        functools.partial(cut_kernel, many=len(pieces), halo=halo),
        in_specs=[pl.BlockSpec(memory_space=pltpu.VMEM)] * len(pieces) + [pl.BlockSpec(memory_space=pl.ANY)] * len(after),
        out_specs=[pl.BlockSpec(memory_space=pltpu.VMEM)] * 2,
        out_shape=[out, out],
        scratch_shapes=[pltpu.VMEM((window + 2 * halo, count * lanes), jnp.bfloat16)],
        compiler_params=pltpu.CompilerParams(vmem_limit_bytes=16 * MIB),
        cost_estimate=pl.CostEstimate(flops=0, bytes_accessed=8 * out.size, transcendentals=0),
    )(*pieces, *after)


def time_kernel(segments_ref, pick_ref, taps_ref, spread_ref, frame_ref, *, history, frames, rows):
    chunk, timed = spread_ref.shape[0] // rows, spread_ref.shape[1] // rows
    nseg = pick_ref.shape[0]
    taps = taps_ref.shape[0]
    wide_out, wide_in = chunk * rows, timed * rows

    def count_one(t, totals):
        here = segments_ref[t]
        below = [total + (here < s).astype(jnp.int32) for s, total in enumerate(totals[0])]
        same = [total + (here == s).astype(jnp.int32) for s, total in enumerate(totals[1])]
        return tuple(below), tuple(same)

    zeros = tuple(jnp.int32(0) for _ in range(nseg))
    starts, counts = lax.fori_loop(0, frames, count_one, (zeros, zeros), unroll=8)
    for s in range(nseg):
        frame_ref[s] = starts[s] + lax.rem(pick_ref[s], counts[s])

    lag = history + lax.broadcasted_iota(jnp.int32, (chunk, timed), 0) - lax.broadcasted_iota(
        jnp.int32, (chunk, timed), 1
    )
    if history:
        first = lax.axis_index("chunk") * chunk - history
        real = first + lax.broadcasted_iota(jnp.int32, (chunk, timed), 1) >= 0
        lag = jnp.where(real, lag, -1)
    matrix = jnp.zeros((chunk, timed), jnp.float32)
    for k in range(taps):
        matrix = jnp.where(lag == k, taps_ref[k], matrix)
    repeat_left = (
        lax.broadcasted_iota(jnp.int32, (wide_out, chunk), 0) // rows
        == lax.broadcasted_iota(jnp.int32, (wide_out, chunk), 1)
    ).astype(jnp.bfloat16)
    repeat_right = (
        lax.broadcasted_iota(jnp.int32, (timed, wide_in), 1) // rows
        == lax.broadcasted_iota(jnp.int32, (timed, wide_in), 0)
    ).astype(jnp.bfloat16)
    tall = jnp.dot(repeat_left, matrix.astype(jnp.bfloat16), preferred_element_type=jnp.float32)
    tall = tall.astype(jnp.bfloat16)
    piece = min(128, wide_out)
    for start in range(0, wide_out, piece):
        part = jnp.dot(tall[start : start + piece], repeat_right, preferred_element_type=jnp.float32)
        same_row = (
            lax.broadcasted_iota(jnp.int32, (piece, wide_in), 0) % rows
            == lax.broadcasted_iota(jnp.int32, (piece, wide_in), 1) % rows
        )
        spread_ref[start : start + piece] = jnp.where(same_row, part, 0.0).astype(jnp.bfloat16)


def time_tables(segments, ref_pick, band_taps, rows, chunk, history):
    frames = segments.shape[0]
    wide_out, wide_in = chunk * rows, (history + chunk) * rows
    smem = pl.BlockSpec(memory_space=pltpu.SMEM)
    return pl.pallas_call(
        functools.partial(time_kernel, history=history, frames=frames, rows=rows),
        in_specs=[smem] * 3,
        out_specs=[pl.BlockSpec(memory_space=pltpu.VMEM), smem],
        out_shape=[
            jax.ShapeDtypeStruct((wide_out, wide_in), jnp.bfloat16),
            jax.ShapeDtypeStruct(ref_pick.shape, jnp.int32),
        ],
        compiler_params=pltpu.CompilerParams(vmem_limit_bytes=16 * MIB),
        cost_estimate=pl.CostEstimate(
            flops=2 * wide_out * wide_in * chunk, bytes_accessed=2 * wide_out * wide_in, transcendentals=0
        ),
    )(segments, ref_pick, band_taps.astype(jnp.float32))


def filter_frames(window_refs, left_ref, right_ref, stacked_ref, put):
    groups, deep, _ = right_ref.shape
    lanes = deep // (2 * SHARE)
    rows = left_ref.shape[0] // (2 * SHARE * groups)
    bands = rows // TILE
    pair = window_refs[0].shape[1] // lanes
    many = len(window_refs) * pair * TILE
    for n, window in enumerate(window_refs):
        stacked = jnp.dot(left_ref[...], window[...], preferred_element_type=jnp.float32).astype(jnp.bfloat16)
        for oz in range(2 * SHARE * groups):
            group, place = divmod(oz, 2 * SHARE)
            for band in range(bands):
                begin = oz * rows + band * TILE
                for f in range(pair):
                    row = band * many + (n * pair + f) * TILE
                    stacked_ref[group, row : row + TILE, place * lanes : (place + 1) * lanes] = stacked[
                        begin : begin + TILE, f * lanes : (f + 1) * lanes
                    ]
    block = pair * TILE
    total = bands * many
    step = min(512, total)
    for group in range(groups):
        for start in range(0, total, step):
            stop = min(start + step, total)
            coeff = jnp.dot(
                stacked_ref[group, start:stop], right_ref[group], preferred_element_type=jnp.float32
            ).astype(jnp.bfloat16)
            for place in range(start, stop, block):
                band, row = divmod(place, many)
                put(group, band, row // block, coeff[place - start : place - start + block])


def coeff_kernel(window_ref, left_ref, right_ref, coeff_ref, stacked_ref):
    chips = window_ref.shape[0]
    block = coeff_ref.shape[2] // chips

    def put(group, band, i, values):
        coeff_ref[group, band, i * block : (i + 1) * block] = values

    filter_frames([window_ref.at[chip] for chip in range(chips)], left_ref, right_ref, stacked_ref, put)


def own_coeffs(windows, left, right, rows, frames_here):
    groups, deep, wide = right.shape
    vmem = pl.BlockSpec(memory_space=pltpu.VMEM)
    many = windows.shape[0] * frames_here * TILE
    out = jax.ShapeDtypeStruct((groups, rows // TILE, many, wide), jnp.bfloat16)
    return pl.pallas_call(
        coeff_kernel,
        in_specs=[vmem] * 3,
        out_specs=vmem,
        out_shape=out,
        scratch_shapes=[pltpu.VMEM((groups, rows // TILE * many, deep), jnp.bfloat16)],
        compiler_params=pltpu.CompilerParams(vmem_limit_bytes=8 * out.size + 16 * MIB),
        cost_estimate=pl.CostEstimate(
            flops=4 * out.size * deep, bytes_accessed=2 * (windows.size + out.size), transcendentals=0
        ),
    )(windows, left, right)


def pixel_kernel(
    segments_ref, ref_frame_ref, spread_ref, other_ref, refer_ref, left_ref, right_ref, *refs, places, history, whole
):
    ready_refs, (out_ref, stacked_ref, coeff_ref, phase_ref, filtered_ref) = refs[:-5], refs[-5:]
    chips = other_ref.shape[0]
    groups, bands, _, wide = coeff_ref.shape
    half = wide // 2
    pair = other_ref.shape[2] // (right_ref.shape[1] // (2 * SHARE))
    block = pair * TILE
    chunk = out_ref.shape[0] * pair
    timed = history + chunk
    core = lax.axis_index("core")

    def place_of(exchanges, twin, n):
        chip = n if exchanges is None else lax.bitwise_xor(lax.axis_index("slab"), exchanges[n])
        return pl.ds(pl.multiple_of((chip * CORES + lax.rem(core + twin, CORES)) * block, block), block)

    for ready_ref, (exchanges, twin) in zip(ready_refs, places):
        for n in range(ready_ref.shape[2] // block):
            for group in range(groups):
                for band in range(bands):
                    coeff_ref[group, band, place_of(exchanges, twin, n)] = ready_ref[group, band, n * block : (n + 1) * block]

    def put(group, band, i, values):
        if i < chips:
            place = place_of(*places[-1], i)
        else:
            place = slice(timed * TILE + (i - chips) * block, timed * TILE + (i - chips + 1) * block)
        coeff_ref[group, band, place] = values

    windows = [other_ref.at[chip] for chip in range(chips)]
    if not whole:
        windows += [refer_ref.at[i] for i in range(refer_ref.shape[0])]
    filter_frames(windows, left_ref, right_ref, stacked_ref, put)

    def phase_one(slot, carry):
        place = pl.ds(pl.multiple_of(slot * TILE, TILE), TILE)
        if whole:
            source = ref_frame_ref[segments_ref[slot]]
        else:
            first = lax.axis_index("chunk") * chunk - history
            source = timed + segments_ref[jnp.maximum(first + slot, 0)]
        refer = pl.ds(pl.multiple_of(source * TILE, TILE), TILE)
        for group in range(groups):
            for band in range(bands):
                coeff_real = coeff_ref[group, band, place, 0:half].astype(jnp.float32)
                coeff_imag = coeff_ref[group, band, place, half:wide].astype(jnp.float32)
                ref_real = coeff_ref[group, band, refer, 0:half].astype(jnp.float32)
                ref_imag = coeff_ref[group, band, refer, half:wide].astype(jnp.float32)
                prod_real = coeff_real * ref_real + coeff_imag * ref_imag
                prod_imag = coeff_imag * ref_real - coeff_real * ref_imag
                square = prod_real * prod_real + prod_imag * prod_imag + 1.0
                phase = (prod_imag * lax.rsqrt(square)).astype(jnp.bfloat16)
                phase_ref[band, place, group * half : (group + 1) * half] = phase
        return carry

    lax.fori_loop(0, timed, phase_one, 0, unroll=2)

    piece = min(128, chunk * TILE)
    columns = half // SHARE
    left_half = lax.broadcasted_iota(jnp.int32, (TILE, half), 1) < columns
    step = min(256, chunk * TILE)
    for band in range(bands):
        for start in range(0, chunk * TILE, step):
            stop = start + step
            filtered_ref[start:stop] = jnp.dot(
                spread_ref[start:stop, : history * TILE + stop],
                phase_ref[band, : history * TILE + stop],
                preferred_element_type=jnp.float32,
            ).astype(jnp.bfloat16)
        for start in range(0, chunk * TILE, piece):
            here = slice(history * TILE + start, history * TILE + start + piece)
            filtered = filtered_ref[start : start + piece].astype(jnp.float32)
            above = jnp.zeros((piece, half), jnp.float32)
            below = jnp.zeros((piece, half), jnp.float32)
            for group in range(groups):
                coeff_real = coeff_ref[group, band, here, 0:half].astype(jnp.float32)
                coeff_imag = coeff_ref[group, band, here, half:wide].astype(jnp.float32)
                amplitude = coeff_real * coeff_real + coeff_imag * coeff_imag
                above = above + amplitude * filtered[:, group * half : (group + 1) * half]
                below = below + amplitude
            for i in range(piece // block):
                sums = []
                for value in (above, below):
                    one, two = value[i * block : i * block + TILE], value[i * block + TILE : (i + 1) * block]
                    sums.append(jnp.where(left_half, one, two) + pltpu.roll(jnp.where(left_half, two, one), columns, 1))
                both = (sums[0] / (sums[1] + 1.0)).astype(out_ref.dtype)
                out_ref[start // block + i, band * TILE : (band + 1) * TILE] = both


def pixel_motion(segments, ref_frames, spread, ready, other, refer, left, right, places, chunk, history):
    groups, bands, _, wide = ready[0].shape
    deep = right.shape[1]
    timed = history + chunk
    whole = refer is None
    slots = timed if whole else timed + NSEG
    pair = other.shape[2] // (deep // (2 * SHARE))
    fresh = other.shape[0] * pair + slots - timed
    smem = pl.BlockSpec(memory_space=pltpu.SMEM)
    vmem = pl.BlockSpec(memory_space=pltpu.VMEM)
    return pl.pallas_call(
        functools.partial(pixel_kernel, places=places, history=history, whole=whole),
        in_specs=[smem] * 2 + [vmem] * (5 + len(ready)),
        out_specs=vmem,
        out_shape=jax.ShapeDtypeStruct((chunk // pair, bands * TILE, wide // 2), jnp.bfloat16),
        scratch_shapes=[
            pltpu.VMEM((groups, bands * fresh * TILE, deep), jnp.bfloat16),
            pltpu.VMEM((groups, bands, slots * TILE, wide), jnp.bfloat16),
            pltpu.VMEM((bands, timed * TILE, groups * wide // 2), jnp.bfloat16),
            pltpu.VMEM((chunk * TILE, groups * wide // 2), jnp.bfloat16),
        ],
        compiler_params=pltpu.CompilerParams(vmem_limit_bytes=8 * groups * bands * slots * TILE * wide + 16 * MIB),
        cost_estimate=pl.CostEstimate(
            flops=2 * groups * bands * TILE * wide * (fresh * deep + chunk * timed * TILE // 2),
            bytes_accessed=2 * (other.size + sum(one.size for one in ready) + right.size),
            transcendentals=groups * bands * TILE * timed * wide // 2,
        ),
    )(segments, ref_frames, spread, other, other if whole else refer, left, right, *ready)


def join_kernel(tiles_ref, out_ref):
    count, quarter, _ = out_ref.shape
    devices, rows, lanes = tiles_ref.shape
    columns = lanes // count
    strips = quarter // columns
    left = lax.broadcasted_iota(jnp.int32, (rows, lanes), 1) < columns
    for strip in range(0, strips, 2):
        for i in range(devices // strips):
            one = tiles_ref[strip * devices // strips + i].astype(jnp.float32)
            two = tiles_ref[(strip + 1) * devices // strips + i].astype(jnp.float32)
            here = slice(strip * columns, (strip + 2) * columns)
            out_ref[0, i * rows : (i + 1) * rows, here] = jnp.where(left, one, pltpu.roll(two, columns, 1))
            out_ref[1, i * rows : (i + 1) * rows, here] = jnp.where(left, pltpu.roll(one, columns, 1), two)


def join_tiles(tiles, quarter):
    vmem = pl.BlockSpec(memory_space=pltpu.VMEM)
    return pl.pallas_call(
        join_kernel,
        in_specs=[vmem],
        out_specs=vmem,
        out_shape=jax.ShapeDtypeStruct((2, quarter, quarter), jnp.float32),
        compiler_params=pltpu.CompilerParams(vmem_limit_bytes=16 * MIB),
        cost_estimate=pl.CostEstimate(flops=tiles.size, bytes_accessed=6 * tiles.size, transcendentals=0),
    )(tiles)


def chunk_windows(mine, other, ref_frames, frames_here, history_chips, chips):
    mine = lax.all_gather(mine, "chunk", axis=0, tiled=True)
    other = lax.all_gather(other, "chunk", axis=0, tiled=True)
    height = mine.shape[1]
    core = lax.axis_index("core")
    device, f = ref_frames // frames_here, ref_frames % frames_here
    own = (device % CORES == core)[:, None, None]

    def pick(windows):
        return windows.reshape(windows.shape[0], height, frames_here, -1)[device // CORES, :, f]

    refer = jnp.where(own, pick(mine), pick(other))
    refer = refer.reshape(NSEG // frames_here, frames_here, height, -1)
    refer = jnp.swapaxes(refer, 1, 2).reshape(NSEG // frames_here, height, -1)

    def cut(windows):
        before = jnp.zeros((history_chips,) + windows.shape[1:], windows.dtype)
        windows = jnp.concatenate([before, windows])
        return lax.dynamic_slice_in_dim(windows, lax.axis_index("chunk") * chips, history_chips + chips)

    return cut(mine), cut(other), refer


def body(video_frames, segments, ref_pick, band_taps, *, chunks, slabs):
    frames_here, size, _ = video_frames.shape
    quarter = size // 4
    rows = quarter // (DOWN * CORES)
    columns = quarter * DOWN // slabs
    chunk = slabs * CORES * frames_here
    history = min(chunk * -(-(band_taps.shape[0] - 1) // chunk), segments.shape[0] - chunk)
    left = jnp.asarray(slab_left_table(rows, HALO, ORIENT))
    right = jnp.asarray(make_right_table(columns, HALO, ORIENT))
    half = slabs // 2
    far, near = list(range(half, slabs, DOWN)), list(range(2, half)) + [1, 0]

    def exchange(array, k):
        return lax.ppermute(array, "slab", [(chip, chip ^ k) for chip in range(slabs)]) if k else array

    def swap(array):
        return lax.ppermute(array, "core", [(0, 1), (1, 0)])

    windows = reduce_frames(video_frames, far, near, slabs, HALO)
    spread, ref_frames = time_tables(segments, ref_pick, band_taps, TILE, chunk, history)
    strips = [exchange(strip, k) for k, strip in zip(far, windows)]
    windows, spread = lax.optimization_barrier((windows[len(far) :], spread))
    pieces = [exchange(window, k) for k, window in zip(near, windows)]
    for strip in strips:
        own, following = pass_on(strip, HALO)
        pieces += [own, exchange(following, 1)]
    order = near + [k + i for k in far for i in range(DOWN)]
    if chunks > 1:
        mine, other = cut_windows(pieces, HALO, [])
        by_chip = jnp.asarray(np.argsort(order))[lax.axis_index("slab") ^ jnp.arange(slabs)]
        mine, other = mine[by_chip], swap(other)[by_chip]
        history_chips = history // (CORES * frames_here)
        mine, other, refer = chunk_windows(mine, other, ref_frames, frames_here, history_chips, slabs)
        ready = [own_coeffs(mine, left, right, rows, frames_here)]
        places = [(None, 0), (None, 1)]
    else:
        first = len(near)
        mine, other = cut_windows(pieces[:first], HALO, [spread])
        ready = [own_coeffs(one, left, right, rows, frames_here) for one in (mine, swap(other))]
        mine, other = cut_windows(pieces[first:], HALO, ready[:1])
        other, refer = swap(other), None
        ready.append(own_coeffs(mine, left, right, rows, frames_here))
        places = [(exchanges, twin) for exchanges in (order[:first], order[first:]) for twin in range(CORES)]
    motion = pixel_motion(segments, ref_frames, spread, ready, other, refer, left, right, places, chunk, history)
    motion = lax.all_to_all(motion, ("slab", "core"), split_axis=0, concat_axis=0, tiled=True)
    return join_tiles(motion, quarter)


def solution(mesh):
    chips = mesh.shape["frames"] // CORES
    slabs = min(chips, QUART * DOWN // (2 * HALO))
    chunks = chips // slabs
    names = ("groups", "chunk", "slab", "core")
    cut = jax.sharding.Mesh(mesh.devices.reshape(mesh.shape["groups"], chunks, slabs, CORES), names)
    in_specs = (P(names, None, None), P("groups"), P("groups"), P())
    return jax.shard_map(
        functools.partial(body, chunks=chunks, slabs=slabs),
        mesh=cut, in_specs=in_specs, out_specs=P(names, None, None), check_vma=False,
    )
```

```python
import functools
import math

import jax
import jax.numpy as jnp
import numpy as np
from jax import lax
from jax.experimental import pallas as pl
from jax.experimental.pallas import tpu as pltpu
from jax.sharding import PartitionSpec as P

IMG = 1024
ORIENT = 4
NSEG = 4
QUART = 256


blur_sigma = 2.0
gabor_sigma = 2.0
wave_number = math.pi / 2.0
gabor_gain = 2.0

HALO = 32
TILE = 16
DOWN = 2
SHARE = 2
CORES = 2
MIB = 1024 * 1024


def envelope_of(offset_grid):
    return np.float32(gabor_gain) * np.exp(
        -offset_grid * offset_grid / np.float32(2.0 * gabor_sigma * gabor_sigma)
    )


def waves(orient):
    angles = np.arange(orient, dtype=np.float32) * np.float32(math.pi / orient)
    wave_x = np.float32(wave_number) * np.cos(angles)
    wave_y = np.float32(wave_number) * np.sin(angles)
    return wave_x, wave_y


def slab_left_table(rows, halo, orient):
    offset = (
        np.arange(rows + 2 * halo, dtype=np.float32)[None, :]
        - np.float32(halo)
        - np.arange(rows, dtype=np.float32)[:, None]
    )
    wave_y = waves(orient)[1]
    phase = wave_y[:, None, None] * offset[None]
    envelope = envelope_of(offset)[None]
    table = np.stack([envelope * np.cos(phase), envelope * np.sin(phase)], axis=1)
    return table.reshape(orient * 2 * rows, rows + 2 * halo).astype(jnp.bfloat16)


def make_right_table(columns, halo, orient):
    window = columns + 2 * halo
    offset = (
        np.arange(window, dtype=np.float32)[:, None] - np.float32(halo) - np.arange(columns, dtype=np.float32)[None, :]
    )
    wave_x = waves(orient)[0]
    phase_x = wave_x[:, None, None] * offset[None]
    envelope = envelope_of(offset)[None]
    real_part = envelope * np.cos(phase_x)
    imag_part = envelope * np.sin(phase_x)
    table = np.zeros((orient // SHARE, SHARE, 2, window, 2, SHARE, columns), np.float32)
    for o in range(orient):
        group, i = divmod(o, SHARE)
        table[group, i, 0, :, 0, i] = real_part[o]
        table[group, i, 0, :, 1, i] = imag_part[o]
        table[group, i, 1, :, 0, i] = -imag_part[o]
        table[group, i, 1, :, 1, i] = real_part[o]
    return table.reshape(orient // SHARE, SHARE * 2 * window, 2 * SHARE * columns).astype(jnp.bfloat16)


def down_sums(full_size, quarter):
    position = np.arange(quarter, dtype=np.float32)[:, None]
    columns = np.arange(full_size, dtype=np.float32)[None, :]
    offset_grid = columns - np.float32(4.0) * position - np.float32(1.5)
    weight = np.exp(-offset_grid * offset_grid / np.float32(2.0 * blur_sigma * blur_sigma))
    return np.sum(weight, axis=1)


def down_block(position, column, shape, axis, sums):
    positions = position + lax.broadcasted_iota(jnp.int32, shape, 1 - axis)
    columns = column + lax.broadcasted_iota(jnp.int32, shape, axis)
    offset_grid = columns.astype(jnp.float32) - 4.0 * positions.astype(jnp.float32) - 1.5
    weight = jnp.exp(-offset_grid * offset_grid / (2.0 * blur_sigma * blur_sigma))
    inner = float(sums[len(sums) // 2])
    line = position + lax.broadcasted_iota(jnp.int32, tuple(1 if i == axis else n for i, n in enumerate(shape)), 1 - axis)
    scale = jnp.full(line.shape, 1.0 / inner, jnp.float32)
    for q in range(position, min(position + shape[1 - axis], len(sums))):
        if abs(float(sums[q]) - inner) > 1e-7 * inner:
            scale = jnp.where(line == q, 1.0 / float(sums[q]), scale)
    return (weight * scale).astype(jnp.bfloat16)


def build_down(table_ref, axis):
    size, quarter = table_ref.shape[axis], table_ref.shape[1 - axis]
    sums = down_sums(size, quarter)
    table_ref[...] = jnp.zeros_like(table_ref)
    tall, wide = (128, 32)[axis], min(128, table_ref.shape[1])
    for row in range(0, table_ref.shape[0], tall):
        for lane in range(0, table_ref.shape[1], wide):
            position, column = (row, lane) if axis else (lane, row)
            positions, columns = (tall, wide) if axis else (wide, tall)
            if 4 * (position + positions - 1) + 30 >= column and 4 * position - 27 <= column + columns - 1:
                block = down_block(position, column, (tall, wide), axis, sums)
                table_ref[row : row + tall, lane : lane + wide] = block


def reduce_kernel(frames_ref, *refs, order, halo, block):
    out_refs = refs[: len(order)]
    picture_ref, down_t_ref, down_ref, half_ref, total_ref, strip_ref, sems = refs[len(order) :]
    count, size, _ = picture_ref.shape
    quarter = down_ref.shape[0]
    _, strips, _, lanes = strip_ref.shape
    columns = lanes - 2 * halo
    window = out_refs[0].shape[1]

    copies = []
    for f in range(count):
        for i in range(size // block):
            here = pl.ds(i * block, block)
            copy = pltpu.make_async_copy(frames_ref.at[f, here], picture_ref.at[f, here], sems.at[f, i])
            copy.start()
            copies.append(copy)
    build_down(down_t_ref, 0)

    me = lax.axis_index("slab")
    reach = quarter
    blocks = size // block
    copies[0].wait()
    for f in range(count):
        total_ref[f] = jnp.zeros(total_ref.shape[1:], jnp.float32)
        for i in range(blocks):
            half_ref[i] = jnp.dot(
                picture_ref[f, i * block : (i + 1) * block], down_t_ref[...], preferred_element_type=jnp.float32
            ).astype(jnp.bfloat16)
            if f == i == 0:
                build_down(down_ref, 1)
            for row in range(0, block, reach):
                begin = i * block + row
                near = slice(max(begin // 4 - TILE, 0), min((begin + reach) // 4 + TILE, quarter))
                total_ref[f, near] += jnp.dot(
                    down_ref[near, begin : begin + reach], half_ref[i, row : row + reach], preferred_element_type=jnp.float32
                )
            if f * blocks + i + 1 < len(copies):
                copies[f * blocks + i + 1].wait()
        for strip in range(strips):
            begin = strip * columns - halo
            moved = pltpu.roll(total_ref[f], (-begin) % quarter, 1)[:, 0:lanes]
            column = begin + lax.broadcasted_iota(jnp.int32, (quarter, lanes), 1)
            inside = (column >= 0) & (column < quarter)
            strip_ref[f, strip] = jnp.where(inside, moved, 0.0).astype(jnp.bfloat16)
        for k, out_ref in zip(order, out_refs):
            slab = lax.bitwise_xor(me, k)
            begin = pl.multiple_of(lax.rem(slab, DOWN) * (quarter - window), TILE)
            out_ref[f] = strip_ref[f, slab // DOWN, pl.ds(begin, window)]


def reduce_frames(video_frames, order, halo):
    count, size, _ = video_frames.shape
    quarter = size // 4
    strips = len(order) // DOWN
    lanes = quarter // strips + 2 * halo
    block = size // 2
    out = jax.ShapeDtypeStruct((count, quarter // DOWN + halo, lanes), jnp.bfloat16)
    return pl.pallas_call(
        functools.partial(reduce_kernel, order=order, halo=halo, block=block),
        in_specs=[pl.BlockSpec(memory_space=pltpu.HBM)],
        out_specs=[pl.BlockSpec(memory_space=pltpu.VMEM)] * len(order),
        out_shape=[out] * len(order),
        scratch_shapes=[
            pltpu.VMEM((count, size, size), jnp.bfloat16),
            pltpu.VMEM((size, quarter), jnp.bfloat16),
            pltpu.VMEM((quarter, size), jnp.bfloat16),
            pltpu.VMEM((size // block, block, quarter), jnp.bfloat16),
            pltpu.VMEM((count, quarter, quarter), jnp.float32),
            pltpu.VMEM((count, strips, quarter, lanes), jnp.bfloat16),
            pltpu.SemaphoreType.DMA((count, size // block)),
        ],
        compiler_params=pltpu.CompilerParams(vmem_limit_bytes=52 * MIB),
        cost_estimate=pl.CostEstimate(
            flops=2 * count * size * quarter * (size + quarter),
            bytes_accessed=2 * count * size * size,
            transcendentals=0,
        ),
    )(video_frames)


def exchange_order(slabs):
    far = sorted(range(slabs // 2, slabs), key=lambda k: k % 2)
    near = list(range(2, slabs // 2))
    turns = [k for pair in zip(far, near) for k in pair]
    return [0] + turns + far[len(near) :] + [k for k in (1,) if k < slabs // 2]


def cut_kernel(*refs, many, halo):
    in_refs, (mine_ref, other_ref), padded_ref = refs[:many], refs[-3:-1], refs[-1]
    count, window, lanes = in_refs[0].shape
    height = mine_ref.shape[1]
    rows = height - 2 * halo
    me, core = lax.axis_index("slab"), lax.axis_index("core")
    edge = jnp.zeros((halo, count * lanes), jnp.bfloat16)
    padded_ref[0:halo] = edge
    padded_ref[halo + window :] = edge
    above = lax.rem(me, DOWN) * halo
    for n, in_ref in enumerate(in_refs):
        for f in range(count):
            padded_ref[halo : halo + window, f * lanes : (f + 1) * lanes] = in_ref[f]
        for out_ref, number in ((mine_ref, core), (other_ref, 1 - core)):
            out_ref[n] = padded_ref[pl.ds(pl.multiple_of(above + number * rows, TILE), height)]


def cut_windows(pieces, halo, after):
    count, window, lanes = pieces[0].shape
    height = (window - halo) // CORES + 2 * halo
    out = jax.ShapeDtypeStruct((len(pieces), height, count * lanes), jnp.bfloat16)
    return pl.pallas_call(
        functools.partial(cut_kernel, many=len(pieces), halo=halo),
        in_specs=[pl.BlockSpec(memory_space=pltpu.VMEM)] * len(pieces) + [pl.BlockSpec(memory_space=pl.ANY)] * len(after),
        out_specs=[pl.BlockSpec(memory_space=pltpu.VMEM)] * 2,
        out_shape=[out, out],
        scratch_shapes=[pltpu.VMEM((window + 2 * halo, count * lanes), jnp.bfloat16)],
        compiler_params=pltpu.CompilerParams(vmem_limit_bytes=16 * MIB),
        cost_estimate=pl.CostEstimate(flops=0, bytes_accessed=8 * out.size, transcendentals=0),
    )(*pieces, *after)


def time_kernel(segments_ref, pick_ref, taps_ref, spread_ref, frame_ref, source_ref, *, history, frames, rows):
    chunk, timed = spread_ref.shape[0] // rows, spread_ref.shape[1] // rows
    nseg = pick_ref.shape[0]
    taps = taps_ref.shape[0]
    wide_out, wide_in = chunk * rows, timed * rows

    def count_one(t, totals):
        here = segments_ref[t]
        below = [total + (here < s).astype(jnp.int32) for s, total in enumerate(totals[0])]
        same = [total + (here == s).astype(jnp.int32) for s, total in enumerate(totals[1])]
        return tuple(below), tuple(same)

    zeros = tuple(jnp.int32(0) for _ in range(nseg))
    starts, counts = lax.fori_loop(0, frames, count_one, (zeros, zeros), unroll=8)
    for s in range(nseg):
        frame_ref[s] = starts[s] + lax.rem(pick_ref[s], counts[s])

    def source_one(slot, carry):
        if timed == frames:
            source_ref[slot] = frame_ref[segments_ref[slot]]
        else:
            before = lax.axis_index("chunk") * chunk - history
            source_ref[slot] = timed + segments_ref[jnp.maximum(before + slot, 0)]
        return carry

    lax.fori_loop(0, timed, source_one, 0)

    lag = history + lax.broadcasted_iota(jnp.int32, (chunk, timed), 0) - lax.broadcasted_iota(
        jnp.int32, (chunk, timed), 1
    )
    if history:
        first = lax.axis_index("chunk") * chunk - history
        real = first + lax.broadcasted_iota(jnp.int32, (chunk, timed), 1) >= 0
        lag = jnp.where(real, lag, -1)
    matrix = jnp.zeros((chunk, timed), jnp.float32)
    for k in range(taps):
        matrix = jnp.where(lag == k, taps_ref[k], matrix)
    repeat_left = (
        lax.broadcasted_iota(jnp.int32, (wide_out, chunk), 0) // rows
        == lax.broadcasted_iota(jnp.int32, (wide_out, chunk), 1)
    ).astype(jnp.bfloat16)
    repeat_right = (
        lax.broadcasted_iota(jnp.int32, (timed, wide_in), 1) // rows
        == lax.broadcasted_iota(jnp.int32, (timed, wide_in), 0)
    ).astype(jnp.bfloat16)
    tall = jnp.dot(repeat_left, matrix.astype(jnp.bfloat16), preferred_element_type=jnp.float32)
    tall = tall.astype(jnp.bfloat16)
    piece = min(128, wide_out)
    for start in range(0, wide_out, piece):
        part = jnp.dot(tall[start : start + piece], repeat_right, preferred_element_type=jnp.float32)
        same_row = (
            lax.broadcasted_iota(jnp.int32, (piece, wide_in), 0) % rows
            == lax.broadcasted_iota(jnp.int32, (piece, wide_in), 1) % rows
        )
        spread_ref[start : start + piece] = jnp.where(same_row, part, 0.0).astype(jnp.bfloat16)


def time_tables(segments, ref_pick, band_taps, rows, chunk, history):
    frames = segments.shape[0]
    wide_out, wide_in = chunk * rows, (history + chunk) * rows
    smem = pl.BlockSpec(memory_space=pltpu.SMEM)
    return pl.pallas_call(
        functools.partial(time_kernel, history=history, frames=frames, rows=rows),
        in_specs=[smem] * 3,
        out_specs=[pl.BlockSpec(memory_space=pltpu.VMEM), smem, smem],
        out_shape=[
            jax.ShapeDtypeStruct((wide_out, wide_in), jnp.bfloat16),
            jax.ShapeDtypeStruct(ref_pick.shape, jnp.int32),
            jax.ShapeDtypeStruct((history + chunk,), jnp.int32),
        ],
        compiler_params=pltpu.CompilerParams(vmem_limit_bytes=16 * MIB),
        cost_estimate=pl.CostEstimate(
            flops=2 * wide_out * wide_in * chunk, bytes_accessed=2 * wide_out * wide_in, transcendentals=0
        ),
    )(segments, ref_pick, band_taps.astype(jnp.float32))


def filter_frames(window_refs, left_ref, right_ref, stacked_ref, put):
    groups, deep, _ = right_ref.shape
    lanes = deep // (2 * SHARE)
    rows = left_ref.shape[0] // (2 * SHARE * groups)
    bands = rows // TILE
    pair = window_refs[0].shape[1] // lanes
    many = len(window_refs) * pair * TILE
    for n, window in enumerate(window_refs):
        stacked = jnp.dot(left_ref[...], window[...], preferred_element_type=jnp.float32).astype(jnp.bfloat16)
        for oz in range(2 * SHARE * groups):
            group, place = divmod(oz, 2 * SHARE)
            for band in range(bands):
                begin = oz * rows + band * TILE
                for f in range(pair):
                    row = band * many + (n * pair + f) * TILE
                    stacked_ref[group, row : row + TILE, place * lanes : (place + 1) * lanes] = stacked[
                        begin : begin + TILE, f * lanes : (f + 1) * lanes
                    ]
    block = pair * TILE
    total = bands * many
    step = min(512, total)
    for group in range(groups):
        for start in range(0, total, step):
            stop = min(start + step, total)
            coeff = jnp.dot(
                stacked_ref[group, start:stop], right_ref[group], preferred_element_type=jnp.float32
            ).astype(jnp.bfloat16)
            for place in range(start, stop, block):
                band, row = divmod(place, many)
                put(group, band, row // block, coeff[place - start : place - start + block])


def coeff_kernel(window_ref, left_ref, right_ref, coeff_ref, stacked_ref):
    chips = window_ref.shape[0]
    block = coeff_ref.shape[2] // chips

    def put(group, band, i, values):
        coeff_ref[group, band, i * block : (i + 1) * block] = values

    filter_frames([window_ref.at[chip] for chip in range(chips)], left_ref, right_ref, stacked_ref, put)


def own_coeffs(windows, left, right, rows, frames_here):
    groups, deep, wide = right.shape
    vmem = pl.BlockSpec(memory_space=pltpu.VMEM)
    many = windows.shape[0] * frames_here * TILE
    out = jax.ShapeDtypeStruct((groups, rows // TILE, many, wide), jnp.bfloat16)
    return pl.pallas_call(
        coeff_kernel,
        in_specs=[vmem] * 3,
        out_specs=vmem,
        out_shape=out,
        scratch_shapes=[pltpu.VMEM((groups, rows // TILE * many, deep), jnp.bfloat16)],
        compiler_params=pltpu.CompilerParams(vmem_limit_bytes=8 * out.size + 16 * MIB),
        cost_estimate=pl.CostEstimate(
            flops=4 * out.size * deep, bytes_accessed=2 * (windows.size + out.size), transcendentals=0
        ),
    )(windows, left, right)


def pixel_kernel(
    sources_ref, spread_ref, other_ref, refer_ref, left_ref, right_ref, *refs, places, history, whole
):
    ready_refs, (out_ref, stacked_ref, coeff_ref, phase_ref, filtered_ref, source_ref, sem) = refs[:-7], refs[-7:]
    sources = pltpu.make_async_copy(sources_ref, source_ref, sem)
    sources.start()
    chips = other_ref.shape[0]
    groups, bands, _, wide = coeff_ref.shape
    half = wide // 2
    pair = other_ref.shape[2] // (right_ref.shape[1] // (2 * SHARE))
    block = pair * TILE
    chunk = out_ref.shape[0] * pair
    timed = history + chunk
    core = lax.axis_index("core")

    def place_of(exchanges, twin, n):
        chip = n if exchanges is None else lax.bitwise_xor(lax.axis_index("slab"), exchanges[n])
        return pl.ds(pl.multiple_of((chip * CORES + lax.rem(core + twin, CORES)) * block, block), block)

    for ready_ref, (exchanges, twin) in zip(ready_refs, places):
        for n in range(ready_ref.shape[2] // block):
            for group in range(groups):
                for band in range(bands):
                    coeff_ref[group, band, place_of(exchanges, twin, n)] = ready_ref[group, band, n * block : (n + 1) * block]

    def put(group, band, i, values):
        if i < chips:
            place = place_of(*places[-1], i)
        else:
            place = slice(timed * TILE + (i - chips) * block, timed * TILE + (i - chips + 1) * block)
        coeff_ref[group, band, place] = values

    windows = [other_ref.at[chip] for chip in range(chips)]
    if not whole:
        windows += [refer_ref.at[i] for i in range(refer_ref.shape[0])]
    filter_frames(windows, left_ref, right_ref, stacked_ref, put)

    sources.wait()

    def phase_one(slot, carry):
        place = pl.ds(pl.multiple_of(slot * TILE, TILE), TILE)
        source = source_ref[slot]
        refer = pl.ds(pl.multiple_of(source * TILE, TILE), TILE)
        for group in range(groups):
            for band in range(bands):
                coeff_real = coeff_ref[group, band, place, 0:half].astype(jnp.float32)
                coeff_imag = coeff_ref[group, band, place, half:wide].astype(jnp.float32)
                ref_real = coeff_ref[group, band, refer, 0:half].astype(jnp.float32)
                ref_imag = coeff_ref[group, band, refer, half:wide].astype(jnp.float32)
                prod_real = coeff_real * ref_real + coeff_imag * ref_imag
                prod_imag = coeff_imag * ref_real - coeff_real * ref_imag
                square = prod_real * prod_real + prod_imag * prod_imag + 1.0
                phase = (prod_imag * lax.rsqrt(square)).astype(jnp.bfloat16)
                phase_ref[band, place, group * half : (group + 1) * half] = phase
        return carry

    lax.fori_loop(0, timed, phase_one, 0, unroll=2)

    piece = min(128, chunk * TILE)
    columns = half // SHARE
    left_half = lax.broadcasted_iota(jnp.int32, (TILE, half), 1) < columns
    step = min(256, chunk * TILE)
    for band in range(bands):
        for start in range(0, chunk * TILE, step):
            stop = start + step
            filtered_ref[start:stop] = jnp.dot(
                spread_ref[start:stop, : history * TILE + stop],
                phase_ref[band, : history * TILE + stop],
                preferred_element_type=jnp.float32,
            ).astype(jnp.bfloat16)
        for start in range(0, chunk * TILE, piece):
            here = slice(history * TILE + start, history * TILE + start + piece)
            filtered = filtered_ref[start : start + piece].astype(jnp.float32)
            above = jnp.zeros((piece, half), jnp.float32)
            below = jnp.zeros((piece, half), jnp.float32)
            for group in range(groups):
                coeff_real = coeff_ref[group, band, here, 0:half].astype(jnp.float32)
                coeff_imag = coeff_ref[group, band, here, half:wide].astype(jnp.float32)
                amplitude = coeff_real * coeff_real + coeff_imag * coeff_imag
                above = above + amplitude * filtered[:, group * half : (group + 1) * half]
                below = below + amplitude
            for i in range(piece // block):
                sums = []
                for value in (above, below):
                    one, two = value[i * block : i * block + TILE], value[i * block + TILE : (i + 1) * block]
                    sums.append(jnp.where(left_half, one, two) + pltpu.roll(jnp.where(left_half, two, one), columns, 1))
                both = (sums[0] / (sums[1] + 1.0)).astype(out_ref.dtype)
                out_ref[start // block + i, band * TILE : (band + 1) * TILE] = both


def pixel_motion(sources, spread, ready, other, refer, left, right, places, chunk, history):
    groups, bands, _, wide = ready[0].shape
    deep = right.shape[1]
    timed = history + chunk
    whole = refer is None
    slots = timed if whole else timed + NSEG
    pair = other.shape[2] // (deep // (2 * SHARE))
    fresh = other.shape[0] * pair + slots - timed
    vmem = pl.BlockSpec(memory_space=pltpu.VMEM)
    return pl.pallas_call(
        functools.partial(pixel_kernel, places=places, history=history, whole=whole),
        in_specs=[pl.BlockSpec(memory_space=pl.ANY)] + [vmem] * (5 + len(ready)),
        out_specs=vmem,
        out_shape=jax.ShapeDtypeStruct((chunk // pair, bands * TILE, wide // 2), jnp.bfloat16),
        scratch_shapes=[
            pltpu.VMEM((groups, bands * fresh * TILE, deep), jnp.bfloat16),
            pltpu.VMEM((groups, bands, slots * TILE, wide), jnp.bfloat16),
            pltpu.VMEM((bands, timed * TILE, groups * wide // 2), jnp.bfloat16),
            pltpu.VMEM((chunk * TILE, groups * wide // 2), jnp.bfloat16),
            pltpu.SMEM((timed,), jnp.int32),
            pltpu.SemaphoreType.DMA,
        ],
        compiler_params=pltpu.CompilerParams(vmem_limit_bytes=8 * groups * bands * slots * TILE * wide + 16 * MIB),
        cost_estimate=pl.CostEstimate(
            flops=2 * groups * bands * TILE * wide * (fresh * deep + chunk * timed * TILE // 2),
            bytes_accessed=2 * (other.size + sum(one.size for one in ready) + right.size),
            transcendentals=groups * bands * TILE * timed * wide // 2,
        ),
    )(sources, spread, other, other if whole else refer, left, right, *ready)


def join_kernel(tiles_ref, out_ref, frames_ref, sems):
    count, quarter, _ = out_ref.shape
    devices, rows, lanes = tiles_ref.shape
    columns = lanes // count
    strips = quarter // columns
    left = lax.broadcasted_iota(jnp.int32, (rows, lanes), 1) < columns
    copies = []
    for i in range(devices // strips):
        down = slice(i * rows, (i + 1) * rows)
        for strip in range(0, strips, 2):
            one = tiles_ref[strip * devices // strips + i].astype(jnp.float32)
            two = tiles_ref[(strip + 1) * devices // strips + i].astype(jnp.float32)
            here = slice(strip * columns, (strip + 2) * columns)
            frames_ref[0, down, here] = jnp.where(left, one, pltpu.roll(two, columns, 1))
            frames_ref[1, down, here] = jnp.where(left, pltpu.roll(one, columns, 1), two)
        for f in range(count):
            copies.append(pltpu.make_async_copy(frames_ref.at[f, down], out_ref.at[f, down], sems.at[f, i]))
            copies[-1].start()
    for copy in copies:
        copy.wait()


def join_tiles(tiles, quarter):
    strips = quarter * 2 // tiles.shape[2]
    out = jax.ShapeDtypeStruct((2, quarter, quarter), jnp.float32)
    return pl.pallas_call(
        join_kernel,
        in_specs=[pl.BlockSpec(memory_space=pltpu.VMEM)],
        out_specs=pl.BlockSpec(memory_space=pltpu.HBM),
        out_shape=out,
        scratch_shapes=[
            pltpu.VMEM(out.shape, jnp.float32),
            pltpu.SemaphoreType.DMA((2, tiles.shape[0] // strips)),
        ],
        compiler_params=pltpu.CompilerParams(vmem_limit_bytes=16 * MIB),
        cost_estimate=pl.CostEstimate(flops=tiles.size, bytes_accessed=6 * tiles.size, transcendentals=0),
    )(tiles)


def chunk_windows(mine, other, ref_frames, frames_here, history_chips, chips):
    mine = lax.all_gather(mine, "chunk", axis=0, tiled=True)
    other = lax.all_gather(other, "chunk", axis=0, tiled=True)
    height = mine.shape[1]
    core = lax.axis_index("core")
    device, f = ref_frames // frames_here, ref_frames % frames_here
    own = (device % CORES == core)[:, None, None]

    def pick(windows):
        return windows.reshape(windows.shape[0], height, frames_here, -1)[device // CORES, :, f]

    refer = jnp.where(own, pick(mine), pick(other))
    refer = refer.reshape(NSEG // frames_here, frames_here, height, -1)
    refer = jnp.swapaxes(refer, 1, 2).reshape(NSEG // frames_here, height, -1)

    def cut(windows):
        before = jnp.zeros((history_chips,) + windows.shape[1:], windows.dtype)
        windows = jnp.concatenate([before, windows])
        return lax.dynamic_slice_in_dim(windows, lax.axis_index("chunk") * chips, history_chips + chips)

    return cut(mine), cut(other), refer


def body(video_frames, segments, ref_pick, band_taps, *, chunks, slabs):
    frames_here, size, _ = video_frames.shape
    quarter = size // 4
    rows = quarter // (DOWN * CORES)
    columns = quarter * DOWN // slabs
    chunk = slabs * CORES * frames_here
    history = min(chunk * -(-(band_taps.shape[0] - 1) // chunk), segments.shape[0] - chunk)
    left = jnp.asarray(slab_left_table(rows, HALO, ORIENT))
    right = jnp.asarray(make_right_table(columns, HALO, ORIENT))
    order = exchange_order(slabs)

    def exchange(array, k):
        return lax.ppermute(array, "slab", [(chip, chip ^ k) for chip in range(slabs)]) if k else array

    def swap(array):
        return lax.ppermute(array, "core", [(0, 1), (1, 0)])

    windows = reduce_frames(video_frames, order, HALO)
    spread, ref_frames, sources = time_tables(segments, ref_pick, band_taps, TILE, chunk, history)
    pieces = [exchange(window, k) for k, window in zip(order, windows)]
    if chunks > 1:
        mine, other = cut_windows(pieces, HALO, [])
        by_chip = jnp.asarray(np.argsort(order))[lax.axis_index("slab") ^ jnp.arange(slabs)]
        mine, other = mine[by_chip], swap(other)[by_chip]
        history_chips = history // (CORES * frames_here)
        mine, other, refer = chunk_windows(mine, other, ref_frames, frames_here, history_chips, slabs)
        ready = [own_coeffs(mine, left, right, rows, frames_here)]
        places = [(None, 0), (None, 1)]
    else:
        first = slabs // 2
        mine, other = cut_windows(pieces[:first], HALO, [spread])
        ready = [own_coeffs(one, left, right, rows, frames_here) for one in (mine, swap(other))]
        mine, other = cut_windows(pieces[first:], HALO, ready[:1])
        other, refer = swap(other), None
        ready.append(own_coeffs(mine, left, right, rows, frames_here))
        places = [(exchanges, twin) for exchanges in (order[:first], order[first:]) for twin in range(CORES)]
    motion = pixel_motion(sources, spread, ready, other, refer, left, right, places, chunk, history)
    motion = lax.all_to_all(motion, ("slab", "core"), split_axis=0, concat_axis=0, tiled=True)
    return join_tiles(motion, quarter)


def solution(mesh):
    chips = mesh.shape["frames"] // CORES
    slabs = min(chips, QUART * DOWN // (2 * HALO))
    chunks = chips // slabs
    names = ("groups", "chunk", "slab", "core")
    cut = jax.sharding.Mesh(mesh.devices.reshape(mesh.shape["groups"], chunks, slabs, CORES), names)
    in_specs = (P(names, None, None), P("groups"), P("groups"), P())
    return jax.shard_map(
        functools.partial(body, chunks=chunks, slabs=slabs),
        mesh=cut, in_specs=in_specs, out_specs=P(names, None, None), check_vma=False,
    )
```

```python
import functools
import math

import jax
import jax.numpy as jnp
import numpy as np
from jax import lax
from jax.experimental import pallas as pl
from jax.experimental.pallas import tpu as pltpu
from jax.sharding import PartitionSpec as P

IMG = 1024
ORIENT = 4
NSEG = 4
QUART = 256


blur_sigma = 2.0
gabor_sigma = 2.0
wave_number = math.pi / 2.0
gabor_gain = 2.0

HALO = 32
TILE = 16
DOWN = 2
SHARE = 2
CORES = 2
MIB = 1024 * 1024


def envelope_of(offset_grid):
    return np.float32(gabor_gain) * np.exp(
        -offset_grid * offset_grid / np.float32(2.0 * gabor_sigma * gabor_sigma)
    )


def waves(orient):
    angles = np.arange(orient, dtype=np.float32) * np.float32(math.pi / orient)
    wave_x = np.float32(wave_number) * np.cos(angles)
    wave_y = np.float32(wave_number) * np.sin(angles)
    return wave_x, wave_y


def slab_left_table(rows, halo, orient):
    offset = (
        np.arange(rows + 2 * halo, dtype=np.float32)[None, :]
        - np.float32(halo)
        - np.arange(rows, dtype=np.float32)[:, None]
    )
    wave_y = waves(orient)[1]
    phase = wave_y[:, None, None] * offset[None]
    envelope = envelope_of(offset)[None]
    table = np.stack([envelope * np.cos(phase), envelope * np.sin(phase)], axis=1)
    return table.reshape(orient * 2 * rows, rows + 2 * halo).astype(jnp.bfloat16)


def make_right_table(columns, halo, orient):
    window = columns + 2 * halo
    offset = (
        np.arange(window, dtype=np.float32)[:, None] - np.float32(halo) - np.arange(columns, dtype=np.float32)[None, :]
    )
    wave_x = waves(orient)[0]
    phase_x = wave_x[:, None, None] * offset[None]
    envelope = envelope_of(offset)[None]
    real_part = envelope * np.cos(phase_x)
    imag_part = envelope * np.sin(phase_x)
    table = np.zeros((orient // SHARE, SHARE, 2, window, 2, SHARE, columns), np.float32)
    for o in range(orient):
        group, i = divmod(o, SHARE)
        table[group, i, 0, :, 0, i] = real_part[o]
        table[group, i, 0, :, 1, i] = imag_part[o]
        table[group, i, 1, :, 0, i] = -imag_part[o]
        table[group, i, 1, :, 1, i] = real_part[o]
    return table.reshape(orient // SHARE, SHARE * 2 * window, 2 * SHARE * columns).astype(jnp.bfloat16)


def down_sums(full_size, quarter):
    position = np.arange(quarter, dtype=np.float32)[:, None]
    columns = np.arange(full_size, dtype=np.float32)[None, :]
    offset_grid = columns - np.float32(4.0) * position - np.float32(1.5)
    weight = np.exp(-offset_grid * offset_grid / np.float32(2.0 * blur_sigma * blur_sigma))
    return np.sum(weight, axis=1)


def down_block(position, column, shape, axis, sums):
    positions = position + lax.broadcasted_iota(jnp.int32, shape, 1 - axis)
    columns = column + lax.broadcasted_iota(jnp.int32, shape, axis)
    offset_grid = columns.astype(jnp.float32) - 4.0 * positions.astype(jnp.float32) - 1.5
    weight = jnp.exp(-offset_grid * offset_grid / (2.0 * blur_sigma * blur_sigma))
    inner = float(sums[len(sums) // 2])
    line = position + lax.broadcasted_iota(jnp.int32, tuple(1 if i == axis else n for i, n in enumerate(shape)), 1 - axis)
    scale = jnp.full(line.shape, 1.0 / inner, jnp.float32)
    for q in range(position, min(position + shape[1 - axis], len(sums))):
        if abs(float(sums[q]) - inner) > 1e-7 * inner:
            scale = jnp.where(line == q, 1.0 / float(sums[q]), scale)
    return (weight * scale).astype(jnp.bfloat16)


def build_down(table_ref, axis):
    size, quarter = table_ref.shape[axis], table_ref.shape[1 - axis]
    sums = down_sums(size, quarter)
    table_ref[...] = jnp.zeros_like(table_ref)
    tall, wide = (128, 32)[axis], min(128, table_ref.shape[1])
    for row in range(0, table_ref.shape[0], tall):
        for lane in range(0, table_ref.shape[1], wide):
            position, column = (row, lane) if axis else (lane, row)
            positions, columns = (tall, wide) if axis else (wide, tall)
            if 4 * (position + positions - 1) + 30 >= column and 4 * position - 27 <= column + columns - 1:
                block = down_block(position, column, (tall, wide), axis, sums)
                table_ref[row : row + tall, lane : lane + wide] = block


def reduce_kernel(frames_ref, *refs, order, halo, block):
    out_refs = refs[: len(order)]
    picture_ref, down_t_ref, down_ref, half_ref, total_ref, strip_ref, sems = refs[len(order) :]
    count, size, _ = picture_ref.shape
    quarter = down_ref.shape[0]
    _, strips, _, lanes = strip_ref.shape
    columns = lanes - 2 * halo
    window = out_refs[0].shape[1]

    copies = []
    for f in range(count):
        for i in range(size // block):
            here = pl.ds(i * block, block)
            copy = pltpu.make_async_copy(frames_ref.at[f, here], picture_ref.at[f, here], sems.at[f, i])
            copy.start()
            copies.append(copy)
    build_down(down_t_ref, 0)

    me = lax.axis_index("slab")
    blocks = size // block
    for f in range(count):
        step = block if f == 0 else size
        for begin in range(0, size, step):
            for i in range(begin // block, (begin + step) // block):
                copies[f * blocks + i].wait()
            half_ref[f, begin : begin + step] = jnp.dot(
                picture_ref[f, begin : begin + step], down_t_ref[...], preferred_element_type=jnp.float32
            ).astype(jnp.bfloat16)
            if f == begin == 0:
                build_down(down_ref, 1)
        total_ref[f] = jnp.dot(down_ref[...], half_ref[f], preferred_element_type=jnp.float32)
        for strip in range(strips):
            begin = strip * columns - halo
            moved = pltpu.roll(total_ref[f], (-begin) % quarter, 1)[:, 0:lanes]
            column = begin + lax.broadcasted_iota(jnp.int32, (quarter, lanes), 1)
            inside = (column >= 0) & (column < quarter)
            strip_ref[f, strip] = jnp.where(inside, moved, 0.0).astype(jnp.bfloat16)
        for k, out_ref in zip(order, out_refs):
            slab = lax.bitwise_xor(me, k)
            begin = pl.multiple_of(lax.rem(slab, DOWN) * (quarter - window), TILE)
            out_ref[f] = strip_ref[f, slab // DOWN, pl.ds(begin, window)]


def reduce_frames(video_frames, order, halo):
    count, size, _ = video_frames.shape
    quarter = size // 4
    strips = len(order) // DOWN
    lanes = quarter // strips + 2 * halo
    block = size // 2
    out = jax.ShapeDtypeStruct((count, quarter // DOWN + halo, lanes), jnp.bfloat16)
    return pl.pallas_call(
        functools.partial(reduce_kernel, order=order, halo=halo, block=block),
        in_specs=[pl.BlockSpec(memory_space=pltpu.HBM)],
        out_specs=[pl.BlockSpec(memory_space=pltpu.VMEM)] * len(order),
        out_shape=[out] * len(order),
        scratch_shapes=[
            pltpu.VMEM((count, size, size), jnp.bfloat16),
            pltpu.VMEM((size, quarter), jnp.bfloat16),
            pltpu.VMEM((quarter, size), jnp.bfloat16),
            pltpu.VMEM((count, size, quarter), jnp.bfloat16),
            pltpu.VMEM((count, quarter, quarter), jnp.float32),
            pltpu.VMEM((count, strips, quarter, lanes), jnp.bfloat16),
            pltpu.SemaphoreType.DMA((count, size // block)),
        ],
        compiler_params=pltpu.CompilerParams(vmem_limit_bytes=52 * MIB),
        cost_estimate=pl.CostEstimate(
            flops=2 * count * size * quarter * (size + quarter),
            bytes_accessed=2 * count * size * size,
            transcendentals=0,
        ),
    )(video_frames)


def exchange_order(slabs):
    far = sorted(range(slabs // 2, slabs), key=lambda k: k % 2)
    near = list(range(2, slabs // 2))
    turns = [k for pair in zip(far, near) for k in pair]
    return [0] + turns + far[len(near) :] + [k for k in (1,) if k < slabs // 2]


def cut_kernel(*refs, many, halo):
    in_refs, (mine_ref, other_ref), padded_ref = refs[:many], refs[-3:-1], refs[-1]
    count, window, lanes = in_refs[0].shape
    height = mine_ref.shape[0]
    rows = height - 2 * halo
    wide = count * lanes
    me, core = lax.axis_index("slab"), lax.axis_index("core")
    edge = jnp.zeros((halo, count * lanes), jnp.bfloat16)
    padded_ref[0:halo] = edge
    padded_ref[halo + window :] = edge
    above = lax.rem(me, DOWN) * halo
    for n, in_ref in enumerate(in_refs):
        for f in range(count):
            padded_ref[halo : halo + window, f * lanes : (f + 1) * lanes] = in_ref[f]
        for out_ref, number in ((mine_ref, core), (other_ref, 1 - core)):
            place = pl.ds(pl.multiple_of(above + number * rows, TILE), height)
            out_ref[:, n * wide : (n + 1) * wide] = padded_ref[place]


def cut_windows(pieces, halo, after):
    count, window, lanes = pieces[0].shape
    height = (window - halo) // CORES + 2 * halo
    out = jax.ShapeDtypeStruct((height, len(pieces) * count * lanes), jnp.bfloat16)
    return pl.pallas_call(
        functools.partial(cut_kernel, many=len(pieces), halo=halo),
        in_specs=[pl.BlockSpec(memory_space=pltpu.VMEM)] * len(pieces) + [pl.BlockSpec(memory_space=pl.ANY)] * len(after),
        out_specs=[pl.BlockSpec(memory_space=pltpu.VMEM)] * 2,
        out_shape=[out, out],
        scratch_shapes=[pltpu.VMEM((window + 2 * halo, count * lanes), jnp.bfloat16)],
        compiler_params=pltpu.CompilerParams(vmem_limit_bytes=16 * MIB),
        cost_estimate=pl.CostEstimate(flops=0, bytes_accessed=8 * out.size, transcendentals=0),
    )(*pieces, *after)


def time_kernel(segments_ref, pick_ref, taps_ref, spread_ref, frame_ref, source_ref, *, history, frames, rows):
    chunk, timed = spread_ref.shape[0] // rows, spread_ref.shape[1] // rows
    nseg = pick_ref.shape[0]
    taps = taps_ref.shape[0]
    wide_out, wide_in = chunk * rows, timed * rows

    def count_one(t, totals):
        here = segments_ref[t]
        below = [total + (here < s).astype(jnp.int32) for s, total in enumerate(totals[0])]
        same = [total + (here == s).astype(jnp.int32) for s, total in enumerate(totals[1])]
        return tuple(below), tuple(same)

    zeros = tuple(jnp.int32(0) for _ in range(nseg))
    starts, counts = lax.fori_loop(0, frames, count_one, (zeros, zeros), unroll=8)
    for s in range(nseg):
        frame_ref[s] = starts[s] + lax.rem(pick_ref[s], counts[s])

    def source_one(slot, carry):
        if chunk == frames:
            source_ref[slot] = frame_ref[segments_ref[slot]]
        else:
            before = lax.axis_index("chunk") * chunk - history
            source_ref[slot] = timed + segments_ref[jnp.maximum(before + slot, 0)]
        return carry

    lax.fori_loop(0, timed, source_one, 0)

    lag = history + lax.broadcasted_iota(jnp.int32, (chunk, timed), 0) - lax.broadcasted_iota(
        jnp.int32, (chunk, timed), 1
    )
    if history:
        first = lax.axis_index("chunk") * chunk - history
        real = first + lax.broadcasted_iota(jnp.int32, (chunk, timed), 1) >= 0
        lag = jnp.where(real, lag, -1)
    matrix = jnp.zeros((chunk, timed), jnp.float32)
    for k in range(taps):
        matrix = jnp.where(lag == k, taps_ref[k], matrix)
    repeat_left = (
        lax.broadcasted_iota(jnp.int32, (wide_out, chunk), 0) // rows
        == lax.broadcasted_iota(jnp.int32, (wide_out, chunk), 1)
    ).astype(jnp.bfloat16)
    repeat_right = (
        lax.broadcasted_iota(jnp.int32, (timed, wide_in), 1) // rows
        == lax.broadcasted_iota(jnp.int32, (timed, wide_in), 0)
    ).astype(jnp.bfloat16)
    tall = jnp.dot(repeat_left, matrix.astype(jnp.bfloat16), preferred_element_type=jnp.float32)
    tall = tall.astype(jnp.bfloat16)
    piece = min(128, wide_out)
    for start in range(0, wide_out, piece):
        part = jnp.dot(tall[start : start + piece], repeat_right, preferred_element_type=jnp.float32)
        same_row = (
            lax.broadcasted_iota(jnp.int32, (piece, wide_in), 0) % rows
            == lax.broadcasted_iota(jnp.int32, (piece, wide_in), 1) % rows
        )
        spread_ref[start : start + piece] = jnp.where(same_row, part, 0.0).astype(jnp.bfloat16)


def time_tables(segments, ref_pick, band_taps, rows, chunk, history):
    frames = segments.shape[0]
    wide_out, wide_in = chunk * rows, (history + chunk) * rows
    smem = pl.BlockSpec(memory_space=pltpu.SMEM)
    return pl.pallas_call(
        functools.partial(time_kernel, history=history, frames=frames, rows=rows),
        in_specs=[smem] * 3,
        out_specs=[pl.BlockSpec(memory_space=pltpu.VMEM), smem, smem],
        out_shape=[
            jax.ShapeDtypeStruct((wide_out, wide_in), jnp.bfloat16),
            jax.ShapeDtypeStruct(ref_pick.shape, jnp.int32),
            jax.ShapeDtypeStruct((history + chunk,), jnp.int32),
        ],
        compiler_params=pltpu.CompilerParams(vmem_limit_bytes=16 * MIB),
        cost_estimate=pl.CostEstimate(
            flops=2 * wide_out * wide_in * chunk, bytes_accessed=2 * wide_out * wide_in, transcendentals=0
        ),
    )(segments, ref_pick, band_taps.astype(jnp.float32))


def filter_frames(window_ref, pair, left_ref, right_ref, stacked_ref, put):
    groups, deep, _ = right_ref.shape
    lanes = deep // (2 * SHARE)
    rows = left_ref.shape[0] // (2 * SHARE * groups)
    bands = rows // TILE
    frames = window_ref.shape[1] // lanes
    many = frames * TILE
    for first in range(0, frames, 8):
        last = min(first + 8, frames)
        stacked = jnp.dot(
            left_ref[...], window_ref[:, first * lanes : last * lanes], preferred_element_type=jnp.float32
        ).astype(jnp.bfloat16)
        for oz in range(2 * SHARE * groups):
            group, place = divmod(oz, 2 * SHARE)
            for band in range(bands):
                begin = oz * rows + band * TILE
                for f in range(first, last):
                    row = band * many + f * TILE
                    stacked_ref[group, row : row + TILE, place * lanes : (place + 1) * lanes] = stacked[
                        begin : begin + TILE, (f - first) * lanes : (f - first + 1) * lanes
                    ]
    block = pair * TILE
    total = bands * many
    step = min(512, total)
    for group in range(groups):
        for start in range(0, total, step):
            stop = min(start + step, total)
            coeff = jnp.dot(
                stacked_ref[group, start:stop], right_ref[group], preferred_element_type=jnp.float32
            ).astype(jnp.bfloat16)
            for place in range(start, stop, block):
                band, row = divmod(place, many)
                put(group, band, row // block, coeff[place - start : place - start + block])


def coeff_kernel(window_ref, left_ref, right_ref, coeff_ref, stacked_ref, *, pair):
    block = pair * TILE

    def put(group, band, i, values):
        coeff_ref[group, band, i * block : (i + 1) * block] = values

    filter_frames(window_ref, pair, left_ref, right_ref, stacked_ref, put)


def own_coeffs(windows, left, right, rows, frames_here):
    groups, deep, wide = right.shape
    vmem = pl.BlockSpec(memory_space=pltpu.VMEM)
    many = windows.shape[1] // (deep // (2 * SHARE)) * TILE
    out = jax.ShapeDtypeStruct((groups, rows // TILE, many, wide), jnp.bfloat16)
    return pl.pallas_call(
        functools.partial(coeff_kernel, pair=frames_here),
        in_specs=[vmem] * 3,
        out_specs=vmem,
        out_shape=out,
        scratch_shapes=[pltpu.VMEM((groups, rows // TILE * many, deep), jnp.bfloat16)],
        compiler_params=pltpu.CompilerParams(vmem_limit_bytes=8 * out.size + 16 * MIB),
        cost_estimate=pl.CostEstimate(
            flops=4 * out.size * deep, bytes_accessed=2 * (windows.size + out.size), transcendentals=0
        ),
    )(windows, left, right)


def pixel_kernel(
    sources_ref, spread_ref, other_ref, left_ref, right_ref, *refs, places, pair, chips, history
):
    ready_refs, (out_ref, stacked_ref, coeff_ref, phase_ref, filtered_ref, source_ref, sem) = refs[:-7], refs[-7:]
    sources = pltpu.make_async_copy(sources_ref, source_ref, sem)
    sources.start()
    groups, bands, _, wide = coeff_ref.shape
    half = wide // 2
    block = pair * TILE
    chunk = out_ref.shape[0] * pair
    timed = history + chunk
    core = lax.axis_index("core")

    def place_of(exchanges, twin, n):
        chip = n if exchanges is None else lax.bitwise_xor(lax.axis_index("slab"), exchanges[n])
        return pl.ds(pl.multiple_of((chip * CORES + lax.rem(core + twin, CORES)) * block, block), block)

    for ready_ref, (exchanges, twin) in zip(ready_refs, places):
        for n in range(ready_ref.shape[2] // block):
            for group in range(groups):
                for band in range(bands):
                    coeff_ref[group, band, place_of(exchanges, twin, n)] = ready_ref[group, band, n * block : (n + 1) * block]

    def put(group, band, i, values):
        if i < chips:
            place = place_of(*places[-1], i)
        else:
            place = slice(timed * TILE + (i - chips) * block, timed * TILE + (i - chips + 1) * block)
        coeff_ref[group, band, place] = values

    filter_frames(other_ref, pair, left_ref, right_ref, stacked_ref, put)

    sources.wait()

    def phase_one(slot, carry):
        place = pl.ds(pl.multiple_of(slot * TILE, TILE), TILE)
        source = source_ref[slot]
        refer = pl.ds(pl.multiple_of(source * TILE, TILE), TILE)
        for group in range(groups):
            for band in range(bands):
                coeff_real = coeff_ref[group, band, place, 0:half].astype(jnp.float32)
                coeff_imag = coeff_ref[group, band, place, half:wide].astype(jnp.float32)
                ref_real = coeff_ref[group, band, refer, 0:half].astype(jnp.float32)
                ref_imag = coeff_ref[group, band, refer, half:wide].astype(jnp.float32)
                prod_real = coeff_real * ref_real + coeff_imag * ref_imag
                prod_imag = coeff_imag * ref_real - coeff_real * ref_imag
                square = prod_real * prod_real + prod_imag * prod_imag + 1.0
                phase = (prod_imag * lax.rsqrt(square)).astype(jnp.bfloat16)
                lane = (band * groups + group) * half
                phase_ref[place, lane : lane + half] = phase
        return carry

    lax.fori_loop(0, timed, phase_one, 0, unroll=2)

    piece = min(128, chunk * TILE)
    columns = half // SHARE
    left_half = lax.broadcasted_iota(jnp.int32, (TILE, half), 1) < columns
    step = min(256, chunk * TILE)
    for start in range(0, chunk * TILE, step):
        stop = start + step
        filtered_ref[start:stop] = jnp.dot(
            spread_ref[start:stop, : history * TILE + stop],
            phase_ref[: history * TILE + stop],
            preferred_element_type=jnp.float32,
        ).astype(jnp.bfloat16)
    for band in range(bands):
        for start in range(0, chunk * TILE, piece):
            here = slice(history * TILE + start, history * TILE + start + piece)
            lane = band * groups * half
            filtered = filtered_ref[start : start + piece, lane : lane + groups * half].astype(jnp.float32)
            above = jnp.zeros((piece, half), jnp.float32)
            below = jnp.zeros((piece, half), jnp.float32)
            for group in range(groups):
                coeff_real = coeff_ref[group, band, here, 0:half].astype(jnp.float32)
                coeff_imag = coeff_ref[group, band, here, half:wide].astype(jnp.float32)
                amplitude = coeff_real * coeff_real + coeff_imag * coeff_imag
                above = above + amplitude * filtered[:, group * half : (group + 1) * half]
                below = below + amplitude
            for i in range(piece // block):
                sums = []
                for value in (above, below):
                    one, two = value[i * block : i * block + TILE], value[i * block + TILE : (i + 1) * block]
                    sums.append(jnp.where(left_half, one, two) + pltpu.roll(jnp.where(left_half, two, one), columns, 1))
                both = (sums[0] / (sums[1] + 1.0)).astype(out_ref.dtype)
                out_ref[start // block + i, band * TILE : (band + 1) * TILE] = both


def pixel_motion(sources, spread, ready, other, left, right, places, pair, chips, chunk, history):
    groups, bands, _, wide = ready[0].shape
    deep = right.shape[1]
    timed = history + chunk
    fresh = other.shape[1] // (deep // (2 * SHARE))
    slots = timed + fresh - chips * pair
    vmem = pl.BlockSpec(memory_space=pltpu.VMEM)
    return pl.pallas_call(
        functools.partial(pixel_kernel, places=places, pair=pair, chips=chips, history=history),
        in_specs=[pl.BlockSpec(memory_space=pl.ANY)] + [vmem] * (4 + len(ready)),
        out_specs=vmem,
        out_shape=jax.ShapeDtypeStruct((chunk // pair, bands * TILE, wide // 2), jnp.bfloat16),
        scratch_shapes=[
            pltpu.VMEM((groups, bands * fresh * TILE, deep), jnp.bfloat16),
            pltpu.VMEM((groups, bands, slots * TILE, wide), jnp.bfloat16),
            pltpu.VMEM((timed * TILE, bands * groups * wide // 2), jnp.bfloat16),
            pltpu.VMEM((chunk * TILE, bands * groups * wide // 2), jnp.bfloat16),
            pltpu.SMEM((timed,), jnp.int32),
            pltpu.SemaphoreType.DMA,
        ],
        compiler_params=pltpu.CompilerParams(vmem_limit_bytes=8 * groups * bands * slots * TILE * wide + 16 * MIB),
        cost_estimate=pl.CostEstimate(
            flops=2 * groups * bands * TILE * wide * (fresh * deep + chunk * timed * TILE // 2),
            bytes_accessed=2 * (other.size + sum(one.size for one in ready) + right.size),
            transcendentals=groups * bands * TILE * timed * wide // 2,
        ),
    )(sources, spread, other, left, right, *ready)


def join_kernel(tiles_ref, out_ref, frames_ref, sems):
    count, quarter, _ = out_ref.shape
    devices, rows, lanes = tiles_ref.shape
    columns = lanes // count
    strips = quarter // columns
    left = lax.broadcasted_iota(jnp.int32, (rows, lanes), 1) < columns
    copies = []
    for i in range(devices // strips):
        down = slice(i * rows, (i + 1) * rows)
        for strip in range(0, strips, 2):
            one = tiles_ref[strip * devices // strips + i].astype(jnp.float32)
            two = tiles_ref[(strip + 1) * devices // strips + i].astype(jnp.float32)
            here = slice(strip * columns, (strip + 2) * columns)
            frames_ref[0, down, here] = jnp.where(left, one, pltpu.roll(two, columns, 1))
            frames_ref[1, down, here] = jnp.where(left, pltpu.roll(one, columns, 1), two)
        for f in range(count):
            copies.append(pltpu.make_async_copy(frames_ref.at[f, down], out_ref.at[f, down], sems.at[f, i]))
            copies[-1].start()
    for copy in copies:
        copy.wait()


def join_tiles(tiles, quarter):
    strips = quarter * 2 // tiles.shape[2]
    out = jax.ShapeDtypeStruct((2, quarter, quarter), jnp.float32)
    return pl.pallas_call(
        join_kernel,
        in_specs=[pl.BlockSpec(memory_space=pltpu.VMEM)],
        out_specs=pl.BlockSpec(memory_space=pltpu.HBM),
        out_shape=out,
        scratch_shapes=[
            pltpu.VMEM(out.shape, jnp.float32),
            pltpu.SemaphoreType.DMA((2, tiles.shape[0] // strips)),
        ],
        compiler_params=pltpu.CompilerParams(vmem_limit_bytes=16 * MIB),
        cost_estimate=pl.CostEstimate(flops=tiles.size, bytes_accessed=6 * tiles.size, transcendentals=0),
    )(tiles)


def chunk_windows(mine, other, ref_frames, frames_here, history_chips, chips):
    mine = lax.all_gather(mine, "chunk", axis=0, tiled=True)
    other = lax.all_gather(other, "chunk", axis=0, tiled=True)
    height = mine.shape[1]
    core = lax.axis_index("core")
    device, f = ref_frames // frames_here, ref_frames % frames_here
    own = (device % CORES == core)[:, None, None]

    def pick(windows):
        return windows.reshape(windows.shape[0], height, frames_here, -1)[device // CORES, :, f]

    refer = jnp.where(own, pick(mine), pick(other))
    refer = refer.reshape(NSEG // frames_here, frames_here, height, -1)
    refer = jnp.swapaxes(refer, 1, 2).reshape(NSEG // frames_here, height, -1)

    def cut(windows):
        before = jnp.zeros((history_chips,) + windows.shape[1:], windows.dtype)
        windows = jnp.concatenate([before, windows])
        return lax.dynamic_slice_in_dim(windows, lax.axis_index("chunk") * chips, history_chips + chips)

    return cut(mine), cut(other), refer


def body(video_frames, segments, ref_pick, band_taps, *, chunks, slabs):
    frames_here, size, _ = video_frames.shape
    quarter = size // 4
    rows = quarter // (DOWN * CORES)
    columns = quarter * DOWN // slabs
    chunk = slabs * CORES * frames_here
    history = min(chunk * -(-(band_taps.shape[0] - 1) // chunk), segments.shape[0] - chunk)
    left = jnp.asarray(slab_left_table(rows, HALO, ORIENT))
    right = jnp.asarray(make_right_table(columns, HALO, ORIENT))
    order = exchange_order(slabs)

    def exchange(array, k):
        return lax.ppermute(array, "slab", [(chip, chip ^ k) for chip in range(slabs)]) if k else array

    def swap(array):
        return lax.ppermute(array, "core", [(0, 1), (1, 0)])

    windows = reduce_frames(video_frames, order, HALO)
    spread, ref_frames, sources = time_tables(segments, ref_pick, band_taps, TILE, chunk, history)
    pieces = [exchange(window, k) for k, window in zip(order, windows)]
    if chunks > 1:

        def by_chip(windows):
            apart = jnp.moveaxis(windows.reshape(windows.shape[0], slabs, -1), 1, 0)
            return apart[jnp.asarray(np.argsort(order))[lax.axis_index("slab") ^ jnp.arange(slabs)]]

        def side_by_side(windows):
            return jnp.moveaxis(windows, 0, 1).reshape(windows.shape[1], -1)

        mine, other = cut_windows(pieces, HALO, [])
        chips = slabs + history // (CORES * frames_here)
        windows = chunk_windows(by_chip(mine), by_chip(swap(other)), ref_frames, frames_here, chips - slabs, slabs)
        mine, other, refer = [side_by_side(one) for one in windows]
        other = jnp.concatenate([other, refer], axis=1)
        ready = [own_coeffs(mine, left, right, rows, frames_here)]
        places = [(None, 0), (None, 1)]
    else:
        first = slabs // 2
        chips = slabs - first
        mine, other = cut_windows(pieces[:first], HALO, [spread])
        ready = [own_coeffs(one, left, right, rows, frames_here) for one in (mine, swap(other))]
        mine, other = cut_windows(pieces[first:], HALO, ready[:1])
        other = swap(other)
        ready.append(own_coeffs(mine, left, right, rows, frames_here))
        places = [(exchanges, twin) for exchanges in (order[:first], order[first:]) for twin in range(CORES)]
    motion = pixel_motion(sources, spread, ready, other, left, right, places, frames_here, chips, chunk, history)
    motion = lax.all_to_all(motion, ("slab", "core"), split_axis=0, concat_axis=0, tiled=True)
    return join_tiles(motion, quarter)


def solution(mesh):
    chips = mesh.shape["frames"] // CORES
    slabs = min(chips, QUART * DOWN // (2 * HALO))
    chunks = chips // slabs
    names = ("groups", "chunk", "slab", "core")
    cut = jax.sharding.Mesh(mesh.devices.reshape(mesh.shape["groups"], chunks, slabs, CORES), names)
    in_specs = (P(names, None, None), P("groups"), P("groups"), P())
    return jax.shard_map(
        functools.partial(body, chunks=chunks, slabs=slabs),
        mesh=cut, in_specs=in_specs, out_specs=P(names, None, None), check_vma=False,
    )
```

```python
import functools
import math

import jax
import jax.numpy as jnp
import numpy as np
from jax import lax
from jax.experimental import pallas as pl
from jax.experimental.pallas import tpu as pltpu
from jax.sharding import PartitionSpec as P

IMG = 1024
ORIENT = 4
NSEG = 4
QUART = 256


blur_sigma = 2.0
gabor_sigma = 2.0
wave_number = math.pi / 2.0
gabor_gain = 2.0

HALO = 32
TILE = 16
DOWN = 2
SHARE = 2
CORES = 2
MIB = 1024 * 1024


def envelope_of(offset_grid):
    return np.float32(gabor_gain) * np.exp(
        -offset_grid * offset_grid / np.float32(2.0 * gabor_sigma * gabor_sigma)
    )


def waves(orient):
    angles = np.arange(orient, dtype=np.float32) * np.float32(math.pi / orient)
    wave_x = np.float32(wave_number) * np.cos(angles)
    wave_y = np.float32(wave_number) * np.sin(angles)
    return wave_x, wave_y


def slab_left_table(rows, halo, orient):
    offset = (
        np.arange(rows + 2 * halo, dtype=np.float32)[None, :]
        - np.float32(halo)
        - np.arange(rows, dtype=np.float32)[:, None]
    )
    wave_y = waves(orient)[1]
    phase = wave_y[:, None, None] * offset[None]
    envelope = envelope_of(offset)[None]
    table = np.stack([envelope * np.cos(phase), envelope * np.sin(phase)], axis=1)
    return table.reshape(orient * 2 * rows, rows + 2 * halo).astype(jnp.bfloat16)


def make_right_table(columns, halo, orient):
    window = columns + 2 * halo
    offset = (
        np.arange(window, dtype=np.float32)[:, None] - np.float32(halo) - np.arange(columns, dtype=np.float32)[None, :]
    )
    wave_x = waves(orient)[0]
    phase_x = wave_x[:, None, None] * offset[None]
    envelope = envelope_of(offset)[None]
    real_part = envelope * np.cos(phase_x)
    imag_part = envelope * np.sin(phase_x)
    table = np.zeros((orient // SHARE, SHARE, 2, window, 2, SHARE, columns), np.float32)
    for o in range(orient):
        group, i = divmod(o, SHARE)
        table[group, i, 0, :, 0, i] = real_part[o]
        table[group, i, 0, :, 1, i] = imag_part[o]
        table[group, i, 1, :, 0, i] = -imag_part[o]
        table[group, i, 1, :, 1, i] = real_part[o]
    return table.reshape(orient // SHARE, SHARE * 2 * window, 2 * SHARE * columns).astype(jnp.bfloat16)


def down_sums(full_size, quarter):
    position = np.arange(quarter, dtype=np.float32)[:, None]
    columns = np.arange(full_size, dtype=np.float32)[None, :]
    offset_grid = columns - np.float32(4.0) * position - np.float32(1.5)
    weight = np.exp(-offset_grid * offset_grid / np.float32(2.0 * blur_sigma * blur_sigma))
    return np.sum(weight, axis=1)


def down_block(position, column, shape, axis, sums):
    positions = position + lax.broadcasted_iota(jnp.int32, shape, 1 - axis)
    columns = column + lax.broadcasted_iota(jnp.int32, shape, axis)
    offset_grid = columns.astype(jnp.float32) - 4.0 * positions.astype(jnp.float32) - 1.5
    weight = jnp.exp(-offset_grid * offset_grid / (2.0 * blur_sigma * blur_sigma))
    inner = float(sums[len(sums) // 2])
    line = position + lax.broadcasted_iota(jnp.int32, tuple(1 if i == axis else n for i, n in enumerate(shape)), 1 - axis)
    scale = jnp.full(line.shape, 1.0 / inner, jnp.float32)
    for q in range(position, min(position + shape[1 - axis], len(sums))):
        if abs(float(sums[q]) - inner) > 1e-7 * inner:
            scale = jnp.where(line == q, 1.0 / float(sums[q]), scale)
    return (weight * scale).astype(jnp.bfloat16)


def build_down(table_ref, axis):
    size, quarter = table_ref.shape[axis], table_ref.shape[1 - axis]
    sums = down_sums(size, quarter)
    table_ref[...] = jnp.zeros_like(table_ref)
    tall, wide = (128, 32)[axis], min(128, table_ref.shape[1])
    for row in range(0, table_ref.shape[0], tall):
        for lane in range(0, table_ref.shape[1], wide):
            position, column = (row, lane) if axis else (lane, row)
            positions, columns = (tall, wide) if axis else (wide, tall)
            if 4 * (position + positions - 1) + 30 >= column and 4 * position - 27 <= column + columns - 1:
                block = down_block(position, column, (tall, wide), axis, sums)
                table_ref[row : row + tall, lane : lane + wide] = block


def reduce_kernel(frames_ref, *refs, far, direct, halo, block):
    out_refs = refs[: 1 + len(direct)]
    picture_ref, down_t_ref, down_ref, half_ref, total_ref, strip_ref, sems = refs[1 + len(direct) :]
    count, size, _ = picture_ref.shape
    quarter = down_ref.shape[0]
    _, strips, _, lanes = strip_ref.shape
    columns = lanes - 2 * halo
    window = out_refs[-1].shape[1]

    copies = []
    for f in range(count):
        for i in range(size // block):
            here = pl.ds(i * block, block)
            copy = pltpu.make_async_copy(frames_ref.at[f, here], picture_ref.at[f, here], sems.at[f, i])
            copy.start()
            copies.append(copy)
    build_down(down_t_ref, 0)

    me = lax.axis_index("slab")
    blocks = size // block
    for f in range(count):
        step = block if f == 0 else size
        for begin in range(0, size, step):
            for i in range(begin // block, (begin + step) // block):
                copies[f * blocks + i].wait()
            half_ref[f, begin : begin + step] = jnp.dot(
                picture_ref[f, begin : begin + step], down_t_ref[...], preferred_element_type=jnp.float32
            ).astype(jnp.bfloat16)
            if f == begin == 0:
                build_down(down_ref, 1)
        total_ref[f] = jnp.dot(down_ref[...], half_ref[f], preferred_element_type=jnp.float32)
        for strip in range(strips):
            begin = strip * columns - halo
            moved = pltpu.roll(total_ref[f], (-begin) % quarter, 1)[:, 0:lanes]
            column = begin + lax.broadcasted_iota(jnp.int32, (quarter, lanes), 1)
            inside = (column >= 0) & (column < quarter)
            strip_ref[f, strip] = jnp.where(inside, moved, 0.0).astype(jnp.bfloat16)
        out_refs[0][f] = strip_ref[f, lax.bitwise_xor(me, far) // DOWN]
        for k, out_ref in zip(direct, out_refs[1:]):
            slab = lax.bitwise_xor(me, k)
            begin = pl.multiple_of(lax.rem(slab, DOWN) * (quarter - window), TILE)
            out_ref[f] = strip_ref[f, slab // DOWN, pl.ds(begin, window)]


def reduce_frames(video_frames, far, direct, slabs, halo):
    count, size, _ = video_frames.shape
    quarter = size // 4
    strips = slabs // DOWN
    lanes = quarter // strips + 2 * halo
    block = size // 2
    out = [jax.ShapeDtypeStruct((count, quarter, lanes), jnp.bfloat16)]
    out += [jax.ShapeDtypeStruct((count, quarter // DOWN + halo, lanes), jnp.bfloat16)] * len(direct)
    return pl.pallas_call(
        functools.partial(reduce_kernel, far=far, direct=direct, halo=halo, block=block),
        in_specs=[pl.BlockSpec(memory_space=pltpu.HBM)],
        out_specs=[pl.BlockSpec(memory_space=pltpu.VMEM)] * len(out),
        out_shape=out,
        scratch_shapes=[
            pltpu.VMEM((count, size, size), jnp.bfloat16),
            pltpu.VMEM((size, quarter), jnp.bfloat16),
            pltpu.VMEM((quarter, size), jnp.bfloat16),
            pltpu.VMEM((count, size, quarter), jnp.bfloat16),
            pltpu.VMEM((count, quarter, quarter), jnp.float32),
            pltpu.VMEM((count, strips, quarter, lanes), jnp.bfloat16),
            pltpu.SemaphoreType.DMA((count, size // block)),
        ],
        compiler_params=pltpu.CompilerParams(vmem_limit_bytes=52 * MIB),
        cost_estimate=pl.CostEstimate(
            flops=2 * count * size * quarter * (size + quarter),
            bytes_accessed=2 * count * size * size,
            transcendentals=0,
        ),
    )(video_frames)


def pass_kernel(strip_ref, window_ref, *refs):
    own_ref, next_ref = refs[-2:]
    count, window, _ = own_ref.shape
    down = lax.rem(lax.axis_index("slab"), DOWN)
    spare = strip_ref.shape[1] - window
    for f in range(count):
        own_ref[f] = strip_ref[f, pl.ds(pl.multiple_of(down * spare, TILE), window)]
        next_ref[f] = window_ref[f]
        next_ref[count + f] = strip_ref[f, pl.ds(pl.multiple_of((1 - down) * spare, TILE), window)]


def pass_on(strip, window, after):
    vmem = pl.BlockSpec(memory_space=pltpu.VMEM)
    count, height, lanes = window.shape
    return pl.pallas_call(
        pass_kernel,
        in_specs=[vmem] * 2 + [pl.BlockSpec(memory_space=pl.ANY)] * len(after),
        out_specs=[vmem] * 2,
        out_shape=[jax.ShapeDtypeStruct((n * count, height, lanes), jnp.bfloat16) for n in (1, 2)],
        compiler_params=pltpu.CompilerParams(vmem_limit_bytes=16 * MIB),
        cost_estimate=pl.CostEstimate(flops=0, bytes_accessed=12 * window.size, transcendentals=0),
    )(strip, window, *after)


def cut_kernel(*refs, many, count, halo):
    in_refs, (mine_ref, other_ref), padded_ref = refs[:many], refs[-3:-1], refs[-1]
    _, window, lanes = in_refs[0].shape
    height = mine_ref.shape[0]
    rows = height - 2 * halo
    wide = count * lanes
    me, core = lax.axis_index("slab"), lax.axis_index("core")
    edge = jnp.zeros((halo, count * lanes), jnp.bfloat16)
    padded_ref[0:halo] = edge
    padded_ref[halo + window :] = edge
    above = lax.rem(me, DOWN) * halo
    for n, (in_ref, first) in enumerate([(ref, i) for ref in in_refs for i in range(0, ref.shape[0], count)]):
        for f in range(count):
            padded_ref[halo : halo + window, f * lanes : (f + 1) * lanes] = in_ref[first + f]
        for out_ref, number in ((mine_ref, core), (other_ref, 1 - core)):
            place = pl.ds(pl.multiple_of(above + number * rows, TILE), height)
            out_ref[:, n * wide : (n + 1) * wide] = padded_ref[place]


def cut_windows(pieces, count, halo, after):
    _, window, lanes = pieces[0].shape
    height = (window - halo) // CORES + 2 * halo
    frames = sum(piece.shape[0] for piece in pieces)
    out = jax.ShapeDtypeStruct((height, frames * lanes), jnp.bfloat16)
    return pl.pallas_call(
        functools.partial(cut_kernel, many=len(pieces), count=count, halo=halo),
        in_specs=[pl.BlockSpec(memory_space=pltpu.VMEM)] * len(pieces) + [pl.BlockSpec(memory_space=pl.ANY)] * len(after),
        out_specs=[pl.BlockSpec(memory_space=pltpu.VMEM)] * 2,
        out_shape=[out, out],
        scratch_shapes=[pltpu.VMEM((window + 2 * halo, count * lanes), jnp.bfloat16)],
        compiler_params=pltpu.CompilerParams(vmem_limit_bytes=16 * MIB),
        cost_estimate=pl.CostEstimate(flops=0, bytes_accessed=8 * out.size, transcendentals=0),
    )(*pieces, *after)


def time_kernel(segments_ref, pick_ref, taps_ref, spread_ref, frame_ref, source_ref, *, history, frames, rows):
    chunk, timed = spread_ref.shape[0] // rows, spread_ref.shape[1] // rows
    nseg = pick_ref.shape[0]
    taps = taps_ref.shape[0]
    wide_out, wide_in = chunk * rows, timed * rows

    def count_one(t, totals):
        here = segments_ref[t]
        below = [total + (here < s).astype(jnp.int32) for s, total in enumerate(totals[0])]
        same = [total + (here == s).astype(jnp.int32) for s, total in enumerate(totals[1])]
        return tuple(below), tuple(same)

    zeros = tuple(jnp.int32(0) for _ in range(nseg))
    starts, counts = lax.fori_loop(0, frames, count_one, (zeros, zeros), unroll=8)
    for s in range(nseg):
        frame_ref[s] = starts[s] + lax.rem(pick_ref[s], counts[s])

    def source_one(slot, carry):
        if chunk == frames:
            source_ref[slot] = frame_ref[segments_ref[slot]]
        else:
            before = lax.axis_index("chunk") * chunk - history
            source_ref[slot] = timed + segments_ref[jnp.maximum(before + slot, 0)]
        return carry

    lax.fori_loop(0, timed, source_one, 0)

    lag = history + lax.broadcasted_iota(jnp.int32, (chunk, timed), 0) - lax.broadcasted_iota(
        jnp.int32, (chunk, timed), 1
    )
    if history:
        first = lax.axis_index("chunk") * chunk - history
        real = first + lax.broadcasted_iota(jnp.int32, (chunk, timed), 1) >= 0
        lag = jnp.where(real, lag, -1)
    matrix = jnp.zeros((chunk, timed), jnp.float32)
    for k in range(taps):
        matrix = jnp.where(lag == k, taps_ref[k], matrix)
    repeat_left = (
        lax.broadcasted_iota(jnp.int32, (wide_out, chunk), 0) // rows
        == lax.broadcasted_iota(jnp.int32, (wide_out, chunk), 1)
    ).astype(jnp.bfloat16)
    repeat_right = (
        lax.broadcasted_iota(jnp.int32, (timed, wide_in), 1) // rows
        == lax.broadcasted_iota(jnp.int32, (timed, wide_in), 0)
    ).astype(jnp.bfloat16)
    tall = jnp.dot(repeat_left, matrix.astype(jnp.bfloat16), preferred_element_type=jnp.float32)
    tall = tall.astype(jnp.bfloat16)
    piece = min(128, wide_out)
    for start in range(0, wide_out, piece):
        part = jnp.dot(tall[start : start + piece], repeat_right, preferred_element_type=jnp.float32)
        same_row = (
            lax.broadcasted_iota(jnp.int32, (piece, wide_in), 0) % rows
            == lax.broadcasted_iota(jnp.int32, (piece, wide_in), 1) % rows
        )
        spread_ref[start : start + piece] = jnp.where(same_row, part, 0.0).astype(jnp.bfloat16)


def time_tables(segments, ref_pick, band_taps, rows, chunk, history):
    frames = segments.shape[0]
    wide_out, wide_in = chunk * rows, (history + chunk) * rows
    smem = pl.BlockSpec(memory_space=pltpu.SMEM)
    return pl.pallas_call(
        functools.partial(time_kernel, history=history, frames=frames, rows=rows),
        in_specs=[smem] * 3,
        out_specs=[pl.BlockSpec(memory_space=pltpu.VMEM), smem, smem],
        out_shape=[
            jax.ShapeDtypeStruct((wide_out, wide_in), jnp.bfloat16),
            jax.ShapeDtypeStruct(ref_pick.shape, jnp.int32),
            jax.ShapeDtypeStruct((history + chunk,), jnp.int32),
        ],
        compiler_params=pltpu.CompilerParams(vmem_limit_bytes=16 * MIB),
        cost_estimate=pl.CostEstimate(
            flops=2 * wide_out * wide_in * chunk, bytes_accessed=2 * wide_out * wide_in, transcendentals=0
        ),
    )(segments, ref_pick, band_taps.astype(jnp.float32))


def filter_frames(window_ref, pair, left_ref, right_ref, stacked_ref, put):
    groups, deep, _ = right_ref.shape
    lanes = deep // (2 * SHARE)
    rows = left_ref.shape[0] // (2 * SHARE * groups)
    bands = rows // TILE
    frames = window_ref.shape[1] // lanes
    many = frames * TILE
    for first in range(0, frames, 8):
        last = min(first + 8, frames)
        stacked = jnp.dot(
            left_ref[...], window_ref[:, first * lanes : last * lanes], preferred_element_type=jnp.float32
        ).astype(jnp.bfloat16)
        for oz in range(2 * SHARE * groups):
            group, place = divmod(oz, 2 * SHARE)
            for band in range(bands):
                begin = oz * rows + band * TILE
                for f in range(first, last):
                    row = band * many + f * TILE
                    stacked_ref[group, row : row + TILE, place * lanes : (place + 1) * lanes] = stacked[
                        begin : begin + TILE, (f - first) * lanes : (f - first + 1) * lanes
                    ]
    block = pair * TILE
    total = bands * many
    step = min(512, total)
    for group in range(groups):
        for start in range(0, total, step):
            stop = min(start + step, total)
            coeff = jnp.dot(
                stacked_ref[group, start:stop], right_ref[group], preferred_element_type=jnp.float32
            ).astype(jnp.bfloat16)
            for place in range(start, stop, block):
                band, row = divmod(place, many)
                put(group, band, row // block, coeff[place - start : place - start + block])


def coeff_kernel(window_ref, left_ref, right_ref, coeff_ref, stacked_ref, *, pair):
    block = pair * TILE

    def put(group, band, i, values):
        coeff_ref[group, band, i * block : (i + 1) * block] = values

    filter_frames(window_ref, pair, left_ref, right_ref, stacked_ref, put)


def own_coeffs(windows, left, right, rows, frames_here):
    groups, deep, wide = right.shape
    vmem = pl.BlockSpec(memory_space=pltpu.VMEM)
    many = windows.shape[1] // (deep // (2 * SHARE)) * TILE
    out = jax.ShapeDtypeStruct((groups, rows // TILE, many, wide), jnp.bfloat16)
    return pl.pallas_call(
        functools.partial(coeff_kernel, pair=frames_here),
        in_specs=[vmem] * 3,
        out_specs=vmem,
        out_shape=out,
        scratch_shapes=[pltpu.VMEM((groups, rows // TILE * many, deep), jnp.bfloat16)],
        compiler_params=pltpu.CompilerParams(vmem_limit_bytes=8 * out.size + 16 * MIB),
        cost_estimate=pl.CostEstimate(
            flops=4 * out.size * deep, bytes_accessed=2 * (windows.size + out.size), transcendentals=0
        ),
    )(windows, left, right)


def pixel_kernel(
    sources_ref, spread_ref, other_ref, left_ref, right_ref, *refs, places, pair, chips, history
):
    ready_refs, (out_ref, stacked_ref, coeff_ref, phase_ref, filtered_ref, source_ref, sem) = refs[:-7], refs[-7:]
    sources = pltpu.make_async_copy(sources_ref, source_ref, sem)
    sources.start()
    groups, bands, _, wide = coeff_ref.shape
    half = wide // 2
    block = pair * TILE
    chunk = out_ref.shape[0] * pair
    timed = history + chunk
    core = lax.axis_index("core")

    def place_of(exchanges, twin, n):
        chip = n if exchanges is None else lax.bitwise_xor(lax.axis_index("slab"), exchanges[n])
        return pl.ds(pl.multiple_of((chip * CORES + lax.rem(core + twin, CORES)) * block, block), block)

    for ready_ref, (exchanges, twin) in zip(ready_refs, places):
        for n in range(ready_ref.shape[2] // block):
            for group in range(groups):
                for band in range(bands):
                    coeff_ref[group, band, place_of(exchanges, twin, n)] = ready_ref[group, band, n * block : (n + 1) * block]

    def put(group, band, i, values):
        if i < chips:
            place = place_of(*places[-1], i)
        else:
            place = slice(timed * TILE + (i - chips) * block, timed * TILE + (i - chips + 1) * block)
        coeff_ref[group, band, place] = values

    filter_frames(other_ref, pair, left_ref, right_ref, stacked_ref, put)

    sources.wait()

    def phase_one(slot, carry):
        place = pl.ds(pl.multiple_of(slot * TILE, TILE), TILE)
        source = source_ref[slot]
        refer = pl.ds(pl.multiple_of(source * TILE, TILE), TILE)
        for group in range(groups):
            for band in range(bands):
                coeff_real = coeff_ref[group, band, place, 0:half].astype(jnp.float32)
                coeff_imag = coeff_ref[group, band, place, half:wide].astype(jnp.float32)
                ref_real = coeff_ref[group, band, refer, 0:half].astype(jnp.float32)
                ref_imag = coeff_ref[group, band, refer, half:wide].astype(jnp.float32)
                prod_real = coeff_real * ref_real + coeff_imag * ref_imag
                prod_imag = coeff_imag * ref_real - coeff_real * ref_imag
                square = prod_real * prod_real + prod_imag * prod_imag + 1.0
                phase = (prod_imag * lax.rsqrt(square)).astype(jnp.bfloat16)
                lane = (band * groups + group) * half
                phase_ref[place, lane : lane + half] = phase
        return carry

    lax.fori_loop(0, timed, phase_one, 0, unroll=2)

    piece = min(128, chunk * TILE)
    columns = half // SHARE
    left_half = lax.broadcasted_iota(jnp.int32, (TILE, half), 1) < columns
    step = min(256, chunk * TILE)
    for start in range(0, chunk * TILE, step):
        stop = start + step
        filtered_ref[start:stop] = jnp.dot(
            spread_ref[start:stop, : history * TILE + stop],
            phase_ref[: history * TILE + stop],
            preferred_element_type=jnp.float32,
        ).astype(jnp.bfloat16)
    for band in range(bands):
        for start in range(0, chunk * TILE, piece):
            here = slice(history * TILE + start, history * TILE + start + piece)
            lane = band * groups * half
            filtered = filtered_ref[start : start + piece, lane : lane + groups * half].astype(jnp.float32)
            above = jnp.zeros((piece, half), jnp.float32)
            below = jnp.zeros((piece, half), jnp.float32)
            for group in range(groups):
                coeff_real = coeff_ref[group, band, here, 0:half].astype(jnp.float32)
                coeff_imag = coeff_ref[group, band, here, half:wide].astype(jnp.float32)
                amplitude = coeff_real * coeff_real + coeff_imag * coeff_imag
                above = above + amplitude * filtered[:, group * half : (group + 1) * half]
                below = below + amplitude
            for i in range(piece // block):
                sums = []
                for value in (above, below):
                    one, two = value[i * block : i * block + TILE], value[i * block + TILE : (i + 1) * block]
                    sums.append(jnp.where(left_half, one, two) + pltpu.roll(jnp.where(left_half, two, one), columns, 1))
                both = (sums[0] / (sums[1] + 1.0)).astype(out_ref.dtype)
                out_ref[start // block + i, band * TILE : (band + 1) * TILE] = both


def pixel_motion(sources, spread, ready, other, left, right, places, pair, chips, chunk, history):
    groups, bands, _, wide = ready[0].shape
    deep = right.shape[1]
    timed = history + chunk
    fresh = other.shape[1] // (deep // (2 * SHARE))
    slots = timed + fresh - chips * pair
    vmem = pl.BlockSpec(memory_space=pltpu.VMEM)
    return pl.pallas_call(
        functools.partial(pixel_kernel, places=places, pair=pair, chips=chips, history=history),
        in_specs=[pl.BlockSpec(memory_space=pl.ANY)] + [vmem] * (4 + len(ready)),
        out_specs=vmem,
        out_shape=jax.ShapeDtypeStruct((chunk // pair, bands * TILE, wide // 2), jnp.bfloat16),
        scratch_shapes=[
            pltpu.VMEM((groups, bands * fresh * TILE, deep), jnp.bfloat16),
            pltpu.VMEM((groups, bands, slots * TILE, wide), jnp.bfloat16),
            pltpu.VMEM((timed * TILE, bands * groups * wide // 2), jnp.bfloat16),
            pltpu.VMEM((chunk * TILE, bands * groups * wide // 2), jnp.bfloat16),
            pltpu.SMEM((timed,), jnp.int32),
            pltpu.SemaphoreType.DMA,
        ],
        compiler_params=pltpu.CompilerParams(vmem_limit_bytes=8 * groups * bands * slots * TILE * wide + 16 * MIB),
        cost_estimate=pl.CostEstimate(
            flops=2 * groups * bands * TILE * wide * (fresh * deep + chunk * timed * TILE // 2),
            bytes_accessed=2 * (other.size + sum(one.size for one in ready) + right.size),
            transcendentals=groups * bands * TILE * timed * wide // 2,
        ),
    )(sources, spread, other, left, right, *ready)


def join_kernel(tiles_ref, out_ref, frames_ref, sems):
    count, quarter, _ = out_ref.shape
    devices, rows, lanes = tiles_ref.shape
    columns = lanes // count
    strips = quarter // columns
    left = lax.broadcasted_iota(jnp.int32, (rows, lanes), 1) < columns
    copies = []
    for i in range(devices // strips):
        down = slice(i * rows, (i + 1) * rows)
        for strip in range(0, strips, 2):
            one = tiles_ref[strip * devices // strips + i].astype(jnp.float32)
            two = tiles_ref[(strip + 1) * devices // strips + i].astype(jnp.float32)
            here = slice(strip * columns, (strip + 2) * columns)
            frames_ref[0, down, here] = jnp.where(left, one, pltpu.roll(two, columns, 1))
            frames_ref[1, down, here] = jnp.where(left, pltpu.roll(one, columns, 1), two)
        for f in range(count):
            copies.append(pltpu.make_async_copy(frames_ref.at[f, down], out_ref.at[f, down], sems.at[f, i]))
            copies[-1].start()
    for copy in copies:
        copy.wait()


def join_tiles(tiles, quarter):
    strips = quarter * 2 // tiles.shape[2]
    out = jax.ShapeDtypeStruct((2, quarter, quarter), jnp.float32)
    return pl.pallas_call(
        join_kernel,
        in_specs=[pl.BlockSpec(memory_space=pltpu.VMEM)],
        out_specs=pl.BlockSpec(memory_space=pltpu.HBM),
        out_shape=out,
        scratch_shapes=[
            pltpu.VMEM(out.shape, jnp.float32),
            pltpu.SemaphoreType.DMA((2, tiles.shape[0] // strips)),
        ],
        compiler_params=pltpu.CompilerParams(vmem_limit_bytes=16 * MIB),
        cost_estimate=pl.CostEstimate(flops=tiles.size, bytes_accessed=6 * tiles.size, transcendentals=0),
    )(tiles)


def chunk_windows(mine, other, ref_frames, frames_here, history_chips, chips):
    mine = lax.all_gather(mine, "chunk", axis=0, tiled=True)
    other = lax.all_gather(other, "chunk", axis=0, tiled=True)
    height = mine.shape[1]
    core = lax.axis_index("core")
    device, f = ref_frames // frames_here, ref_frames % frames_here
    own = (device % CORES == core)[:, None, None]

    def pick(windows):
        return windows.reshape(windows.shape[0], height, frames_here, -1)[device // CORES, :, f]

    refer = jnp.where(own, pick(mine), pick(other))
    refer = refer.reshape(NSEG // frames_here, frames_here, height, -1)
    refer = jnp.swapaxes(refer, 1, 2).reshape(NSEG // frames_here, height, -1)

    def cut(windows):
        before = jnp.zeros((history_chips,) + windows.shape[1:], windows.dtype)
        windows = jnp.concatenate([before, windows])
        return lax.dynamic_slice_in_dim(windows, lax.axis_index("chunk") * chips, history_chips + chips)

    return cut(mine), cut(other), refer


def body(video_frames, segments, ref_pick, band_taps, *, chunks, slabs):
    frames_here, size, _ = video_frames.shape
    quarter = size // 4
    rows = quarter // (DOWN * CORES)
    columns = quarter * DOWN // slabs
    chunk = slabs * CORES * frames_here
    history = min(chunk * -(-(band_taps.shape[0] - 1) // chunk), segments.shape[0] - chunk)
    left = jnp.asarray(slab_left_table(rows, HALO, ORIENT))
    right = jnp.asarray(make_right_table(columns, HALO, ORIENT))
    half = slabs // 2
    turns = [k for pair in zip(range(half + DOWN, slabs), range(DOWN, half)) for k in pair]

    def exchange(array, k):
        return lax.ppermute(array, "slab", [(chip, chip ^ k) for chip in range(slabs)]) if k else array

    def swap(array):
        return lax.ppermute(array, "core", [(0, 1), (1, 0)])

    strip, *windows, beside, own = reduce_frames(video_frames, half, turns + [1, 0], slabs, HALO)
    spread, ref_frames, sources = time_tables(segments, ref_pick, band_taps, TILE, chunk, history)
    strip = exchange(strip, half)
    windows = [exchange(window, k) for k, window in zip(turns, windows)]
    across, following = pass_on(strip, beside, [spread])
    batches = [[across, exchange(following, 1)], windows + [own]]
    orders = [[half, 1, half + 1], turns + [0]]

    if chunks > 1:
        order = orders[0] + orders[1]

        def by_chip(windows):
            apart = jnp.moveaxis(windows.reshape(windows.shape[0], slabs, -1), 1, 0)
            return apart[jnp.asarray(np.argsort(order))[lax.axis_index("slab") ^ jnp.arange(slabs)]]

        def side_by_side(windows):
            return jnp.moveaxis(windows, 0, 1).reshape(windows.shape[1], -1)

        mine, other = cut_windows(batches[0] + batches[1], frames_here, HALO, [])
        chips = slabs + history // (CORES * frames_here)
        windows = chunk_windows(by_chip(mine), by_chip(swap(other)), ref_frames, frames_here, chips - slabs, slabs)
        mine, other, refer = [side_by_side(one) for one in windows]
        other = jnp.concatenate([other, refer], axis=1)
        ready = [own_coeffs(mine, left, right, rows, frames_here)]
        places = [(None, 0), (None, 1)]
    else:
        chips = len(orders[1])
        mine, other = cut_windows(batches[0], frames_here, HALO, [])
        ready = [own_coeffs(one, left, right, rows, frames_here) for one in (mine, swap(other))]
        mine, other = cut_windows(batches[1], frames_here, HALO, [])
        other = swap(other)
        ready.append(own_coeffs(mine, left, right, rows, frames_here))
        places = [(order, twin) for order in orders for twin in range(CORES)]
    motion = pixel_motion(sources, spread, ready, other, left, right, places, frames_here, chips, chunk, history)
    motion = lax.all_to_all(motion, ("slab", "core"), split_axis=0, concat_axis=0, tiled=True)
    return join_tiles(motion, quarter)


def solution(mesh):
    chips = mesh.shape["frames"] // CORES
    slabs = min(chips, QUART * DOWN // (2 * HALO))
    chunks = chips // slabs
    names = ("groups", "chunk", "slab", "core")
    cut = jax.sharding.Mesh(mesh.devices.reshape(mesh.shape["groups"], chunks, slabs, CORES), names)
    in_specs = (P(names, None, None), P("groups"), P("groups"), P())
    return jax.shard_map(
        functools.partial(body, chunks=chunks, slabs=slabs),
        mesh=cut, in_specs=in_specs, out_specs=P(names, None, None), check_vma=False,
    )
```

```python
import functools
import math

import jax
import jax.numpy as jnp
import numpy as np
from jax import lax
from jax.experimental import pallas as pl
from jax.experimental.pallas import tpu as pltpu
from jax.sharding import PartitionSpec as P

IMG = 1024
ORIENT = 4
NSEG = 4
QUART = 256


blur_sigma = 2.0
gabor_sigma = 2.0
wave_number = math.pi / 2.0
gabor_gain = 2.0

HALO = 32
TILE = 16
DOWN = 2
SHARE = 2
CORES = 2
MIB = 1024 * 1024


def envelope_of(offset_grid):
    return np.float32(gabor_gain) * np.exp(
        -offset_grid * offset_grid / np.float32(2.0 * gabor_sigma * gabor_sigma)
    )


def waves(orient):
    angles = np.arange(orient, dtype=np.float32) * np.float32(math.pi / orient)
    wave_x = np.float32(wave_number) * np.cos(angles)
    wave_y = np.float32(wave_number) * np.sin(angles)
    return wave_x, wave_y


def slab_left_table(rows, halo, orient):
    offset = (
        np.arange(rows + 2 * halo, dtype=np.float32)[None, :]
        - np.float32(halo)
        - np.arange(rows, dtype=np.float32)[:, None]
    )
    wave_y = waves(orient)[1]
    phase = wave_y[:, None, None] * offset[None]
    envelope = envelope_of(offset)[None]
    table = np.stack([envelope * np.cos(phase), envelope * np.sin(phase)], axis=1)
    return table.reshape(orient * 2 * rows, rows + 2 * halo).astype(jnp.bfloat16)


def make_right_table(columns, halo, orient):
    window = columns + 2 * halo
    offset = (
        np.arange(window, dtype=np.float32)[:, None] - np.float32(halo) - np.arange(columns, dtype=np.float32)[None, :]
    )
    wave_x = waves(orient)[0]
    phase_x = wave_x[:, None, None] * offset[None]
    envelope = envelope_of(offset)[None]
    real_part = envelope * np.cos(phase_x)
    imag_part = envelope * np.sin(phase_x)
    table = np.zeros((orient // SHARE, SHARE, 2, window, 2, SHARE, columns), np.float32)
    for o in range(orient):
        group, i = divmod(o, SHARE)
        table[group, i, 0, :, 0, i] = real_part[o]
        table[group, i, 0, :, 1, i] = imag_part[o]
        table[group, i, 1, :, 0, i] = -imag_part[o]
        table[group, i, 1, :, 1, i] = real_part[o]
    return table.reshape(orient // SHARE, SHARE * 2 * window, 2 * SHARE * columns).astype(jnp.bfloat16)


def down_sums(full_size, quarter):
    position = np.arange(quarter, dtype=np.float32)[:, None]
    columns = np.arange(full_size, dtype=np.float32)[None, :]
    offset_grid = columns - np.float32(4.0) * position - np.float32(1.5)
    weight = np.exp(-offset_grid * offset_grid / np.float32(2.0 * blur_sigma * blur_sigma))
    return np.sum(weight, axis=1)


def down_block(position, column, shape, axis, sums):
    positions = position + lax.broadcasted_iota(jnp.int32, shape, 1 - axis)
    columns = column + lax.broadcasted_iota(jnp.int32, shape, axis)
    offset_grid = columns.astype(jnp.float32) - 4.0 * positions.astype(jnp.float32) - 1.5
    weight = jnp.exp(-offset_grid * offset_grid / (2.0 * blur_sigma * blur_sigma))
    inner = float(sums[len(sums) // 2])
    line = position + lax.broadcasted_iota(jnp.int32, tuple(1 if i == axis else n for i, n in enumerate(shape)), 1 - axis)
    scale = jnp.full(line.shape, 1.0 / inner, jnp.float32)
    for q in range(position, min(position + shape[1 - axis], len(sums))):
        if abs(float(sums[q]) - inner) > 1e-7 * inner:
            scale = jnp.where(line == q, 1.0 / float(sums[q]), scale)
    return (weight * scale).astype(jnp.bfloat16)


def build_down(table_ref, axis):
    size, quarter = table_ref.shape[axis], table_ref.shape[1 - axis]
    sums = down_sums(size, quarter)
    table_ref[...] = jnp.zeros_like(table_ref)
    tall, wide = (128, 32)[axis], min(128, table_ref.shape[1])
    for row in range(0, table_ref.shape[0], tall):
        for lane in range(0, table_ref.shape[1], wide):
            position, column = (row, lane) if axis else (lane, row)
            positions, columns = (tall, wide) if axis else (wide, tall)
            if 4 * (position + positions - 1) + 30 >= column and 4 * position - 27 <= column + columns - 1:
                block = down_block(position, column, (tall, wide), axis, sums)
                table_ref[row : row + tall, lane : lane + wide] = block


def reduce_kernel(frames_ref, *refs, order, halo, block):
    out_refs = refs[: len(order)]
    picture_ref, down_t_ref, down_ref, half_ref, total_ref, strip_ref, sems = refs[len(order) :]
    count, size, _ = picture_ref.shape
    quarter = down_ref.shape[0]
    _, strips, _, lanes = strip_ref.shape
    columns = lanes - 2 * halo
    window = out_refs[0].shape[1]

    copies = []
    for f in range(count):
        for i in range(size // block):
            here = pl.ds(i * block, block)
            copy = pltpu.make_async_copy(frames_ref.at[f, here], picture_ref.at[f, here], sems.at[f, i])
            copy.start()
            copies.append(copy)
    build_down(down_t_ref, 0)

    me = lax.axis_index("slab")
    blocks = size // block
    for f in range(count):
        for i in range(blocks):
            copies[f * blocks + i].wait()
            here = slice(i * block, (i + 1) * block)
            half_ref[f, here] = jnp.dot(
                picture_ref[f, here], down_t_ref[...], preferred_element_type=jnp.float32
            ).astype(jnp.bfloat16)
            if f == i == 0:
                build_down(down_ref, 1)
        total_ref[f] = jnp.dot(down_ref[...], half_ref[f], preferred_element_type=jnp.float32)
        for strip in range(strips):
            begin = strip * columns - halo
            moved = pltpu.roll(total_ref[f], (-begin) % quarter, 1)[:, 0:lanes]
            column = begin + lax.broadcasted_iota(jnp.int32, (quarter, lanes), 1)
            inside = (column >= 0) & (column < quarter)
            strip_ref[f, strip] = jnp.where(inside, moved, 0.0).astype(jnp.bfloat16)
        for k, out_ref in zip(order, out_refs):
            slab = lax.bitwise_xor(me, k)
            begin = pl.multiple_of(lax.rem(slab, DOWN) * (quarter - window), TILE)
            out_ref[f] = strip_ref[f, slab // DOWN, pl.ds(begin, window)]


def reduce_frames(video_frames, order, halo):
    count, size, _ = video_frames.shape
    quarter = size // 4
    strips = len(order) // DOWN
    lanes = quarter // strips + 2 * halo
    block = size // 2
    out = jax.ShapeDtypeStruct((count, quarter // DOWN + halo, lanes), jnp.bfloat16)
    return pl.pallas_call(
        functools.partial(reduce_kernel, order=order, halo=halo, block=block),
        in_specs=[pl.BlockSpec(memory_space=pltpu.HBM)],
        out_specs=[pl.BlockSpec(memory_space=pltpu.VMEM)] * len(order),
        out_shape=[out] * len(order),
        scratch_shapes=[
            pltpu.VMEM((count, size, size), jnp.bfloat16),
            pltpu.VMEM((size, quarter), jnp.bfloat16),
            pltpu.VMEM((quarter, size), jnp.bfloat16),
            pltpu.VMEM((count, size, quarter), jnp.bfloat16),
            pltpu.VMEM((count, quarter, quarter), jnp.float32),
            pltpu.VMEM((count, strips, quarter, lanes), jnp.bfloat16),
            pltpu.SemaphoreType.DMA((count, size // block)),
        ],
        compiler_params=pltpu.CompilerParams(vmem_limit_bytes=52 * MIB),
        cost_estimate=pl.CostEstimate(
            flops=2 * count * size * quarter * (size + quarter),
            bytes_accessed=2 * count * size * size,
            transcendentals=0,
        ),
    )(video_frames)


def exchange_order(slabs):
    far = sorted(range(slabs // 2, slabs), key=lambda k: k % 2)
    near = list(range(2, slabs // 2))
    turns = far[:1] + near[:1] + far[1:3] + near[1:] + far[3:]
    return [0] + turns + [k for k in (1,) if k < slabs // 2]


def cut_kernel(*refs, many, halo):
    in_refs, (mine_ref, other_ref), padded_ref = refs[:many], refs[-3:-1], refs[-1]
    count, window, lanes = in_refs[0].shape
    height = mine_ref.shape[0]
    rows = height - 2 * halo
    wide = count * lanes
    me, core = lax.axis_index("slab"), lax.axis_index("core")
    edge = jnp.zeros((halo, count * lanes), jnp.bfloat16)
    padded_ref[0:halo] = edge
    padded_ref[halo + window :] = edge
    above = lax.rem(me, DOWN) * halo
    for n, in_ref in enumerate(in_refs):
        for f in range(count):
            padded_ref[halo : halo + window, f * lanes : (f + 1) * lanes] = in_ref[f]
        for out_ref, number in ((mine_ref, core), (other_ref, 1 - core)):
            place = pl.ds(pl.multiple_of(above + number * rows, TILE), height)
            out_ref[:, n * wide : (n + 1) * wide] = padded_ref[place]


def cut_windows(pieces, halo, after):
    count, window, lanes = pieces[0].shape
    height = (window - halo) // CORES + 2 * halo
    out = jax.ShapeDtypeStruct((height, len(pieces) * count * lanes), jnp.bfloat16)
    return pl.pallas_call(
        functools.partial(cut_kernel, many=len(pieces), halo=halo),
        in_specs=[pl.BlockSpec(memory_space=pltpu.VMEM)] * len(pieces) + [pl.BlockSpec(memory_space=pl.ANY)] * len(after),
        out_specs=[pl.BlockSpec(memory_space=pltpu.VMEM)] * 2,
        out_shape=[out, out],
        scratch_shapes=[pltpu.VMEM((window + 2 * halo, count * lanes), jnp.bfloat16)],
        compiler_params=pltpu.CompilerParams(vmem_limit_bytes=16 * MIB),
        cost_estimate=pl.CostEstimate(flops=0, bytes_accessed=8 * out.size, transcendentals=0),
    )(*pieces, *after)


def time_kernel(segments_ref, pick_ref, taps_ref, spread_ref, frame_ref, source_ref, *, history, frames, rows):
    chunk, timed = spread_ref.shape[0] // rows, spread_ref.shape[1] // rows
    nseg = pick_ref.shape[0]
    taps = taps_ref.shape[0]
    wide_out, wide_in = chunk * rows, timed * rows

    def count_one(t, totals):
        here = segments_ref[t]
        below = [total + (here < s).astype(jnp.int32) for s, total in enumerate(totals[0])]
        same = [total + (here == s).astype(jnp.int32) for s, total in enumerate(totals[1])]
        return tuple(below), tuple(same)

    zeros = tuple(jnp.int32(0) for _ in range(nseg))
    starts, counts = lax.fori_loop(0, frames, count_one, (zeros, zeros), unroll=8)
    for s in range(nseg):
        frame_ref[s] = starts[s] + lax.rem(pick_ref[s], counts[s])

    def source_one(slot, carry):
        if chunk == frames:
            source_ref[slot] = frame_ref[segments_ref[slot]]
        else:
            before = lax.axis_index("chunk") * chunk - history
            source_ref[slot] = timed + segments_ref[jnp.maximum(before + slot, 0)]
        return carry

    lax.fori_loop(0, timed, source_one, 0)

    lag = history + lax.broadcasted_iota(jnp.int32, (chunk, timed), 0) - lax.broadcasted_iota(
        jnp.int32, (chunk, timed), 1
    )
    if history:
        first = lax.axis_index("chunk") * chunk - history
        real = first + lax.broadcasted_iota(jnp.int32, (chunk, timed), 1) >= 0
        lag = jnp.where(real, lag, -1)
    matrix = jnp.zeros((chunk, timed), jnp.float32)
    for k in range(taps):
        matrix = jnp.where(lag == k, taps_ref[k], matrix)
    repeat_left = (
        lax.broadcasted_iota(jnp.int32, (wide_out, chunk), 0) // rows
        == lax.broadcasted_iota(jnp.int32, (wide_out, chunk), 1)
    ).astype(jnp.bfloat16)
    repeat_right = (
        lax.broadcasted_iota(jnp.int32, (timed, wide_in), 1) // rows
        == lax.broadcasted_iota(jnp.int32, (timed, wide_in), 0)
    ).astype(jnp.bfloat16)
    tall = jnp.dot(repeat_left, matrix.astype(jnp.bfloat16), preferred_element_type=jnp.float32)
    tall = tall.astype(jnp.bfloat16)
    piece = min(128, wide_out)
    for start in range(0, wide_out, piece):
        part = jnp.dot(tall[start : start + piece], repeat_right, preferred_element_type=jnp.float32)
        same_row = (
            lax.broadcasted_iota(jnp.int32, (piece, wide_in), 0) % rows
            == lax.broadcasted_iota(jnp.int32, (piece, wide_in), 1) % rows
        )
        spread_ref[start : start + piece] = jnp.where(same_row, part, 0.0).astype(jnp.bfloat16)


def time_tables(segments, ref_pick, band_taps, rows, chunk, history):
    frames = segments.shape[0]
    wide_out, wide_in = chunk * rows, (history + chunk) * rows
    smem = pl.BlockSpec(memory_space=pltpu.SMEM)
    return pl.pallas_call(
        functools.partial(time_kernel, history=history, frames=frames, rows=rows),
        in_specs=[smem] * 3,
        out_specs=[pl.BlockSpec(memory_space=pltpu.VMEM), smem, smem],
        out_shape=[
            jax.ShapeDtypeStruct((wide_out, wide_in), jnp.bfloat16),
            jax.ShapeDtypeStruct(ref_pick.shape, jnp.int32),
            jax.ShapeDtypeStruct((history + chunk,), jnp.int32),
        ],
        compiler_params=pltpu.CompilerParams(vmem_limit_bytes=16 * MIB),
        cost_estimate=pl.CostEstimate(
            flops=2 * wide_out * wide_in * chunk, bytes_accessed=2 * wide_out * wide_in, transcendentals=0
        ),
    )(segments, ref_pick, band_taps.astype(jnp.float32))


def filter_frames(window_ref, pair, left_ref, right_ref, stacked_ref, put):
    groups, deep, _ = right_ref.shape
    lanes = deep // (2 * SHARE)
    rows = left_ref.shape[0] // (2 * SHARE * groups)
    bands = rows // TILE
    frames = window_ref.shape[1] // lanes
    many = frames * TILE
    for first in range(0, frames, 8):
        last = min(first + 8, frames)
        stacked = jnp.dot(
            left_ref[...], window_ref[:, first * lanes : last * lanes], preferred_element_type=jnp.float32
        ).astype(jnp.bfloat16)
        for oz in range(2 * SHARE * groups):
            group, place = divmod(oz, 2 * SHARE)
            for band in range(bands):
                begin = oz * rows + band * TILE
                for f in range(first, last):
                    row = band * many + f * TILE
                    stacked_ref[group, row : row + TILE, place * lanes : (place + 1) * lanes] = stacked[
                        begin : begin + TILE, (f - first) * lanes : (f - first + 1) * lanes
                    ]
    block = pair * TILE
    total = bands * many
    step = min(512, total)
    for group in range(groups):
        for start in range(0, total, step):
            stop = min(start + step, total)
            coeff = jnp.dot(
                stacked_ref[group, start:stop], right_ref[group], preferred_element_type=jnp.float32
            ).astype(jnp.bfloat16)
            for place in range(start, stop, block):
                band, row = divmod(place, many)
                put(group, band, row // block, coeff[place - start : place - start + block])


def coeff_kernel(window_ref, left_ref, right_ref, coeff_ref, stacked_ref, *, pair):
    block = pair * TILE

    def put(group, band, i, values):
        coeff_ref[group, band, i * block : (i + 1) * block] = values

    filter_frames(window_ref, pair, left_ref, right_ref, stacked_ref, put)


def own_coeffs(windows, left, right, rows, frames_here):
    groups, deep, wide = right.shape
    vmem = pl.BlockSpec(memory_space=pltpu.VMEM)
    many = windows.shape[1] // (deep // (2 * SHARE)) * TILE
    out = jax.ShapeDtypeStruct((groups, rows // TILE, many, wide), jnp.bfloat16)
    return pl.pallas_call(
        functools.partial(coeff_kernel, pair=frames_here),
        in_specs=[vmem] * 3,
        out_specs=vmem,
        out_shape=out,
        scratch_shapes=[pltpu.VMEM((groups, rows // TILE * many, deep), jnp.bfloat16)],
        compiler_params=pltpu.CompilerParams(vmem_limit_bytes=8 * out.size + 16 * MIB),
        cost_estimate=pl.CostEstimate(
            flops=4 * out.size * deep, bytes_accessed=2 * (windows.size + out.size), transcendentals=0
        ),
    )(windows, left, right)


def pixel_kernel(
    sources_ref, spread_ref, other_ref, left_ref, right_ref, *refs, places, pair, chips, history
):
    ready_refs, (out_ref, stacked_ref, coeff_ref, phase_ref, filtered_ref, source_ref, sem) = refs[:-7], refs[-7:]
    sources = pltpu.make_async_copy(sources_ref, source_ref, sem)
    sources.start()
    groups, bands, _, wide = coeff_ref.shape
    half = wide // 2
    block = pair * TILE
    chunk = out_ref.shape[0] * pair
    timed = history + chunk
    core = lax.axis_index("core")

    def place_of(exchanges, twin, n):
        chip = n if exchanges is None else lax.bitwise_xor(lax.axis_index("slab"), exchanges[n])
        return pl.ds(pl.multiple_of((chip * CORES + lax.rem(core + twin, CORES)) * block, block), block)

    for ready_ref, (exchanges, twin) in zip(ready_refs, places):
        for n in range(ready_ref.shape[2] // block):
            for group in range(groups):
                for band in range(bands):
                    coeff_ref[group, band, place_of(exchanges, twin, n)] = ready_ref[group, band, n * block : (n + 1) * block]

    def put(group, band, i, values):
        if i < chips:
            place = place_of(*places[-1], i)
        else:
            place = slice(timed * TILE + (i - chips) * block, timed * TILE + (i - chips + 1) * block)
        coeff_ref[group, band, place] = values

    filter_frames(other_ref, pair, left_ref, right_ref, stacked_ref, put)

    sources.wait()

    def phase_one(slot, carry):
        place = pl.ds(pl.multiple_of(slot * TILE, TILE), TILE)
        source = source_ref[slot]
        refer = pl.ds(pl.multiple_of(source * TILE, TILE), TILE)
        for group in range(groups):
            for band in range(bands):
                coeff_real = coeff_ref[group, band, place, 0:half].astype(jnp.float32)
                coeff_imag = coeff_ref[group, band, place, half:wide].astype(jnp.float32)
                ref_real = coeff_ref[group, band, refer, 0:half].astype(jnp.float32)
                ref_imag = coeff_ref[group, band, refer, half:wide].astype(jnp.float32)
                prod_real = coeff_real * ref_real + coeff_imag * ref_imag
                prod_imag = coeff_imag * ref_real - coeff_real * ref_imag
                square = prod_real * prod_real + prod_imag * prod_imag + 1.0
                phase = (prod_imag * lax.rsqrt(square)).astype(jnp.bfloat16)
                lane = (band * groups + group) * half
                phase_ref[place, lane : lane + half] = phase
        return carry

    lax.fori_loop(0, timed, phase_one, 0, unroll=2)

    piece = min(128, chunk * TILE)
    columns = half // SHARE
    left_half = lax.broadcasted_iota(jnp.int32, (TILE, half), 1) < columns
    step = min(256, chunk * TILE)
    for start in range(0, chunk * TILE, step):
        stop = start + step
        filtered_ref[start:stop] = jnp.dot(
            spread_ref[start:stop, : history * TILE + stop],
            phase_ref[: history * TILE + stop],
            preferred_element_type=jnp.float32,
        ).astype(jnp.bfloat16)
    for band in range(bands):
        for start in range(0, chunk * TILE, piece):
            here = slice(history * TILE + start, history * TILE + start + piece)
            lane = band * groups * half
            filtered = filtered_ref[start : start + piece, lane : lane + groups * half].astype(jnp.float32)
            above = jnp.zeros((piece, half), jnp.float32)
            below = jnp.zeros((piece, half), jnp.float32)
            for group in range(groups):
                coeff_real = coeff_ref[group, band, here, 0:half].astype(jnp.float32)
                coeff_imag = coeff_ref[group, band, here, half:wide].astype(jnp.float32)
                amplitude = coeff_real * coeff_real + coeff_imag * coeff_imag
                above = above + amplitude * filtered[:, group * half : (group + 1) * half]
                below = below + amplitude
            for i in range(piece // block):
                sums = []
                for value in (above, below):
                    one, two = value[i * block : i * block + TILE], value[i * block + TILE : (i + 1) * block]
                    sums.append(jnp.where(left_half, one, two) + pltpu.roll(jnp.where(left_half, two, one), columns, 1))
                both = (sums[0] / (sums[1] + 1.0)).astype(out_ref.dtype)
                out_ref[start // block + i, band * TILE : (band + 1) * TILE] = both


def pixel_motion(sources, spread, ready, other, left, right, places, pair, chips, chunk, history):
    groups, bands, _, wide = ready[0].shape
    deep = right.shape[1]
    timed = history + chunk
    fresh = other.shape[1] // (deep // (2 * SHARE))
    slots = timed + fresh - chips * pair
    vmem = pl.BlockSpec(memory_space=pltpu.VMEM)
    return pl.pallas_call(
        functools.partial(pixel_kernel, places=places, pair=pair, chips=chips, history=history),
        in_specs=[pl.BlockSpec(memory_space=pl.ANY)] + [vmem] * (4 + len(ready)),
        out_specs=vmem,
        out_shape=jax.ShapeDtypeStruct((chunk // pair, bands * TILE, wide // 2), jnp.bfloat16),
        scratch_shapes=[
            pltpu.VMEM((groups, bands * fresh * TILE, deep), jnp.bfloat16),
            pltpu.VMEM((groups, bands, slots * TILE, wide), jnp.bfloat16),
            pltpu.VMEM((timed * TILE, bands * groups * wide // 2), jnp.bfloat16),
            pltpu.VMEM((chunk * TILE, bands * groups * wide // 2), jnp.bfloat16),
            pltpu.SMEM((timed,), jnp.int32),
            pltpu.SemaphoreType.DMA,
        ],
        compiler_params=pltpu.CompilerParams(vmem_limit_bytes=8 * groups * bands * slots * TILE * wide + 16 * MIB),
        cost_estimate=pl.CostEstimate(
            flops=2 * groups * bands * TILE * wide * (fresh * deep + chunk * timed * TILE // 2),
            bytes_accessed=2 * (other.size + sum(one.size for one in ready) + right.size),
            transcendentals=groups * bands * TILE * timed * wide // 2,
        ),
    )(sources, spread, other, left, right, *ready)


def join_kernel(tiles_ref, out_ref, frames_ref, sems):
    count, quarter, _ = out_ref.shape
    devices, rows, lanes = tiles_ref.shape
    columns = lanes // count
    strips = quarter // columns
    left = lax.broadcasted_iota(jnp.int32, (rows, lanes), 1) < columns
    copies = []
    for i in range(devices // strips):
        down = slice(i * rows, (i + 1) * rows)
        for strip in range(0, strips, 2):
            one = tiles_ref[strip * devices // strips + i].astype(jnp.float32)
            two = tiles_ref[(strip + 1) * devices // strips + i].astype(jnp.float32)
            here = slice(strip * columns, (strip + 2) * columns)
            frames_ref[0, down, here] = jnp.where(left, one, pltpu.roll(two, columns, 1))
            frames_ref[1, down, here] = jnp.where(left, pltpu.roll(one, columns, 1), two)
        for f in range(count):
            copies.append(pltpu.make_async_copy(frames_ref.at[f, down], out_ref.at[f, down], sems.at[f, i]))
            copies[-1].start()
    for copy in copies:
        copy.wait()


def join_tiles(tiles, quarter):
    strips = quarter * 2 // tiles.shape[2]
    out = jax.ShapeDtypeStruct((2, quarter, quarter), jnp.float32)
    return pl.pallas_call(
        join_kernel,
        in_specs=[pl.BlockSpec(memory_space=pltpu.VMEM)],
        out_specs=pl.BlockSpec(memory_space=pltpu.HBM),
        out_shape=out,
        scratch_shapes=[
            pltpu.VMEM(out.shape, jnp.float32),
            pltpu.SemaphoreType.DMA((2, tiles.shape[0] // strips)),
        ],
        compiler_params=pltpu.CompilerParams(vmem_limit_bytes=16 * MIB),
        cost_estimate=pl.CostEstimate(flops=tiles.size, bytes_accessed=6 * tiles.size, transcendentals=0),
    )(tiles)


def chunk_windows(mine, other, ref_frames, frames_here, history_chips, chips):
    mine = lax.all_gather(mine, "chunk", axis=0, tiled=True)
    other = lax.all_gather(other, "chunk", axis=0, tiled=True)
    height = mine.shape[1]
    core = lax.axis_index("core")
    device, f = ref_frames // frames_here, ref_frames % frames_here
    own = (device % CORES == core)[:, None, None]

    def pick(windows):
        return windows.reshape(windows.shape[0], height, frames_here, -1)[device // CORES, :, f]

    refer = jnp.where(own, pick(mine), pick(other))
    refer = refer.reshape(NSEG // frames_here, frames_here, height, -1)
    refer = jnp.swapaxes(refer, 1, 2).reshape(NSEG // frames_here, height, -1)

    def cut(windows):
        before = jnp.zeros((history_chips,) + windows.shape[1:], windows.dtype)
        windows = jnp.concatenate([before, windows])
        return lax.dynamic_slice_in_dim(windows, lax.axis_index("chunk") * chips, history_chips + chips)

    return cut(mine), cut(other), refer


def body(video_frames, segments, ref_pick, band_taps, *, chunks, slabs):
    frames_here, size, _ = video_frames.shape
    quarter = size // 4
    rows = quarter // (DOWN * CORES)
    columns = quarter * DOWN // slabs
    chunk = slabs * CORES * frames_here
    history = min(chunk * -(-(band_taps.shape[0] - 1) // chunk), segments.shape[0] - chunk)
    left = jnp.asarray(slab_left_table(rows, HALO, ORIENT))
    right = jnp.asarray(make_right_table(columns, HALO, ORIENT))
    order = exchange_order(slabs)

    def exchange(array, k):
        return lax.ppermute(array, "slab", [(chip, chip ^ k) for chip in range(slabs)]) if k else array

    def swap(array):
        return lax.ppermute(array, "core", [(0, 1), (1, 0)])

    windows = reduce_frames(video_frames, order, HALO)
    spread, ref_frames, sources = time_tables(segments, ref_pick, band_taps, TILE, chunk, history)
    pieces = [exchange(window, k) for k, window in zip(order, windows)]
    if chunks > 1:

        def by_chip(windows):
            apart = jnp.moveaxis(windows.reshape(windows.shape[0], slabs, -1), 1, 0)
            return apart[jnp.asarray(np.argsort(order))[lax.axis_index("slab") ^ jnp.arange(slabs)]]

        def side_by_side(windows):
            return jnp.moveaxis(windows, 0, 1).reshape(windows.shape[1], -1)

        mine, other = cut_windows(pieces, HALO, [])
        chips = slabs + history // (CORES * frames_here)
        windows = chunk_windows(by_chip(mine), by_chip(swap(other)), ref_frames, frames_here, chips - slabs, slabs)
        mine, other, refer = [side_by_side(one) for one in windows]
        other = jnp.concatenate([other, refer], axis=1)
        ready = [own_coeffs(mine, left, right, rows, frames_here)]
        places = [(None, 0), (None, 1)]
    else:
        first = slabs // 2
        chips = slabs - first
        mine, other = cut_windows(pieces[:first], HALO, [spread])
        ready = [own_coeffs(one, left, right, rows, frames_here) for one in (mine, swap(other))]
        mine, other = cut_windows(pieces[first:], HALO, ready[:1])
        other = swap(other)
        ready.append(own_coeffs(mine, left, right, rows, frames_here))
        places = [(exchanges, twin) for exchanges in (order[:first], order[first:]) for twin in range(CORES)]
    motion = pixel_motion(sources, spread, ready, other, left, right, places, frames_here, chips, chunk, history)
    motion = lax.all_to_all(motion, ("slab", "core"), split_axis=0, concat_axis=0, tiled=True)
    return join_tiles(motion, quarter)


def solution(mesh):
    chips = mesh.shape["frames"] // CORES
    slabs = min(chips, QUART * DOWN // (2 * HALO))
    chunks = chips // slabs
    names = ("groups", "chunk", "slab", "core")
    cut = jax.sharding.Mesh(mesh.devices.reshape(mesh.shape["groups"], chunks, slabs, CORES), names)
    in_specs = (P(names, None, None), P("groups"), P("groups"), P())
    return jax.shard_map(
        functools.partial(body, chunks=chunks, slabs=slabs),
        mesh=cut, in_specs=in_specs, out_specs=P(names, None, None), check_vma=False,
    )
```

```python
import functools
import math

import jax
import jax.numpy as jnp
import numpy as np
from jax import lax
from jax.experimental import pallas as pl
from jax.experimental.pallas import tpu as pltpu
from jax.sharding import PartitionSpec as P

IMG = 1024
ORIENT = 4
NSEG = 4
QUART = 256


blur_sigma = 2.0
gabor_sigma = 2.0
wave_number = math.pi / 2.0
gabor_gain = 2.0

HALO = 32
TILE = 16
DOWN = 2
SHARE = 2
CORES = 2
MIB = 1024 * 1024


def envelope_of(offset_grid):
    return np.float32(gabor_gain) * np.exp(
        -offset_grid * offset_grid / np.float32(2.0 * gabor_sigma * gabor_sigma)
    )


def waves(orient):
    angles = np.arange(orient, dtype=np.float32) * np.float32(math.pi / orient)
    wave_x = np.float32(wave_number) * np.cos(angles)
    wave_y = np.float32(wave_number) * np.sin(angles)
    return wave_x, wave_y


def slab_left_table(rows, halo, orient):
    offset = (
        np.arange(rows + 2 * halo, dtype=np.float32)[None, :]
        - np.float32(halo)
        - np.arange(rows, dtype=np.float32)[:, None]
    )
    wave_y = waves(orient)[1]
    phase = wave_y[:, None, None] * offset[None]
    envelope = envelope_of(offset)[None]
    table = np.stack([envelope * np.cos(phase), envelope * np.sin(phase)], axis=1)
    return table.reshape(orient * 2 * rows, rows + 2 * halo).astype(jnp.bfloat16)


def make_right_table(columns, halo, orient):
    window = columns + 2 * halo
    offset = (
        np.arange(window, dtype=np.float32)[:, None] - np.float32(halo) - np.arange(columns, dtype=np.float32)[None, :]
    )
    wave_x = waves(orient)[0]
    phase_x = wave_x[:, None, None] * offset[None]
    envelope = envelope_of(offset)[None]
    real_part = envelope * np.cos(phase_x)
    imag_part = envelope * np.sin(phase_x)
    table = np.zeros((orient // SHARE, SHARE, 2, window, 2, SHARE, columns), np.float32)
    for o in range(orient):
        group, i = divmod(o, SHARE)
        table[group, i, 0, :, 0, i] = real_part[o]
        table[group, i, 0, :, 1, i] = imag_part[o]
        table[group, i, 1, :, 0, i] = -imag_part[o]
        table[group, i, 1, :, 1, i] = real_part[o]
    return table.reshape(orient // SHARE, SHARE * 2 * window, 2 * SHARE * columns).astype(jnp.bfloat16)


def down_sums(full_size, quarter):
    position = np.arange(quarter, dtype=np.float32)[:, None]
    columns = np.arange(full_size, dtype=np.float32)[None, :]
    offset_grid = columns - np.float32(4.0) * position - np.float32(1.5)
    weight = np.exp(-offset_grid * offset_grid / np.float32(2.0 * blur_sigma * blur_sigma))
    return np.sum(weight, axis=1)


def down_block(position, column, shape, axis, sums):
    positions = position + lax.broadcasted_iota(jnp.int32, shape, 1 - axis)
    columns = column + lax.broadcasted_iota(jnp.int32, shape, axis)
    offset_grid = columns.astype(jnp.float32) - 4.0 * positions.astype(jnp.float32) - 1.5
    weight = jnp.exp(-offset_grid * offset_grid / (2.0 * blur_sigma * blur_sigma))
    inner = float(sums[len(sums) // 2])
    line = position + lax.broadcasted_iota(jnp.int32, tuple(1 if i == axis else n for i, n in enumerate(shape)), 1 - axis)
    scale = jnp.full(line.shape, 1.0 / inner, jnp.float32)
    for q in range(position, min(position + shape[1 - axis], len(sums))):
        if abs(float(sums[q]) - inner) > 1e-7 * inner:
            scale = jnp.where(line == q, 1.0 / float(sums[q]), scale)
    return (weight * scale).astype(jnp.bfloat16)


def build_down(table_ref, axis):
    size, quarter = table_ref.shape[axis], table_ref.shape[1 - axis]
    sums = down_sums(size, quarter)
    table_ref[...] = jnp.zeros_like(table_ref)
    tall, wide = (128, 32)[axis], min(128, table_ref.shape[1])
    for row in range(0, table_ref.shape[0], tall):
        for lane in range(0, table_ref.shape[1], wide):
            position, column = (row, lane) if axis else (lane, row)
            positions, columns = (tall, wide) if axis else (wide, tall)
            if 4 * (position + positions - 1) + 30 >= column and 4 * position - 27 <= column + columns - 1:
                block = down_block(position, column, (tall, wide), axis, sums)
                table_ref[row : row + tall, lane : lane + wide] = block


def reduce_kernel(frames_ref, *refs, order, halo, block):
    out_refs = refs[: len(order)]
    picture_ref, down_t_ref, down_ref, half_ref, total_ref, strip_ref, sems = refs[len(order) :]
    count, size, _ = picture_ref.shape
    quarter = down_ref.shape[0]
    _, strips, _, lanes = strip_ref.shape
    columns = lanes - 2 * halo
    window = out_refs[0].shape[1]

    copies = []
    for f in range(count):
        for i in range(size // block):
            here = pl.ds(i * block, block)
            copy = pltpu.make_async_copy(frames_ref.at[f, here], picture_ref.at[f, here], sems.at[f, i])
            copy.start()
            copies.append(copy)
    build_down(down_t_ref, 0)

    me = lax.axis_index("slab")
    blocks = size // block
    for f in range(count):
        for i in range(blocks):
            copies[f * blocks + i].wait()
        half_ref[f] = jnp.dot(picture_ref[f], down_t_ref[...], preferred_element_type=jnp.float32).astype(jnp.bfloat16)
        if f == 0:
            build_down(down_ref, 1)
        total_ref[f] = jnp.dot(down_ref[...], half_ref[f], preferred_element_type=jnp.float32)
        for strip in range(strips):
            begin = strip * columns - halo
            moved = pltpu.roll(total_ref[f], (-begin) % quarter, 1)[:, 0:lanes]
            column = begin + lax.broadcasted_iota(jnp.int32, (quarter, lanes), 1)
            inside = (column >= 0) & (column < quarter)
            strip_ref[f, strip] = jnp.where(inside, moved, 0.0).astype(jnp.bfloat16)
        for k, out_ref in zip(order, out_refs):
            slab = lax.bitwise_xor(me, k)
            begin = pl.multiple_of(lax.rem(slab, DOWN) * (quarter - window), TILE)
            out_ref[f] = strip_ref[f, slab // DOWN, pl.ds(begin, window)]


def reduce_frames(video_frames, order, halo):
    count, size, _ = video_frames.shape
    quarter = size // 4
    strips = len(order) // DOWN
    lanes = quarter // strips + 2 * halo
    block = size // 2
    out = jax.ShapeDtypeStruct((count, quarter // DOWN + halo, lanes), jnp.bfloat16)
    return pl.pallas_call(
        functools.partial(reduce_kernel, order=order, halo=halo, block=block),
        in_specs=[pl.BlockSpec(memory_space=pltpu.HBM)],
        out_specs=[pl.BlockSpec(memory_space=pltpu.VMEM)] * len(order),
        out_shape=[out] * len(order),
        scratch_shapes=[
            pltpu.VMEM((count, size, size), jnp.bfloat16),
            pltpu.VMEM((size, quarter), jnp.bfloat16),
            pltpu.VMEM((quarter, size), jnp.bfloat16),
            pltpu.VMEM((count, size, quarter), jnp.bfloat16),
            pltpu.VMEM((count, quarter, quarter), jnp.float32),
            pltpu.VMEM((count, strips, quarter, lanes), jnp.bfloat16),
            pltpu.SemaphoreType.DMA((count, size // block)),
        ],
        compiler_params=pltpu.CompilerParams(vmem_limit_bytes=52 * MIB),
        cost_estimate=pl.CostEstimate(
            flops=2 * count * size * quarter * (size + quarter),
            bytes_accessed=2 * count * size * size,
            transcendentals=0,
        ),
    )(video_frames)


def exchange_order(slabs):
    far = sorted(range(slabs // 2, slabs), key=lambda k: k % 2)
    near = list(range(2, slabs // 2))
    turns = [k for pair in zip(far, near) for k in pair]
    return [0] + turns + far[len(near) :] + [k for k in (1,) if k < slabs // 2]


def cut_kernel(*refs, many, halo):
    in_refs, (mine_ref, other_ref), padded_ref = refs[:many], refs[-3:-1], refs[-1]
    count, window, lanes = in_refs[0].shape
    height = mine_ref.shape[0]
    rows = height - 2 * halo
    wide = count * lanes
    me, core = lax.axis_index("slab"), lax.axis_index("core")
    edge = jnp.zeros((halo, count * lanes), jnp.bfloat16)
    padded_ref[0:halo] = edge
    padded_ref[halo + window :] = edge
    above = lax.rem(me, DOWN) * halo
    for n, in_ref in enumerate(in_refs):
        for f in range(count):
            padded_ref[halo : halo + window, f * lanes : (f + 1) * lanes] = in_ref[f]
        for out_ref, number in ((mine_ref, core), (other_ref, 1 - core)):
            place = pl.ds(pl.multiple_of(above + number * rows, TILE), height)
            out_ref[:, n * wide : (n + 1) * wide] = padded_ref[place]


def cut_windows(pieces, halo, after):
    count, window, lanes = pieces[0].shape
    height = (window - halo) // CORES + 2 * halo
    out = jax.ShapeDtypeStruct((height, len(pieces) * count * lanes), jnp.bfloat16)
    return pl.pallas_call(
        functools.partial(cut_kernel, many=len(pieces), halo=halo),
        in_specs=[pl.BlockSpec(memory_space=pltpu.VMEM)] * len(pieces) + [pl.BlockSpec(memory_space=pl.ANY)] * len(after),
        out_specs=[pl.BlockSpec(memory_space=pltpu.VMEM)] * 2,
        out_shape=[out, out],
        scratch_shapes=[pltpu.VMEM((window + 2 * halo, count * lanes), jnp.bfloat16)],
        compiler_params=pltpu.CompilerParams(vmem_limit_bytes=16 * MIB),
        cost_estimate=pl.CostEstimate(flops=0, bytes_accessed=8 * out.size, transcendentals=0),
    )(*pieces, *after)


def time_kernel(segments_ref, pick_ref, taps_ref, spread_ref, frame_ref, source_ref, *, history, frames, rows):
    chunk, timed = spread_ref.shape[0] // rows, spread_ref.shape[1] // rows
    nseg = pick_ref.shape[0]
    taps = taps_ref.shape[0]
    wide_out, wide_in = chunk * rows, timed * rows

    def count_one(t, totals):
        here = segments_ref[t]
        below = [total + (here < s).astype(jnp.int32) for s, total in enumerate(totals[0])]
        same = [total + (here == s).astype(jnp.int32) for s, total in enumerate(totals[1])]
        return tuple(below), tuple(same)

    zeros = tuple(jnp.int32(0) for _ in range(nseg))
    starts, counts = lax.fori_loop(0, frames, count_one, (zeros, zeros), unroll=8)
    for s in range(nseg):
        frame_ref[s] = starts[s] + lax.rem(pick_ref[s], counts[s])

    def source_one(slot, carry):
        if chunk == frames:
            source_ref[slot] = frame_ref[segments_ref[slot]]
        else:
            before = lax.axis_index("chunk") * chunk - history
            source_ref[slot] = timed + segments_ref[jnp.maximum(before + slot, 0)]
        return carry

    lax.fori_loop(0, timed, source_one, 0)

    lag = history + lax.broadcasted_iota(jnp.int32, (chunk, timed), 0) - lax.broadcasted_iota(
        jnp.int32, (chunk, timed), 1
    )
    if history:
        first = lax.axis_index("chunk") * chunk - history
        real = first + lax.broadcasted_iota(jnp.int32, (chunk, timed), 1) >= 0
        lag = jnp.where(real, lag, -1)
    matrix = jnp.zeros((chunk, timed), jnp.float32)
    for k in range(taps):
        matrix = jnp.where(lag == k, taps_ref[k], matrix)
    repeat_left = (
        lax.broadcasted_iota(jnp.int32, (wide_out, chunk), 0) // rows
        == lax.broadcasted_iota(jnp.int32, (wide_out, chunk), 1)
    ).astype(jnp.bfloat16)
    repeat_right = (
        lax.broadcasted_iota(jnp.int32, (timed, wide_in), 1) // rows
        == lax.broadcasted_iota(jnp.int32, (timed, wide_in), 0)
    ).astype(jnp.bfloat16)
    tall = jnp.dot(repeat_left, matrix.astype(jnp.bfloat16), preferred_element_type=jnp.float32)
    tall = tall.astype(jnp.bfloat16)
    piece = min(128, wide_out)
    for start in range(0, wide_out, piece):
        part = jnp.dot(tall[start : start + piece], repeat_right, preferred_element_type=jnp.float32)
        same_row = (
            lax.broadcasted_iota(jnp.int32, (piece, wide_in), 0) % rows
            == lax.broadcasted_iota(jnp.int32, (piece, wide_in), 1) % rows
        )
        spread_ref[start : start + piece] = jnp.where(same_row, part, 0.0).astype(jnp.bfloat16)


def time_tables(segments, ref_pick, band_taps, rows, chunk, history):
    frames = segments.shape[0]
    wide_out, wide_in = chunk * rows, (history + chunk) * rows
    smem = pl.BlockSpec(memory_space=pltpu.SMEM)
    return pl.pallas_call(
        functools.partial(time_kernel, history=history, frames=frames, rows=rows),
        in_specs=[smem] * 3,
        out_specs=[pl.BlockSpec(memory_space=pltpu.VMEM), smem, smem],
        out_shape=[
            jax.ShapeDtypeStruct((wide_out, wide_in), jnp.bfloat16),
            jax.ShapeDtypeStruct(ref_pick.shape, jnp.int32),
            jax.ShapeDtypeStruct((history + chunk,), jnp.int32),
        ],
        compiler_params=pltpu.CompilerParams(vmem_limit_bytes=16 * MIB),
        cost_estimate=pl.CostEstimate(
            flops=2 * wide_out * wide_in * chunk, bytes_accessed=2 * wide_out * wide_in, transcendentals=0
        ),
    )(segments, ref_pick, band_taps.astype(jnp.float32))


def filter_frames(window_ref, pair, left_ref, right_ref, stacked_ref, put):
    groups, deep, _ = right_ref.shape
    lanes = deep // (2 * SHARE)
    rows = left_ref.shape[0] // (2 * SHARE * groups)
    bands = rows // TILE
    frames = window_ref.shape[1] // lanes
    many = frames * TILE
    for first in range(0, frames, 8):
        last = min(first + 8, frames)
        stacked = jnp.dot(
            left_ref[...], window_ref[:, first * lanes : last * lanes], preferred_element_type=jnp.float32
        ).astype(jnp.bfloat16)
        for oz in range(2 * SHARE * groups):
            group, place = divmod(oz, 2 * SHARE)
            for band in range(bands):
                begin = oz * rows + band * TILE
                for f in range(first, last):
                    row = band * many + f * TILE
                    stacked_ref[group, row : row + TILE, place * lanes : (place + 1) * lanes] = stacked[
                        begin : begin + TILE, (f - first) * lanes : (f - first + 1) * lanes
                    ]
    block = pair * TILE
    total = bands * many
    step = min(512, total)
    for group in range(groups):
        for start in range(0, total, step):
            stop = min(start + step, total)
            coeff = jnp.dot(
                stacked_ref[group, start:stop], right_ref[group], preferred_element_type=jnp.float32
            ).astype(jnp.bfloat16)
            for place in range(start, stop, block):
                band, row = divmod(place, many)
                put(group, band, row // block, coeff[place - start : place - start + block])


def coeff_kernel(window_ref, left_ref, right_ref, coeff_ref, stacked_ref, *, pair):
    block = pair * TILE

    def put(group, band, i, values):
        coeff_ref[group, band, i * block : (i + 1) * block] = values

    filter_frames(window_ref, pair, left_ref, right_ref, stacked_ref, put)


def own_coeffs(windows, left, right, rows, frames_here):
    groups, deep, wide = right.shape
    vmem = pl.BlockSpec(memory_space=pltpu.VMEM)
    many = windows.shape[1] // (deep // (2 * SHARE)) * TILE
    out = jax.ShapeDtypeStruct((groups, rows // TILE, many, wide), jnp.bfloat16)
    return pl.pallas_call(
        functools.partial(coeff_kernel, pair=frames_here),
        in_specs=[vmem] * 3,
        out_specs=vmem,
        out_shape=out,
        scratch_shapes=[pltpu.VMEM((groups, rows // TILE * many, deep), jnp.bfloat16)],
        compiler_params=pltpu.CompilerParams(vmem_limit_bytes=8 * out.size + 16 * MIB),
        cost_estimate=pl.CostEstimate(
            flops=4 * out.size * deep, bytes_accessed=2 * (windows.size + out.size), transcendentals=0
        ),
    )(windows, left, right)


def pixel_kernel(
    sources_ref, spread_ref, other_ref, left_ref, right_ref, *refs, places, pair, chips, history
):
    ready_refs, (out_ref, stacked_ref, coeff_ref, phase_ref, filtered_ref, source_ref, sem) = refs[:-7], refs[-7:]
    sources = pltpu.make_async_copy(sources_ref, source_ref, sem)
    sources.start()
    groups, bands, _, wide = coeff_ref.shape
    half = wide // 2
    block = pair * TILE
    chunk = out_ref.shape[0] * pair
    timed = history + chunk
    core = lax.axis_index("core")

    def place_of(exchanges, twin, n):
        chip = n if exchanges is None else lax.bitwise_xor(lax.axis_index("slab"), exchanges[n])
        return pl.ds(pl.multiple_of((chip * CORES + lax.rem(core + twin, CORES)) * block, block), block)

    for ready_ref, (exchanges, twin) in zip(ready_refs, places):
        for n in range(ready_ref.shape[2] // block):
            for group in range(groups):
                for band in range(bands):
                    coeff_ref[group, band, place_of(exchanges, twin, n)] = ready_ref[group, band, n * block : (n + 1) * block]

    def put(group, band, i, values):
        if i < chips:
            place = place_of(*places[-1], i)
        else:
            place = slice(timed * TILE + (i - chips) * block, timed * TILE + (i - chips + 1) * block)
        coeff_ref[group, band, place] = values

    filter_frames(other_ref, pair, left_ref, right_ref, stacked_ref, put)

    sources.wait()

    def phase_one(slot, carry):
        place = pl.ds(pl.multiple_of(slot * TILE, TILE), TILE)
        source = source_ref[slot]
        refer = pl.ds(pl.multiple_of(source * TILE, TILE), TILE)
        for group in range(groups):
            for band in range(bands):
                coeff_real = coeff_ref[group, band, place, 0:half].astype(jnp.float32)
                coeff_imag = coeff_ref[group, band, place, half:wide].astype(jnp.float32)
                ref_real = coeff_ref[group, band, refer, 0:half].astype(jnp.float32)
                ref_imag = coeff_ref[group, band, refer, half:wide].astype(jnp.float32)
                prod_real = coeff_real * ref_real + coeff_imag * ref_imag
                prod_imag = coeff_imag * ref_real - coeff_real * ref_imag
                square = prod_real * prod_real + prod_imag * prod_imag + 1.0
                phase = (prod_imag * lax.rsqrt(square)).astype(jnp.bfloat16)
                lane = (band * groups + group) * half
                phase_ref[place, lane : lane + half] = phase
        return carry

    lax.fori_loop(0, timed, phase_one, 0, unroll=2)

    piece = min(128, chunk * TILE)
    columns = half // SHARE
    left_half = lax.broadcasted_iota(jnp.int32, (TILE, half), 1) < columns
    step = min(256, chunk * TILE)
    for start in range(0, chunk * TILE, step):
        stop = start + step
        filtered_ref[start:stop] = jnp.dot(
            spread_ref[start:stop, : history * TILE + stop],
            phase_ref[: history * TILE + stop],
            preferred_element_type=jnp.float32,
        ).astype(jnp.bfloat16)
    for band in range(bands):
        for start in range(0, chunk * TILE, piece):
            here = slice(history * TILE + start, history * TILE + start + piece)
            lane = band * groups * half
            filtered = filtered_ref[start : start + piece, lane : lane + groups * half].astype(jnp.float32)
            above = jnp.zeros((piece, half), jnp.float32)
            below = jnp.zeros((piece, half), jnp.float32)
            for group in range(groups):
                coeff_real = coeff_ref[group, band, here, 0:half].astype(jnp.float32)
                coeff_imag = coeff_ref[group, band, here, half:wide].astype(jnp.float32)
                amplitude = coeff_real * coeff_real + coeff_imag * coeff_imag
                above = above + amplitude * filtered[:, group * half : (group + 1) * half]
                below = below + amplitude
            for i in range(piece // block):
                sums = []
                for value in (above, below):
                    one, two = value[i * block : i * block + TILE], value[i * block + TILE : (i + 1) * block]
                    sums.append(jnp.where(left_half, one, two) + pltpu.roll(jnp.where(left_half, two, one), columns, 1))
                both = (sums[0] / (sums[1] + 1.0)).astype(out_ref.dtype)
                out_ref[start // block + i, band * TILE : (band + 1) * TILE] = both


def pixel_motion(sources, spread, ready, other, left, right, places, pair, chips, chunk, history):
    groups, bands, _, wide = ready[0].shape
    deep = right.shape[1]
    timed = history + chunk
    fresh = other.shape[1] // (deep // (2 * SHARE))
    slots = timed + fresh - chips * pair
    vmem = pl.BlockSpec(memory_space=pltpu.VMEM)
    return pl.pallas_call(
        functools.partial(pixel_kernel, places=places, pair=pair, chips=chips, history=history),
        in_specs=[pl.BlockSpec(memory_space=pl.ANY)] + [vmem] * (4 + len(ready)),
        out_specs=vmem,
        out_shape=jax.ShapeDtypeStruct((chunk // pair, bands * TILE, wide // 2), jnp.bfloat16),
        scratch_shapes=[
            pltpu.VMEM((groups, bands * fresh * TILE, deep), jnp.bfloat16),
            pltpu.VMEM((groups, bands, slots * TILE, wide), jnp.bfloat16),
            pltpu.VMEM((timed * TILE, bands * groups * wide // 2), jnp.bfloat16),
            pltpu.VMEM((chunk * TILE, bands * groups * wide // 2), jnp.bfloat16),
            pltpu.SMEM((timed,), jnp.int32),
            pltpu.SemaphoreType.DMA,
        ],
        compiler_params=pltpu.CompilerParams(vmem_limit_bytes=8 * groups * bands * slots * TILE * wide + 16 * MIB),
        cost_estimate=pl.CostEstimate(
            flops=2 * groups * bands * TILE * wide * (fresh * deep + chunk * timed * TILE // 2),
            bytes_accessed=2 * (other.size + sum(one.size for one in ready) + right.size),
            transcendentals=groups * bands * TILE * timed * wide // 2,
        ),
    )(sources, spread, other, left, right, *ready)


def join_kernel(tiles_ref, out_ref, frames_ref, sems):
    count, quarter, _ = out_ref.shape
    devices, rows, lanes = tiles_ref.shape
    columns = lanes // count
    strips = quarter // columns
    left = lax.broadcasted_iota(jnp.int32, (rows, lanes), 1) < columns
    copies = []
    for i in range(devices // strips):
        down = slice(i * rows, (i + 1) * rows)
        for strip in range(0, strips, 2):
            one = tiles_ref[strip * devices // strips + i].astype(jnp.float32)
            two = tiles_ref[(strip + 1) * devices // strips + i].astype(jnp.float32)
            here = slice(strip * columns, (strip + 2) * columns)
            frames_ref[0, down, here] = jnp.where(left, one, pltpu.roll(two, columns, 1))
            frames_ref[1, down, here] = jnp.where(left, pltpu.roll(one, columns, 1), two)
        for f in range(count):
            copies.append(pltpu.make_async_copy(frames_ref.at[f, down], out_ref.at[f, down], sems.at[f, i]))
            copies[-1].start()
    for copy in copies:
        copy.wait()


def join_tiles(tiles, quarter):
    strips = quarter * 2 // tiles.shape[2]
    out = jax.ShapeDtypeStruct((2, quarter, quarter), jnp.float32)
    return pl.pallas_call(
        join_kernel,
        in_specs=[pl.BlockSpec(memory_space=pltpu.VMEM)],
        out_specs=pl.BlockSpec(memory_space=pltpu.HBM),
        out_shape=out,
        scratch_shapes=[
            pltpu.VMEM(out.shape, jnp.float32),
            pltpu.SemaphoreType.DMA((2, tiles.shape[0] // strips)),
        ],
        compiler_params=pltpu.CompilerParams(vmem_limit_bytes=16 * MIB),
        cost_estimate=pl.CostEstimate(flops=tiles.size, bytes_accessed=6 * tiles.size, transcendentals=0),
    )(tiles)


def chunk_windows(mine, other, ref_frames, frames_here, history_chips, chips):
    mine = lax.all_gather(mine, "chunk", axis=0, tiled=True)
    other = lax.all_gather(other, "chunk", axis=0, tiled=True)
    height = mine.shape[1]
    core = lax.axis_index("core")
    device, f = ref_frames // frames_here, ref_frames % frames_here
    own = (device % CORES == core)[:, None, None]

    def pick(windows):
        return windows.reshape(windows.shape[0], height, frames_here, -1)[device // CORES, :, f]

    refer = jnp.where(own, pick(mine), pick(other))
    refer = refer.reshape(NSEG // frames_here, frames_here, height, -1)
    refer = jnp.swapaxes(refer, 1, 2).reshape(NSEG // frames_here, height, -1)

    def cut(windows):
        before = jnp.zeros((history_chips,) + windows.shape[1:], windows.dtype)
        windows = jnp.concatenate([before, windows])
        return lax.dynamic_slice_in_dim(windows, lax.axis_index("chunk") * chips, history_chips + chips)

    return cut(mine), cut(other), refer


def body(video_frames, segments, ref_pick, band_taps, *, chunks, slabs):
    frames_here, size, _ = video_frames.shape
    quarter = size // 4
    rows = quarter // (DOWN * CORES)
    columns = quarter * DOWN // slabs
    chunk = slabs * CORES * frames_here
    history = min(chunk * -(-(band_taps.shape[0] - 1) // chunk), segments.shape[0] - chunk)
    left = jnp.asarray(slab_left_table(rows, HALO, ORIENT))
    right = jnp.asarray(make_right_table(columns, HALO, ORIENT))
    order = exchange_order(slabs)

    def exchange(array, k):
        return lax.ppermute(array, "slab", [(chip, chip ^ k) for chip in range(slabs)]) if k else array

    def swap(array):
        return lax.ppermute(array, "core", [(0, 1), (1, 0)])

    windows = reduce_frames(video_frames, order, HALO)
    spread, ref_frames, sources = time_tables(segments, ref_pick, band_taps, TILE, chunk, history)
    pieces = [exchange(window, k) for k, window in zip(order, windows)]
    if chunks > 1:

        def by_chip(windows):
            apart = jnp.moveaxis(windows.reshape(windows.shape[0], slabs, -1), 1, 0)
            return apart[jnp.asarray(np.argsort(order))[lax.axis_index("slab") ^ jnp.arange(slabs)]]

        def side_by_side(windows):
            return jnp.moveaxis(windows, 0, 1).reshape(windows.shape[1], -1)

        mine, other = cut_windows(pieces, HALO, [])
        chips = slabs + history // (CORES * frames_here)
        windows = chunk_windows(by_chip(mine), by_chip(swap(other)), ref_frames, frames_here, chips - slabs, slabs)
        mine, other, refer = [side_by_side(one) for one in windows]
        other = jnp.concatenate([other, refer], axis=1)
        ready = [own_coeffs(mine, left, right, rows, frames_here)]
        places = [(None, 0), (None, 1)]
    else:
        first = slabs // 2
        chips = slabs - first
        mine, other = cut_windows(pieces[:first], HALO, [spread])
        ready = [own_coeffs(one, left, right, rows, frames_here) for one in (mine, swap(other))]
        mine, other = cut_windows(pieces[first:], HALO, ready[:1])
        other = swap(other)
        ready.append(own_coeffs(mine, left, right, rows, frames_here))
        places = [(exchanges, twin) for exchanges in (order[:first], order[first:]) for twin in range(CORES)]
    motion = pixel_motion(sources, spread, ready, other, left, right, places, frames_here, chips, chunk, history)
    motion = lax.all_to_all(motion, ("slab", "core"), split_axis=0, concat_axis=0, tiled=True)
    return join_tiles(motion, quarter)


def solution(mesh):
    chips = mesh.shape["frames"] // CORES
    slabs = min(chips, QUART * DOWN // (2 * HALO))
    chunks = chips // slabs
    names = ("groups", "chunk", "slab", "core")
    cut = jax.sharding.Mesh(mesh.devices.reshape(mesh.shape["groups"], chunks, slabs, CORES), names)
    in_specs = (P(names, None, None), P("groups"), P("groups"), P())
    return jax.shard_map(
        functools.partial(body, chunks=chunks, slabs=slabs),
        mesh=cut, in_specs=in_specs, out_specs=P(names, None, None), check_vma=False,
    )
```

```python
import functools
import math

import jax
import jax.numpy as jnp
import numpy as np
from jax import lax
from jax.experimental import pallas as pl
from jax.experimental.pallas import tpu as pltpu
from jax.sharding import PartitionSpec as P

IMG = 1024
ORIENT = 4
NSEG = 4
QUART = 256


blur_sigma = 2.0
gabor_sigma = 2.0
wave_number = math.pi / 2.0
gabor_gain = 2.0

HALO = 32
TILE = 16
DOWN = 2
SHARE = 2
CORES = 2
MIB = 1024 * 1024


def envelope_of(offset_grid):
    return np.float32(gabor_gain) * np.exp(
        -offset_grid * offset_grid / np.float32(2.0 * gabor_sigma * gabor_sigma)
    )


def waves(orient):
    angles = np.arange(orient, dtype=np.float32) * np.float32(math.pi / orient)
    wave_x = np.float32(wave_number) * np.cos(angles)
    wave_y = np.float32(wave_number) * np.sin(angles)
    return wave_x, wave_y


def slab_left_table(rows, halo, orient):
    offset = (
        np.arange(rows + 2 * halo, dtype=np.float32)[None, :]
        - np.float32(halo)
        - np.arange(rows, dtype=np.float32)[:, None]
    )
    wave_y = waves(orient)[1]
    phase = wave_y[:, None, None] * offset[None]
    envelope = envelope_of(offset)[None]
    table = np.stack([envelope * np.cos(phase), envelope * np.sin(phase)], axis=1)
    return table.reshape(orient * 2 * rows, rows + 2 * halo).astype(jnp.bfloat16)


def make_right_table(columns, halo, orient):
    window = columns + 2 * halo
    offset = (
        np.arange(window, dtype=np.float32)[:, None] - np.float32(halo) - np.arange(columns, dtype=np.float32)[None, :]
    )
    wave_x = waves(orient)[0]
    phase_x = wave_x[:, None, None] * offset[None]
    envelope = envelope_of(offset)[None]
    real_part = envelope * np.cos(phase_x)
    imag_part = envelope * np.sin(phase_x)
    table = np.zeros((orient // SHARE, SHARE, 2, window, 2, SHARE, columns), np.float32)
    for o in range(orient):
        group, i = divmod(o, SHARE)
        table[group, i, 0, :, 0, i] = real_part[o]
        table[group, i, 0, :, 1, i] = imag_part[o]
        table[group, i, 1, :, 0, i] = -imag_part[o]
        table[group, i, 1, :, 1, i] = real_part[o]
    return table.reshape(orient // SHARE, SHARE * 2 * window, 2 * SHARE * columns).astype(jnp.bfloat16)


def down_sums(full_size, quarter):
    position = np.arange(quarter, dtype=np.float32)[:, None]
    columns = np.arange(full_size, dtype=np.float32)[None, :]
    offset_grid = columns - np.float32(4.0) * position - np.float32(1.5)
    weight = np.exp(-offset_grid * offset_grid / np.float32(2.0 * blur_sigma * blur_sigma))
    return np.sum(weight, axis=1)


def down_block(position, column, shape, axis, sums):
    positions = position + lax.broadcasted_iota(jnp.int32, shape, 1 - axis)
    columns = column + lax.broadcasted_iota(jnp.int32, shape, axis)
    offset_grid = columns.astype(jnp.float32) - 4.0 * positions.astype(jnp.float32) - 1.5
    weight = jnp.exp(-offset_grid * offset_grid / (2.0 * blur_sigma * blur_sigma))
    inner = float(sums[len(sums) // 2])
    line = position + lax.broadcasted_iota(jnp.int32, tuple(1 if i == axis else n for i, n in enumerate(shape)), 1 - axis)
    scale = jnp.full(line.shape, 1.0 / inner, jnp.float32)
    for q in range(position, min(position + shape[1 - axis], len(sums))):
        if abs(float(sums[q]) - inner) > 1e-7 * inner:
            scale = jnp.where(line == q, 1.0 / float(sums[q]), scale)
    return (weight * scale).astype(jnp.bfloat16)


def build_down(table_ref, axis):
    size, quarter = table_ref.shape[axis], table_ref.shape[1 - axis]
    sums = down_sums(size, quarter)
    cut = np.abs(sums - sums[quarter // 2]) > 1e-7 * sums[quarter // 2]
    blocks = {}
    table_ref[...] = jnp.zeros_like(table_ref)
    tall, wide = (128, 32)[axis], min(128, table_ref.shape[1])
    for row in range(0, table_ref.shape[0], tall):
        for lane in range(0, table_ref.shape[1], wide):
            position, column = (row, lane) if axis else (lane, row)
            positions, columns = (tall, wide) if axis else (wide, tall)
            if 4 * (position + positions - 1) + 30 >= column and 4 * position - 27 <= column + columns - 1:
                kind = (column - 4 * position, position if cut[position : position + positions].any() else None)
                if kind not in blocks:
                    blocks[kind] = down_block(position, column, (tall, wide), axis, sums)
                table_ref[row : row + tall, lane : lane + wide] = blocks[kind]


def reduce_kernel(frames_ref, *refs, order, halo, block):
    out_refs = refs[: len(order)]
    picture_ref, down_t_ref, down_ref, half_ref, total_ref, strip_ref, sems = refs[len(order) :]
    count, size, _ = picture_ref.shape
    quarter = down_ref.shape[0]
    _, strips, _, lanes = strip_ref.shape
    columns = lanes - 2 * halo
    window = out_refs[0].shape[1]

    copies = []
    for f in range(count):
        for i in range(size // block):
            here = pl.ds(i * block, block)
            copy = pltpu.make_async_copy(frames_ref.at[f, here], picture_ref.at[f, here], sems.at[f, i])
            copy.start()
            copies.append(copy)
    build_down(down_t_ref, 0)

    me = lax.axis_index("slab")
    blocks = size // block
    for f in range(count):
        step = block if f == 0 else size
        for begin in range(0, size, step):
            for i in range(begin // block, (begin + step) // block):
                copies[f * blocks + i].wait()
            half_ref[f, begin : begin + step] = jnp.dot(
                picture_ref[f, begin : begin + step], down_t_ref[...], preferred_element_type=jnp.float32
            ).astype(jnp.bfloat16)
            if f == begin == 0:
                build_down(down_ref, 1)
        total_ref[f] = jnp.dot(down_ref[...], half_ref[f], preferred_element_type=jnp.float32)
        for strip in range(strips):
            begin = strip * columns - halo
            moved = pltpu.roll(total_ref[f], (-begin) % quarter, 1)[:, 0:lanes]
            column = begin + lax.broadcasted_iota(jnp.int32, (quarter, lanes), 1)
            inside = (column >= 0) & (column < quarter)
            strip_ref[f, strip] = jnp.where(inside, moved, 0.0).astype(jnp.bfloat16)
        for k, out_ref in zip(order, out_refs):
            slab = lax.bitwise_xor(me, k)
            begin = pl.multiple_of(lax.rem(slab, DOWN) * (quarter - window), TILE)
            out_ref[f] = strip_ref[f, slab // DOWN, pl.ds(begin, window)]


def reduce_frames(video_frames, order, halo):
    count, size, _ = video_frames.shape
    quarter = size // 4
    strips = len(order) // DOWN
    lanes = quarter // strips + 2 * halo
    block = size // 2
    out = jax.ShapeDtypeStruct((count, quarter // DOWN + halo, lanes), jnp.bfloat16)
    return pl.pallas_call(
        functools.partial(reduce_kernel, order=order, halo=halo, block=block),
        in_specs=[pl.BlockSpec(memory_space=pltpu.HBM)],
        out_specs=[pl.BlockSpec(memory_space=pltpu.VMEM)] * len(order),
        out_shape=[out] * len(order),
        scratch_shapes=[
            pltpu.VMEM((count, size, size), jnp.bfloat16),
            pltpu.VMEM((size, quarter), jnp.bfloat16),
            pltpu.VMEM((quarter, size), jnp.bfloat16),
            pltpu.VMEM((count, size, quarter), jnp.bfloat16),
            pltpu.VMEM((count, quarter, quarter), jnp.float32),
            pltpu.VMEM((count, strips, quarter, lanes), jnp.bfloat16),
            pltpu.SemaphoreType.DMA((count, size // block)),
        ],
        compiler_params=pltpu.CompilerParams(vmem_limit_bytes=52 * MIB),
        cost_estimate=pl.CostEstimate(
            flops=2 * count * size * quarter * (size + quarter),
            bytes_accessed=2 * count * size * size,
            transcendentals=0,
        ),
    )(video_frames)


def exchange_order(slabs):
    far = sorted(range(slabs // 2, slabs), key=lambda k: k % 2)
    near = list(range(2, slabs // 2))
    turns = [k for pair in zip(far, near) for k in pair]
    return [0] + turns + far[len(near) :] + [k for k in (1,) if k < slabs // 2]


def cut_kernel(*refs, many, halo):
    in_refs, (mine_ref, other_ref), padded_ref = refs[:many], refs[-3:-1], refs[-1]
    count, window, lanes = in_refs[0].shape
    height = mine_ref.shape[0]
    rows = height - 2 * halo
    wide = count * lanes
    me, core = lax.axis_index("slab"), lax.axis_index("core")
    edge = jnp.zeros((halo, count * lanes), jnp.bfloat16)
    padded_ref[0:halo] = edge
    padded_ref[halo + window :] = edge
    above = lax.rem(me, DOWN) * halo
    for n, in_ref in enumerate(in_refs):
        for f in range(count):
            padded_ref[halo : halo + window, f * lanes : (f + 1) * lanes] = in_ref[f]
        for out_ref, number in ((mine_ref, core), (other_ref, 1 - core)):
            place = pl.ds(pl.multiple_of(above + number * rows, TILE), height)
            out_ref[:, n * wide : (n + 1) * wide] = padded_ref[place]


def cut_windows(pieces, halo, after):
    count, window, lanes = pieces[0].shape
    height = (window - halo) // CORES + 2 * halo
    out = jax.ShapeDtypeStruct((height, len(pieces) * count * lanes), jnp.bfloat16)
    return pl.pallas_call(
        functools.partial(cut_kernel, many=len(pieces), halo=halo),
        in_specs=[pl.BlockSpec(memory_space=pltpu.VMEM)] * len(pieces) + [pl.BlockSpec(memory_space=pl.ANY)] * len(after),
        out_specs=[pl.BlockSpec(memory_space=pltpu.VMEM)] * 2,
        out_shape=[out, out],
        scratch_shapes=[pltpu.VMEM((window + 2 * halo, count * lanes), jnp.bfloat16)],
        compiler_params=pltpu.CompilerParams(vmem_limit_bytes=16 * MIB),
        cost_estimate=pl.CostEstimate(flops=0, bytes_accessed=8 * out.size, transcendentals=0),
    )(*pieces, *after)


def time_kernel(segments_ref, pick_ref, taps_ref, spread_ref, frame_ref, source_ref, *, history, frames, rows):
    chunk, timed = spread_ref.shape[0] // rows, spread_ref.shape[1] // rows
    nseg = pick_ref.shape[0]
    taps = taps_ref.shape[0]
    wide_out, wide_in = chunk * rows, timed * rows

    def count_one(t, totals):
        here = segments_ref[t]
        below = [total + (here < s).astype(jnp.int32) for s, total in enumerate(totals[0])]
        same = [total + (here == s).astype(jnp.int32) for s, total in enumerate(totals[1])]
        return tuple(below), tuple(same)

    zeros = tuple(jnp.int32(0) for _ in range(nseg))
    starts, counts = lax.fori_loop(0, frames, count_one, (zeros, zeros), unroll=8)
    for s in range(nseg):
        frame_ref[s] = starts[s] + lax.rem(pick_ref[s], counts[s])

    def source_one(slot, carry):
        if chunk == frames:
            source_ref[slot] = frame_ref[segments_ref[slot]]
        else:
            before = lax.axis_index("chunk") * chunk - history
            source_ref[slot] = timed + segments_ref[jnp.maximum(before + slot, 0)]
        return carry

    lax.fori_loop(0, timed, source_one, 0)

    lag = history + lax.broadcasted_iota(jnp.int32, (chunk, timed), 0) - lax.broadcasted_iota(
        jnp.int32, (chunk, timed), 1
    )
    if history:
        first = lax.axis_index("chunk") * chunk - history
        real = first + lax.broadcasted_iota(jnp.int32, (chunk, timed), 1) >= 0
        lag = jnp.where(real, lag, -1)
    matrix = jnp.zeros((chunk, timed), jnp.float32)
    for k in range(taps):
        matrix = jnp.where(lag == k, taps_ref[k], matrix)
    repeat_left = (
        lax.broadcasted_iota(jnp.int32, (wide_out, chunk), 0) // rows
        == lax.broadcasted_iota(jnp.int32, (wide_out, chunk), 1)
    ).astype(jnp.bfloat16)
    repeat_right = (
        lax.broadcasted_iota(jnp.int32, (timed, wide_in), 1) // rows
        == lax.broadcasted_iota(jnp.int32, (timed, wide_in), 0)
    ).astype(jnp.bfloat16)
    tall = jnp.dot(repeat_left, matrix.astype(jnp.bfloat16), preferred_element_type=jnp.float32)
    tall = tall.astype(jnp.bfloat16)
    piece = min(128, wide_out)
    for start in range(0, wide_out, piece):
        part = jnp.dot(tall[start : start + piece], repeat_right, preferred_element_type=jnp.float32)
        same_row = (
            lax.broadcasted_iota(jnp.int32, (piece, wide_in), 0) % rows
            == lax.broadcasted_iota(jnp.int32, (piece, wide_in), 1) % rows
        )
        spread_ref[start : start + piece] = jnp.where(same_row, part, 0.0).astype(jnp.bfloat16)


def time_tables(segments, ref_pick, band_taps, rows, chunk, history):
    frames = segments.shape[0]
    wide_out, wide_in = chunk * rows, (history + chunk) * rows
    smem = pl.BlockSpec(memory_space=pltpu.SMEM)
    return pl.pallas_call(
        functools.partial(time_kernel, history=history, frames=frames, rows=rows),
        in_specs=[smem] * 3,
        out_specs=[pl.BlockSpec(memory_space=pltpu.VMEM), smem, smem],
        out_shape=[
            jax.ShapeDtypeStruct((wide_out, wide_in), jnp.bfloat16),
            jax.ShapeDtypeStruct(ref_pick.shape, jnp.int32),
            jax.ShapeDtypeStruct((history + chunk,), jnp.int32),
        ],
        compiler_params=pltpu.CompilerParams(vmem_limit_bytes=16 * MIB),
        cost_estimate=pl.CostEstimate(
            flops=2 * wide_out * wide_in * chunk, bytes_accessed=2 * wide_out * wide_in, transcendentals=0
        ),
    )(segments, ref_pick, band_taps.astype(jnp.float32))


def filter_frames(window_ref, pair, left_ref, right_ref, stacked_ref, put):
    groups, deep, _ = right_ref.shape
    lanes = deep // (2 * SHARE)
    rows = left_ref.shape[0] // (2 * SHARE * groups)
    bands = rows // TILE
    frames = window_ref.shape[1] // lanes
    many = frames * TILE
    for first in range(0, frames, 8):
        last = min(first + 8, frames)
        stacked = jnp.dot(
            left_ref[...], window_ref[:, first * lanes : last * lanes], preferred_element_type=jnp.float32
        ).astype(jnp.bfloat16)
        for oz in range(2 * SHARE * groups):
            group, place = divmod(oz, 2 * SHARE)
            for band in range(bands):
                begin = oz * rows + band * TILE
                for f in range(first, last):
                    row = band * many + f * TILE
                    stacked_ref[group, row : row + TILE, place * lanes : (place + 1) * lanes] = stacked[
                        begin : begin + TILE, (f - first) * lanes : (f - first + 1) * lanes
                    ]
    block = pair * TILE
    total = bands * many
    step = min(512, total)
    for group in range(groups):
        for start in range(0, total, step):
            stop = min(start + step, total)
            coeff = jnp.dot(
                stacked_ref[group, start:stop], right_ref[group], preferred_element_type=jnp.float32
            ).astype(jnp.bfloat16)
            for place in range(start, stop, block):
                band, row = divmod(place, many)
                put(group, band, row // block, coeff[place - start : place - start + block])


def coeff_kernel(window_ref, left_ref, right_ref, coeff_ref, stacked_ref, *, pair):
    block = pair * TILE

    def put(group, band, i, values):
        coeff_ref[group, band, i * block : (i + 1) * block] = values

    filter_frames(window_ref, pair, left_ref, right_ref, stacked_ref, put)


def own_coeffs(windows, left, right, rows, frames_here):
    groups, deep, wide = right.shape
    vmem = pl.BlockSpec(memory_space=pltpu.VMEM)
    many = windows.shape[1] // (deep // (2 * SHARE)) * TILE
    out = jax.ShapeDtypeStruct((groups, rows // TILE, many, wide), jnp.bfloat16)
    return pl.pallas_call(
        functools.partial(coeff_kernel, pair=frames_here),
        in_specs=[vmem] * 3,
        out_specs=vmem,
        out_shape=out,
        scratch_shapes=[pltpu.VMEM((groups, rows // TILE * many, deep), jnp.bfloat16)],
        compiler_params=pltpu.CompilerParams(vmem_limit_bytes=8 * out.size + 16 * MIB),
        cost_estimate=pl.CostEstimate(
            flops=4 * out.size * deep, bytes_accessed=2 * (windows.size + out.size), transcendentals=0
        ),
    )(windows, left, right)


def pixel_kernel(
    sources_ref, spread_ref, other_ref, left_ref, right_ref, *refs, places, pair, chips, history
):
    ready_refs, (out_ref, stacked_ref, coeff_ref, phase_ref, filtered_ref, source_ref, sem) = refs[:-7], refs[-7:]
    sources = pltpu.make_async_copy(sources_ref, source_ref, sem)
    sources.start()
    groups, bands, _, wide = coeff_ref.shape
    half = wide // 2
    block = pair * TILE
    chunk = out_ref.shape[0] * pair
    timed = history + chunk
    core = lax.axis_index("core")

    def place_of(exchanges, twin, n):
        chip = n if exchanges is None else lax.bitwise_xor(lax.axis_index("slab"), exchanges[n])
        return pl.ds(pl.multiple_of((chip * CORES + lax.rem(core + twin, CORES)) * block, block), block)

    for ready_ref, (exchanges, twin) in zip(ready_refs, places):
        for n in range(ready_ref.shape[2] // block):
            for group in range(groups):
                for band in range(bands):
                    coeff_ref[group, band, place_of(exchanges, twin, n)] = ready_ref[group, band, n * block : (n + 1) * block]

    def put(group, band, i, values):
        if i < chips:
            place = place_of(*places[-1], i)
        else:
            place = slice(timed * TILE + (i - chips) * block, timed * TILE + (i - chips + 1) * block)
        coeff_ref[group, band, place] = values

    filter_frames(other_ref, pair, left_ref, right_ref, stacked_ref, put)

    sources.wait()

    def phase_one(slot, carry):
        place = pl.ds(pl.multiple_of(slot * TILE, TILE), TILE)
        source = source_ref[slot]
        refer = pl.ds(pl.multiple_of(source * TILE, TILE), TILE)
        for group in range(groups):
            for band in range(bands):
                coeff_real = coeff_ref[group, band, place, 0:half].astype(jnp.float32)
                coeff_imag = coeff_ref[group, band, place, half:wide].astype(jnp.float32)
                ref_real = coeff_ref[group, band, refer, 0:half].astype(jnp.float32)
                ref_imag = coeff_ref[group, band, refer, half:wide].astype(jnp.float32)
                prod_real = coeff_real * ref_real + coeff_imag * ref_imag
                prod_imag = coeff_imag * ref_real - coeff_real * ref_imag
                square = prod_real * prod_real + prod_imag * prod_imag + 1.0
                phase = (prod_imag * lax.rsqrt(square)).astype(jnp.bfloat16)
                lane = (band * groups + group) * half
                phase_ref[place, lane : lane + half] = phase
        return carry

    lax.fori_loop(0, timed, phase_one, 0, unroll=2)

    piece = min(128, chunk * TILE)
    columns = half // SHARE
    left_half = lax.broadcasted_iota(jnp.int32, (TILE, half), 1) < columns
    step = min(256, chunk * TILE)
    for start in range(0, chunk * TILE, step):
        stop = start + step
        filtered_ref[start:stop] = jnp.dot(
            spread_ref[start:stop, : history * TILE + stop],
            phase_ref[: history * TILE + stop],
            preferred_element_type=jnp.float32,
        ).astype(jnp.bfloat16)
    for band in range(bands):
        for start in range(0, chunk * TILE, piece):
            here = slice(history * TILE + start, history * TILE + start + piece)
            lane = band * groups * half
            filtered = filtered_ref[start : start + piece, lane : lane + groups * half].astype(jnp.float32)
            above = jnp.zeros((piece, half), jnp.float32)
            below = jnp.zeros((piece, half), jnp.float32)
            for group in range(groups):
                coeff_real = coeff_ref[group, band, here, 0:half].astype(jnp.float32)
                coeff_imag = coeff_ref[group, band, here, half:wide].astype(jnp.float32)
                amplitude = coeff_real * coeff_real + coeff_imag * coeff_imag
                above = above + amplitude * filtered[:, group * half : (group + 1) * half]
                below = below + amplitude
            for i in range(piece // block):
                sums = []
                for value in (above, below):
                    one, two = value[i * block : i * block + TILE], value[i * block + TILE : (i + 1) * block]
                    sums.append(jnp.where(left_half, one, two) + pltpu.roll(jnp.where(left_half, two, one), columns, 1))
                both = (sums[0] / (sums[1] + 1.0)).astype(out_ref.dtype)
                out_ref[start // block + i, band * TILE : (band + 1) * TILE] = both


def pixel_motion(sources, spread, ready, other, left, right, places, pair, chips, chunk, history):
    groups, bands, _, wide = ready[0].shape
    deep = right.shape[1]
    timed = history + chunk
    fresh = other.shape[1] // (deep // (2 * SHARE))
    slots = timed + fresh - chips * pair
    vmem = pl.BlockSpec(memory_space=pltpu.VMEM)
    return pl.pallas_call(
        functools.partial(pixel_kernel, places=places, pair=pair, chips=chips, history=history),
        in_specs=[pl.BlockSpec(memory_space=pl.ANY)] + [vmem] * (4 + len(ready)),
        out_specs=vmem,
        out_shape=jax.ShapeDtypeStruct((chunk // pair, bands * TILE, wide // 2), jnp.bfloat16),
        scratch_shapes=[
            pltpu.VMEM((groups, bands * fresh * TILE, deep), jnp.bfloat16),
            pltpu.VMEM((groups, bands, slots * TILE, wide), jnp.bfloat16),
            pltpu.VMEM((timed * TILE, bands * groups * wide // 2), jnp.bfloat16),
            pltpu.VMEM((chunk * TILE, bands * groups * wide // 2), jnp.bfloat16),
            pltpu.SMEM((timed,), jnp.int32),
            pltpu.SemaphoreType.DMA,
        ],
        compiler_params=pltpu.CompilerParams(vmem_limit_bytes=8 * groups * bands * slots * TILE * wide + 16 * MIB),
        cost_estimate=pl.CostEstimate(
            flops=2 * groups * bands * TILE * wide * (fresh * deep + chunk * timed * TILE // 2),
            bytes_accessed=2 * (other.size + sum(one.size for one in ready) + right.size),
            transcendentals=groups * bands * TILE * timed * wide // 2,
        ),
    )(sources, spread, other, left, right, *ready)


def join_kernel(tiles_ref, out_ref, frames_ref, sems):
    count, quarter, _ = out_ref.shape
    devices, rows, lanes = tiles_ref.shape
    columns = lanes // count
    strips = quarter // columns
    left = lax.broadcasted_iota(jnp.int32, (rows, lanes), 1) < columns
    copies = []
    for i in range(devices // strips):
        down = slice(i * rows, (i + 1) * rows)
        for strip in range(0, strips, 2):
            one = tiles_ref[strip * devices // strips + i].astype(jnp.float32)
            two = tiles_ref[(strip + 1) * devices // strips + i].astype(jnp.float32)
            here = slice(strip * columns, (strip + 2) * columns)
            frames_ref[0, down, here] = jnp.where(left, one, pltpu.roll(two, columns, 1))
            frames_ref[1, down, here] = jnp.where(left, pltpu.roll(one, columns, 1), two)
        for f in range(count):
            copies.append(pltpu.make_async_copy(frames_ref.at[f, down], out_ref.at[f, down], sems.at[f, i]))
            copies[-1].start()
    for copy in copies:
        copy.wait()


def join_tiles(tiles, quarter):
    strips = quarter * 2 // tiles.shape[2]
    out = jax.ShapeDtypeStruct((2, quarter, quarter), jnp.float32)
    return pl.pallas_call(
        join_kernel,
        in_specs=[pl.BlockSpec(memory_space=pltpu.VMEM)],
        out_specs=pl.BlockSpec(memory_space=pltpu.HBM),
        out_shape=out,
        scratch_shapes=[
            pltpu.VMEM(out.shape, jnp.float32),
            pltpu.SemaphoreType.DMA((2, tiles.shape[0] // strips)),
        ],
        compiler_params=pltpu.CompilerParams(vmem_limit_bytes=16 * MIB),
        cost_estimate=pl.CostEstimate(flops=tiles.size, bytes_accessed=6 * tiles.size, transcendentals=0),
    )(tiles)


def chunk_windows(mine, other, ref_frames, frames_here, history_chips, chips):
    mine = lax.all_gather(mine, "chunk", axis=0, tiled=True)
    other = lax.all_gather(other, "chunk", axis=0, tiled=True)
    height = mine.shape[1]
    core = lax.axis_index("core")
    device, f = ref_frames // frames_here, ref_frames % frames_here
    own = (device % CORES == core)[:, None, None]

    def pick(windows):
        return windows.reshape(windows.shape[0], height, frames_here, -1)[device // CORES, :, f]

    refer = jnp.where(own, pick(mine), pick(other))
    refer = refer.reshape(NSEG // frames_here, frames_here, height, -1)
    refer = jnp.swapaxes(refer, 1, 2).reshape(NSEG // frames_here, height, -1)

    def cut(windows):
        before = jnp.zeros((history_chips,) + windows.shape[1:], windows.dtype)
        windows = jnp.concatenate([before, windows])
        return lax.dynamic_slice_in_dim(windows, lax.axis_index("chunk") * chips, history_chips + chips)

    return cut(mine), cut(other), refer


def body(video_frames, segments, ref_pick, band_taps, *, chunks, slabs):
    frames_here, size, _ = video_frames.shape
    quarter = size // 4
    rows = quarter // (DOWN * CORES)
    columns = quarter * DOWN // slabs
    chunk = slabs * CORES * frames_here
    history = min(chunk * -(-(band_taps.shape[0] - 1) // chunk), segments.shape[0] - chunk)
    left = jnp.asarray(slab_left_table(rows, HALO, ORIENT))
    right = jnp.asarray(make_right_table(columns, HALO, ORIENT))
    order = exchange_order(slabs)

    def exchange(array, k):
        return lax.ppermute(array, "slab", [(chip, chip ^ k) for chip in range(slabs)]) if k else array

    def swap(array):
        return lax.ppermute(array, "core", [(0, 1), (1, 0)])

    windows = reduce_frames(video_frames, order, HALO)
    spread, ref_frames, sources = time_tables(segments, ref_pick, band_taps, TILE, chunk, history)
    pieces = [exchange(window, k) for k, window in zip(order, windows)]
    if chunks > 1:

        def by_chip(windows):
            apart = jnp.moveaxis(windows.reshape(windows.shape[0], slabs, -1), 1, 0)
            return apart[jnp.asarray(np.argsort(order))[lax.axis_index("slab") ^ jnp.arange(slabs)]]

        def side_by_side(windows):
            return jnp.moveaxis(windows, 0, 1).reshape(windows.shape[1], -1)

        mine, other = cut_windows(pieces, HALO, [])
        chips = slabs + history // (CORES * frames_here)
        windows = chunk_windows(by_chip(mine), by_chip(swap(other)), ref_frames, frames_here, chips - slabs, slabs)
        mine, other, refer = [side_by_side(one) for one in windows]
        other = jnp.concatenate([other, refer], axis=1)
        ready = [own_coeffs(mine, left, right, rows, frames_here)]
        places = [(None, 0), (None, 1)]
    else:
        first = slabs // 2
        chips = slabs - first
        mine, other = cut_windows(pieces[:first], HALO, [spread])
        ready = [own_coeffs(one, left, right, rows, frames_here) for one in (mine, swap(other))]
        mine, other = cut_windows(pieces[first:], HALO, ready[:1])
        other = swap(other)
        ready.append(own_coeffs(mine, left, right, rows, frames_here))
        places = [(exchanges, twin) for exchanges in (order[:first], order[first:]) for twin in range(CORES)]
    motion = pixel_motion(sources, spread, ready, other, left, right, places, frames_here, chips, chunk, history)
    motion = lax.all_to_all(motion, ("slab", "core"), split_axis=0, concat_axis=0, tiled=True)
    return join_tiles(motion, quarter)


def solution(mesh):
    chips = mesh.shape["frames"] // CORES
    slabs = min(chips, QUART * DOWN // (2 * HALO))
    chunks = chips // slabs
    names = ("groups", "chunk", "slab", "core")
    cut = jax.sharding.Mesh(mesh.devices.reshape(mesh.shape["groups"], chunks, slabs, CORES), names)
    in_specs = (P(names, None, None), P("groups"), P("groups"), P())
    return jax.shard_map(
        functools.partial(body, chunks=chunks, slabs=slabs),
        mesh=cut, in_specs=in_specs, out_specs=P(names, None, None), check_vma=False,
    )
```

```python
import functools
import math

import jax
import jax.numpy as jnp
import numpy as np
from jax import lax
from jax.experimental import pallas as pl
from jax.experimental.pallas import tpu as pltpu
from jax.sharding import PartitionSpec as P

IMG = 1024
ORIENT = 4
NSEG = 4
QUART = 256


blur_sigma = 2.0
gabor_sigma = 2.0
wave_number = math.pi / 2.0
gabor_gain = 2.0

HALO = 32
TILE = 16
DOWN = 2
SHARE = 2
CORES = 2
MIB = 1024 * 1024


def envelope_of(offset_grid):
    return np.float32(gabor_gain) * np.exp(
        -offset_grid * offset_grid / np.float32(2.0 * gabor_sigma * gabor_sigma)
    )


def waves(orient):
    angles = np.arange(orient, dtype=np.float32) * np.float32(math.pi / orient)
    wave_x = np.float32(wave_number) * np.cos(angles)
    wave_y = np.float32(wave_number) * np.sin(angles)
    return wave_x, wave_y


def slab_left_table(rows, halo, orient):
    offset = (
        np.arange(rows + 2 * halo, dtype=np.float32)[None, :]
        - np.float32(halo)
        - np.arange(rows, dtype=np.float32)[:, None]
    )
    wave_y = waves(orient)[1]
    phase = wave_y[:, None, None] * offset[None]
    envelope = envelope_of(offset)[None]
    table = np.stack([envelope * np.cos(phase), envelope * np.sin(phase)], axis=1)
    return table.reshape(orient * 2 * rows, rows + 2 * halo).astype(jnp.bfloat16)


def make_right_table(columns, halo, orient):
    window = columns + 2 * halo
    offset = (
        np.arange(window, dtype=np.float32)[:, None] - np.float32(halo) - np.arange(columns, dtype=np.float32)[None, :]
    )
    wave_x = waves(orient)[0]
    phase_x = wave_x[:, None, None] * offset[None]
    envelope = envelope_of(offset)[None]
    real_part = envelope * np.cos(phase_x)
    imag_part = envelope * np.sin(phase_x)
    table = np.zeros((orient // SHARE, SHARE, 2, window, 2, SHARE, columns), np.float32)
    for o in range(orient):
        group, i = divmod(o, SHARE)
        table[group, i, 0, :, 0, i] = real_part[o]
        table[group, i, 0, :, 1, i] = imag_part[o]
        table[group, i, 1, :, 0, i] = -imag_part[o]
        table[group, i, 1, :, 1, i] = real_part[o]
    return table.reshape(orient // SHARE, SHARE * 2 * window, 2 * SHARE * columns).astype(jnp.bfloat16)


def down_sums(full_size, quarter):
    position = np.arange(quarter, dtype=np.float32)[:, None]
    columns = np.arange(full_size, dtype=np.float32)[None, :]
    offset_grid = columns - np.float32(4.0) * position - np.float32(1.5)
    weight = np.exp(-offset_grid * offset_grid / np.float32(2.0 * blur_sigma * blur_sigma))
    return np.sum(weight, axis=1)


def down_block(position, column, shape, axis, sums):
    positions = position + lax.broadcasted_iota(jnp.int32, shape, 1 - axis)
    columns = column + lax.broadcasted_iota(jnp.int32, shape, axis)
    offset_grid = columns.astype(jnp.float32) - 4.0 * positions.astype(jnp.float32) - 1.5
    weight = jnp.exp(-offset_grid * offset_grid / (2.0 * blur_sigma * blur_sigma))
    inner = float(sums[len(sums) // 2])
    line = position + lax.broadcasted_iota(jnp.int32, tuple(1 if i == axis else n for i, n in enumerate(shape)), 1 - axis)
    scale = jnp.full(line.shape, 1.0 / inner, jnp.float32)
    for q in range(position, min(position + shape[1 - axis], len(sums))):
        if abs(float(sums[q]) - inner) > 1e-7 * inner:
            scale = jnp.where(line == q, 1.0 / float(sums[q]), scale)
    return (weight * scale).astype(jnp.bfloat16)


def build_down(table_ref, axis):
    size, quarter = table_ref.shape[axis], table_ref.shape[1 - axis]
    sums = down_sums(size, quarter)
    cut = np.abs(sums - sums[quarter // 2]) > 1e-7 * sums[quarter // 2]
    blocks = {}
    table_ref[...] = jnp.zeros_like(table_ref)
    tall, wide = (128, 32)[axis], min(128, table_ref.shape[1])
    for row in range(0, table_ref.shape[0], tall):
        for lane in range(0, table_ref.shape[1], wide):
            position, column = (row, lane) if axis else (lane, row)
            positions, columns = (tall, wide) if axis else (wide, tall)
            if 4 * (position + positions - 1) + 30 >= column and 4 * position - 27 <= column + columns - 1:
                kind = (column - 4 * position, position if cut[position : position + positions].any() else None)
                if kind not in blocks:
                    blocks[kind] = down_block(position, column, (tall, wide), axis, sums)
                table_ref[row : row + tall, lane : lane + wide] = blocks[kind]


def reduce_kernel(frames_ref, *refs, order, halo, block):
    out_refs = refs[: len(order)]
    picture_ref, down_t_ref, down_ref, half_ref, total_ref, strip_ref, sems = refs[len(order) :]
    count, size, _ = picture_ref.shape
    quarter = down_ref.shape[0]
    _, strips, _, lanes = strip_ref.shape
    columns = lanes - 2 * halo
    window = out_refs[0].shape[1]

    copies = []
    for f in range(count):
        for i in range(size // block):
            here = pl.ds(i * block, block)
            copy = pltpu.make_async_copy(frames_ref.at[f, here], picture_ref.at[f, here], sems.at[f, i])
            copy.start()
            copies.append(copy)
    build_down(down_t_ref, 0)

    me = lax.axis_index("slab")
    blocks = size // block
    for f in range(count):
        step = block if f == 0 else size
        for begin in range(0, size, step):
            for i in range(begin // block, (begin + step) // block):
                copies[f * blocks + i].wait()
            half_ref[f, begin : begin + step] = jnp.dot(
                picture_ref[f, begin : begin + step], down_t_ref[...], preferred_element_type=jnp.float32
            ).astype(jnp.bfloat16)
            if f == begin == 0:
                build_down(down_ref, 1)
        total_ref[f] = jnp.dot(down_ref[...], half_ref[f], preferred_element_type=jnp.float32)
        for strip in range(strips):
            begin = strip * columns - halo
            moved = pltpu.roll(total_ref[f], (-begin) % quarter, 1)[:, 0:lanes]
            column = begin + lax.broadcasted_iota(jnp.int32, (quarter, lanes), 1)
            inside = (column >= 0) & (column < quarter)
            strip_ref[f, strip] = jnp.where(inside, moved, 0.0).astype(jnp.bfloat16)
        for k, out_ref in zip(order, out_refs):
            slab = lax.bitwise_xor(me, k)
            begin = pl.multiple_of(lax.rem(slab, DOWN) * (quarter - window), TILE)
            out_ref[f] = strip_ref[f, slab // DOWN, pl.ds(begin, window)]


def reduce_frames(video_frames, order, halo):
    count, size, _ = video_frames.shape
    quarter = size // 4
    strips = len(order) // DOWN
    lanes = quarter // strips + 2 * halo
    block = size // 2
    out = jax.ShapeDtypeStruct((count, quarter // DOWN + halo, lanes), jnp.bfloat16)
    return pl.pallas_call(
        functools.partial(reduce_kernel, order=order, halo=halo, block=block),
        in_specs=[pl.BlockSpec(memory_space=pltpu.HBM)],
        out_specs=[pl.BlockSpec(memory_space=pltpu.VMEM)] * len(order),
        out_shape=[out] * len(order),
        scratch_shapes=[
            pltpu.VMEM((count, size, size), jnp.bfloat16),
            pltpu.VMEM((size, quarter), jnp.bfloat16),
            pltpu.VMEM((quarter, size), jnp.bfloat16),
            pltpu.VMEM((count, size, quarter), jnp.bfloat16),
            pltpu.VMEM((count, quarter, quarter), jnp.float32),
            pltpu.VMEM((count, strips, quarter, lanes), jnp.bfloat16),
            pltpu.SemaphoreType.DMA((count, size // block)),
        ],
        compiler_params=pltpu.CompilerParams(vmem_limit_bytes=52 * MIB),
        cost_estimate=pl.CostEstimate(
            flops=2 * count * size * quarter * (size + quarter),
            bytes_accessed=2 * count * size * size,
            transcendentals=0,
        ),
    )(video_frames)


def exchange_order(slabs):
    far = sorted(range(slabs // 2, slabs), key=lambda k: k % 2)
    near = list(range(2, slabs // 2))
    turns = [k for pair in zip(far, near) for k in pair]
    return [0] + turns + far[len(near) :] + [k for k in (1,) if k < slabs // 2]


def cut_kernel(*refs, many, halo):
    in_refs, (mine_ref, other_ref), padded_ref = refs[:many], refs[-3:-1], refs[-1]
    count, window, lanes = in_refs[0].shape
    height = mine_ref.shape[0]
    rows = height - 2 * halo
    wide = count * lanes
    me, core = lax.axis_index("slab"), lax.axis_index("core")
    edge = jnp.zeros((halo, count * lanes), jnp.bfloat16)
    padded_ref[0:halo] = edge
    padded_ref[halo + window :] = edge
    above = lax.rem(me, DOWN) * halo
    for n, in_ref in enumerate(in_refs):
        for f in range(count):
            padded_ref[halo : halo + window, f * lanes : (f + 1) * lanes] = in_ref[f]
        for out_ref, number in ((mine_ref, core), (other_ref, 1 - core)):
            place = pl.ds(pl.multiple_of(above + number * rows, TILE), height)
            out_ref[:, n * wide : (n + 1) * wide] = padded_ref[place]


def cut_windows(pieces, halo, after):
    count, window, lanes = pieces[0].shape
    height = (window - halo) // CORES + 2 * halo
    out = jax.ShapeDtypeStruct((height, len(pieces) * count * lanes), jnp.bfloat16)
    return pl.pallas_call(
        functools.partial(cut_kernel, many=len(pieces), halo=halo),
        in_specs=[pl.BlockSpec(memory_space=pltpu.VMEM)] * len(pieces) + [pl.BlockSpec(memory_space=pl.ANY)] * len(after),
        out_specs=[pl.BlockSpec(memory_space=pltpu.VMEM)] * 2,
        out_shape=[out, out],
        scratch_shapes=[pltpu.VMEM((window + 2 * halo, count * lanes), jnp.bfloat16)],
        compiler_params=pltpu.CompilerParams(vmem_limit_bytes=16 * MIB),
        cost_estimate=pl.CostEstimate(flops=0, bytes_accessed=8 * out.size, transcendentals=0),
    )(*pieces, *after)


def time_kernel(segments_ref, pick_ref, taps_ref, spread_ref, frame_ref, source_ref, *, history, frames, rows):
    chunk, timed = spread_ref.shape[0] // rows, spread_ref.shape[1] // rows
    nseg = pick_ref.shape[0]
    taps = taps_ref.shape[0]
    wide_out, wide_in = chunk * rows, timed * rows

    def count_one(t, totals):
        here = segments_ref[t]
        below = [total + (here < s).astype(jnp.int32) for s, total in enumerate(totals[0])]
        same = [total + (here == s).astype(jnp.int32) for s, total in enumerate(totals[1])]
        return tuple(below), tuple(same)

    zeros = tuple(jnp.int32(0) for _ in range(nseg))
    starts, counts = lax.fori_loop(0, frames, count_one, (zeros, zeros), unroll=8)
    for s in range(nseg):
        frame_ref[s] = starts[s] + lax.rem(pick_ref[s], counts[s])

    def source_one(slot, carry):
        if chunk == frames:
            source_ref[slot] = frame_ref[segments_ref[slot]]
        else:
            before = lax.axis_index("chunk") * chunk - history
            source_ref[slot] = timed + segments_ref[jnp.maximum(before + slot, 0)]
        return carry

    lax.fori_loop(0, timed, source_one, 0)

    lag = history + lax.broadcasted_iota(jnp.int32, (chunk, timed), 0) - lax.broadcasted_iota(
        jnp.int32, (chunk, timed), 1
    )
    if history:
        first = lax.axis_index("chunk") * chunk - history
        real = first + lax.broadcasted_iota(jnp.int32, (chunk, timed), 1) >= 0
        lag = jnp.where(real, lag, -1)
    matrix = jnp.zeros((chunk, timed), jnp.float32)
    for k in range(taps):
        matrix = jnp.where(lag == k, taps_ref[k], matrix)
    repeat_left = (
        lax.broadcasted_iota(jnp.int32, (wide_out, chunk), 0) // rows
        == lax.broadcasted_iota(jnp.int32, (wide_out, chunk), 1)
    ).astype(jnp.bfloat16)
    repeat_right = (
        lax.broadcasted_iota(jnp.int32, (timed, wide_in), 1) // rows
        == lax.broadcasted_iota(jnp.int32, (timed, wide_in), 0)
    ).astype(jnp.bfloat16)
    tall = jnp.dot(repeat_left, matrix.astype(jnp.bfloat16), preferred_element_type=jnp.float32)
    tall = tall.astype(jnp.bfloat16)
    piece = min(128, wide_out)
    for start in range(0, wide_out, piece):
        part = jnp.dot(tall[start : start + piece], repeat_right, preferred_element_type=jnp.float32)
        same_row = (
            lax.broadcasted_iota(jnp.int32, (piece, wide_in), 0) % rows
            == lax.broadcasted_iota(jnp.int32, (piece, wide_in), 1) % rows
        )
        spread_ref[start : start + piece] = jnp.where(same_row, part, 0.0).astype(jnp.bfloat16)


def time_tables(segments, ref_pick, band_taps, rows, chunk, history):
    frames = segments.shape[0]
    wide_out, wide_in = chunk * rows, (history + chunk) * rows
    smem = pl.BlockSpec(memory_space=pltpu.SMEM)
    return pl.pallas_call(
        functools.partial(time_kernel, history=history, frames=frames, rows=rows),
        in_specs=[smem] * 3,
        out_specs=[pl.BlockSpec(memory_space=pltpu.VMEM), smem, smem],
        out_shape=[
            jax.ShapeDtypeStruct((wide_out, wide_in), jnp.bfloat16),
            jax.ShapeDtypeStruct(ref_pick.shape, jnp.int32),
            jax.ShapeDtypeStruct((history + chunk,), jnp.int32),
        ],
        compiler_params=pltpu.CompilerParams(vmem_limit_bytes=16 * MIB),
        cost_estimate=pl.CostEstimate(
            flops=2 * wide_out * wide_in * chunk, bytes_accessed=2 * wide_out * wide_in, transcendentals=0
        ),
    )(segments, ref_pick, band_taps.astype(jnp.float32))


def filter_frames(window_ref, pair, left_ref, right_ref, stacked_ref, put):
    groups, deep, _ = right_ref.shape
    lanes = deep // (2 * SHARE)
    rows = left_ref.shape[0] // (2 * SHARE * groups)
    bands = rows // TILE
    frames = window_ref.shape[1] // lanes
    many = frames * TILE
    for first in range(0, frames, 8):
        last = min(first + 8, frames)
        stacked = jnp.dot(
            left_ref[...], window_ref[:, first * lanes : last * lanes], preferred_element_type=jnp.float32
        ).astype(jnp.bfloat16)
        for oz in range(2 * SHARE * groups):
            group, place = divmod(oz, 2 * SHARE)
            for band in range(bands):
                begin = oz * rows + band * TILE
                for f in range(first, last):
                    row = band * many + f * TILE
                    stacked_ref[group, row : row + TILE, place * lanes : (place + 1) * lanes] = stacked[
                        begin : begin + TILE, (f - first) * lanes : (f - first + 1) * lanes
                    ]
    block = pair * TILE
    total = bands * many
    step = min(512, total)
    for group in range(groups):
        for start in range(0, total, step):
            stop = min(start + step, total)
            coeff = jnp.dot(
                stacked_ref[group, start:stop], right_ref[group], preferred_element_type=jnp.float32
            ).astype(jnp.bfloat16)
            for place in range(start, stop, block):
                band, row = divmod(place, many)
                put(group, band, row // block, coeff[place - start : place - start + block])


def coeff_kernel(window_ref, left_ref, right_ref, coeff_ref, stacked_ref, *, pair):
    block = pair * TILE

    def put(group, band, i, values):
        coeff_ref[group, band, i * block : (i + 1) * block] = values

    filter_frames(window_ref, pair, left_ref, right_ref, stacked_ref, put)


def own_coeffs(windows, left, right, rows, frames_here):
    groups, deep, wide = right.shape
    vmem = pl.BlockSpec(memory_space=pltpu.VMEM)
    many = windows.shape[1] // (deep // (2 * SHARE)) * TILE
    out = jax.ShapeDtypeStruct((groups, rows // TILE, many, wide), jnp.bfloat16)
    return pl.pallas_call(
        functools.partial(coeff_kernel, pair=frames_here),
        in_specs=[vmem] * 3,
        out_specs=vmem,
        out_shape=out,
        scratch_shapes=[pltpu.VMEM((groups, rows // TILE * many, deep), jnp.bfloat16)],
        compiler_params=pltpu.CompilerParams(vmem_limit_bytes=8 * out.size + 16 * MIB),
        cost_estimate=pl.CostEstimate(
            flops=4 * out.size * deep, bytes_accessed=2 * (windows.size + out.size), transcendentals=0
        ),
    )(windows, left, right)


def pixel_kernel(
    sources_ref, spread_ref, other_ref, left_ref, right_ref, *refs, places, pair, chips, history
):
    ready_refs, (out_ref, stacked_ref, coeff_ref, phase_ref, filtered_ref, source_ref, sem, sems) = refs[:-8], refs[-8:]
    sources = pltpu.make_async_copy(sources_ref, source_ref, sem)
    sources.start()
    groups, bands, _, wide = coeff_ref.shape
    half = wide // 2
    block = pair * TILE
    chunk = out_ref.shape[0] * pair
    timed = history + chunk
    core = lax.axis_index("core")

    def place_of(exchanges, twin, n):
        chip = n if exchanges is None else lax.bitwise_xor(lax.axis_index("slab"), exchanges[n])
        return pl.ds(pl.multiple_of((chip * CORES + lax.rem(core + twin, CORES)) * block, block), block)

    copies = []
    for ready_ref, (exchanges, twin) in zip(ready_refs, places):
        for n in range(ready_ref.shape[2] // block):
            copies.append(
                pltpu.make_async_copy(
                    ready_ref.at[:, :, n * block : (n + 1) * block],
                    coeff_ref.at[:, :, place_of(exchanges, twin, n)],
                    sems.at[len(copies)],
                )
            )
            copies[-1].start()

    def put(group, band, i, values):
        if i < chips:
            place = place_of(*places[-1], i)
        else:
            place = slice(timed * TILE + (i - chips) * block, timed * TILE + (i - chips + 1) * block)
        coeff_ref[group, band, place] = values

    filter_frames(other_ref, pair, left_ref, right_ref, stacked_ref, put)

    for copy in copies:
        copy.wait()
    sources.wait()

    def phase_one(slot, carry):
        place = pl.ds(pl.multiple_of(slot * TILE, TILE), TILE)
        source = source_ref[slot]
        refer = pl.ds(pl.multiple_of(source * TILE, TILE), TILE)
        for group in range(groups):
            for band in range(bands):
                coeff_real = coeff_ref[group, band, place, 0:half].astype(jnp.float32)
                coeff_imag = coeff_ref[group, band, place, half:wide].astype(jnp.float32)
                ref_real = coeff_ref[group, band, refer, 0:half].astype(jnp.float32)
                ref_imag = coeff_ref[group, band, refer, half:wide].astype(jnp.float32)
                prod_real = coeff_real * ref_real + coeff_imag * ref_imag
                prod_imag = coeff_imag * ref_real - coeff_real * ref_imag
                square = prod_real * prod_real + prod_imag * prod_imag + 1.0
                phase = (prod_imag * lax.rsqrt(square)).astype(jnp.bfloat16)
                lane = (band * groups + group) * half
                phase_ref[place, lane : lane + half] = phase
        return carry

    lax.fori_loop(0, timed, phase_one, 0, unroll=2)

    piece = min(128, chunk * TILE)
    columns = half // SHARE
    left_half = lax.broadcasted_iota(jnp.int32, (TILE, half), 1) < columns
    step = min(256, chunk * TILE)
    for start in range(0, chunk * TILE, step):
        stop = start + step
        filtered_ref[start:stop] = jnp.dot(
            spread_ref[start:stop, : history * TILE + stop],
            phase_ref[: history * TILE + stop],
            preferred_element_type=jnp.float32,
        ).astype(jnp.bfloat16)
    for band in range(bands):
        for start in range(0, chunk * TILE, piece):
            here = slice(history * TILE + start, history * TILE + start + piece)
            lane = band * groups * half
            filtered = filtered_ref[start : start + piece, lane : lane + groups * half].astype(jnp.float32)
            above = jnp.zeros((piece, half), jnp.float32)
            below = jnp.zeros((piece, half), jnp.float32)
            for group in range(groups):
                coeff_real = coeff_ref[group, band, here, 0:half].astype(jnp.float32)
                coeff_imag = coeff_ref[group, band, here, half:wide].astype(jnp.float32)
                amplitude = coeff_real * coeff_real + coeff_imag * coeff_imag
                above = above + amplitude * filtered[:, group * half : (group + 1) * half]
                below = below + amplitude
            for i in range(piece // block):
                sums = []
                for value in (above, below):
                    one, two = value[i * block : i * block + TILE], value[i * block + TILE : (i + 1) * block]
                    sums.append(jnp.where(left_half, one, two) + pltpu.roll(jnp.where(left_half, two, one), columns, 1))
                both = (sums[0] / (sums[1] + 1.0)).astype(out_ref.dtype)
                out_ref[start // block + i, band * TILE : (band + 1) * TILE] = both


def pixel_motion(sources, spread, ready, other, left, right, places, pair, chips, chunk, history):
    groups, bands, _, wide = ready[0].shape
    deep = right.shape[1]
    timed = history + chunk
    fresh = other.shape[1] // (deep // (2 * SHARE))
    slots = timed + fresh - chips * pair
    vmem = pl.BlockSpec(memory_space=pltpu.VMEM)
    return pl.pallas_call(
        functools.partial(pixel_kernel, places=places, pair=pair, chips=chips, history=history),
        in_specs=[pl.BlockSpec(memory_space=pl.ANY)] + [vmem] * (4 + len(ready)),
        out_specs=vmem,
        out_shape=jax.ShapeDtypeStruct((chunk // pair, bands * TILE, wide // 2), jnp.bfloat16),
        scratch_shapes=[
            pltpu.VMEM((groups, bands * fresh * TILE, deep), jnp.bfloat16),
            pltpu.VMEM((groups, bands, slots * TILE, wide), jnp.bfloat16),
            pltpu.VMEM((timed * TILE, bands * groups * wide // 2), jnp.bfloat16),
            pltpu.VMEM((chunk * TILE, bands * groups * wide // 2), jnp.bfloat16),
            pltpu.SMEM((timed,), jnp.int32),
            pltpu.SemaphoreType.DMA,
            pltpu.SemaphoreType.DMA((sum(one.shape[2] for one in ready) // (pair * TILE),)),
        ],
        compiler_params=pltpu.CompilerParams(vmem_limit_bytes=8 * groups * bands * slots * TILE * wide + 16 * MIB),
        cost_estimate=pl.CostEstimate(
            flops=2 * groups * bands * TILE * wide * (fresh * deep + chunk * timed * TILE // 2),
            bytes_accessed=2 * (other.size + sum(one.size for one in ready) + right.size),
            transcendentals=groups * bands * TILE * timed * wide // 2,
        ),
    )(sources, spread, other, left, right, *ready)


def join_kernel(tiles_ref, out_ref, frames_ref, sems):
    count, quarter, _ = out_ref.shape
    devices, rows, lanes = tiles_ref.shape
    columns = lanes // count
    strips = quarter // columns
    left = lax.broadcasted_iota(jnp.int32, (rows, lanes), 1) < columns
    copies = []
    for i in range(devices // strips):
        down = slice(i * rows, (i + 1) * rows)
        for strip in range(0, strips, 2):
            one = tiles_ref[strip * devices // strips + i].astype(jnp.float32)
            two = tiles_ref[(strip + 1) * devices // strips + i].astype(jnp.float32)
            here = slice(strip * columns, (strip + 2) * columns)
            frames_ref[0, down, here] = jnp.where(left, one, pltpu.roll(two, columns, 1))
            frames_ref[1, down, here] = jnp.where(left, pltpu.roll(one, columns, 1), two)
        for f in range(count):
            copies.append(pltpu.make_async_copy(frames_ref.at[f, down], out_ref.at[f, down], sems.at[f, i]))
            copies[-1].start()
    for copy in copies:
        copy.wait()


def join_tiles(tiles, quarter):
    strips = quarter * 2 // tiles.shape[2]
    out = jax.ShapeDtypeStruct((2, quarter, quarter), jnp.float32)
    return pl.pallas_call(
        join_kernel,
        in_specs=[pl.BlockSpec(memory_space=pltpu.VMEM)],
        out_specs=pl.BlockSpec(memory_space=pltpu.HBM),
        out_shape=out,
        scratch_shapes=[
            pltpu.VMEM(out.shape, jnp.float32),
            pltpu.SemaphoreType.DMA((2, tiles.shape[0] // strips)),
        ],
        compiler_params=pltpu.CompilerParams(vmem_limit_bytes=16 * MIB),
        cost_estimate=pl.CostEstimate(flops=tiles.size, bytes_accessed=6 * tiles.size, transcendentals=0),
    )(tiles)


def chunk_windows(mine, other, ref_frames, frames_here, history_chips, chips):
    mine = lax.all_gather(mine, "chunk", axis=0, tiled=True)
    other = lax.all_gather(other, "chunk", axis=0, tiled=True)
    height = mine.shape[1]
    core = lax.axis_index("core")
    device, f = ref_frames // frames_here, ref_frames % frames_here
    own = (device % CORES == core)[:, None, None]

    def pick(windows):
        return windows.reshape(windows.shape[0], height, frames_here, -1)[device // CORES, :, f]

    refer = jnp.where(own, pick(mine), pick(other))
    refer = refer.reshape(NSEG // frames_here, frames_here, height, -1)
    refer = jnp.swapaxes(refer, 1, 2).reshape(NSEG // frames_here, height, -1)

    def cut(windows):
        before = jnp.zeros((history_chips,) + windows.shape[1:], windows.dtype)
        windows = jnp.concatenate([before, windows])
        return lax.dynamic_slice_in_dim(windows, lax.axis_index("chunk") * chips, history_chips + chips)

    return cut(mine), cut(other), refer


def body(video_frames, segments, ref_pick, band_taps, *, chunks, slabs):
    frames_here, size, _ = video_frames.shape
    quarter = size // 4
    rows = quarter // (DOWN * CORES)
    columns = quarter * DOWN // slabs
    chunk = slabs * CORES * frames_here
    history = min(chunk * -(-(band_taps.shape[0] - 1) // chunk), segments.shape[0] - chunk)
    left = jnp.asarray(slab_left_table(rows, HALO, ORIENT))
    right = jnp.asarray(make_right_table(columns, HALO, ORIENT))
    order = exchange_order(slabs)

    def exchange(array, k):
        return lax.ppermute(array, "slab", [(chip, chip ^ k) for chip in range(slabs)]) if k else array

    def swap(array):
        return lax.ppermute(array, "core", [(0, 1), (1, 0)])

    windows = reduce_frames(video_frames, order, HALO)
    spread, ref_frames, sources = time_tables(segments, ref_pick, band_taps, TILE, chunk, history)
    pieces = [exchange(window, k) for k, window in zip(order, windows)]
    if chunks > 1:

        def by_chip(windows):
            apart = jnp.moveaxis(windows.reshape(windows.shape[0], slabs, -1), 1, 0)
            return apart[jnp.asarray(np.argsort(order))[lax.axis_index("slab") ^ jnp.arange(slabs)]]

        def side_by_side(windows):
            return jnp.moveaxis(windows, 0, 1).reshape(windows.shape[1], -1)

        mine, other = cut_windows(pieces, HALO, [])
        chips = slabs + history // (CORES * frames_here)
        windows = chunk_windows(by_chip(mine), by_chip(swap(other)), ref_frames, frames_here, chips - slabs, slabs)
        mine, other, refer = [side_by_side(one) for one in windows]
        other = jnp.concatenate([other, refer], axis=1)
        ready = [own_coeffs(mine, left, right, rows, frames_here)]
        places = [(None, 0), (None, 1)]
    else:
        first = slabs // 2
        chips = slabs - first
        mine, other = cut_windows(pieces[:first], HALO, [spread])
        ready = [own_coeffs(one, left, right, rows, frames_here) for one in (mine, swap(other))]
        mine, other = cut_windows(pieces[first:], HALO, ready[:1])
        other = swap(other)
        ready.append(own_coeffs(mine, left, right, rows, frames_here))
        places = [(exchanges, twin) for exchanges in (order[:first], order[first:]) for twin in range(CORES)]
    motion = pixel_motion(sources, spread, ready, other, left, right, places, frames_here, chips, chunk, history)
    motion = lax.all_to_all(motion, ("slab", "core"), split_axis=0, concat_axis=0, tiled=True)
    return join_tiles(motion, quarter)


def solution(mesh):
    chips = mesh.shape["frames"] // CORES
    slabs = min(chips, QUART * DOWN // (2 * HALO))
    chunks = chips // slabs
    names = ("groups", "chunk", "slab", "core")
    cut = jax.sharding.Mesh(mesh.devices.reshape(mesh.shape["groups"], chunks, slabs, CORES), names)
    in_specs = (P(names, None, None), P("groups"), P("groups"), P())
    return jax.shard_map(
        functools.partial(body, chunks=chunks, slabs=slabs),
        mesh=cut, in_specs=in_specs, out_specs=P(names, None, None), check_vma=False,
    )
```

```python
import functools
import math

import jax
import jax.numpy as jnp
import numpy as np
from jax import lax
from jax.experimental import pallas as pl
from jax.experimental.pallas import tpu as pltpu
from jax.sharding import PartitionSpec as P

IMG = 1024
ORIENT = 4
NSEG = 4
QUART = 256


blur_sigma = 2.0
gabor_sigma = 2.0
wave_number = math.pi / 2.0
gabor_gain = 2.0

HALO = 32
TILE = 16
DOWN = 2
SHARE = 2
CORES = 2
MIB = 1024 * 1024


def envelope_of(offset_grid):
    return np.float32(gabor_gain) * np.exp(
        -offset_grid * offset_grid / np.float32(2.0 * gabor_sigma * gabor_sigma)
    )


def waves(orient):
    angles = np.arange(orient, dtype=np.float32) * np.float32(math.pi / orient)
    wave_x = np.float32(wave_number) * np.cos(angles)
    wave_y = np.float32(wave_number) * np.sin(angles)
    return wave_x, wave_y


def slab_left_table(rows, halo, orient):
    offset = (
        np.arange(rows + 2 * halo, dtype=np.float32)[None, :]
        - np.float32(halo)
        - np.arange(rows, dtype=np.float32)[:, None]
    )
    wave_y = waves(orient)[1]
    phase = wave_y[:, None, None] * offset[None]
    envelope = envelope_of(offset)[None]
    table = np.stack([envelope * np.cos(phase), envelope * np.sin(phase)], axis=1)
    return table.reshape(orient * 2 * rows, rows + 2 * halo).astype(jnp.bfloat16)


def make_right_table(columns, halo, orient):
    window = columns + 2 * halo
    offset = (
        np.arange(window, dtype=np.float32)[:, None] - np.float32(halo) - np.arange(columns, dtype=np.float32)[None, :]
    )
    wave_x = waves(orient)[0]
    phase_x = wave_x[:, None, None] * offset[None]
    envelope = envelope_of(offset)[None]
    real_part = envelope * np.cos(phase_x)
    imag_part = envelope * np.sin(phase_x)
    table = np.zeros((orient // SHARE, SHARE, 2, window, 2, SHARE, columns), np.float32)
    for o in range(orient):
        group, i = divmod(o, SHARE)
        table[group, i, 0, :, 0, i] = real_part[o]
        table[group, i, 0, :, 1, i] = imag_part[o]
        table[group, i, 1, :, 0, i] = -imag_part[o]
        table[group, i, 1, :, 1, i] = real_part[o]
    return table.reshape(orient // SHARE, SHARE * 2 * window, 2 * SHARE * columns).astype(jnp.bfloat16)


def down_sums(full_size, quarter):
    position = np.arange(quarter, dtype=np.float32)[:, None]
    columns = np.arange(full_size, dtype=np.float32)[None, :]
    offset_grid = columns - np.float32(4.0) * position - np.float32(1.5)
    weight = np.exp(-offset_grid * offset_grid / np.float32(2.0 * blur_sigma * blur_sigma))
    return np.sum(weight, axis=1)


def down_block(position, column, shape, axis, sums):
    positions = position + lax.broadcasted_iota(jnp.int32, shape, 1 - axis)
    columns = column + lax.broadcasted_iota(jnp.int32, shape, axis)
    offset_grid = columns.astype(jnp.float32) - 4.0 * positions.astype(jnp.float32) - 1.5
    weight = jnp.exp(-offset_grid * offset_grid / (2.0 * blur_sigma * blur_sigma))
    inner = float(sums[len(sums) // 2])
    line = position + lax.broadcasted_iota(jnp.int32, tuple(1 if i == axis else n for i, n in enumerate(shape)), 1 - axis)
    scale = jnp.full(line.shape, 1.0 / inner, jnp.float32)
    for q in range(position, min(position + shape[1 - axis], len(sums))):
        if abs(float(sums[q]) - inner) > 1e-7 * inner:
            scale = jnp.where(line == q, 1.0 / float(sums[q]), scale)
    return (weight * scale).astype(jnp.bfloat16)


def build_down(table_ref, axis):
    size, quarter = table_ref.shape[axis], table_ref.shape[1 - axis]
    sums = down_sums(size, quarter)
    cut = np.abs(sums - sums[quarter // 2]) > 1e-7 * sums[quarter // 2]
    blocks = {}
    table_ref[...] = jnp.zeros_like(table_ref)
    tall, wide = (128, 32)[axis], min(128, table_ref.shape[1])
    for row in range(0, table_ref.shape[0], tall):
        for lane in range(0, table_ref.shape[1], wide):
            position, column = (row, lane) if axis else (lane, row)
            positions, columns = (tall, wide) if axis else (wide, tall)
            if 4 * (position + positions - 1) + 30 >= column and 4 * position - 27 <= column + columns - 1:
                kind = (column - 4 * position, position if cut[position : position + positions].any() else None)
                if kind not in blocks:
                    blocks[kind] = down_block(position, column, (tall, wide), axis, sums)
                table_ref[row : row + tall, lane : lane + wide] = blocks[kind]


def reduce_kernel(frames_ref, *refs, order, halo, block):
    out_refs = refs[: len(order)]
    picture_ref, down_t_ref, down_ref, half_ref, total_ref, strip_ref, sems = refs[len(order) :]
    count, size, _ = picture_ref.shape
    quarter = down_ref.shape[0]
    _, strips, _, lanes = strip_ref.shape
    columns = lanes - 2 * halo
    window = out_refs[0].shape[1]

    copies = []
    for f in range(count):
        for i in range(size // block):
            here = pl.ds(i * block, block)
            copy = pltpu.make_async_copy(frames_ref.at[f, here], picture_ref.at[f, here], sems.at[f, i])
            copy.start()
            copies.append(copy)
    build_down(down_t_ref, 0)

    me = lax.axis_index("slab")
    blocks = size // block
    for f in range(count):
        step = block if f == 0 else size
        for begin in range(0, size, step):
            for i in range(begin // block, (begin + step) // block):
                copies[f * blocks + i].wait()
            half_ref[f, begin : begin + step] = jnp.dot(
                picture_ref[f, begin : begin + step], down_t_ref[...], preferred_element_type=jnp.float32
            ).astype(jnp.bfloat16)
            if f == begin == 0:
                build_down(down_ref, 1)
        total_ref[f] = jnp.dot(down_ref[...], half_ref[f], preferred_element_type=jnp.float32)
        for strip in range(strips):
            begin = strip * columns - halo
            moved = pltpu.roll(total_ref[f], (-begin) % quarter, 1)[:, 0:lanes]
            column = begin + lax.broadcasted_iota(jnp.int32, (quarter, lanes), 1)
            inside = (column >= 0) & (column < quarter)
            strip_ref[f, strip] = jnp.where(inside, moved, 0.0).astype(jnp.bfloat16)
        for k, out_ref in zip(order, out_refs):
            slab = lax.bitwise_xor(me, k)
            begin = pl.multiple_of(lax.rem(slab, DOWN) * (quarter - window), TILE)
            out_ref[f] = strip_ref[f, slab // DOWN, pl.ds(begin, window)]


def reduce_frames(video_frames, order, halo):
    count, size, _ = video_frames.shape
    quarter = size // 4
    strips = len(order) // DOWN
    lanes = quarter // strips + 2 * halo
    block = size // 2
    out = jax.ShapeDtypeStruct((count, quarter // DOWN + halo, lanes), jnp.bfloat16)
    return pl.pallas_call(
        functools.partial(reduce_kernel, order=order, halo=halo, block=block),
        in_specs=[pl.BlockSpec(memory_space=pltpu.HBM)],
        out_specs=[pl.BlockSpec(memory_space=pltpu.VMEM)] * len(order),
        out_shape=[out] * len(order),
        scratch_shapes=[
            pltpu.VMEM((count, size, size), jnp.bfloat16),
            pltpu.VMEM((size, quarter), jnp.bfloat16),
            pltpu.VMEM((quarter, size), jnp.bfloat16),
            pltpu.VMEM((count, size, quarter), jnp.bfloat16),
            pltpu.VMEM((count, quarter, quarter), jnp.float32),
            pltpu.VMEM((count, strips, quarter, lanes), jnp.bfloat16),
            pltpu.SemaphoreType.DMA((count, size // block)),
        ],
        compiler_params=pltpu.CompilerParams(vmem_limit_bytes=52 * MIB),
        cost_estimate=pl.CostEstimate(
            flops=2 * count * size * quarter * (size + quarter),
            bytes_accessed=2 * count * size * size,
            transcendentals=0,
        ),
    )(video_frames)


def exchange_order(slabs):
    far = sorted(range(slabs // 2, slabs), key=lambda k: k % 2)
    near = list(range(2, slabs // 2))
    turns = [k for pair in zip(far, near) for k in pair]
    return [0] + turns + far[len(near) :] + [k for k in (1,) if k < slabs // 2]


def cut_kernel(*refs, many, halo):
    in_refs, (mine_ref, other_ref), padded_ref = refs[:many], refs[-3:-1], refs[-1]
    count, window, lanes = in_refs[0].shape
    height = mine_ref.shape[0]
    rows = height - 2 * halo
    wide = count * lanes
    me, core = lax.axis_index("slab"), lax.axis_index("core")
    edge = jnp.zeros((halo, count * lanes), jnp.bfloat16)
    padded_ref[0:halo] = edge
    padded_ref[halo + window :] = edge
    above = lax.rem(me, DOWN) * halo
    for n, in_ref in enumerate(in_refs):
        for f in range(count):
            padded_ref[halo : halo + window, f * lanes : (f + 1) * lanes] = in_ref[f]
        for out_ref, number in ((mine_ref, core), (other_ref, 1 - core)):
            place = pl.ds(pl.multiple_of(above + number * rows, TILE), height)
            out_ref[:, n * wide : (n + 1) * wide] = padded_ref[place]


def cut_windows(pieces, halo, after):
    count, window, lanes = pieces[0].shape
    height = (window - halo) // CORES + 2 * halo
    out = jax.ShapeDtypeStruct((height, len(pieces) * count * lanes), jnp.bfloat16)
    return pl.pallas_call(
        functools.partial(cut_kernel, many=len(pieces), halo=halo),
        in_specs=[pl.BlockSpec(memory_space=pltpu.VMEM)] * len(pieces) + [pl.BlockSpec(memory_space=pl.ANY)] * len(after),
        out_specs=[pl.BlockSpec(memory_space=pltpu.VMEM)] * 2,
        out_shape=[out, out],
        scratch_shapes=[pltpu.VMEM((window + 2 * halo, count * lanes), jnp.bfloat16)],
        compiler_params=pltpu.CompilerParams(vmem_limit_bytes=16 * MIB),
        cost_estimate=pl.CostEstimate(flops=0, bytes_accessed=8 * out.size, transcendentals=0),
    )(*pieces, *after)


def time_kernel(segments_ref, pick_ref, taps_ref, spread_ref, frame_ref, source_ref, *, history, frames, rows):
    chunk, timed = spread_ref.shape[0] // rows, spread_ref.shape[1] // rows
    nseg = pick_ref.shape[0]
    taps = taps_ref.shape[0]
    wide_out, wide_in = chunk * rows, timed * rows

    def count_one(t, totals):
        here = segments_ref[t]
        below = [total + (here < s).astype(jnp.int32) for s, total in enumerate(totals[0])]
        same = [total + (here == s).astype(jnp.int32) for s, total in enumerate(totals[1])]
        return tuple(below), tuple(same)

    zeros = tuple(jnp.int32(0) for _ in range(nseg))
    starts, counts = lax.fori_loop(0, frames, count_one, (zeros, zeros), unroll=8)
    for s in range(nseg):
        frame_ref[s] = starts[s] + lax.rem(pick_ref[s], counts[s])

    def source_one(slot, carry):
        if chunk == frames:
            source_ref[slot] = frame_ref[segments_ref[slot]]
        else:
            before = lax.axis_index("chunk") * chunk - history
            source_ref[slot] = timed + segments_ref[jnp.maximum(before + slot, 0)]
        return carry

    lax.fori_loop(0, timed, source_one, 0)

    lag = history + lax.broadcasted_iota(jnp.int32, (chunk, timed), 0) - lax.broadcasted_iota(
        jnp.int32, (chunk, timed), 1
    )
    if history:
        first = lax.axis_index("chunk") * chunk - history
        real = first + lax.broadcasted_iota(jnp.int32, (chunk, timed), 1) >= 0
        lag = jnp.where(real, lag, -1)
    matrix = jnp.zeros((chunk, timed), jnp.float32)
    for k in range(taps):
        matrix = jnp.where(lag == k, taps_ref[k], matrix)
    repeat_left = (
        lax.broadcasted_iota(jnp.int32, (wide_out, chunk), 0) // rows
        == lax.broadcasted_iota(jnp.int32, (wide_out, chunk), 1)
    ).astype(jnp.bfloat16)
    repeat_right = (
        lax.broadcasted_iota(jnp.int32, (timed, wide_in), 1) // rows
        == lax.broadcasted_iota(jnp.int32, (timed, wide_in), 0)
    ).astype(jnp.bfloat16)
    tall = jnp.dot(repeat_left, matrix.astype(jnp.bfloat16), preferred_element_type=jnp.float32)
    tall = tall.astype(jnp.bfloat16)
    piece = min(128, wide_out)
    for start in range(0, wide_out, piece):
        part = jnp.dot(tall[start : start + piece], repeat_right, preferred_element_type=jnp.float32)
        same_row = (
            lax.broadcasted_iota(jnp.int32, (piece, wide_in), 0) % rows
            == lax.broadcasted_iota(jnp.int32, (piece, wide_in), 1) % rows
        )
        spread_ref[start : start + piece] = jnp.where(same_row, part, 0.0).astype(jnp.bfloat16)


def time_tables(segments, ref_pick, band_taps, rows, chunk, history):
    frames = segments.shape[0]
    wide_out, wide_in = chunk * rows, (history + chunk) * rows
    smem = pl.BlockSpec(memory_space=pltpu.SMEM)
    return pl.pallas_call(
        functools.partial(time_kernel, history=history, frames=frames, rows=rows),
        in_specs=[smem] * 3,
        out_specs=[pl.BlockSpec(memory_space=pltpu.VMEM), smem, smem],
        out_shape=[
            jax.ShapeDtypeStruct((wide_out, wide_in), jnp.bfloat16),
            jax.ShapeDtypeStruct(ref_pick.shape, jnp.int32),
            jax.ShapeDtypeStruct((history + chunk,), jnp.int32),
        ],
        compiler_params=pltpu.CompilerParams(vmem_limit_bytes=16 * MIB),
        cost_estimate=pl.CostEstimate(
            flops=2 * wide_out * wide_in * chunk, bytes_accessed=2 * wide_out * wide_in, transcendentals=0
        ),
    )(segments, ref_pick, band_taps.astype(jnp.float32))


def filter_frames(window_ref, pair, left_ref, right_ref, stacked_ref, put):
    groups, deep, _ = right_ref.shape
    lanes = deep // (2 * SHARE)
    rows = left_ref.shape[0] // (2 * SHARE * groups)
    bands = rows // TILE
    frames = window_ref.shape[1] // lanes
    many = frames * TILE
    for first in range(0, frames, 8):
        last = min(first + 8, frames)
        stacked = jnp.dot(
            left_ref[...], window_ref[:, first * lanes : last * lanes], preferred_element_type=jnp.float32
        ).astype(jnp.bfloat16)
        for oz in range(2 * SHARE * groups):
            group, place = divmod(oz, 2 * SHARE)
            for band in range(bands):
                begin = oz * rows + band * TILE
                for f in range(first, last):
                    row = band * many + f * TILE
                    stacked_ref[group, row : row + TILE, place * lanes : (place + 1) * lanes] = stacked[
                        begin : begin + TILE, (f - first) * lanes : (f - first + 1) * lanes
                    ]
    block = pair * TILE
    total = bands * many
    step = min(512, total)
    for group in range(groups):
        for start in range(0, total, step):
            stop = min(start + step, total)
            coeff = jnp.dot(
                stacked_ref[group, start:stop], right_ref[group], preferred_element_type=jnp.float32
            ).astype(jnp.bfloat16)
            for place in range(start, stop, block):
                band, row = divmod(place, many)
                put(group, band, row // block, coeff[place - start : place - start + block])


def coeff_kernel(window_ref, left_ref, right_ref, coeff_ref, stacked_ref, *, pair):
    block = pair * TILE

    def put(group, band, i, values):
        coeff_ref[group, band, i * block : (i + 1) * block] = values

    filter_frames(window_ref, pair, left_ref, right_ref, stacked_ref, put)


def own_coeffs(windows, left, right, rows, frames_here):
    groups, deep, wide = right.shape
    vmem = pl.BlockSpec(memory_space=pltpu.VMEM)
    many = windows.shape[1] // (deep // (2 * SHARE)) * TILE
    out = jax.ShapeDtypeStruct((groups, rows // TILE, many, wide), jnp.bfloat16)
    return pl.pallas_call(
        functools.partial(coeff_kernel, pair=frames_here),
        in_specs=[vmem] * 3,
        out_specs=vmem,
        out_shape=out,
        scratch_shapes=[pltpu.VMEM((groups, rows // TILE * many, deep), jnp.bfloat16)],
        compiler_params=pltpu.CompilerParams(vmem_limit_bytes=8 * out.size + 16 * MIB),
        cost_estimate=pl.CostEstimate(
            flops=4 * out.size * deep, bytes_accessed=2 * (windows.size + out.size), transcendentals=0
        ),
    )(windows, left, right)


def pixel_kernel(
    sources_ref, spread_ref, other_ref, left_ref, right_ref, *refs, places, pair, chips, history
):
    ready_refs, (out_ref, stacked_ref, coeff_ref, phase_ref, filtered_ref, source_ref, sem) = refs[:-7], refs[-7:]
    sources = pltpu.make_async_copy(sources_ref, source_ref, sem)
    sources.start()
    groups, bands, _, wide = coeff_ref.shape
    half = wide // 2
    block = pair * TILE
    chunk = out_ref.shape[0] * pair
    timed = history + chunk
    core = lax.axis_index("core")

    def place_of(exchanges, twin, n):
        chip = n if exchanges is None else lax.bitwise_xor(lax.axis_index("slab"), exchanges[n])
        return pl.ds(pl.multiple_of((chip * CORES + lax.rem(core + twin, CORES)) * block, block), block)

    for ready_ref, (exchanges, twin) in zip(ready_refs, places):
        for n in range(ready_ref.shape[2] // block):
            for group in range(groups):
                for band in range(bands):
                    coeff_ref[group, band, place_of(exchanges, twin, n)] = ready_ref[group, band, n * block : (n + 1) * block]

    def put(group, band, i, values):
        if i < chips:
            place = place_of(*places[-1], i)
        else:
            place = slice(timed * TILE + (i - chips) * block, timed * TILE + (i - chips + 1) * block)
        coeff_ref[group, band, place] = values

    filter_frames(other_ref, pair, left_ref, right_ref, stacked_ref, put)

    sources.wait()

    def phase_one(slot, carry):
        place = pl.ds(pl.multiple_of(slot * TILE, TILE), TILE)
        source = source_ref[slot]
        refer = pl.ds(pl.multiple_of(source * TILE, TILE), TILE)
        for group in range(groups):
            for band in range(bands):
                coeff_real = coeff_ref[group, band, place, 0:half].astype(jnp.float32)
                coeff_imag = coeff_ref[group, band, place, half:wide].astype(jnp.float32)
                ref_real = coeff_ref[group, band, refer, 0:half].astype(jnp.float32)
                ref_imag = coeff_ref[group, band, refer, half:wide].astype(jnp.float32)
                prod_real = coeff_real * ref_real + coeff_imag * ref_imag
                prod_imag = coeff_imag * ref_real - coeff_real * ref_imag
                square = prod_real * prod_real + prod_imag * prod_imag + 1.0
                phase = (prod_imag * lax.rsqrt(square)).astype(jnp.bfloat16)
                lane = (band * groups + group) * half
                phase_ref[place, lane : lane + half] = phase
        return carry

    lax.fori_loop(0, timed, phase_one, 0, unroll=2)

    piece = min(128, chunk * TILE)
    columns = half // SHARE
    left_half = lax.broadcasted_iota(jnp.int32, (TILE, half), 1) < columns
    step = min(512, chunk * TILE)
    for start in range(0, chunk * TILE, step):
        stop = start + step
        filtered_ref[start:stop] = jnp.dot(
            spread_ref[start:stop, : history * TILE + stop],
            phase_ref[: history * TILE + stop],
            preferred_element_type=jnp.float32,
        ).astype(jnp.bfloat16)
    for band in range(bands):
        for start in range(0, chunk * TILE, piece):
            here = slice(history * TILE + start, history * TILE + start + piece)
            lane = band * groups * half
            filtered = filtered_ref[start : start + piece, lane : lane + groups * half].astype(jnp.float32)
            above = jnp.zeros((piece, half), jnp.float32)
            below = jnp.zeros((piece, half), jnp.float32)
            for group in range(groups):
                coeff_real = coeff_ref[group, band, here, 0:half].astype(jnp.float32)
                coeff_imag = coeff_ref[group, band, here, half:wide].astype(jnp.float32)
                amplitude = coeff_real * coeff_real + coeff_imag * coeff_imag
                above = above + amplitude * filtered[:, group * half : (group + 1) * half]
                below = below + amplitude
            for i in range(piece // block):
                sums = []
                for value in (above, below):
                    one, two = value[i * block : i * block + TILE], value[i * block + TILE : (i + 1) * block]
                    sums.append(jnp.where(left_half, one, two) + pltpu.roll(jnp.where(left_half, two, one), columns, 1))
                both = (sums[0] / (sums[1] + 1.0)).astype(out_ref.dtype)
                out_ref[start // block + i, band * TILE : (band + 1) * TILE] = both


def pixel_motion(sources, spread, ready, other, left, right, places, pair, chips, chunk, history):
    groups, bands, _, wide = ready[0].shape
    deep = right.shape[1]
    timed = history + chunk
    fresh = other.shape[1] // (deep // (2 * SHARE))
    slots = timed + fresh - chips * pair
    vmem = pl.BlockSpec(memory_space=pltpu.VMEM)
    return pl.pallas_call(
        functools.partial(pixel_kernel, places=places, pair=pair, chips=chips, history=history),
        in_specs=[pl.BlockSpec(memory_space=pl.ANY)] + [vmem] * (4 + len(ready)),
        out_specs=vmem,
        out_shape=jax.ShapeDtypeStruct((chunk // pair, bands * TILE, wide // 2), jnp.bfloat16),
        scratch_shapes=[
            pltpu.VMEM((groups, bands * fresh * TILE, deep), jnp.bfloat16),
            pltpu.VMEM((groups, bands, slots * TILE, wide), jnp.bfloat16),
            pltpu.VMEM((timed * TILE, bands * groups * wide // 2), jnp.bfloat16),
            pltpu.VMEM((chunk * TILE, bands * groups * wide // 2), jnp.bfloat16),
            pltpu.SMEM((timed,), jnp.int32),
            pltpu.SemaphoreType.DMA,
        ],
        compiler_params=pltpu.CompilerParams(vmem_limit_bytes=8 * groups * bands * slots * TILE * wide + 16 * MIB),
        cost_estimate=pl.CostEstimate(
            flops=2 * groups * bands * TILE * wide * (fresh * deep + chunk * timed * TILE // 2),
            bytes_accessed=2 * (other.size + sum(one.size for one in ready) + right.size),
            transcendentals=groups * bands * TILE * timed * wide // 2,
        ),
    )(sources, spread, other, left, right, *ready)


def join_kernel(tiles_ref, out_ref, frames_ref, sems):
    count, quarter, _ = out_ref.shape
    devices, rows, lanes = tiles_ref.shape
    columns = lanes // count
    strips = quarter // columns
    left = lax.broadcasted_iota(jnp.int32, (rows, lanes), 1) < columns
    copies = []
    for i in range(devices // strips):
        down = slice(i * rows, (i + 1) * rows)
        for strip in range(0, strips, 2):
            one = tiles_ref[strip * devices // strips + i].astype(jnp.float32)
            two = tiles_ref[(strip + 1) * devices // strips + i].astype(jnp.float32)
            here = slice(strip * columns, (strip + 2) * columns)
            frames_ref[0, down, here] = jnp.where(left, one, pltpu.roll(two, columns, 1))
            frames_ref[1, down, here] = jnp.where(left, pltpu.roll(one, columns, 1), two)
        for f in range(count):
            copies.append(pltpu.make_async_copy(frames_ref.at[f, down], out_ref.at[f, down], sems.at[f, i]))
            copies[-1].start()
    for copy in copies:
        copy.wait()


def join_tiles(tiles, quarter):
    strips = quarter * 2 // tiles.shape[2]
    out = jax.ShapeDtypeStruct((2, quarter, quarter), jnp.float32)
    return pl.pallas_call(
        join_kernel,
        in_specs=[pl.BlockSpec(memory_space=pltpu.VMEM)],
        out_specs=pl.BlockSpec(memory_space=pltpu.HBM),
        out_shape=out,
        scratch_shapes=[
            pltpu.VMEM(out.shape, jnp.float32),
            pltpu.SemaphoreType.DMA((2, tiles.shape[0] // strips)),
        ],
        compiler_params=pltpu.CompilerParams(vmem_limit_bytes=16 * MIB),
        cost_estimate=pl.CostEstimate(flops=tiles.size, bytes_accessed=6 * tiles.size, transcendentals=0),
    )(tiles)


def chunk_windows(mine, other, ref_frames, frames_here, history_chips, chips):
    mine = lax.all_gather(mine, "chunk", axis=0, tiled=True)
    other = lax.all_gather(other, "chunk", axis=0, tiled=True)
    height = mine.shape[1]
    core = lax.axis_index("core")
    device, f = ref_frames // frames_here, ref_frames % frames_here
    own = (device % CORES == core)[:, None, None]

    def pick(windows):
        return windows.reshape(windows.shape[0], height, frames_here, -1)[device // CORES, :, f]

    refer = jnp.where(own, pick(mine), pick(other))
    refer = refer.reshape(NSEG // frames_here, frames_here, height, -1)
    refer = jnp.swapaxes(refer, 1, 2).reshape(NSEG // frames_here, height, -1)

    def cut(windows):
        before = jnp.zeros((history_chips,) + windows.shape[1:], windows.dtype)
        windows = jnp.concatenate([before, windows])
        return lax.dynamic_slice_in_dim(windows, lax.axis_index("chunk") * chips, history_chips + chips)

    return cut(mine), cut(other), refer


def body(video_frames, segments, ref_pick, band_taps, *, chunks, slabs):
    frames_here, size, _ = video_frames.shape
    quarter = size // 4
    rows = quarter // (DOWN * CORES)
    columns = quarter * DOWN // slabs
    chunk = slabs * CORES * frames_here
    history = min(chunk * -(-(band_taps.shape[0] - 1) // chunk), segments.shape[0] - chunk)
    left = jnp.asarray(slab_left_table(rows, HALO, ORIENT))
    right = jnp.asarray(make_right_table(columns, HALO, ORIENT))
    order = exchange_order(slabs)

    def exchange(array, k):
        return lax.ppermute(array, "slab", [(chip, chip ^ k) for chip in range(slabs)]) if k else array

    def swap(array):
        return lax.ppermute(array, "core", [(0, 1), (1, 0)])

    windows = reduce_frames(video_frames, order, HALO)
    spread, ref_frames, sources = time_tables(segments, ref_pick, band_taps, TILE, chunk, history)
    pieces = [exchange(window, k) for k, window in zip(order, windows)]
    if chunks > 1:

        def by_chip(windows):
            apart = jnp.moveaxis(windows.reshape(windows.shape[0], slabs, -1), 1, 0)
            return apart[jnp.asarray(np.argsort(order))[lax.axis_index("slab") ^ jnp.arange(slabs)]]

        def side_by_side(windows):
            return jnp.moveaxis(windows, 0, 1).reshape(windows.shape[1], -1)

        mine, other = cut_windows(pieces, HALO, [])
        chips = slabs + history // (CORES * frames_here)
        windows = chunk_windows(by_chip(mine), by_chip(swap(other)), ref_frames, frames_here, chips - slabs, slabs)
        mine, other, refer = [side_by_side(one) for one in windows]
        other = jnp.concatenate([other, refer], axis=1)
        ready = [own_coeffs(mine, left, right, rows, frames_here)]
        places = [(None, 0), (None, 1)]
    else:
        first = slabs // 2
        chips = slabs - first
        mine, other = cut_windows(pieces[:first], HALO, [spread])
        ready = [own_coeffs(one, left, right, rows, frames_here) for one in (mine, swap(other))]
        mine, other = cut_windows(pieces[first:], HALO, ready[:1])
        other = swap(other)
        ready.append(own_coeffs(mine, left, right, rows, frames_here))
        places = [(exchanges, twin) for exchanges in (order[:first], order[first:]) for twin in range(CORES)]
    motion = pixel_motion(sources, spread, ready, other, left, right, places, frames_here, chips, chunk, history)
    motion = lax.all_to_all(motion, ("slab", "core"), split_axis=0, concat_axis=0, tiled=True)
    return join_tiles(motion, quarter)


def solution(mesh):
    chips = mesh.shape["frames"] // CORES
    slabs = min(chips, QUART * DOWN // (2 * HALO))
    chunks = chips // slabs
    names = ("groups", "chunk", "slab", "core")
    cut = jax.sharding.Mesh(mesh.devices.reshape(mesh.shape["groups"], chunks, slabs, CORES), names)
    in_specs = (P(names, None, None), P("groups"), P("groups"), P())
    return jax.shard_map(
        functools.partial(body, chunks=chunks, slabs=slabs),
        mesh=cut, in_specs=in_specs, out_specs=P(names, None, None), check_vma=False,
    )
```

```python
import functools
import math

import jax
import jax.numpy as jnp
import numpy as np
from jax import lax
from jax.experimental import pallas as pl
from jax.experimental.pallas import tpu as pltpu
from jax.sharding import PartitionSpec as P

IMG = 1024
ORIENT = 4
NSEG = 4
QUART = 256


blur_sigma = 2.0
gabor_sigma = 2.0
wave_number = math.pi / 2.0
gabor_gain = 2.0

HALO = 32
TILE = 16
DOWN = 2
SHARE = 2
CORES = 2
MIB = 1024 * 1024


def envelope_of(offset_grid):
    return np.float32(gabor_gain) * np.exp(
        -offset_grid * offset_grid / np.float32(2.0 * gabor_sigma * gabor_sigma)
    )


def waves(orient):
    angles = np.arange(orient, dtype=np.float32) * np.float32(math.pi / orient)
    wave_x = np.float32(wave_number) * np.cos(angles)
    wave_y = np.float32(wave_number) * np.sin(angles)
    return wave_x, wave_y


def slab_left_table(rows, halo, orient):
    offset = (
        np.arange(rows + 2 * halo, dtype=np.float32)[None, :]
        - np.float32(halo)
        - np.arange(rows, dtype=np.float32)[:, None]
    )
    wave_y = waves(orient)[1]
    phase = wave_y[:, None, None] * offset[None]
    envelope = envelope_of(offset)[None]
    table = np.stack([envelope * np.cos(phase), envelope * np.sin(phase)], axis=1)
    return table.reshape(orient * 2 * rows, rows + 2 * halo).astype(jnp.bfloat16)


def make_right_table(columns, halo, orient):
    window = columns + 2 * halo
    offset = (
        np.arange(window, dtype=np.float32)[:, None] - np.float32(halo) - np.arange(columns, dtype=np.float32)[None, :]
    )
    wave_x = waves(orient)[0]
    phase_x = wave_x[:, None, None] * offset[None]
    envelope = envelope_of(offset)[None]
    real_part = envelope * np.cos(phase_x)
    imag_part = envelope * np.sin(phase_x)
    table = np.zeros((orient // SHARE, SHARE, 2, window, 2, SHARE, columns), np.float32)
    for o in range(orient):
        group, i = divmod(o, SHARE)
        table[group, i, 0, :, 0, i] = real_part[o]
        table[group, i, 0, :, 1, i] = imag_part[o]
        table[group, i, 1, :, 0, i] = -imag_part[o]
        table[group, i, 1, :, 1, i] = real_part[o]
    return table.reshape(orient // SHARE, SHARE * 2 * window, 2 * SHARE * columns).astype(jnp.bfloat16)


def down_sums(full_size, quarter):
    position = np.arange(quarter, dtype=np.float32)[:, None]
    columns = np.arange(full_size, dtype=np.float32)[None, :]
    offset_grid = columns - np.float32(4.0) * position - np.float32(1.5)
    weight = np.exp(-offset_grid * offset_grid / np.float32(2.0 * blur_sigma * blur_sigma))
    return np.sum(weight, axis=1)


def down_block(position, column, shape, axis, sums):
    positions = position + lax.broadcasted_iota(jnp.int32, shape, 1 - axis)
    columns = column + lax.broadcasted_iota(jnp.int32, shape, axis)
    offset_grid = columns.astype(jnp.float32) - 4.0 * positions.astype(jnp.float32) - 1.5
    weight = jnp.exp(-offset_grid * offset_grid / (2.0 * blur_sigma * blur_sigma))
    inner = float(sums[len(sums) // 2])
    line = position + lax.broadcasted_iota(jnp.int32, tuple(1 if i == axis else n for i, n in enumerate(shape)), 1 - axis)
    scale = jnp.full(line.shape, 1.0 / inner, jnp.float32)
    for q in range(position, min(position + shape[1 - axis], len(sums))):
        if abs(float(sums[q]) - inner) > 1e-7 * inner:
            scale = jnp.where(line == q, 1.0 / float(sums[q]), scale)
    return (weight * scale).astype(jnp.bfloat16)


def build_down(table_ref, axis):
    size, quarter = table_ref.shape[axis], table_ref.shape[1 - axis]
    sums = down_sums(size, quarter)
    cut = np.abs(sums - sums[quarter // 2]) > 1e-7 * sums[quarter // 2]
    blocks = {}
    table_ref[...] = jnp.zeros_like(table_ref)
    tall, wide = (128, 32)[axis], min(128, table_ref.shape[1])
    for row in range(0, table_ref.shape[0], tall):
        for lane in range(0, table_ref.shape[1], wide):
            position, column = (row, lane) if axis else (lane, row)
            positions, columns = (tall, wide) if axis else (wide, tall)
            if 4 * (position + positions - 1) + 30 >= column and 4 * position - 27 <= column + columns - 1:
                kind = (column - 4 * position, position if cut[position : position + positions].any() else None)
                if kind not in blocks:
                    blocks[kind] = down_block(position, column, (tall, wide), axis, sums)
                table_ref[row : row + tall, lane : lane + wide] = blocks[kind]


def reduce_kernel(frames_ref, *refs, order, halo, block):
    out_refs = refs[: len(order)]
    picture_ref, down_t_ref, down_ref, half_ref, total_ref, strip_ref, sems = refs[len(order) :]
    count, size, _ = picture_ref.shape
    quarter = down_ref.shape[0]
    _, strips, _, lanes = strip_ref.shape
    columns = lanes - 2 * halo
    window = out_refs[0].shape[1]

    copies = []
    for f in range(count):
        for i in range(size // block):
            here = pl.ds(i * block, block)
            copy = pltpu.make_async_copy(frames_ref.at[f, here], picture_ref.at[f, here], sems.at[f, i])
            copy.start()
            copies.append(copy)
    build_down(down_t_ref, 0)

    me = lax.axis_index("slab")
    blocks = size // block
    for f in range(count):
        step = block if f == 0 else size
        for begin in range(0, size, step):
            for i in range(begin // block, (begin + step) // block):
                copies[f * blocks + i].wait()
            half_ref[f, begin : begin + step] = jnp.dot(
                picture_ref[f, begin : begin + step], down_t_ref[...], preferred_element_type=jnp.float32
            ).astype(jnp.bfloat16)
            if f == begin == 0:
                build_down(down_ref, 1)
        total_ref[f] = jnp.dot(down_ref[...], half_ref[f], preferred_element_type=jnp.float32)
        for strip in range(strips):
            begin = strip * columns - halo
            moved = pltpu.roll(total_ref[f], (-begin) % quarter, 1)[:, 0:lanes]
            column = begin + lax.broadcasted_iota(jnp.int32, (quarter, lanes), 1)
            inside = (column >= 0) & (column < quarter)
            strip_ref[f, strip] = jnp.where(inside, moved, 0.0).astype(jnp.bfloat16)
        for k, out_ref in zip(order, out_refs):
            slab = lax.bitwise_xor(me, k)
            begin = pl.multiple_of(lax.rem(slab, DOWN) * (quarter - window), TILE)
            out_ref[f] = strip_ref[f, slab // DOWN, pl.ds(begin, window)]


def reduce_frames(video_frames, order, halo):
    count, size, _ = video_frames.shape
    quarter = size // 4
    strips = len(order) // DOWN
    lanes = quarter // strips + 2 * halo
    block = size // 2
    out = jax.ShapeDtypeStruct((count, quarter // DOWN + halo, lanes), jnp.bfloat16)
    return pl.pallas_call(
        functools.partial(reduce_kernel, order=order, halo=halo, block=block),
        in_specs=[pl.BlockSpec(memory_space=pltpu.HBM)],
        out_specs=[pl.BlockSpec(memory_space=pltpu.VMEM)] * len(order),
        out_shape=[out] * len(order),
        scratch_shapes=[
            pltpu.VMEM((count, size, size), jnp.bfloat16),
            pltpu.VMEM((size, quarter), jnp.bfloat16),
            pltpu.VMEM((quarter, size), jnp.bfloat16),
            pltpu.VMEM((count, size, quarter), jnp.bfloat16),
            pltpu.VMEM((count, quarter, quarter), jnp.float32),
            pltpu.VMEM((count, strips, quarter, lanes), jnp.bfloat16),
            pltpu.SemaphoreType.DMA((count, size // block)),
        ],
        compiler_params=pltpu.CompilerParams(vmem_limit_bytes=52 * MIB),
        cost_estimate=pl.CostEstimate(
            flops=2 * count * size * quarter * (size + quarter),
            bytes_accessed=2 * count * size * size,
            transcendentals=0,
        ),
    )(video_frames)


def exchange_order(slabs):
    far = sorted(range(slabs // 2, slabs), key=lambda k: k % 2)
    near = list(range(2, slabs // 2))
    turns = [k for pair in zip(far, near) for k in pair]
    return [0] + turns + far[len(near) :] + [k for k in (1,) if k < slabs // 2]


def cut_kernel(*refs, many, halo):
    in_refs, (mine_ref, other_ref), padded_ref = refs[:many], refs[-3:-1], refs[-1]
    count, window, lanes = in_refs[0].shape
    height = mine_ref.shape[0]
    rows = height - 2 * halo
    wide = count * lanes
    me, core = lax.axis_index("slab"), lax.axis_index("core")
    edge = jnp.zeros((halo, count * lanes), jnp.bfloat16)
    padded_ref[0:halo] = edge
    padded_ref[halo + window :] = edge
    above = lax.rem(me, DOWN) * halo
    for n, in_ref in enumerate(in_refs):
        for f in range(count):
            padded_ref[halo : halo + window, f * lanes : (f + 1) * lanes] = in_ref[f]
        for out_ref, number in ((mine_ref, core), (other_ref, 1 - core)):
            place = pl.ds(pl.multiple_of(above + number * rows, TILE), height)
            out_ref[:, n * wide : (n + 1) * wide] = padded_ref[place]


def cut_windows(pieces, halo, after):
    count, window, lanes = pieces[0].shape
    height = (window - halo) // CORES + 2 * halo
    out = jax.ShapeDtypeStruct((height, len(pieces) * count * lanes), jnp.bfloat16)
    return pl.pallas_call(
        functools.partial(cut_kernel, many=len(pieces), halo=halo),
        in_specs=[pl.BlockSpec(memory_space=pltpu.VMEM)] * len(pieces) + [pl.BlockSpec(memory_space=pl.ANY)] * len(after),
        out_specs=[pl.BlockSpec(memory_space=pltpu.VMEM)] * 2,
        out_shape=[out, out],
        scratch_shapes=[pltpu.VMEM((window + 2 * halo, count * lanes), jnp.bfloat16)],
        compiler_params=pltpu.CompilerParams(vmem_limit_bytes=16 * MIB),
        cost_estimate=pl.CostEstimate(flops=0, bytes_accessed=8 * out.size, transcendentals=0),
    )(*pieces, *after)


def time_kernel(segments_ref, pick_ref, taps_ref, spread_ref, frame_ref, source_ref, *, history, frames, rows):
    chunk, timed = spread_ref.shape[0] // rows, spread_ref.shape[1] // rows
    nseg = pick_ref.shape[0]
    taps = taps_ref.shape[0]
    wide_out, wide_in = chunk * rows, timed * rows

    def count_one(t, totals):
        here = segments_ref[t]
        below = [total + (here < s).astype(jnp.int32) for s, total in enumerate(totals[0])]
        same = [total + (here == s).astype(jnp.int32) for s, total in enumerate(totals[1])]
        return tuple(below), tuple(same)

    zeros = tuple(jnp.int32(0) for _ in range(nseg))
    starts, counts = lax.fori_loop(0, frames, count_one, (zeros, zeros), unroll=8)
    for s in range(nseg):
        frame_ref[s] = starts[s] + lax.rem(pick_ref[s], counts[s])

    def source_one(slot, carry):
        if chunk == frames:
            source_ref[slot] = frame_ref[segments_ref[slot]]
        else:
            before = lax.axis_index("chunk") * chunk - history
            source_ref[slot] = timed + segments_ref[jnp.maximum(before + slot, 0)]
        return carry

    lax.fori_loop(0, timed, source_one, 0)

    lag = history + lax.broadcasted_iota(jnp.int32, (chunk, timed), 0) - lax.broadcasted_iota(
        jnp.int32, (chunk, timed), 1
    )
    if history:
        first = lax.axis_index("chunk") * chunk - history
        real = first + lax.broadcasted_iota(jnp.int32, (chunk, timed), 1) >= 0
        lag = jnp.where(real, lag, -1)
    matrix = jnp.zeros((chunk, timed), jnp.float32)
    for k in range(taps):
        matrix = jnp.where(lag == k, taps_ref[k], matrix)
    repeat_left = (
        lax.broadcasted_iota(jnp.int32, (wide_out, chunk), 0) // rows
        == lax.broadcasted_iota(jnp.int32, (wide_out, chunk), 1)
    ).astype(jnp.bfloat16)
    repeat_right = (
        lax.broadcasted_iota(jnp.int32, (timed, wide_in), 1) // rows
        == lax.broadcasted_iota(jnp.int32, (timed, wide_in), 0)
    ).astype(jnp.bfloat16)
    tall = jnp.dot(repeat_left, matrix.astype(jnp.bfloat16), preferred_element_type=jnp.float32)
    tall = tall.astype(jnp.bfloat16)
    piece = min(128, wide_out)
    for start in range(0, wide_out, piece):
        part = jnp.dot(tall[start : start + piece], repeat_right, preferred_element_type=jnp.float32)
        same_row = (
            lax.broadcasted_iota(jnp.int32, (piece, wide_in), 0) % rows
            == lax.broadcasted_iota(jnp.int32, (piece, wide_in), 1) % rows
        )
        spread_ref[start : start + piece] = jnp.where(same_row, part, 0.0).astype(jnp.bfloat16)


def time_tables(segments, ref_pick, band_taps, rows, chunk, history):
    frames = segments.shape[0]
    wide_out, wide_in = chunk * rows, (history + chunk) * rows
    smem = pl.BlockSpec(memory_space=pltpu.SMEM)
    return pl.pallas_call(
        functools.partial(time_kernel, history=history, frames=frames, rows=rows),
        in_specs=[smem] * 3,
        out_specs=[pl.BlockSpec(memory_space=pltpu.VMEM), smem, smem],
        out_shape=[
            jax.ShapeDtypeStruct((wide_out, wide_in), jnp.bfloat16),
            jax.ShapeDtypeStruct(ref_pick.shape, jnp.int32),
            jax.ShapeDtypeStruct((history + chunk,), jnp.int32),
        ],
        compiler_params=pltpu.CompilerParams(vmem_limit_bytes=16 * MIB),
        cost_estimate=pl.CostEstimate(
            flops=2 * wide_out * wide_in * chunk, bytes_accessed=2 * wide_out * wide_in, transcendentals=0
        ),
    )(segments, ref_pick, band_taps.astype(jnp.float32))


def filter_frames(window_ref, pair, left_ref, right_ref, stacked_ref, put):
    groups, deep, _ = right_ref.shape
    lanes = deep // (2 * SHARE)
    rows = left_ref.shape[0] // (2 * SHARE * groups)
    bands = rows // TILE
    frames = window_ref.shape[1] // lanes
    many = frames * TILE
    for first in range(0, frames, 8):
        last = min(first + 8, frames)
        stacked = jnp.dot(
            left_ref[...], window_ref[:, first * lanes : last * lanes], preferred_element_type=jnp.float32
        ).astype(jnp.bfloat16)
        for oz in range(2 * SHARE * groups):
            group, place = divmod(oz, 2 * SHARE)
            for band in range(bands):
                begin = oz * rows + band * TILE
                for f in range(first, last):
                    row = band * many + f * TILE
                    stacked_ref[group, row : row + TILE, place * lanes : (place + 1) * lanes] = stacked[
                        begin : begin + TILE, (f - first) * lanes : (f - first + 1) * lanes
                    ]
    block = pair * TILE
    total = bands * many
    step = min(512, total)
    for group in range(groups):
        for start in range(0, total, step):
            stop = min(start + step, total)
            coeff = jnp.dot(
                stacked_ref[group, start:stop], right_ref[group], preferred_element_type=jnp.float32
            ).astype(jnp.bfloat16)
            for place in range(start, stop, block):
                band, row = divmod(place, many)
                put(group, band, row // block, coeff[place - start : place - start + block])


def coeff_kernel(window_ref, left_ref, right_ref, coeff_ref, stacked_ref, *, pair):
    block = pair * TILE

    def put(group, band, i, values):
        coeff_ref[group, band, i * block : (i + 1) * block] = values

    filter_frames(window_ref, pair, left_ref, right_ref, stacked_ref, put)


def own_coeffs(windows, left, right, rows, frames_here):
    groups, deep, wide = right.shape
    vmem = pl.BlockSpec(memory_space=pltpu.VMEM)
    many = windows.shape[1] // (deep // (2 * SHARE)) * TILE
    out = jax.ShapeDtypeStruct((groups, rows // TILE, many, wide), jnp.bfloat16)
    return pl.pallas_call(
        functools.partial(coeff_kernel, pair=frames_here),
        in_specs=[vmem] * 3,
        out_specs=vmem,
        out_shape=out,
        scratch_shapes=[pltpu.VMEM((groups, rows // TILE * many, deep), jnp.bfloat16)],
        compiler_params=pltpu.CompilerParams(vmem_limit_bytes=8 * out.size + 16 * MIB),
        cost_estimate=pl.CostEstimate(
            flops=4 * out.size * deep, bytes_accessed=2 * (windows.size + out.size), transcendentals=0
        ),
    )(windows, left, right)


def pixel_kernel(
    sources_ref, spread_ref, other_ref, left_ref, right_ref, *refs, places, pair, chips, history
):
    ready_refs, (out_ref, stacked_ref, coeff_ref, phase_ref, filtered_ref, source_ref, sem) = refs[:-7], refs[-7:]
    sources = pltpu.make_async_copy(sources_ref, source_ref, sem)
    sources.start()
    groups, bands, _, wide = coeff_ref.shape
    half = wide // 2
    block = pair * TILE
    chunk = out_ref.shape[0] * pair
    timed = history + chunk
    core = lax.axis_index("core")

    def place_of(exchanges, twin, n):
        chip = n if exchanges is None else lax.bitwise_xor(lax.axis_index("slab"), exchanges[n])
        return pl.ds(pl.multiple_of((chip * CORES + lax.rem(core + twin, CORES)) * block, block), block)

    for ready_ref, (exchanges, twin) in zip(ready_refs, places):
        for n in range(ready_ref.shape[2] // block):
            for group in range(groups):
                for band in range(bands):
                    coeff_ref[group, band, place_of(exchanges, twin, n)] = ready_ref[group, band, n * block : (n + 1) * block]

    def put(group, band, i, values):
        if i < chips:
            place = place_of(*places[-1], i)
        else:
            place = slice(timed * TILE + (i - chips) * block, timed * TILE + (i - chips + 1) * block)
        coeff_ref[group, band, place] = values

    filter_frames(other_ref, pair, left_ref, right_ref, stacked_ref, put)

    sources.wait()

    def phase_one(slot, carry):
        place = pl.ds(pl.multiple_of(slot * TILE, TILE), TILE)
        source = source_ref[slot]
        refer = pl.ds(pl.multiple_of(source * TILE, TILE), TILE)
        for group in range(groups):
            for band in range(bands):
                coeff_real = coeff_ref[group, band, place, 0:half].astype(jnp.float32)
                coeff_imag = coeff_ref[group, band, place, half:wide].astype(jnp.float32)
                ref_real = coeff_ref[group, band, refer, 0:half].astype(jnp.float32)
                ref_imag = coeff_ref[group, band, refer, half:wide].astype(jnp.float32)
                prod_real = coeff_real * ref_real + coeff_imag * ref_imag
                prod_imag = coeff_imag * ref_real - coeff_real * ref_imag
                square = prod_real * prod_real + prod_imag * prod_imag + 1.0
                phase = (prod_imag * lax.rsqrt(square)).astype(jnp.bfloat16)
                lane = (band * groups + group) * half
                phase_ref[place, lane : lane + half] = phase
        return carry

    lax.fori_loop(0, timed, phase_one, 0, unroll=2)

    piece = min(64, chunk * TILE)
    columns = half // SHARE
    left_half = lax.broadcasted_iota(jnp.int32, (TILE, half), 1) < columns
    step = min(256, chunk * TILE)
    for start in range(0, chunk * TILE, step):
        stop = start + step
        filtered_ref[start:stop] = jnp.dot(
            spread_ref[start:stop, : history * TILE + stop],
            phase_ref[: history * TILE + stop],
            preferred_element_type=jnp.float32,
        ).astype(jnp.bfloat16)
    for band in range(bands):
        for start in range(0, chunk * TILE, piece):
            here = slice(history * TILE + start, history * TILE + start + piece)
            lane = band * groups * half
            filtered = filtered_ref[start : start + piece, lane : lane + groups * half].astype(jnp.float32)
            above = jnp.zeros((piece, half), jnp.float32)
            below = jnp.zeros((piece, half), jnp.float32)
            for group in range(groups):
                coeff_real = coeff_ref[group, band, here, 0:half].astype(jnp.float32)
                coeff_imag = coeff_ref[group, band, here, half:wide].astype(jnp.float32)
                amplitude = coeff_real * coeff_real + coeff_imag * coeff_imag
                above = above + amplitude * filtered[:, group * half : (group + 1) * half]
                below = below + amplitude
            for i in range(piece // block):
                sums = []
                for value in (above, below):
                    one, two = value[i * block : i * block + TILE], value[i * block + TILE : (i + 1) * block]
                    sums.append(jnp.where(left_half, one, two) + pltpu.roll(jnp.where(left_half, two, one), columns, 1))
                both = (sums[0] / (sums[1] + 1.0)).astype(out_ref.dtype)
                out_ref[start // block + i, band * TILE : (band + 1) * TILE] = both


def pixel_motion(sources, spread, ready, other, left, right, places, pair, chips, chunk, history):
    groups, bands, _, wide = ready[0].shape
    deep = right.shape[1]
    timed = history + chunk
    fresh = other.shape[1] // (deep // (2 * SHARE))
    slots = timed + fresh - chips * pair
    vmem = pl.BlockSpec(memory_space=pltpu.VMEM)
    return pl.pallas_call(
        functools.partial(pixel_kernel, places=places, pair=pair, chips=chips, history=history),
        in_specs=[pl.BlockSpec(memory_space=pl.ANY)] + [vmem] * (4 + len(ready)),
        out_specs=vmem,
        out_shape=jax.ShapeDtypeStruct((chunk // pair, bands * TILE, wide // 2), jnp.bfloat16),
        scratch_shapes=[
            pltpu.VMEM((groups, bands * fresh * TILE, deep), jnp.bfloat16),
            pltpu.VMEM((groups, bands, slots * TILE, wide), jnp.bfloat16),
            pltpu.VMEM((timed * TILE, bands * groups * wide // 2), jnp.bfloat16),
            pltpu.VMEM((chunk * TILE, bands * groups * wide // 2), jnp.bfloat16),
            pltpu.SMEM((timed,), jnp.int32),
            pltpu.SemaphoreType.DMA,
        ],
        compiler_params=pltpu.CompilerParams(vmem_limit_bytes=8 * groups * bands * slots * TILE * wide + 16 * MIB),
        cost_estimate=pl.CostEstimate(
            flops=2 * groups * bands * TILE * wide * (fresh * deep + chunk * timed * TILE // 2),
            bytes_accessed=2 * (other.size + sum(one.size for one in ready) + right.size),
            transcendentals=groups * bands * TILE * timed * wide // 2,
        ),
    )(sources, spread, other, left, right, *ready)


def join_kernel(tiles_ref, out_ref, frames_ref, sems):
    count, quarter, _ = out_ref.shape
    devices, rows, lanes = tiles_ref.shape
    columns = lanes // count
    strips = quarter // columns
    left = lax.broadcasted_iota(jnp.int32, (rows, lanes), 1) < columns
    copies = []
    for i in range(devices // strips):
        down = slice(i * rows, (i + 1) * rows)
        for strip in range(0, strips, 2):
            one = tiles_ref[strip * devices // strips + i].astype(jnp.float32)
            two = tiles_ref[(strip + 1) * devices // strips + i].astype(jnp.float32)
            here = slice(strip * columns, (strip + 2) * columns)
            frames_ref[0, down, here] = jnp.where(left, one, pltpu.roll(two, columns, 1))
            frames_ref[1, down, here] = jnp.where(left, pltpu.roll(one, columns, 1), two)
        for f in range(count):
            copies.append(pltpu.make_async_copy(frames_ref.at[f, down], out_ref.at[f, down], sems.at[f, i]))
            copies[-1].start()
    for copy in copies:
        copy.wait()


def join_tiles(tiles, quarter):
    strips = quarter * 2 // tiles.shape[2]
    out = jax.ShapeDtypeStruct((2, quarter, quarter), jnp.float32)
    return pl.pallas_call(
        join_kernel,
        in_specs=[pl.BlockSpec(memory_space=pltpu.VMEM)],
        out_specs=pl.BlockSpec(memory_space=pltpu.HBM),
        out_shape=out,
        scratch_shapes=[
            pltpu.VMEM(out.shape, jnp.float32),
            pltpu.SemaphoreType.DMA((2, tiles.shape[0] // strips)),
        ],
        compiler_params=pltpu.CompilerParams(vmem_limit_bytes=16 * MIB),
        cost_estimate=pl.CostEstimate(flops=tiles.size, bytes_accessed=6 * tiles.size, transcendentals=0),
    )(tiles)


def chunk_windows(mine, other, ref_frames, frames_here, history_chips, chips):
    mine = lax.all_gather(mine, "chunk", axis=0, tiled=True)
    other = lax.all_gather(other, "chunk", axis=0, tiled=True)
    height = mine.shape[1]
    core = lax.axis_index("core")
    device, f = ref_frames // frames_here, ref_frames % frames_here
    own = (device % CORES == core)[:, None, None]

    def pick(windows):
        return windows.reshape(windows.shape[0], height, frames_here, -1)[device // CORES, :, f]

    refer = jnp.where(own, pick(mine), pick(other))
    refer = refer.reshape(NSEG // frames_here, frames_here, height, -1)
    refer = jnp.swapaxes(refer, 1, 2).reshape(NSEG // frames_here, height, -1)

    def cut(windows):
        before = jnp.zeros((history_chips,) + windows.shape[1:], windows.dtype)
        windows = jnp.concatenate([before, windows])
        return lax.dynamic_slice_in_dim(windows, lax.axis_index("chunk") * chips, history_chips + chips)

    return cut(mine), cut(other), refer


def body(video_frames, segments, ref_pick, band_taps, *, chunks, slabs):
    frames_here, size, _ = video_frames.shape
    quarter = size // 4
    rows = quarter // (DOWN * CORES)
    columns = quarter * DOWN // slabs
    chunk = slabs * CORES * frames_here
    history = min(chunk * -(-(band_taps.shape[0] - 1) // chunk), segments.shape[0] - chunk)
    left = jnp.asarray(slab_left_table(rows, HALO, ORIENT))
    right = jnp.asarray(make_right_table(columns, HALO, ORIENT))
    order = exchange_order(slabs)

    def exchange(array, k):
        return lax.ppermute(array, "slab", [(chip, chip ^ k) for chip in range(slabs)]) if k else array

    def swap(array):
        return lax.ppermute(array, "core", [(0, 1), (1, 0)])

    windows = reduce_frames(video_frames, order, HALO)
    spread, ref_frames, sources = time_tables(segments, ref_pick, band_taps, TILE, chunk, history)
    pieces = [exchange(window, k) for k, window in zip(order, windows)]
    if chunks > 1:

        def by_chip(windows):
            apart = jnp.moveaxis(windows.reshape(windows.shape[0], slabs, -1), 1, 0)
            return apart[jnp.asarray(np.argsort(order))[lax.axis_index("slab") ^ jnp.arange(slabs)]]

        def side_by_side(windows):
            return jnp.moveaxis(windows, 0, 1).reshape(windows.shape[1], -1)

        mine, other = cut_windows(pieces, HALO, [])
        chips = slabs + history // (CORES * frames_here)
        windows = chunk_windows(by_chip(mine), by_chip(swap(other)), ref_frames, frames_here, chips - slabs, slabs)
        mine, other, refer = [side_by_side(one) for one in windows]
        other = jnp.concatenate([other, refer], axis=1)
        ready = [own_coeffs(mine, left, right, rows, frames_here)]
        places = [(None, 0), (None, 1)]
    else:
        first = slabs // 2
        chips = slabs - first
        mine, other = cut_windows(pieces[:first], HALO, [spread])
        ready = [own_coeffs(one, left, right, rows, frames_here) for one in (mine, swap(other))]
        mine, other = cut_windows(pieces[first:], HALO, ready[:1])
        other = swap(other)
        ready.append(own_coeffs(mine, left, right, rows, frames_here))
        places = [(exchanges, twin) for exchanges in (order[:first], order[first:]) for twin in range(CORES)]
    motion = pixel_motion(sources, spread, ready, other, left, right, places, frames_here, chips, chunk, history)
    motion = lax.all_to_all(motion, ("slab", "core"), split_axis=0, concat_axis=0, tiled=True)
    return join_tiles(motion, quarter)


def solution(mesh):
    chips = mesh.shape["frames"] // CORES
    slabs = min(chips, QUART * DOWN // (2 * HALO))
    chunks = chips // slabs
    names = ("groups", "chunk", "slab", "core")
    cut = jax.sharding.Mesh(mesh.devices.reshape(mesh.shape["groups"], chunks, slabs, CORES), names)
    in_specs = (P(names, None, None), P("groups"), P("groups"), P())
    return jax.shard_map(
        functools.partial(body, chunks=chunks, slabs=slabs),
        mesh=cut, in_specs=in_specs, out_specs=P(names, None, None), check_vma=False,
    )
```
